32 devices in a mesh: dp: 4 (over z), context: 2 (over x), tensor: 4 (over y, core).
Axes of the slice: x: 2, y: 2, z: 4, core: 2. Of those that a mesh axis runs over, the one named last changes fastest.
Arguments:
- stream: bfloat16 [8, 1024, 1536], P('dp', 'context'), may hold values from -6 to 6
- seg_ids: int32 [8, 1024], P('dp', 'context'), may hold values from 0 to 3, as said below
- input_weight: bfloat16 [2, 1536, 2, 3072], P(None, ('dp', 'context'), None, 'tensor'), may hold values from -0.15625 to 0.15625
- step_size_weight: bfloat16 [2, 1536, 48], P(None, ('dp', 'context'), 'tensor'), may hold values from -0.15625 to 0.15625
- coefficient_weight: bfloat16 [2, 1536, 256], P(None, ('dp', 'context', 'tensor')), may hold values from -0.15625 to 0.15625
- pre_gain: bfloat16 [2, 1536], P(None, ('dp', 'context', 'tensor')), may hold values from 0.5 to 1.5
- conv_bc: bfloat16 [2, 4, 256], P(None, None, ('dp', 'context', 'tensor')), may hold values from -2 to 2
- bias_bc: bfloat16 [2, 256], P(None, ('dp', 'context', 'tensor')), may hold values from -2 to 2
- output_weight: bfloat16 [2, 3072, 1536], P(None, 'tensor', ('dp', 'context')), may hold values from -0.109375 to 0.109375
- conv_x: float32 [2, 4, 3072], P(None, None, 'tensor'), may hold values from -2 to 2
- bias_x: float32 [2, 3072], P(None, 'tensor'), may hold values from -2 to 2
- dt_bias: float32 [2, 48], P(None, 'tensor'), may hold values from -1 to 1
- a_log: float32 [2, 48], P(None, 'tensor'), may hold values from -12 to -2, as said below
- skip: float32 [2, 48], P(None, 'tensor'), may hold values from 0.5 to 1.5
- gate_gain: float32 [2, 3072], P(None, 'tensor'), may hold values from 0.5 to 1.5
- cotangent: bfloat16 [8, 1024, 1536], P('dp', 'context'), may hold values from -6 to 6
Outputs:
- layer_out: bfloat16 [8, 1024, 1536], P('dp', 'context')
- grad_stream: bfloat16 [8, 1024, 1536], P('dp', 'context')
- grad_w_in: float32 [2, 1536, 2, 3072], P(None, ('dp', 'context'), None, 'tensor')
- grad_w_dt: float32 [2, 1536, 48], P(None, ('dp', 'context'), 'tensor')
- grad_w_bc: float32 [2, 1536, 256], P(None, ('dp', 'context', 'tensor'))
- grad_pre_gain: float32 [2, 1536], P(None, ('dp', 'context', 'tensor'))
- grad_conv_bc: float32 [2, 4, 256], P(None, None, ('dp', 'context', 'tensor'))
- grad_bias_bc: float32 [2, 256], P(None, ('dp', 'context', 'tensor'))
- grad_w_out: float32 [2, 3072, 1536], P(None, 'tensor', ('dp', 'context'))
- grad_conv_x: float32 [2, 4, 3072], P(None, None, 'tensor')
- grad_bias_x: float32 [2, 3072], P(None, 'tensor')
- grad_dt_bias: float32 [2, 48], P(None, 'tensor')
- grad_a_log: float32 [2, 48], P(None, 'tensor')
- grad_skip: float32 [2, 48], P(None, 'tensor')
- grad_gate_gain: float32 [2, 3072], P(None, 'tensor')
The draws below stay inside these ranges and needn't reach their ends.
Inputs may be any that keep to these rules, and one draw needn't show every extreme that they name: `seg_ids`: document numbers start at 0 in every sequence and never fall along it; of each 2 sequences on one index of dp, one drawn from the seed is a single document, the others hold four documents each. `a_log`: Per-head rates, some slow over a whole sequence, some fast.
All inputs are finite; a program needn't handle non-finite values.
Results may differ from the reference program's by a relative error of at most 0.015.
The reference program's roundings to bfloat16 on the way count: a program that leaves them out, or rounds other values in their place, can miss the bound.
Values may be sent and summed in bfloat16 or wider, within the bound.
No kernel may reach another device: no remote copies, remote signals or barrier semaphores. Data moves between devices by JAX's collectives and lax.ppermute only.
A program may use at most 640 MiB of HBM per device.

```python
import math
import jax
import jax.numpy as jnp
from jax import lax

D = 1536
E = 3072
H = 48
N = 128
SPAN = 256
LAYERS = 2
SEQ_DEV = 2
SEQ_LEN = 1024
SEQS = 8


def draw_seg_ids(key, part):
    key = jax.random.fold_in(key, 11)
    quarter = SEQ_LEN // 4
    offsets = jax.random.randint(jax.random.fold_in(key, 1), (SEQS, 3), quarter // 4, 3 * quarter // 4 + 1)
    doc_starts = (jnp.arange(1, 4, dtype=jnp.int32) * quarter)[None, :] + offsets - quarter // 2
    places = jnp.arange(SEQ_LEN, dtype=jnp.int32)
    numbers = jnp.sum((doc_starts[:, None, :] <= places[None, :, None]).astype(jnp.int32), axis=2)
    chosen = jax.random.randint(jax.random.fold_in(key, 2), (SEQS // SEQ_DEV,), 0, SEQ_DEV)
    single = jnp.arange(SEQS) % SEQ_DEV == jnp.repeat(chosen, SEQ_DEV)
    return jnp.where(single[:, None], 0, numbers).astype(jnp.int32)


def draw_a_log(key, part):
    key = jax.random.fold_in(key, 23)
    return jax.random.uniform(jax.random.fold_in(key, 1), (LAYERS, H), minval=math.log(0.3 / SEQ_LEN), maxval=math.log(0.08)).astype(jnp.float32)


def level_of(own_key, shape, split, smallest, high):
    gain = 1.0
    for dim, blocks in split:
        draws = jax.random.uniform(jax.random.fold_in(jax.random.fold_in(own_key, 6), dim), (blocks,), jnp.float32, smallest / len(split), high / len(split))
        gain = gain * jnp.repeat(jnp.exp(draws), shape[dim] // blocks).reshape((-1,) + (1,) * (len(shape) - 1 - dim))
    return gain


def scatter_about(key, dims, deviation, bound, split=(), kind=jnp.bfloat16):
    values = deviation * jax.random.normal(key, dims, jnp.float32)
    if split:
        values = values * level_of(key, dims, split, -0.22, 0.18)
    return jnp.clip(values, -bound, bound).astype(kind)


def setup_inputs(seed: int = 0) -> dict:
    key_of = jax.random.split(jax.random.key(seed), 17)
    stream = scatter_about(key_of[0], (SEQS, SEQ_LEN, D), 1.0, 6.0, ((0, 4), (1, 2)))
    seg_ids = draw_seg_ids(jax.random.fold_in(key_of[16], 71), 0)
    input_weight = scatter_about(key_of[2], (LAYERS, D, 2, E), D ** -0.5, 0.15625, ((1, 8), (3, 4)))
    step_size_weight = scatter_about(key_of[3], (LAYERS, D, H), D ** -0.5, 0.15625, ((1, 8), (2, 4)))
    coefficient_weight = scatter_about(key_of[4], (LAYERS, D, 2 * N), D ** -0.5, 0.15625, ((1, 32),))
    pre_gain = jnp.clip(1.0 + 0.1 * jax.random.normal(key_of[5], (LAYERS, D), jnp.float32), 0.5, 1.5).astype(jnp.bfloat16)
    conv_bc = scatter_about(key_of[6], (LAYERS, 4, 2 * N), 0.5, 2.0, ((2, 32),))
    bias_bc = scatter_about(key_of[7], (LAYERS, 2 * N), 0.5, 2.0, ((1, 32),))
    output_weight = scatter_about(key_of[8], (LAYERS, E, D), E ** -0.5, 0.109375, ((1, 4), (2, 8)))
    conv_x = scatter_about(key_of[9], (LAYERS, 4, E), 0.5, 2.0, ((2, 4),), jnp.float32)
    bias_x = scatter_about(key_of[10], (LAYERS, E), 0.5, 2.0, ((1, 4),), jnp.float32)
    dt_bias = jnp.clip(jax.random.uniform(key_of[11], (LAYERS, H), jnp.float32, -1.0, 1.0) * level_of(key_of[11], (LAYERS, H), ((1, 4),), -0.4, 0.0), -1.0, 1.0)
    a_log = draw_a_log(jax.random.fold_in(key_of[16], 71), 0)
    skip = jnp.clip(0.5 + 1.0 * jax.random.uniform(key_of[13], (LAYERS, H), jnp.float32) ** level_of(key_of[13], (LAYERS, H), ((1, 4),), -0.2, 0.2), 0.5, 1.5)
    gate_gain = jnp.clip(1.0 + 0.1 * jax.random.normal(key_of[14], (LAYERS, E), jnp.float32), 0.5, 1.5)
    cotangent = scatter_about(key_of[15], (SEQS, SEQ_LEN, D), 1.0, 6.0, ((0, 4), (1, 2)))
    return {"stream": stream, "seg_ids": seg_ids, "input_weight": input_weight, "step_size_weight": step_size_weight, "coefficient_weight": coefficient_weight, "pre_gain": pre_gain, "conv_bc": conv_bc, "bias_bc": bias_bc, "output_weight": output_weight, "conv_x": conv_x, "bias_x": bias_x, "dt_bias": dt_bias, "a_log": a_log, "skip": skip, "gate_gain": gate_gain, "cotangent": cotangent}


PRECISION_HIGH = lax.Precision.HIGHEST
eps = 1e-05

@jax.custom_vjp
def lower_precision(v):
    return lax.optimization_barrier(v.astype(jnp.bfloat16)).astype(jnp.float32)

@jax.custom_vjp
def lower_precision_back(v):
    return v

def low_keep(v):
    return (lower_precision(v), None)

def low_pass(kept, grad):
    return (grad,)

def back_keep(v):
    return (v, None)

def back_low(kept, grad):
    return (lower_precision(grad),)
lower_precision.defvjp(low_keep, low_pass)
lower_precision_back.defvjp(back_keep, back_low)

def prenorm(values, gain_vec):
    return values * lax.rsqrt(lax.optimization_barrier(jnp.mean(values * values, axis=-1, keepdims=True)) + eps) * gain_vec

def conv_local(values, weights, bias_vec, same_doc):
    steps_out = values.shape[1] - 3
    summed = bias_vec + weights[0] * values[:, 0:steps_out] * same_doc[:, :, 0:1]
    for offset in range(1, 4):
        summed = summed + weights[offset] * values[:, offset:offset + steps_out] * same_doc[:, :, offset:offset + 1]
    return jax.nn.silu(summed)

def span_step(state_in, block_in):
    scaled_in, b_proj, c_proj, log_decay, seg_block, before = block_in
    cumulate = jnp.cumsum(log_decay, axis=1)
    positions = seg_block.shape[1]
    causal = jnp.arange(positions)[:, None] >= jnp.arange(positions)[None, :]
    within_doc = (seg_block[:, :, None] == seg_block[:, None, :]) & causal[None]
    spread = cumulate[:, :, None, :] - cumulate[:, None, :, :]
    decays = jnp.where(within_doc[..., None], jnp.exp(jnp.where(within_doc[..., None], spread, 0.0)), 0.0)
    scores = jnp.einsum('stn,sun->stu', c_proj, b_proj, precision=PRECISION_HIGH)
    within = jnp.einsum('stuh,suhp->sthp', decays * scores[..., None], scaled_in, precision=PRECISION_HIGH)
    survive = (seg_block == before[:, None]).astype(jnp.float32)
    growth = jnp.exp(cumulate) * survive[..., None]
    carried = jnp.einsum('stn,shpn->sthp', c_proj, state_in, precision=PRECISION_HIGH) * growth[..., None]
    fresh_state = jnp.einsum('suh,suhp,sun->shpn', decays[:, -1], scaled_in, b_proj, precision=PRECISION_HIGH)
    return (state_in * growth[:, -1][:, :, None, None] + fresh_state, within + carried)

def run_spans(stepper, scaled_in, b_proj, c_proj, log_decay, seg_block, before):
    batch_count, length = seg_block.shape
    span_count = length // SPAN
    prior_ids = jnp.concatenate([before[:, None], seg_block[:, :-1]], axis=1)[:, ::SPAN]

    def split_blocks(values):
        return jnp.moveaxis(values.reshape((batch_count, span_count, SPAN) + values.shape[2:]), 1, 0)
    zero_state = jnp.zeros((batch_count, scaled_in.shape[2], scaled_in.shape[3], b_proj.shape[2]), jnp.float32)
    end_state, outputs = lax.scan(stepper, zero_state, (split_blocks(scaled_in), split_blocks(b_proj), split_blocks(c_proj), split_blocks(log_decay), split_blocks(seg_block), jnp.moveaxis(prior_ids, 1, 0)))
    return (jnp.moveaxis(outputs, 0, 1).reshape(scaled_in.shape), end_state)

def prepare(stepper, x_conv, bc_conv, step_size_raw, bias_dt, log_rate, seg_block, before):
    batch_count, length, channels = x_conv.shape
    head_count = bias_dt.shape[0]
    state_width = bc_conv.shape[2] // 2
    step_size = jax.nn.softplus(step_size_raw + bias_dt)
    log_decay = -jnp.exp(log_rate) * step_size
    x_heads = x_conv.reshape(batch_count, length, head_count, channels // head_count)
    b_proj = bc_conv[:, :, :state_width]
    c_proj = bc_conv[:, :, state_width:]
    y_zero, end_state = run_spans(stepper, x_heads * step_size[..., None], b_proj, c_proj, log_decay, seg_block, before)
    survive = (seg_block == before[:, None]).astype(jnp.float32)
    growth = jnp.exp(jnp.cumsum(log_decay, axis=1)) * survive[..., None]
    return (y_zero, end_state, growth[:, -1], growth, c_proj, x_heads)

def mamba_layer(current, seg_block, input_weight, step_size_weight, coefficient_weight, pre_gain, conv_bc, bias_bc, output_weight, conv_x, bias_x, dt_bias, a_log, skip, gate_gain):
    batch_count = current.shape[0]
    normalized_input = lower_precision(prenorm(current, pre_gain))
    projected_rows = jnp.einsum('qwi,ivu->qwvu', normalized_input, input_weight, precision=PRECISION_HIGH)
    gate_pre = lower_precision_back(projected_rows[:, :, 0])
    inner_vals = lower_precision(lower_precision_back(projected_rows[:, :, 1]))
    bc_unmixed_rows = lower_precision(jnp.einsum('zhw,wg->zhg', normalized_input, coefficient_weight, precision=PRECISION_HIGH))
    step_size_raw = lower_precision_back(jnp.einsum('opf,fy->opy', normalized_input, step_size_weight, precision=PRECISION_HIGH))
    border = jnp.full((batch_count, 3), -1, jnp.int32)
    ext_ids = jnp.concatenate([border, seg_block], axis=1)
    same_doc = jnp.stack([ext_ids[:, offset:offset + SEQ_LEN] == seg_block for offset in range(4)], axis=2).astype(jnp.float32)
    x_conv = conv_local(jnp.pad(inner_vals, ((0, 0), (3, 0), (0, 0))), conv_x, bias_x, same_doc)
    bc_conv = conv_local(jnp.pad(bc_unmixed_rows, ((0, 0), (3, 0), (0, 0))), conv_bc, bias_bc, same_doc)
    before = jnp.full((batch_count,), -1, jnp.int32)
    y_zero, end_state, total_decay, growth, c_proj, x_heads = prepare(jax.checkpoint(span_step), x_conv, bc_conv, step_size_raw, dt_bias, a_log, seg_block, before)
    y_full = y_zero + skip[:, None] * x_heads
    gated_vals = y_full.reshape(gate_pre.shape) * jax.nn.silu(gate_pre)
    scaled_rows = lower_precision(gated_vals * lax.rsqrt(lax.optimization_barrier(jnp.mean(gated_vals * gated_vals, axis=-1, keepdims=True)) + eps) * gate_gain)
    branch_output = lower_precision_back(jnp.einsum('zra,af->zrf', scaled_rows, output_weight, precision=PRECISION_HIGH))
    return current + branch_output

def reference(stream, seg_ids, input_weight, step_size_weight, coefficient_weight, pre_gain, conv_bc, bias_bc, output_weight, conv_x, bias_x, dt_bias, a_log, skip, gate_gain, cotangent):
    param_list = [input_weight, step_size_weight, coefficient_weight, pre_gain, conv_bc, bias_bc, output_weight, conv_x, bias_x, dt_bias, a_log, skip, gate_gain]
    param_list = [element.astype(jnp.float32) for element in param_list]

    def forward(start_stream, *params):

        def one_sequence(carried_in, sequence_item):
            current = sequence_item[0][None]
            ids_one = sequence_item[1][None]
            for layer_pos in range(LAYERS):
                current = mamba_layer(current, ids_one, *[element[layer_pos] for element in params])
            return (carried_in, current[0])
        unused_carry, result = lax.scan(jax.checkpoint(one_sequence), jnp.zeros((), jnp.float32), (start_stream, seg_ids))
        return result
    result, pull_back = jax.vjp(forward, stream.astype(jnp.float32), *param_list)
    grads = pull_back(cotangent.astype(jnp.float32))
    return (result.astype(jnp.bfloat16), grads[0].astype(jnp.bfloat16), grads[1], grads[2], grads[3], grads[4], grads[5], grads[6], grads[7], grads[8], grads[9], grads[10], grads[11], grads[12], grads[13])
```

```python
import functools

import jax
import jax.numpy as jnp
from jax import lax
from jax.experimental import pallas as pl
from jax.experimental.pallas import tpu as pltpu
from jax.sharding import PartitionSpec as P

CHUNK = 128
LANES = 128
eps = 1e-05
F32 = jnp.float32
BF16 = jnp.bfloat16
HIGH = lax.Precision.HIGHEST
NN = (((1,), (0,)), ((), ()))
NT = (((1,), (1,)), ((), ()))
TN = (((0,), (0,)), ((), ()))
NO_LINK = -1e30
FWD_WIDE = True
BWD_WIDE = True
FSTATE = F32


def mm(a, b, dims=NN):
    return lax.dot_general(a, b, dims, preferred_element_type=F32)


def params(mib=48):
    return pltpu.CompilerParams(
        dimension_semantics=("arbitrary",), vmem_limit_bytes=mib * 1024 * 1024
    )


def flipped(value, axis, bit):
    count = lax.axis_size(axis)
    return lax.ppermute(value, axis, [(i, i ^ (1 << bit)) for i in range(count)])


def bits(axis):
    return (lax.axis_size(axis) - 1).bit_length()


def shifted(value, axis, steps):
    count = lax.axis_size(axis)
    leading, last = (max(0, -steps), min(count, count - steps))
    return lax.ppermute(value, axis, [(source, source + steps) for source in range(leading, last)])


def ring(value, axis):
    count = lax.axis_size(axis)
    return lax.ppermute(value, axis, [(i, (i - 1) % count) for i in range(count)])


def summed_over(value, axes):
    for axis in axes:
        for bit in range(bits(axis)):
            value = value + flipped(value, axis, bit)
    return value


def gather_small(value, axes):
    value = value[None]
    for axis in axes:
        index = lax.axis_index(axis)
        for bit in range(bits(axis)):
            other = flipped(value, axis, bit)
            upper = (index >> bit) & 1
            value = jnp.concatenate(
                [jnp.where(upper == 0, value, other), jnp.where(upper == 0, other, value)], axis=0
            )
    return value


def scatter_rows(value):
    index = lax.axis_index("tensor")
    kind = value.dtype
    for bit in range(bits("tensor")):
        mine = (index >> bit) & 1
        half = value.shape[0] // 2
        sent = lax.dynamic_slice_in_dim(value, (1 - mine) * half, half, 0).astype(kind)
        kept = lax.dynamic_slice_in_dim(value, mine * half, half, 0).astype(F32)
        value = kept + flipped(sent, "tensor", bit).astype(F32)
    return value


def own_rows(value):
    index = lax.axis_index("tensor")
    for bit in range(bits("tensor")):
        half = value.shape[0] // 2
        value = lax.dynamic_slice_in_dim(value, ((index >> bit) & 1) * half, half, 0)
    return value


def gather_rows(value):
    index = lax.axis_index("tensor")
    for bit in reversed(range(bits("tensor"))):
        upper = (index >> bit) & 1
        other = flipped(value, "tensor", bit)
        value = jnp.concatenate(
            [jnp.where(upper == 0, value, other), jnp.where(upper == 0, other, value)], axis=0
        )
    return value


def ring_pieces(piece):
    own = [piece]
    for _ in range(lax.axis_size("dp") - 1):
        own.append(ring(own[-1], "dp"))
    table = []
    for arrived in own:
        row = [arrived]
        for _ in range(lax.axis_size("context") - 1):
            row.append(ring(row[-1], "context"))
        table.append(row)
    return table


def place_kernel(count, widths, index_ref, *refs):
    pieces, outs = refs[:count], refs[count:]
    for i in range(count):
        at = 0
        for out, width in zip(outs, widths):
            out[index_ref[i]] = pieces[i][:, at : at + width]
            at += width


def placed(table, widths):
    dp, context = lax.axis_size("dp"), lax.axis_size("context")
    z, x = lax.axis_index("dp"), lax.axis_index("context")
    pieces, index = [], []
    for k, row in enumerate(table):
        for j, piece in enumerate(row):
            pieces.append(piece)
            index.append(((z + k) % dp) * context + (x + j) % context)
    count, rows = len(pieces), pieces[0].shape[0]
    outs = pl.pallas_call(
        functools.partial(place_kernel, count, widths),
        grid_spec=pltpu.PrefetchScalarGridSpec(
            num_scalar_prefetch=1,
            grid=(1,),
            in_specs=[pl.BlockSpec(piece.shape, lambda i, index: (0, 0)) for piece in pieces],
            out_specs=[
                pl.BlockSpec((count, rows, width), lambda i, index: (0, 0, 0)) for width in widths
            ],
        ),
        out_shape=[jax.ShapeDtypeStruct((count, rows, width), BF16) for width in widths],
        compiler_params=params(),
        cost_estimate=pl.CostEstimate(
            flops=0, transcendentals=0, bytes_accessed=4 * count * rows * sum(widths)
        ),
    )(jnp.stack(index).astype(jnp.int32), *pieces)
    return [out.reshape(count * rows, -1) for out in outs]


def ring_scatter(blocks):
    dp, context = lax.axis_size("dp"), lax.axis_size("context")
    z, x = lax.axis_index("dp"), lax.axis_index("context")

    def block(k, j):
        at = ((z + k) % dp) * context + (x + j) % context
        return lax.dynamic_index_in_dim(blocks, at, 0, keepdims=False)

    def over_context(k):
        total = None
        for j in range(1, context):
            part = block(k, j)
            if total is not None:
                part = (total + part.astype(F32)).astype(BF16)
            total = ring(part, "context").astype(F32)
        part = block(k, 0).astype(F32)
        return part if total is None else part + total

    total = None
    for k in list(range(1, dp)) + [0]:
        part = over_context(k)
        if total is not None:
            part = part + total
        if k:
            total = ring(part.astype(BF16), "dp").astype(F32)
        else:
            return part


def silu_parts(value):
    sig = jax.nn.sigmoid(value)
    return value * sig, sig


def softplus(value):
    return jnp.maximum(value, 0.0) + jnp.log1p(jnp.exp(-jnp.abs(value)))


def split_dot(value, table):
    high = value.astype(BF16)
    low = (value - high.astype(F32)).astype(BF16)
    return mm(high, table) + mm(low, table)


def wide_mm(a, b, dims=NN):
    a_high, b_high = a.astype(BF16), b.astype(BF16)
    a_low = (a - a_high.astype(F32)).astype(BF16)
    b_low = (b - b_high.astype(F32)).astype(BF16)
    return mm(a_high, b_high, dims) + (mm(a_low, b_high, dims) + mm(a_high, b_low, dims))


def fmm(a, b, dims=NN):
    return wide_mm(a, b, dims) if FWD_WIDE else mm(a.astype(BF16), b.astype(BF16), dims)


def bmm(a, b, dims=NN):
    return wide_mm(a, b, dims) if BWD_WIDE else mm(a.astype(BF16), b.astype(BF16), dims)


def iota(axis):
    return lax.broadcasted_iota(jnp.int32, (CHUNK, CHUNK), axis)


def rounded(value):
    return value.astype(BF16).astype(F32)


def head_halves(tile, lower):
    zero = jnp.zeros_like(tile)
    return jnp.concatenate([jnp.where(lower, tile, zero), jnp.where(lower, zero, tile)], axis=0)


def column_of(rows):
    pad = jnp.zeros((CHUNK - rows.shape[0], CHUNK), F32)
    return jnp.concatenate([rows, pad], axis=0).T


def scan_forward_kernel(
    heads, width, p_ref, rim_ref, aux_ref, segr_ref, cw_ref, hp_ref, skip_ref, exp_ref,
    z_ref, y_ref, st_ref, end_ref, gr_ref, vbuf, state, offset,
):
    chunk = pl.program_id(0)

    @pl.when(chunk == 0)
    def _():
        vbuf[0:8] = rim_ref[...].astype(F32)
        state[...] = jnp.zeros_like(state)
        offset[...] = jnp.zeros_like(offset)

    @pl.when(chunk > 0)
    def _():
        vbuf[0:8] = vbuf[CHUNK : CHUNK + 8]

    vbuf[8:, :width] = rounded(p_ref[:, :width])
    vbuf[8:, width:] = rounded(p_ref[:, width + LANES :])
    z = cw_ref[4:5] + cw_ref[3:4] * vbuf[8:]
    for k in range(3):
        z = z + cw_ref[k : k + 1] * vbuf[5 + k : 5 + k + CHUNK] * aux_ref[:, k : k + 1]
    z_ref[...] = z
    act = z * jax.nn.sigmoid(z)
    x = act[:, :width]
    b_val, c_val = act[:, width : width + LANES], act[:, width + LANES :]
    lane = iota(1)
    step = jnp.where(
        lane < heads, softplus(p_ref[:, width : width + LANES] + hp_ref[0:1]), 0.0
    )
    decay = hp_ref[1:2] * step
    cum = lax.dot_general(
        (iota(0) >= iota(1)).astype(F32), decay, NN, precision=HIGH, preferred_element_type=F32
    )
    cum_t = cum.T
    seg_col = aux_ref[:, 5:6]
    link = jnp.where((seg_col == segr_ref[0]) & (iota(0) >= iota(1)), 0.0, NO_LINK)
    scores = fmm(c_val, b_val, NT)
    growth = jnp.exp(cum) * aux_ref[:, 3:4]
    last = cum[CHUNK - 1 : CHUNK]
    weight = jnp.exp(last - cum) * (seg_col == seg_col[CHUNK - 1 : CHUNK]).astype(F32)
    wide = split_dot(jnp.concatenate([step, growth, weight], axis=0), exp_ref[...])
    step_e, growth_e, weight_e = wide[:CHUNK], wide[CHUNK : 2 * CHUNK], wide[2 * CHUNK :]
    xd = x * step_e
    lower = lane < LANES // 2
    pieces = []
    for pair in range(heads // 2):
        mats = []
        for head in (2 * pair, 2 * pair + 1):
            spread = cum[:, head : head + 1] - cum_t[head : head + 1, :]
            mats.append(jnp.exp(spread + link) * scores)
        tile = xd[:, pair * LANES : (pair + 1) * LANES]
        pieces.append(fmm(jnp.concatenate(mats, axis=1), head_halves(tile, lower)))
    held = state[...]
    st_ref[0] = held
    carried = fmm(c_val, held) * growth_e
    y_ref[...] = jnp.concatenate(pieces, axis=1) + carried + skip_ref[...] * x
    new = held * growth_e[CHUNK - 1 : CHUNK] + fmm(b_val, xd * weight_e, TN)
    state[...] = new
    end_ref[...] = new
    gr_ref[...] = jnp.exp(offset[...] + cum) * aux_ref[:, 4:5]
    offset[...] = offset[...] + last


def row_spec(width, at=None, rows=CHUNK):
    if at is None:
        return pl.BlockSpec((rows, width), lambda i: (i, 0))
    return pl.BlockSpec((rows, width), lambda i: (i, at))


def whole(shape):
    return pl.BlockSpec(shape, lambda i: (0,) * len(shape))


def scan_forward(proj, rim, aux, seg_rows, consts):
    length, total = proj.shape
    heads, width = consts["heads"], consts["width"]
    chunks, conv = length // CHUNK, total - LANES
    return pl.pallas_call(
        functools.partial(scan_forward_kernel, heads, width),
        grid=(chunks,),
        in_specs=[
            row_spec(total),
            whole((8, conv)),
            row_spec(8),
            pl.BlockSpec((1, 1, CHUNK), lambda i: (i, 0, 0)),
            whole((8, conv)),
            whole((8, LANES)),
            whole((1, width)),
            whole((LANES, width)),
        ],
        out_specs=[
            row_spec(conv),
            row_spec(width),
            pl.BlockSpec((1, LANES, width), lambda i: (i, 0, 0)),
            whole((LANES, width)),
            row_spec(LANES),
        ],
        out_shape=[
            jax.ShapeDtypeStruct((length, conv), F32),
            jax.ShapeDtypeStruct((length, width), F32),
            jax.ShapeDtypeStruct((chunks, LANES, width), F32),
            jax.ShapeDtypeStruct((LANES, width), F32),
            jax.ShapeDtypeStruct((length, LANES), F32),
        ],
        scratch_shapes=[
            pltpu.VMEM((CHUNK + 8, conv), F32),
            pltpu.VMEM((LANES, width), F32),
            pltpu.VMEM((1, LANES), F32),
        ],
        compiler_params=params(),
        cost_estimate=pl.CostEstimate(
            flops=chunks * 400_000_000, transcendentals=0, bytes_accessed=12_000_000
        ),
    )(proj, rim, aux, seg_rows, consts["cw"], consts["hp"], consts["skip"], consts["exp"])


def mix_forward_kernel(y0_ref, zc_ref, gr_ref, sin_ref, gate_ref, exp_ref, y_ref, sq_ref):
    c_val = zc_ref[...] * jax.nn.sigmoid(zc_ref[...])
    carried = fmm(c_val, sin_ref[...].astype(F32))
    y = y0_ref[...] + carried * split_dot(gr_ref[...], exp_ref[...])
    y_ref[...] = y
    gate = gate_ref[...]
    gated = y * (gate * jax.nn.sigmoid(gate))
    square = jnp.sum(gated * gated, axis=1, keepdims=True)
    sq_ref[...] = jnp.broadcast_to(square, (CHUNK, CHUNK)).T[:8]


def mix_forward(y0, z, growth, carried, gate, consts):
    length, width = y0.shape
    last = z.shape[1] // LANES - 1
    return pl.pallas_call(
        mix_forward_kernel,
        grid=(length // CHUNK,),
        in_specs=[
            row_spec(width),
            row_spec(LANES, last),
            row_spec(LANES),
            whole((LANES, width)),
            row_spec(width),
            whole((LANES, width)),
        ],
        out_specs=[row_spec(width), pl.BlockSpec((8, CHUNK), lambda i: (0, i))],
        out_shape=[
            jax.ShapeDtypeStruct((length, width), F32),
            jax.ShapeDtypeStruct((8, length), F32),
        ],
        compiler_params=params(),
        cost_estimate=pl.CostEstimate(
            flops=1_000_000_000, transcendentals=0, bytes_accessed=6_000_000
        ),
    )(y0, z, growth, carried, gate, consts["exp"])


def project_out_kernel(channels, y_ref, gate_ref, sq_ref, gain_ref, w_ref, out_ref):
    scale = lax.rsqrt(column_of(sq_ref[...])[:, 0:1] / channels + eps)
    gate = gate_ref[...]
    gated = y_ref[...] * (gate * jax.nn.sigmoid(gate))
    scaled = (gated * scale * gain_ref[...]).astype(BF16)
    out_ref[...] = mm(scaled, w_ref[...], NT).astype(out_ref.dtype)


def project_out(y, gate, squares, channels, kind, consts):
    length, width = y.shape
    model = consts["out"].shape[0]
    return pl.pallas_call(
        functools.partial(project_out_kernel, float(channels)),
        grid=(length // CHUNK,),
        in_specs=[
            row_spec(width),
            row_spec(width),
            pl.BlockSpec((8, CHUNK), lambda i: (0, i)),
            whole((1, width)),
            whole((model, width)),
        ],
        out_specs=row_spec(model),
        out_shape=jax.ShapeDtypeStruct((length, model), kind),
        compiler_params=params(),
        cost_estimate=pl.CostEstimate(
            flops=4 * length * width * model, transcendentals=0, bytes_accessed=9_000_000
        ),
    )(y, gate, squares, consts["gain"], consts["out"])


def grad_scaled_kernel(g_ref, w_ref, y_ref, gate_ref, gain_ref, gs_ref, dot_ref):
    grad = mm(g_ref[...], w_ref[...])
    gs_ref[...] = grad
    gate = gate_ref[...]
    gated = y_ref[...] * (gate * jax.nn.sigmoid(gate))
    product = jnp.sum(grad * gain_ref[...] * gated, axis=1, keepdims=True)
    dot_ref[...] = jnp.broadcast_to(product, (CHUNK, CHUNK)).T[:8]


def grad_scaled(grad_low, y, gate, consts):
    length, width = y.shape
    model = consts["out"].shape[0]
    return pl.pallas_call(
        grad_scaled_kernel,
        grid=(length // CHUNK,),
        in_specs=[
            row_spec(model),
            whole((model, width)),
            row_spec(width),
            row_spec(width),
            whole((1, width)),
        ],
        out_specs=[row_spec(width), pl.BlockSpec((8, CHUNK), lambda i: (0, i))],
        out_shape=[
            jax.ShapeDtypeStruct((length, width), F32),
            jax.ShapeDtypeStruct((8, length), F32),
        ],
        compiler_params=params(),
        cost_estimate=pl.CostEstimate(
            flops=4 * length * width * model, transcendentals=0, bytes_accessed=9_000_000
        ),
    )(grad_low, consts["out"], y, gate, consts["gain"])


def mix_backward_kernel(
    channels, gs_ref, y_ref, gate_ref, zx_ref, zc_ref, gr_ref, sq_ref, dot_ref, gain_ref, exp_ref,
    scaled_ref, dgate_ref, dy_ref, acc_ref, dsin_ref,
):
    @pl.when(pl.program_id(0) == 0)
    def _():
        acc_ref[...] = jnp.zeros_like(acc_ref)
        dsin_ref[...] = jnp.zeros_like(dsin_ref)

    stats = column_of(jnp.concatenate([sq_ref[...], dot_ref[...]], axis=0))
    scale = lax.rsqrt(stats[:, 0:1] / channels + eps)
    pull = scale * scale * scale * stats[:, 8:9] / channels
    grad, y, gate = gs_ref[...], y_ref[...], gate_ref[...]
    silu, sig = silu_parts(gate)
    gated = y * silu
    unit = gated * scale
    scaled_ref[...] = (unit * gain_ref[...]).astype(BF16)
    dgated = grad * gain_ref[...] * scale - gated * pull
    dy = dgated * silu
    dy_ref[...] = dy
    dgate_ref[...] = (dgated * y * (sig * (1.0 + gate * (1.0 - sig)))).astype(BF16)
    x = zx_ref[...] * jax.nn.sigmoid(zx_ref[...])
    acc_ref[0:1] += jnp.sum(grad * unit, axis=0, keepdims=True)
    acc_ref[1:2] += jnp.sum(dy * x, axis=0, keepdims=True)
    c_low = (zc_ref[...] * jax.nn.sigmoid(zc_ref[...])).astype(BF16)
    dsin_ref[...] += mm(c_low, (dy * split_dot(gr_ref[...], exp_ref[...])).astype(BF16), TN)


def mix_backward(grad, y, gate, z, growth, squares, dots, channels, consts):
    length, width = y.shape
    last = z.shape[1] // LANES - 1
    stat = pl.BlockSpec((8, CHUNK), lambda i: (0, i))
    return pl.pallas_call(
        functools.partial(mix_backward_kernel, float(channels)),
        grid=(length // CHUNK,),
        in_specs=[
            row_spec(width),
            row_spec(width),
            row_spec(width),
            row_spec(width),
            row_spec(LANES, last),
            row_spec(LANES),
            stat,
            stat,
            whole((1, width)),
            whole((LANES, width)),
        ],
        out_specs=[
            row_spec(width),
            row_spec(width),
            row_spec(width),
            whole((8, width)),
            whole((LANES, width)),
        ],
        out_shape=[
            jax.ShapeDtypeStruct((length, width), BF16),
            jax.ShapeDtypeStruct((length, width), BF16),
            jax.ShapeDtypeStruct((length, width), F32),
            jax.ShapeDtypeStruct((8, width), F32),
            jax.ShapeDtypeStruct((LANES, width), F32),
        ],
        compiler_params=params(),
        cost_estimate=pl.CostEstimate(
            flops=1_000_000_000, transcendentals=0, bytes_accessed=12_000_000
        ),
    )(grad, y, gate, z, z, growth, squares, dots, consts["gain"], consts["exp"])


def scan_backward_kernel(
    heads, width, chunks, dy_ref, z_ref, p_ref, before_ref, rim_ref, aux_ref, segr_ref, cw_ref,
    hp_ref, skip_ref, exp_ref, red_ref, st_ref, sin_ref, grprev_ref, dend_ref,
    dproj_ref, wacc_ref, hacc_ref, tail_ref, drim_ref, vbuf, zbuf, dstate,
):
    step_at = pl.program_id(0)
    chunk = chunks - 1 - step_at

    @pl.when(step_at == 0)
    def _():
        dstate[...] = dend_ref[...].astype(F32)
        zbuf[...] = jnp.zeros_like(zbuf)
        wacc_ref[...] = jnp.zeros_like(wacc_ref)
        hacc_ref[...] = jnp.zeros_like(hacc_ref)

    @pl.when(chunk == 0)
    def _():
        vbuf[0:8] = rim_ref[...].astype(F32)

    @pl.when(chunk > 0)
    def _():
        vbuf[0:8, :width] = rounded(before_ref[:, :width])
        vbuf[0:8, width:] = rounded(before_ref[:, width + LANES :])

    vbuf[8:, :width] = rounded(p_ref[:, :width])
    vbuf[8:, width:] = rounded(p_ref[:, width + LANES :])

    z = z_ref[...]
    act, sig = silu_parts(z)
    slope = sig * (1.0 + z * (1.0 - sig))
    x = act[:, :width]
    b_val, c_val = act[:, width : width + LANES], act[:, width + LANES :]
    lane = iota(1)
    pre = p_ref[:, width : width + LANES] + hp_ref[0:1]
    step = jnp.where(lane < heads, softplus(pre), 0.0)
    decay = hp_ref[1:2] * step
    cum = lax.dot_general(
        (iota(0) >= iota(1)).astype(F32), decay, NN, precision=HIGH, preferred_element_type=F32
    )
    cum_t = cum.T
    seg_col = aux_ref[:, 5:6]
    link = jnp.where((seg_col == segr_ref[0]) & (iota(0) <= iota(1)), 0.0, NO_LINK)
    growth = jnp.exp(cum) * aux_ref[:, 3:4]
    last = cum[CHUNK - 1 : CHUNK]
    weight = jnp.exp(last - cum) * (seg_col == seg_col[CHUNK - 1 : CHUNK]).astype(F32)
    reach = jnp.where(chunk == 0, 1.0, grprev_ref[7:8])
    wide = split_dot(
        jnp.concatenate([step, growth, weight, jnp.broadcast_to(reach, (8, LANES))], axis=0),
        exp_ref[...],
    )
    step_e, growth_e = wide[:CHUNK], wide[CHUNK : 2 * CHUNK]
    weight_e, reach_e = wide[2 * CHUNK : 3 * CHUNK], wide[3 * CHUNK : 3 * CHUNK + 1]
    held = st_ref[0] + sin_ref[...].astype(F32) * reach_e
    after = dstate[...]
    xd = x * step_e
    dy = dy_ref[...]
    scores = bmm(b_val, c_val, NT)
    carried = bmm(c_val, held) * growth_e
    fed = bmm(b_val, after) * weight_e
    dy_grown = dy * growth_e
    lower = lane < LANES // 2
    dscores = jnp.zeros((CHUNK, CHUNK), F32)
    into = jnp.zeros((CHUNK, CHUNK), F32)
    rows, pieces = [], []
    for pair in range(heads // 2):
        at = slice(pair * LANES, (pair + 1) * LANES)
        products = bmm(head_halves(xd[:, at], lower), dy[:, at], NT)
        mats = []
        for side, head in enumerate((2 * pair, 2 * pair + 1)):
            spread = cum_t[head : head + 1, :] - cum[:, head : head + 1]
            reachable = jnp.exp(spread + link)
            product = products[side * CHUNK : (side + 1) * CHUNK]
            mat = reachable * scores
            dscores = dscores + reachable * product
            energy = mat * product
            rows.append(jnp.sum(energy, axis=0, keepdims=True))
            into = jnp.where(lane == head, jnp.sum(energy, axis=1, keepdims=True), into)
            mats.append(mat)
        pieces.append(bmm(jnp.concatenate(mats, axis=1), head_halves(dy[:, at], lower)))
    dxd = jnp.concatenate(pieces, axis=1) + fed
    kept = jnp.sum(after * held, axis=0, keepdims=True) * growth_e[CHUNK - 1 : CHUNK]
    sums = split_dot(
        jnp.concatenate(
            [dy * carried, xd * fed, dxd * x, jnp.broadcast_to(kept, (8, width))], axis=0
        ),
        red_ref[...],
    )
    out_of, fed_sum = sums[:CHUNK], sums[CHUNK : 2 * CHUNK]
    dstep, kept_sum = sums[2 * CHUNK : 3 * CHUNK], sums[3 * CHUNK : 3 * CHUNK + 1]
    rows = column_of(jnp.concatenate(rows, axis=0))
    dcum = rows - into + out_of - fed_sum
    end_term = kept_sum + jnp.sum(fed_sum, axis=0, keepdims=True)
    ddecay = (
        lax.dot_general(
            (iota(0) <= iota(1)).astype(F32), dcum, NN, precision=HIGH, preferred_element_type=F32
        )
        + end_term
    )
    ddecay = jnp.where(lane < heads, ddecay, 0.0)
    dpre = jnp.where(lane < heads, (dstep + hp_ref[1:2] * ddecay) * jax.nn.sigmoid(pre), 0.0)
    hacc_ref[0:1] += jnp.sum(dpre, axis=0, keepdims=True)
    hacc_ref[1:2] += jnp.sum(ddecay * decay, axis=0, keepdims=True)
    dx = dxd * step_e + skip_ref[...] * dy
    db = wide_mm(dscores, c_val) + wide_mm(xd * weight_e, after, NT)
    dc = wide_mm(dscores, b_val, TN) + wide_mm(dy_grown, held, NT)
    dstate[...] = after * growth_e[CHUNK - 1 : CHUNK] + bmm(c_val, dy_grown, TN)

    dz = jnp.concatenate([dx, db, dc], axis=1) * slope
    wacc_ref[3:4] += jnp.sum(dz * vbuf[8:], axis=0, keepdims=True)
    wacc_ref[4:5] += jnp.sum(dz, axis=0, keepdims=True)
    dv = cw_ref[3:4] * dz
    for k in range(3):
        masked = dz * aux_ref[:, k : k + 1]
        wacc_ref[k : k + 1] += jnp.sum(
            masked * vbuf[5 + k : 5 + k + CHUNK], axis=0, keepdims=True
        )
        zbuf[k, 8 : 8 + CHUNK] = masked
        dv = dv + cw_ref[k : k + 1] * zbuf[k, 11 - k : 11 - k + CHUNK]
    dproj_ref[:, :width] = dv[:, :width].astype(BF16)
    dproj_ref[:, width : width + LANES] = dpre.astype(BF16)
    dproj_ref[:, width + LANES :] = dv[:, width:].astype(BF16)

    @pl.when(step_at == 0)
    def _():
        tail_ref[...] = dv[CHUNK - 8 :]

    @pl.when(chunk == 0)
    def _():
        drim = cw_ref[0:1] * zbuf[0, 3:11]
        for k in (1, 2):
            drim = drim + cw_ref[k : k + 1] * zbuf[k, 3 - k : 11 - k]
        drim_ref[...] = drim

    for k in range(3):
        zbuf[k, 8 + CHUNK :] = zbuf[k, 8:16]


def scan_backward(dy, z, proj, rim, aux, seg_rows, states, carried, growth, dend, consts):
    length, total = proj.shape
    heads, width = consts["heads"], consts["width"]
    chunks, conv = length // CHUNK, total - LANES
    eights = CHUNK // 8

    def back(columns):
        return pl.BlockSpec((CHUNK, columns), lambda i: (chunks - 1 - i, 0))

    def previous(columns):
        return pl.BlockSpec(
            (8, columns), lambda i: (jnp.maximum((chunks - 1 - i) * eights - 1, 0), 0)
        )

    return pl.pallas_call(
        functools.partial(scan_backward_kernel, heads, width, chunks),
        grid=(chunks,),
        in_specs=[
            back(width),
            back(conv),
            back(total),
            previous(total),
            whole((8, conv)),
            back(8),
            pl.BlockSpec((1, 1, CHUNK), lambda i: (chunks - 1 - i, 0, 0)),
            whole((8, conv)),
            whole((8, LANES)),
            whole((1, width)),
            whole((LANES, width)),
            whole((width, LANES)),
            pl.BlockSpec((1, LANES, width), lambda i: (chunks - 1 - i, 0, 0)),
            whole((LANES, width)),
            previous(LANES),
            whole((LANES, width)),
        ],
        out_specs=[
            back(total),
            whole((8, conv)),
            whole((8, LANES)),
            whole((8, conv)),
            whole((8, conv)),
        ],
        out_shape=[
            jax.ShapeDtypeStruct((length, total), BF16),
            jax.ShapeDtypeStruct((8, conv), F32),
            jax.ShapeDtypeStruct((8, LANES), F32),
            jax.ShapeDtypeStruct((8, conv), F32),
            jax.ShapeDtypeStruct((8, conv), F32),
        ],
        scratch_shapes=[
            pltpu.VMEM((CHUNK + 8, conv), F32),
            pltpu.VMEM((3, CHUNK + 16, conv), F32),
            pltpu.VMEM((LANES, width), F32),
        ],
        compiler_params=params(),
        cost_estimate=pl.CostEstimate(
            flops=chunks * 1_500_000_000, transcendentals=0, bytes_accessed=16_000_000
        ),
    )(
        dy, z, proj, proj, rim, aux, seg_rows, consts["cw"], consts["hp"], consts["skip"],
        consts["exp"], consts["red"], states, carried, growth, dend,
    )


def local(
    stream,
    seg_ids,
    input_weight,
    step_size_weight,
    coefficient_weight,
    pre_gain,
    conv_bc,
    bias_bc,
    output_weight,
    conv_x,
    bias_x,
    dt_bias,
    a_log,
    skip,
    gate_gain,
    cotangent,
):
    layers, rows_in, _, width = input_weight.shape
    sequences, length, model = stream.shape
    heads = dt_bias.shape[1]
    depth = width // heads
    shared = coefficient_weight.shape[2]
    dp, context, tensor = (lax.axis_size(a) for a in ("dp", "context", "tensor"))
    channels = width * tensor
    rows_bc = rows_in // tensor
    bc_part = shared // tensor
    conv = width + shared
    layer_range, seq_range = range(layers), range(sequences)

    def first_piece(layer):
        tile = jnp.concatenate(
            [
                step_size_weight[layer],
                jnp.zeros((rows_in, LANES - heads - bc_part), BF16),
                coefficient_weight[layer].reshape(rows_in, bc_part),
            ],
            axis=1,
        )
        return jnp.concatenate([input_weight[layer, :, 1], tile], axis=1)

    def second_piece(layer):
        return jnp.concatenate([input_weight[layer, :, 0], output_weight[layer].T], axis=1)

    def full_bc(first):
        part = first[:, width + LANES - bc_part :].reshape(dp * context, rows_bc, shared)
        every = gather_small(part, ("tensor",))
        return jnp.moveaxis(every, 0, 1).reshape(model, shared)

    small = jnp.concatenate(
        [pre_gain, conv_bc.reshape(layers, -1), bias_bc], axis=1
    )
    small = gather_small(small, ("tensor", "context", "dp"))
    own_gain, own_conv = pre_gain.shape[1], conv_bc.shape[2]
    gains = jnp.moveaxis(small[:, :, :own_gain], 0, 1).reshape(layers, model).astype(F32)
    conv_all = small[:, :, own_gain : own_gain + 4 * own_conv].reshape(-1, layers, 4, own_conv)
    conv_all = jnp.moveaxis(conv_all, 0, 2).reshape(layers, 4, shared).astype(F32)
    bias_all = jnp.moveaxis(small[:, :, own_gain + 4 * own_conv :], 0, 1)
    bias_all = bias_all.reshape(layers, shared).astype(F32)

    edge_ids = shifted(seg_ids[:, -3:], "context", 1)
    ext_ids = jnp.concatenate([edge_ids, seg_ids], axis=1)
    prior = ext_ids[:, 2 : 2 + length].reshape(sequences, length // CHUNK, CHUNK)[:, :, 0]
    prior = jnp.repeat(prior, CHUNK, axis=1)
    aux_all = jnp.stack(
        [ext_ids[:, k : k + length] == seg_ids for k in range(3)]
        + [seg_ids == prior, seg_ids == edge_ids[:, 2:3], seg_ids, seg_ids, seg_ids],
        axis=2,
    ).astype(F32)
    seg_rows = seg_ids.astype(F32).reshape(sequences, length // CHUNK, 1, CHUNK)

    spread_table = (jnp.arange(LANES)[:, None] == jnp.arange(width)[None, :] // depth).astype(BF16)

    first, second = [None] * layers, [None] * layers
    gate_on = None
    for layer in layer_range:
        piece = first_piece(layer)
        if gate_on is not None:
            piece, gate_on = lax.optimization_barrier((piece, gate_on))
        table = ring_pieces(piece)
        (first[layer],) = placed(table, [width + LANES])
        gate_on = table[-1][0]
        piece, gate_on = lax.optimization_barrier((second_piece(layer), gate_on))
        table = ring_pieces(piece)
        second[layer] = placed(table, [width, width])
        gate_on = table[-1][0]

    consts = []
    for layer in layer_range:
        cw = jnp.concatenate(
            [
                jnp.concatenate([conv_x[layer], conv_all[layer]], axis=1),
                jnp.concatenate([bias_x[layer], bias_all[layer]])[None],
                jnp.zeros((3, conv), F32),
            ],
            axis=0,
        )
        pad = jnp.zeros((LANES - heads,), F32)
        hp = jnp.stack(
            [
                jnp.concatenate([dt_bias[layer], pad]),
                jnp.concatenate([-jnp.exp(a_log[layer]), pad]),
            ]
            + [jnp.zeros((LANES,), F32)] * 6
        )
        consts.append(
            {
                "heads": heads,
                "width": width,
                "cw": cw,
                "hp": hp,
                "skip": jnp.repeat(skip[layer], depth)[None],
                "gain": gate_gain[layer][None],
                "exp": spread_table,
                "red": spread_table.T,
                "front": jnp.concatenate([first[layer], full_bc(first[layer])], axis=1),
                "gate": second[layer][0],
                "out": second[layer][1],
            }
        )

    def chain(value, total, steps, kind):
        carried = shifted(value.astype(kind), "context", steps)
        for _ in range(context - 2):
            whole_value = value + carried.astype(F32) * total
            carried = shifted(whole_value.astype(kind), "context", steps)
        return carried

    def through(growth):
        return jnp.repeat(growth[length - 1, :heads], depth)[None]

    kept = [[None] * sequences for _ in layer_range]
    streams = [own_rows(stream[s]).astype(F32) for s in seq_range]
    normed = []
    for s in seq_range:
        wide = stream[s].astype(F32)
        scale = lax.rsqrt(jnp.mean(wide * wide, axis=-1, keepdims=True) + eps)
        normed.append((wide * scale * gains[0]).astype(BF16))
    finals = []
    for layer in layer_range:
        const = consts[layer]
        nexts = []
        for s in seq_range:
            proj = mm(normed[s], const["front"])
            gate = mm(normed[s], const["gate"])
            rim = shifted(
                jnp.concatenate(
                    [proj[length - 8 :, :width], proj[length - 8 :, width + LANES :]], axis=1
                ).astype(BF16),
                "context",
                1,
            )
            z, y0, states, end, growth = scan_forward(proj, rim, aux_all[s], seg_rows[s], const)
            carried = chain(end, through(growth), 1, FSTATE)
            y, squares = mix_forward(y0, z, growth, carried, gate, const)
            squares = summed_over(squares, ("tensor",))
            kind = F32 if layer + 1 < layers else BF16
            partial = project_out(y, gate, squares, channels, kind, const)
            current = streams[s] + scatter_rows(partial)
            kept[layer][s] = {
                "normed": normed[s], "proj": proj, "gate": gate, "rim": rim, "z": z, "y": y,
                "states": states, "growth": growth, "carried": carried, "squares": squares,
                "stream": streams[s],
            }
            streams[s] = current
            if layer + 1 < layers:
                scale = lax.rsqrt(jnp.mean(current * current, axis=-1, keepdims=True) + eps)
                nexts.append(gather_rows((current * scale * gains[layer + 1]).astype(BF16)))
            else:
                finals.append(gather_rows(current.astype(BF16)))
        normed = nexts
    layer_out = jnp.stack(finals)

    grad_low = [cotangent[s] for s in seq_range]
    grads = [own_rows(cotangent[s]).astype(F32) for s in seq_range]
    out = [None] * layers
    small_local, small_shared = [], []
    for layer in reversed(layer_range):
        const = consts[layer]
        held = kept[layer]
        nexts, back = [], []
        gain_sum = 0.0
        for s in seq_range:
            k = held[s]
            grad, dots = grad_scaled(grad_low[s], k["y"], k["gate"], const)
            dots = summed_over(dots, ("tensor",))
            scaled, dgate, dy, acc, dsin = mix_backward(
                grad, k["y"], k["gate"], k["z"], k["growth"], k["squares"], dots, channels, const
            )
            dend = chain(dsin, through(k["growth"]), -1, BF16)
            dproj, wacc, hacc, tail, drim = scan_backward(
                dy, k["z"], k["proj"], k["rim"], aux_all[s], seg_rows[s], k["states"],
                k["carried"], k["growth"], dend, const,
            )
            fixed = (tail + shifted(drim, "context", -1)).astype(BF16)
            dproj = lax.dynamic_update_slice(dproj, fixed[:, :width], (length - 8, 0))
            dproj = lax.dynamic_update_slice(dproj, fixed[:, width:], (length - 8, width + LANES))
            partial = mm(dproj, const["front"], NT) + mm(dgate, const["gate"], NT)
            total = scatter_rows(partial.astype(BF16))
            current = k["stream"]
            scale = lax.rsqrt(jnp.mean(current * current, axis=-1, keepdims=True) + eps)
            unit = current * scale
            gain_sum = gain_sum + jnp.sum(total * unit, axis=0)
            pulled = total * gains[layer]
            shift = jnp.mean(pulled * unit, axis=-1, keepdims=True)
            grads[s] = grads[s] + scale * (pulled - unit * shift)
            nexts.append(gather_rows(grads[s].astype(BF16)))
            back.append((scaled, dgate, dproj, acc, wacc, hacc))

        def over_tokens(left, right):
            return sum(mm(a, b, TN) for a, b in zip(left, right))

        normed_all = [k["normed"] for k in held]
        front_grad = over_tokens(normed_all, [b[2] for b in back])
        gate_grad = over_tokens(normed_all, [b[1] for b in back]).astype(BF16)
        out_grad = over_tokens(grad_low, [b[0] for b in back]).astype(BF16)
        second_sum = ring_scatter(
            jnp.concatenate([gate_grad, out_grad], axis=1).reshape(dp * context, rows_in, -1)
        )
        bc_grad = front_grad[:, width + LANES :].reshape(dp * context, tensor, rows_bc * shared)
        bc_grad = scatter_rows_of_tensor(bc_grad)
        bc_grad = bc_grad.reshape(model, bc_part).astype(BF16)
        first_blocks = jnp.concatenate(
            [front_grad[:, : width + LANES - bc_part].astype(BF16), bc_grad], axis=1
        )
        first_sum = ring_scatter(first_blocks.reshape(dp * context, rows_in, -1))
        out[layer] = (
            jnp.stack([second_sum[:, :width], first_sum[:, :width]], axis=1),
            first_sum[:, width : width + heads],
            first_sum[:, width + LANES - bc_part :].reshape(rows_bc, shared),
            second_sum[:, width:].T,
        )
        acc, wacc, hacc = (sum(b[i] for b in back) for i in (3, 4, 5))
        small_local.append(
            jnp.concatenate(
                [
                    wacc[:5, :width].reshape(-1),
                    acc[0],
                    acc[1].reshape(heads, depth).sum(axis=1),
                    hacc[0, :heads],
                    hacc[1, :heads],
                ]
            )
        )
        small_shared.append(jnp.concatenate([wacc[:5, width:].reshape(-1), gain_sum]))
        grad_low = nexts
    grad_stream = jnp.stack(grad_low)

    shared_sum = summed_over(jnp.stack(small_shared[::-1]), ("tensor",))
    local_sum = jnp.stack(small_local[::-1])
    cut = local_sum.shape[1]
    both = summed_over(
        jnp.concatenate([local_sum, shared_sum], axis=1), ("context", "dp")
    )
    local_sum, shared_sum = both[:, :cut], both[:, cut:]
    place = (lax.axis_index("dp") * context + lax.axis_index("context")) * tensor
    place = place + lax.axis_index("tensor")
    taps = shared_sum[:, : 5 * shared].reshape(layers, 5, shared)
    taps = lax.dynamic_slice_in_dim(taps, place * own_conv, own_conv, 2)
    grad_gain = lax.dynamic_slice_in_dim(
        shared_sum[:, 5 * shared :], place * own_gain, own_gain, 1
    )
    taps_x = local_sum[:, : 5 * width].reshape(layers, 5, width)
    heads_at = 6 * width
    return (
        layer_out,
        grad_stream,
        jnp.stack([o[0] for o in out]),
        jnp.stack([o[1] for o in out]),
        jnp.stack([o[2] for o in out]),
        grad_gain,
        taps[:, :4],
        taps[:, 4],
        jnp.stack([o[3] for o in out]),
        taps_x[:, :4],
        taps_x[:, 4],
        local_sum[:, heads_at + heads : heads_at + 2 * heads],
        local_sum[:, heads_at + 2 * heads : heads_at + 3 * heads],
        local_sum[:, heads_at : heads_at + heads],
        local_sum[:, 5 * width : 6 * width],
    )


def scatter_rows_of_tensor(value):
    index = lax.axis_index("tensor")
    blocks, _, n = value.shape
    for bit in range(bits("tensor")):
        mine = (index >> bit) & 1
        value = value.reshape(blocks, -1, 2, n)
        sent = lax.dynamic_index_in_dim(value, 1 - mine, 2, keepdims=False).astype(BF16)
        kept = lax.dynamic_index_in_dim(value, mine, 2, keepdims=False).astype(F32)
        value = kept + flipped(sent, "tensor", bit).astype(F32)
    return value.reshape(blocks, n)


def solution(mesh):
    in_specs = (
        P("dp", "context", None),
        P("dp", "context"),
        P(None, ("dp", "context"), None, "tensor"),
        P(None, ("dp", "context"), "tensor"),
        P(None, ("dp", "context", "tensor"), None),
        P(None, ("dp", "context", "tensor")),
        P(None, None, ("dp", "context", "tensor")),
        P(None, ("dp", "context", "tensor")),
        P(None, "tensor", ("dp", "context")),
        P(None, None, "tensor"),
        P(None, "tensor"),
        P(None, "tensor"),
        P(None, "tensor"),
        P(None, "tensor"),
        P(None, "tensor"),
        P("dp", "context", None),
    )
    out_specs = (
        P("dp", "context", None),
        P("dp", "context", None),
        P(None, ("dp", "context"), None, "tensor"),
        P(None, ("dp", "context"), "tensor"),
        P(None, ("dp", "context", "tensor"), None),
        P(None, ("dp", "context", "tensor")),
        P(None, None, ("dp", "context", "tensor")),
        P(None, ("dp", "context", "tensor")),
        P(None, "tensor", ("dp", "context")),
        P(None, None, "tensor"),
        P(None, "tensor"),
        P(None, "tensor"),
        P(None, "tensor"),
        P(None, "tensor"),
        P(None, "tensor"),
        P("dp", "context", None),
    )
    return jax.shard_map(
        local, mesh=mesh, in_specs=in_specs, out_specs=out_specs[:15], check_vma=False
    )
```

```python
import functools

import jax
import jax.numpy as jnp
from jax import lax
from jax.experimental import pallas as pl
from jax.experimental.pallas import tpu as pltpu
from jax.sharding import PartitionSpec as P

CHUNK = 128
LANES = 128
eps = 1e-05
F32 = jnp.float32
BF16 = jnp.bfloat16
HIGH = lax.Precision.HIGHEST
NN = (((1,), (0,)), ((), ()))
NT = (((1,), (1,)), ((), ()))
TN = (((0,), (0,)), ((), ()))
NO_LINK = -1e30
COST_SCALE = 0.5
FWD_WIDE = True
BWD_WIDE = True


def mm(a, b, dims=NN):
    return lax.dot_general(a, b, dims, preferred_element_type=F32)


def params(mib=48):
    return pltpu.CompilerParams(
        dimension_semantics=("arbitrary",), vmem_limit_bytes=mib * 1024 * 1024
    )


PRECEDING = []


def kernel_call(body, cost=2.0, **spec):
    def call(*inputs):
        tokens = list(PRECEDING)
        options = dict(spec)
        grid_spec = options.pop("grid_spec", None)
        unread = [pl.BlockSpec(memory_space=pl.ANY)] * len(tokens)
        prefetched = 0
        if grid_spec is None:
            options["in_specs"] = list(options["in_specs"]) + unread
        else:
            prefetched = grid_spec.num_scalar_prefetch
            options["grid_spec"] = pltpu.PrefetchScalarGridSpec(
                num_scalar_prefetch=prefetched,
                grid=grid_spec.grid,
                in_specs=list(grid_spec.in_specs) + unread,
                out_specs=grid_spec.out_specs,
                scratch_shapes=grid_spec.scratch_shapes,
            )
        first = len(inputs)

        def without_tokens(*refs):
            body(*refs[:first], *refs[first + len(tokens) :])

        out = pl.pallas_call(
            without_tokens,
            cost_estimate=pl.CostEstimate(
                flops=int(cost * 1.0e9 * COST_SCALE), transcendentals=0, bytes_accessed=1024
            ),
            **options,
        )(*inputs, *tokens)
        PRECEDING[:] = [min(jax.tree.leaves(out), key=lambda one: one.size * one.dtype.itemsize)]
        return out

    return call


def precede(*tokens):
    PRECEDING.extend(token for token in tokens if token is not None)


def flipped(value, axis, bit):
    count = lax.axis_size(axis)
    return lax.ppermute(value, axis, [(i, i ^ (1 << bit)) for i in range(count)])


def bits(axis):
    return (lax.axis_size(axis) - 1).bit_length()


def shifted(value, axis, steps):
    count = lax.axis_size(axis)
    leading, last = (max(0, -steps), min(count, count - steps))
    return lax.ppermute(value, axis, [(source, source + steps) for source in range(leading, last)])


def ring(value, axis):
    count = lax.axis_size(axis)
    return lax.ppermute(value, axis, [(i, (i - 1) % count) for i in range(count)])


def summed_over(value, axes):
    for axis in axes:
        for bit in range(bits(axis)):
            value = value + flipped(value, axis, bit)
    return value


def gather_small(value, axes):
    value = value[None]
    for axis in axes:
        index = lax.axis_index(axis)
        for bit in range(bits(axis)):
            other = flipped(value, axis, bit)
            upper = (index >> bit) & 1
            value = jnp.concatenate(
                [jnp.where(upper == 0, value, other), jnp.where(upper == 0, other, value)], axis=0
            )
    return value


def slots():
    count, places = bits("tensor"), []
    for m in range(lax.axis_size("tensor")):
        places.append(sum(((m >> b) & 1) << (count - 1 - b) for b in range(count)))
    return places


def rows_order(first):
    places = slots()
    if first:
        half = len(places) // 2
        places = places[half:] + places[:half]
    return jnp.array(places, jnp.int32) ^ lax.axis_index("tensor")


def own_rows(value):
    rows = value.shape[0] // lax.axis_size("tensor")
    return lax.dynamic_slice_in_dim(value, lax.axis_index("tensor") * rows, rows, 0)


def gathered(value):
    pieces = [value]
    for bit in reversed(range(bits("tensor"))):
        pieces = pieces + [flipped(piece, "tensor", bit) for piece in pieces]
    return pieces


def relay_kernel(from_ref, to_ref):
    to_ref[...] = from_ref[...]


def relayed(piece, *tokens):
    precede(*tokens)
    return kernel_call(
        relay_kernel,
        grid=(1,),
        in_specs=[fixed_block(piece.shape)],
        out_specs=fixed_block(piece.shape),
        out_shape=jax.ShapeDtypeStruct(piece.shape, piece.dtype),
        compiler_params=params(),
    )(piece)


def ring_pieces(piece):
    table, arrived = [], piece
    for k in range(lax.axis_size("dp")):
        if k:
            source = relayed(arrived, table[k - 2][-1]) if k > 1 else arrived
            arrived = ring(source, "dp")
        row = [arrived]
        for _ in range(lax.axis_size("context") - 1):
            row.append(ring(row[-1], "context"))
        table.append(row)
    return table


def place_kernel(count, widths, tile_at, index_ref, *refs):
    pieces, outs = refs[:count], refs[count:]
    for i in range(count):
        at = 0
        for out, width in zip(outs, widths):
            out[index_ref[i]] = pieces[i][:, at : at + width]
            at += width
    if tile_at is not None:
        first, tiles = outs[0], outs[-1]
        rows = first.shape[1]
        whole_rows = jnp.concatenate(
            [first[i, :, tile_at : tile_at + LANES] for i in range(count)], axis=0
        )
        for at in range(0, count * rows, LANES):
            tiles[:, at : at + LANES] = whole_rows[at : at + LANES].astype(F32).T


def placed(table, widths, tile_at=None):
    dp, context = lax.axis_size("dp"), lax.axis_size("context")
    z, x = lax.axis_index("dp"), lax.axis_index("context")
    pieces, index = [], []
    for k, row in enumerate(table):
        for j, piece in enumerate(row):
            pieces.append(piece)
            index.append(((z + k) % dp) * context + (x + j) % context)
    count, rows = len(pieces), pieces[0].shape[0]
    out_specs = [
        pl.BlockSpec((count, rows, width), lambda i, index: (0, 0, 0)) for width in widths
    ]
    out_shape = [jax.ShapeDtypeStruct((count, rows, width), BF16) for width in widths]
    if tile_at is not None:
        out_specs.append(pl.BlockSpec((LANES, count * rows), lambda i, index: (0, 0)))
        out_shape.append(jax.ShapeDtypeStruct((LANES, count * rows), F32))
    outs = kernel_call(
        functools.partial(place_kernel, count, widths, tile_at),
        cost=3.5,
        grid_spec=pltpu.PrefetchScalarGridSpec(
            num_scalar_prefetch=1,
            grid=(1,),
            in_specs=[pl.BlockSpec(piece.shape, lambda i, index: (0, 0)) for piece in pieces],
            out_specs=out_specs,
        ),
        out_shape=out_shape,
        compiler_params=params(),
    )(jnp.stack(index).astype(jnp.int32), *pieces)
    return [
        out.reshape(count * rows, -1) if i < len(widths) else out for i, out in enumerate(outs)
    ]


def after(value, *tokens):
    tokens = tuple(token for token in tokens if token is not None)
    return lax.optimization_barrier((value, *tokens))[0] if tokens else value


def from_others(value, axis):
    count = lax.axis_size(axis)
    return [value] + [
        lax.ppermute(value, axis, [(i, i ^ step) for i in range(count)])
        for step in range(1, count)
    ]


def scatter_places(value):
    index = lax.axis_index("tensor")
    value = value.reshape(-1, value.shape[0] // lax.axis_size("tensor"), value.shape[1])
    for bit in range(bits("tensor")):
        mine = (index >> bit) & 1
        value = value.reshape(-1, 2, *value.shape[1:])
        sent = lax.dynamic_index_in_dim(value, 1 - mine, 1, keepdims=False)
        kept = lax.dynamic_index_in_dim(value, mine, 1, keepdims=False)
        value = kept + flipped(sent, "tensor", bit)
    return value[0]


def silu_parts(value):
    sig = jax.nn.sigmoid(value)
    return value * sig, sig


def softplus(value):
    return jnp.maximum(value, 0.0) + jnp.log1p(jnp.exp(-jnp.abs(value)))


def split_dot(value, table):
    high = value.astype(BF16)
    low = (value - high.astype(F32)).astype(BF16)
    return mm(high, table) + mm(low, table)


def wide_mm(a, b, dims=NN):
    a_high, b_high = a.astype(BF16), b.astype(BF16)
    a_low = (a - a_high.astype(F32)).astype(BF16)
    b_low = (b - b_high.astype(F32)).astype(BF16)
    return mm(a_high, b_high, dims) + (mm(a_low, b_high, dims) + mm(a_high, b_low, dims))


def fmm(a, b, dims=NN):
    return wide_mm(a, b, dims) if FWD_WIDE else mm(a.astype(BF16), b.astype(BF16), dims)


def bmm(a, b, dims=NN):
    return wide_mm(a, b, dims) if BWD_WIDE else mm(a.astype(BF16), b.astype(BF16), dims)


def iota(axis):
    return lax.broadcasted_iota(jnp.int32, (CHUNK, CHUNK), axis)


def rounded(value):
    return value.astype(BF16).astype(F32)


def head_halves(tile, lower):
    zero = jnp.zeros_like(tile)
    return jnp.concatenate([jnp.where(lower, tile, zero), jnp.where(lower, zero, tile)], axis=0)


def column_of(rows):
    pad = jnp.zeros((CHUNK - rows.shape[0], CHUNK), F32)
    return jnp.concatenate([rows, pad], axis=0).T


def row_norm(wide):
    return lax.rsqrt(jnp.mean(wide * wide, axis=-1, keepdims=True) + eps)


def columns(array, at, width):
    return pl.BlockSpec((array.shape[0], width), lambda i, *_: (0, at))


def fixed_block(shape):
    return pl.BlockSpec(shape, lambda i, *_: (0,) * len(shape))


def project_kernel(
    norm, count, width, order_ref, *refs
):
    pieces, rest = refs[:count], refs[count:]
    if norm:
        gain_ref, halo_ref, rest = rest[0], rest[1], rest[2:]
    w_refs, (normed_ref, proj_ref, rim_ref) = rest[:3], rest[3:]
    step = pl.program_id(0)

    def run(rows):
        normed_ref[...] = rows
        for j, w_ref in enumerate(w_refs):
            size = w_ref.shape[1]
            proj_ref[:, j * size : (j + 1) * size] = mm(rows, w_ref[...])

    if norm:
        wide = pieces[0][0].astype(F32)
        run((wide * row_norm(wide) * gain_ref[...]).astype(BF16))

        @pl.when(step == 0)
        def _():
            halo = halo_ref[0].astype(F32)
            halo = (halo * row_norm(halo) * gain_ref[...]).astype(BF16)
            row = jnp.concatenate([mm(halo, w_ref[...]) for w_ref in w_refs], axis=1)
            rim_ref[:, :width] = row[8:, :width].astype(BF16)
            rim_ref[:, width:] = row[8:, width + LANES :].astype(BF16)

    else:
        for m in range(count):

            @pl.when(step == m)
            def _(m=m):
                run(pieces[m][...])

    if norm:
        return

    @pl.when(order_ref[step] == pl.num_programs(0) - 1)
    def _():
        tail = proj_ref[CHUNK - 16 :].astype(BF16)
        rim_ref[:, :width] = tail[8:, :width]
        rim_ref[:, width:] = tail[8:, width + LANES :]


def project(source, gain, order, front, width, total):
    weights, at = front
    third = total // 3
    norm = gain is not None
    if norm:
        stream, halo, sequence = source
        model, length = stream.shape[2], stream.shape[1]
        inputs, count = [stream, gain, halo], 1
        specs = [
            pl.BlockSpec((1, CHUNK, model), lambda i, order: (sequence, order[i], 0)),
            fixed_block((1, model)),
            pl.BlockSpec((1, 16, model), lambda i, order: (sequence, 0, 0)),
        ]
    else:
        model, count = source[0].shape[1], len(source)
        length = count * CHUNK
        inputs = list(source)
        specs = [fixed_block((CHUNK, model))] * count
    conv = total - LANES
    return kernel_call(
        functools.partial(project_kernel, norm, count, width),
        cost=6.5,
        grid_spec=pltpu.PrefetchScalarGridSpec(
            num_scalar_prefetch=1,
            grid=(length // CHUNK,),
            in_specs=specs + [columns(weights, at + j, third) for j in range(3)],
            out_specs=[
                pl.BlockSpec((CHUNK, model), lambda i, order: (order[i], 0)),
                pl.BlockSpec((CHUNK, total), lambda i, order: (order[i], 0)),
                fixed_block((8, conv)),
            ],
        ),
        out_shape=[
            jax.ShapeDtypeStruct((length, model), BF16),
            jax.ShapeDtypeStruct((length, total), F32),
            jax.ShapeDtypeStruct((8, conv), BF16),
        ],
        compiler_params=params(),
    )(order, *inputs, weights, weights, weights)


def plain_kernel(a_ref, w_ref, out_ref):
    out_ref[...] = mm(a_ref[...], w_ref[...])


def plain_product(a, weight, width):
    weights, at = weight
    length, model = a.shape
    return kernel_call(
        plain_kernel,
        cost=3.7,
        grid=(length // CHUNK,),
        in_specs=[row_spec(model), columns(weights, at, width)],
        out_specs=row_spec(width),
        out_shape=jax.ShapeDtypeStruct((length, width), F32),
        compiler_params=params(),
    )(a, weights)


def norm_forward_kernel(stream_ref, keep_ref, first_ref, second_ref, gain_ref, new_ref, low_ref):
    total = keep_ref[0].astype(F32) + first_ref[0].astype(F32) + second_ref[...].astype(F32)
    new = stream_ref[...] + total
    new_ref[...] = new
    low_ref[...] = (new * row_norm(new) * gain_ref[...]).astype(BF16)


def last_forward_kernel(stream_ref, keep_ref, first_ref, second_ref, low_ref):
    total = keep_ref[0].astype(F32) + first_ref[0].astype(F32) + second_ref[...].astype(F32)
    low_ref[...] = (stream_ref[...] + total).astype(BF16)


def pass_on_kernel(keep_ref, first_ref, out_ref):
    total = keep_ref[0].astype(F32) + first_ref[0].astype(F32)
    out_ref[...] = total.astype(out_ref.dtype)


def pass_on(kept, first):
    _, rows, model = kept.shape
    spec = pl.BlockSpec((1, rows, model), lambda i: (1, 0, 0))
    return kernel_call(
        pass_on_kernel,
        grid=(1,),
        in_specs=[spec, spec],
        out_specs=fixed_block((rows, model)),
        out_shape=jax.ShapeDtypeStruct((rows, model), kept.dtype),
        compiler_params=params(),
    )(kept, first)


def term_specs(rows, model):
    return [
        fixed_block((rows, model)),
        fixed_block((1, rows, model)),
        fixed_block((1, rows, model)),
        fixed_block((rows, model)),
    ]


def norm_forward(stream, terms, gain):
    rows, model = stream.shape
    kept, first, second = terms
    if gain is None:
        return stream, kernel_call(
            last_forward_kernel,
            grid=(1,),
            in_specs=term_specs(rows, model),
            out_specs=fixed_block((rows, model)),
            out_shape=jax.ShapeDtypeStruct((rows, model), BF16),
            compiler_params=params(),
        )(stream, kept, first, second)
    return kernel_call(
        norm_forward_kernel,
        grid=(1,),
        in_specs=term_specs(rows, model) + [fixed_block((1, model))],
        out_specs=[fixed_block((rows, model))] * 2,
        out_shape=[
            jax.ShapeDtypeStruct((rows, model), F32),
            jax.ShapeDtypeStruct((rows, model), BF16),
        ],
        compiler_params=params(),
    )(stream, kept, first, second, gain)


def norm_backward_kernel(
    stream_ref, keep_ref, first_ref, second_ref, grad_ref, gain_ref, new_ref, low_ref, dgain_ref
):
    total = keep_ref[0].astype(F32) + first_ref[0].astype(F32) + second_ref[...].astype(F32)
    current = stream_ref[...]
    scale = row_norm(current)
    unit = current * scale
    dgain_ref[...] = jnp.broadcast_to(
        jnp.sum(total * unit, axis=0, keepdims=True), dgain_ref.shape
    )
    pulled = total * gain_ref[...]
    shift = jnp.mean(pulled * unit, axis=-1, keepdims=True)
    new = grad_ref[...] + scale * (pulled - unit * shift)
    new_ref[...] = new
    low_ref[...] = new.astype(BF16)


def norm_backward(stream, terms, grad, gain):
    rows, model = stream.shape
    return kernel_call(
        norm_backward_kernel,
        grid=(1,),
        in_specs=term_specs(rows, model) + [fixed_block((rows, model)), fixed_block((1, model))],
        out_specs=[fixed_block((rows, model))] * 2 + [fixed_block((8, model))],
        out_shape=[
            jax.ShapeDtypeStruct((rows, model), F32),
            jax.ShapeDtypeStruct((rows, model), BF16),
            jax.ShapeDtypeStruct((8, model), F32),
        ],
        compiler_params=params(),
    )(stream, *terms, grad, gain)


def assemble_kernel(count, order_ref, *refs):
    step = pl.program_id(0)
    for m in range(count):

        @pl.when(step == m)
        def _(m=m):
            refs[-1][0] = refs[m][...]


def assembled(groups, order):
    each, (rows, model) = len(groups[0]), groups[0][0].shape
    pieces = [piece for group in groups for piece in group]
    count = len(pieces)
    return kernel_call(
        functools.partial(assemble_kernel, count),
        cost=5.0,
        grid_spec=pltpu.PrefetchScalarGridSpec(
            num_scalar_prefetch=1,
            grid=(count,),
            in_specs=[fixed_block((rows, model))] * count,
            out_specs=pl.BlockSpec(
                (1, rows, model), lambda i, order: (i // each, order[i % each], 0)
            ),
        ),
        out_shape=jax.ShapeDtypeStruct((len(groups), each * rows, model), BF16),
        compiler_params=params(),
    )(order, *pieces)


def input_grad_kernel(parts, width, order_ref, dproj_ref, dgate_ref, tail_ref, rim_ref, *refs):
    w_refs, gate_ref, sent_ref, kept_ref, fixed_ref, rows_p, rows_g = refs[:3], *refs[3:]
    half = parts // 2

    @pl.when(pl.program_id(0) == 0)
    def _():
        fixed_ref[...] = dproj_ref[...]
        tail = (tail_ref[...] + rim_ref[...]).astype(BF16)
        fixed_ref[parts * CHUNK - 16 :, :width] = tail[:, :width]
        fixed_ref[parts * CHUNK - 16 :, width + LANES :] = tail[:, width:]
        for m in range(parts):
            source = pl.ds(pl.multiple_of(order_ref[m] * CHUNK, CHUNK), CHUNK)
            rows_p[m * CHUNK : (m + 1) * CHUNK] = fixed_ref[source]
            rows_g[m * CHUNK : (m + 1) * CHUNK] = dgate_ref[source]

    total = mm(rows_g[...], gate_ref[...], NT)
    for j, w_ref in enumerate(w_refs):
        size = w_ref.shape[1]
        total = total + mm(rows_p[:, j * size : (j + 1) * size], w_ref[...], NT)
    total = total.astype(BF16)
    for m in range(half):
        sent_ref[m] = total[m * CHUNK : (m + 1) * CHUNK]
        kept_ref[m] = total[(half + m) * CHUNK : (half + m + 1) * CHUNK]


def input_grad(dproj, dgate, tail, rim, front, gate, order):
    length, total = dproj.shape
    width = dgate.shape[1]
    (front_w, at), (gate_w, gate_at) = front, gate
    model, third, parts = front_w.shape[0], total // 3, length // CHUNK
    cut = model // 4
    half = pl.BlockSpec((parts // 2, CHUNK, cut), lambda i, order: (0, 0, i))

    def rows(offset, size):
        return pl.BlockSpec((cut, size), lambda i, order: (i, offset))

    return kernel_call(
        functools.partial(input_grad_kernel, parts, width),
        cost=7.6,
        grid_spec=pltpu.PrefetchScalarGridSpec(
            num_scalar_prefetch=1,
            grid=(4,),
            in_specs=[fixed_block(one.shape) for one in (dproj, dgate, tail, rim)]
            + [rows(at + j, third) for j in range(3)]
            + [rows(gate_at, width)],
            out_specs=[half, half, fixed_block((length, total))],
            scratch_shapes=[
                pltpu.VMEM((length, total), BF16),
                pltpu.VMEM((length, width), BF16),
            ],
        ),
        out_shape=[jax.ShapeDtypeStruct((parts // 2, CHUNK, model), BF16)] * 2
        + [jax.ShapeDtypeStruct((length, total), BF16)],
        compiler_params=params(),
    )(order, dproj, dgate, tail, rim, front_w, front_w, front_w, gate_w)


def weight_grad_kernel(segments, sequences, rows, places, order_ref, *refs):
    lefts, rights = refs[: segments * sequences], refs[segments * sequences :]
    rights, outs, total = rights[: segments * sequences], rights[segments * sequences : -1], refs[-1]
    at = 0
    for g in range(segments):
        width = rights[g * sequences].shape[1]
        part = None
        for s in range(sequences):
            left = lefts[g * sequences + s]
            left = left[...] if len(left.shape) == 2 else left[0]
            one = mm(left, rights[g * sequences + s][...], TN)
            part = one if part is None else part + one
        total[:, at : at + width] = part
        at += width
    if places is None:
        outs[0][...] = total[...].astype(BF16)
        return
    dp, context = places
    slot = lax.rem(pl.program_id(0) - order_ref[1] + dp, dp)

    def block(j):
        start = lax.rem(order_ref[0] + j, context) * rows
        return total[pl.ds(pl.multiple_of(start, 8), rows)].astype(BF16)

    outs[0][0] = block(0)
    for j in range(1, context):
        for k in range(dp):

            @pl.when(slot == k)
            def _(j=j, k=k):
                outs[1 + (j - 1) * dp + k][...] = block(j)


def weight_grad(pairs, ordered):
    dp, context = lax.axis_size("dp"), lax.axis_size("context")
    sequences, length = len(pairs[0][0]), pairs[0][1][0].shape[0]
    widths = [right[0].shape[1] for _, right in pairs]
    lefts = [one for left, _ in pairs for one in left]
    rights = [one for _, right in pairs for one in right]
    model = lefts[0].shape[-1]
    total, cut = sum(widths), model // dp
    rows = cut // context
    order = jnp.stack([lax.axis_index("context"), lax.axis_index("dp")]).astype(jnp.int32)
    if ordered:
        others = (context - 1) * dp
        out_specs = [
            pl.BlockSpec(
                (1, rows, total), lambda i, order: (lax.rem(i - order[1] + dp, dp), 0, 0)
            )
        ] + [fixed_block((rows, total))] * others
        out_shape = [jax.ShapeDtypeStruct((dp, rows, total), BF16)] + [
            jax.ShapeDtypeStruct((rows, total), BF16)
        ] * others
    else:
        out_specs = [pl.BlockSpec((cut, total), lambda i, order: (i, 0))]
        out_shape = [jax.ShapeDtypeStruct((model, total), BF16)]
    left_specs, left_arrays = [], []
    for left in lefts:
        if isinstance(left, tuple):
            left_arrays.append(left[0])
            left_specs.append(
                pl.BlockSpec((1, length, cut), lambda i, order, s=left[1]: (s, 0, i))
            )
        else:
            left_arrays.append(left)
            left_specs.append(pl.BlockSpec((length, cut), lambda i, order: (0, i)))
    return kernel_call(
        functools.partial(
            weight_grad_kernel, len(pairs), sequences, rows, (dp, context) if ordered else None
        ),
        cost=10.0,
        grid_spec=pltpu.PrefetchScalarGridSpec(
            num_scalar_prefetch=1,
            grid=(dp,),
            in_specs=left_specs + [fixed_block(one.shape) for one in rights],
            out_specs=out_specs,
            scratch_shapes=[pltpu.VMEM((cut, total), F32)],
        ),
        out_shape=out_shape,
        compiler_params=params(56),
    )(order, *left_arrays, *rights)


def ring_add_kernel(own_ref, *refs):
    total = own_ref[0].astype(F32)
    for one in refs[:-1]:
        total = total + one[...].astype(F32)
    refs[-1][...] = total.astype(refs[-1].dtype)


def ring_add(own, k, terms, kind):
    _, rows, width = own.shape
    return kernel_call(
        ring_add_kernel,
        cost=1.5,
        grid=(1,),
        in_specs=[pl.BlockSpec((1, rows, width), lambda i: (k, 0, 0))]
        + [fixed_block((rows, width))] * len(terms),
        out_specs=fixed_block((rows, width)),
        out_shape=jax.ShapeDtypeStruct((rows, width), kind),
        compiler_params=params(),
    )(own, *terms)


def ring_steps(blocks):
    dp, context = lax.axis_size("dp"), lax.axis_size("context")
    own, others = blocks[0], blocks[1:]
    places = list(range(1, dp)) + [0]
    sides = []
    for k in places:
        side = None
        for j in range(1, context):
            part = others[(j - 1) * dp + k]
            if side is not None:
                part = (side.astype(F32) + part.astype(F32)).astype(BF16)
            side = ring(part, "context")
        sides.append([] if side is None else [side])
    passed = []
    for k, side in zip(places, sides):
        value = ring_add(own, k, side + passed, BF16 if k else F32)
        if k:
            passed = [ring(value, "dp")]
            yield None
        else:
            yield value


def scan_forward_kernel(
    heads, width, p_ref, rim_ref, aux_ref, segr_ref, cw_ref, hp_ref, skip_ref, exp_ref,
    z_ref, y_ref, st_ref, end_ref, gr_ref, vbuf, state, offset,
):
    chunk = pl.program_id(0)

    @pl.when(chunk == 0)
    def _():
        vbuf[0:8] = rim_ref[...].astype(F32)
        state[...] = jnp.zeros_like(state)
        offset[...] = jnp.zeros_like(offset)

    @pl.when(chunk > 0)
    def _():
        vbuf[0:8] = vbuf[CHUNK : CHUNK + 8]

    vbuf[8:, :width] = rounded(p_ref[:, :width])
    vbuf[8:, width:] = rounded(p_ref[:, width + LANES :])
    z = cw_ref[4:5] + cw_ref[3:4] * vbuf[8:]
    for k in range(3):
        z = z + cw_ref[k : k + 1] * vbuf[5 + k : 5 + k + CHUNK] * aux_ref[:, k : k + 1]
    z_ref[...] = z
    act = z * jax.nn.sigmoid(z)
    x = act[:, :width]
    b_val, c_val = act[:, width : width + LANES], act[:, width + LANES :]
    lane = iota(1)
    step = jnp.where(
        lane < heads, softplus(p_ref[:, width : width + LANES] + hp_ref[0:1]), 0.0
    )
    decay = hp_ref[1:2] * step
    cum = lax.dot_general(
        (iota(0) >= iota(1)).astype(F32), decay, NN, precision=HIGH, preferred_element_type=F32
    )
    cum_t = cum.T
    seg_col = aux_ref[:, 5:6]
    link = jnp.where((seg_col == segr_ref[0]) & (iota(0) >= iota(1)), 0.0, NO_LINK)
    scores = fmm(c_val, b_val, NT)
    growth = jnp.exp(cum) * aux_ref[:, 3:4]
    last = cum[CHUNK - 1 : CHUNK]
    weight = jnp.exp(last - cum) * (seg_col == seg_col[CHUNK - 1 : CHUNK]).astype(F32)
    wide = split_dot(jnp.concatenate([step, growth, weight], axis=0), exp_ref[...])
    step_e, growth_e, weight_e = wide[:CHUNK], wide[CHUNK : 2 * CHUNK], wide[2 * CHUNK :]
    xd = x * step_e
    lower = lane < LANES // 2
    pieces = []
    for pair in range(heads // 2):
        mats = []
        for head in (2 * pair, 2 * pair + 1):
            spread = cum[:, head : head + 1] - cum_t[head : head + 1, :]
            mats.append(jnp.exp(spread + link) * scores)
        tile = xd[:, pair * LANES : (pair + 1) * LANES]
        pieces.append(fmm(jnp.concatenate(mats, axis=1), head_halves(tile, lower)))
    held = state[...]
    st_ref[0] = held
    carried = fmm(c_val, held) * growth_e
    y_ref[...] = jnp.concatenate(pieces, axis=1) + carried + skip_ref[...] * x
    new = held * growth_e[CHUNK - 1 : CHUNK] + fmm(b_val, xd * weight_e, TN)
    state[...] = new
    end_ref[...] = new
    gr_ref[...] = jnp.exp(offset[...] + cum) * aux_ref[:, 4:5]
    offset[...] = offset[...] + last


def row_spec(width, at=None, rows=CHUNK):
    if at is None:
        return pl.BlockSpec((rows, width), lambda i: (i, 0))
    return pl.BlockSpec((rows, width), lambda i: (i, at))


def whole(shape):
    return pl.BlockSpec(shape, lambda i: (0,) * len(shape))


def scan_forward(proj, rim, aux, seg_rows, consts):
    length, total = proj.shape
    heads, width = consts["heads"], consts["width"]
    chunks, conv = length // CHUNK, total - LANES
    return kernel_call(
        functools.partial(scan_forward_kernel, heads, width),
        cost=9.5,
        grid=(chunks,),
        in_specs=[
            row_spec(total),
            whole((8, conv)),
            row_spec(8),
            pl.BlockSpec((1, 1, CHUNK), lambda i: (i, 0, 0)),
            whole((8, conv)),
            whole((8, LANES)),
            whole((1, width)),
            whole((LANES, width)),
        ],
        out_specs=[
            row_spec(conv),
            row_spec(width),
            pl.BlockSpec((1, LANES, width), lambda i: (i, 0, 0)),
            whole((LANES, width)),
            row_spec(LANES),
        ],
        out_shape=[
            jax.ShapeDtypeStruct((length, conv), F32),
            jax.ShapeDtypeStruct((length, width), F32),
            jax.ShapeDtypeStruct((chunks, LANES, width), F32),
            jax.ShapeDtypeStruct((LANES, width), F32),
            jax.ShapeDtypeStruct((length, LANES), F32),
        ],
        scratch_shapes=[
            pltpu.VMEM((CHUNK + 8, conv), F32),
            pltpu.VMEM((LANES, width), F32),
            pltpu.VMEM((1, LANES), F32),
        ],
        compiler_params=params(),
    )(proj, rim, aux, seg_rows, consts["cw"], consts["hp"], consts["skip"], consts["exp"])


def mix_forward_kernel(y0_ref, zc_ref, gr_ref, sin_ref, gate_ref, exp_ref, y_ref, sq_ref):
    c_val = zc_ref[...] * jax.nn.sigmoid(zc_ref[...])
    carried = fmm(c_val, sin_ref[...].astype(F32))
    y = y0_ref[...] + carried * split_dot(gr_ref[...], exp_ref[...])
    y_ref[...] = y
    gate = gate_ref[...]
    gated = y * (gate * jax.nn.sigmoid(gate))
    square = jnp.sum(gated * gated, axis=1, keepdims=True)
    sq_ref[...] = jnp.broadcast_to(square, (CHUNK, CHUNK)).T[:8]


def mix_forward(y0, z, growth, carried, gate, consts):
    length, width = y0.shape
    last = z.shape[1] // LANES - 1
    return kernel_call(
        mix_forward_kernel,
        cost=3.6,
        grid=(length // CHUNK,),
        in_specs=[
            row_spec(width),
            row_spec(LANES, last),
            row_spec(LANES),
            whole((LANES, width)),
            row_spec(width),
            whole((LANES, width)),
        ],
        out_specs=[row_spec(width), pl.BlockSpec((8, CHUNK), lambda i: (0, i))],
        out_shape=[
            jax.ShapeDtypeStruct((length, width), F32),
            jax.ShapeDtypeStruct((8, length), F32),
        ],
        compiler_params=params(),
    )(y0, z, growth, carried, gate, consts["exp"])


def project_out_kernel(channels, parts, order_ref, y_ref, gate_ref, gain_ref, w_ref, *refs):
    squares, (sent_ref, kept_ref, rows) = refs[:-3], refs[-3:]
    half = parts // 2

    @pl.when(pl.program_id(0) == 0)
    def _():
        for m in range(parts):
            source = pl.ds(pl.multiple_of(order_ref[m] * CHUNK, CHUNK), CHUNK)
            square = sum(one[:, source] for one in squares)
            scale = lax.rsqrt(column_of(square)[:, 0:1] / channels + eps)
            gate = gate_ref[source]
            gated = y_ref[source] * (gate * jax.nn.sigmoid(gate))
            rows[m * CHUNK : (m + 1) * CHUNK] = (gated * scale * gain_ref[...]).astype(BF16)

    total = mm(rows[...], w_ref[...], NT).astype(sent_ref.dtype)
    for m in range(half):
        sent_ref[m] = total[m * CHUNK : (m + 1) * CHUNK]
        kept_ref[m] = total[(half + m) * CHUNK : (half + m + 1) * CHUNK]


def project_out(y, gate, squares, channels, kind, order, consts):
    length, width = y.shape
    weights, at = consts["out"]
    model, parts = weights.shape[0], length // CHUNK
    cut = model // 4
    half = pl.BlockSpec((parts // 2, CHUNK, cut), lambda i, order: (0, 0, i))
    return kernel_call(
        functools.partial(project_out_kernel, float(channels), parts),
        cost=5.7,
        grid_spec=pltpu.PrefetchScalarGridSpec(
            num_scalar_prefetch=1,
            grid=(4,),
            in_specs=[
                fixed_block((length, width)),
                fixed_block((length, width)),
                fixed_block((1, width)),
                pl.BlockSpec((cut, width), lambda i, order: (i, at)),
            ]
            + [fixed_block((8, length))] * len(squares),
            out_specs=[half, half],
            scratch_shapes=[pltpu.VMEM((length, width), BF16)],
        ),
        out_shape=[jax.ShapeDtypeStruct((parts // 2, CHUNK, model), kind)] * 2,
        compiler_params=params(),
    )(order, y, gate, consts["gain"], weights, *squares)


def grad_scaled_kernel(count, order_ref, *refs):
    pieces, rest = refs[:count], refs[count:]
    w_ref, y_ref, gate_ref, gain_ref, gs_ref, dot_ref = rest[:6]
    gate = gate_ref[...]
    gated = y_ref[...] * (gate * jax.nn.sigmoid(gate))

    def run(rows):
        grad = mm(rows, w_ref[...])
        gs_ref[...] = grad
        product = jnp.sum(grad * gain_ref[...] * gated, axis=1, keepdims=True)
        dot_ref[...] = jnp.broadcast_to(product, (CHUNK, CHUNK)).T[:8]

    if count == 1:
        run(pieces[0][0])
    else:
        for m in range(count):

            @pl.when(pl.program_id(0) == m)
            def _(m=m):
                rest[6][...] = pieces[m][...]
                run(pieces[m][...])


def grad_scaled(source, y, gate, order, consts):
    length, width = y.shape
    weights, at = consts["out"]
    model = weights.shape[0]
    row = pl.BlockSpec((CHUNK, width), lambda i, order: (order[i], 0))
    out_specs = [row, pl.BlockSpec((8, CHUNK), lambda i, order: (0, order[i]))]
    out_shape = [
        jax.ShapeDtypeStruct((length, width), F32),
        jax.ShapeDtypeStruct((8, length), F32),
    ]
    if len(source) == 2:
        stream, sequence = source
        inputs, count = [stream], 1
        specs = [pl.BlockSpec((1, CHUNK, model), lambda i, order: (sequence, order[i], 0))]
    else:
        inputs, count = list(source), len(source)
        specs = [fixed_block((CHUNK, model))] * count
        out_specs.append(pl.BlockSpec((CHUNK, model), lambda i, order: (order[i], 0)))
        out_shape.append(jax.ShapeDtypeStruct((length, model), BF16))
    out = kernel_call(
        functools.partial(grad_scaled_kernel, count),
        cost=5.5,
        grid_spec=pltpu.PrefetchScalarGridSpec(
            num_scalar_prefetch=1,
            grid=(length // CHUNK,),
            in_specs=specs + [columns(weights, at, width), row, row, fixed_block((1, width))],
            out_specs=out_specs,
        ),
        out_shape=out_shape,
        compiler_params=params(),
    )(order, *inputs, weights, y, gate, consts["gain"])
    return out if count > 1 else (*out, source)


def mix_backward_kernel(
    channels, shares, gs_ref, y_ref, gate_ref, zx_ref, zc_ref, gr_ref, gain_ref, exp_ref, *refs
):
    squares, dots, refs = refs[:shares], refs[shares : 2 * shares], refs[2 * shares :]
    scaled_ref, dgate_ref, dy_ref, acc_ref, dsin_ref, dsin = refs
    at = pl.program_id(0)

    @pl.when(at == 0)
    def _():
        acc_ref[...] = jnp.zeros_like(acc_ref)
        dsin[...] = jnp.zeros_like(dsin)

    stats = column_of(
        jnp.concatenate(
            [sum(one[...] for one in squares), sum(one[...] for one in dots)], axis=0
        )
    )
    scale = lax.rsqrt(stats[:, 0:1] / channels + eps)
    pull = scale * scale * scale * stats[:, 8:9] / channels
    grad, y, gate = gs_ref[...], y_ref[...], gate_ref[...]
    silu, sig = silu_parts(gate)
    gated = y * silu
    unit = gated * scale
    scaled_ref[...] = (unit * gain_ref[...]).astype(BF16)
    dgated = grad * gain_ref[...] * scale - gated * pull
    dy = dgated * silu
    dy_ref[...] = dy
    dgate_ref[...] = (dgated * y * (sig * (1.0 + gate * (1.0 - sig)))).astype(BF16)
    x = zx_ref[...] * jax.nn.sigmoid(zx_ref[...])
    acc_ref[0:1] += jnp.sum(grad * unit, axis=0, keepdims=True)
    acc_ref[1:2] += jnp.sum(dy * x, axis=0, keepdims=True)
    c_low = (zc_ref[...] * jax.nn.sigmoid(zc_ref[...])).astype(BF16)
    dsin[...] += mm(c_low, (dy * split_dot(gr_ref[...], exp_ref[...])).astype(BF16), TN)

    @pl.when(at == pl.num_programs(0) - 1)
    def _():
        dsin_ref[...] = dsin[...].astype(BF16)


def mix_backward(grad, y, gate, z, growth, squares, dots, channels, consts):
    length, width = y.shape
    last = z.shape[1] // LANES - 1
    stat = pl.BlockSpec((8, CHUNK), lambda i: (0, i))
    return kernel_call(
        functools.partial(mix_backward_kernel, float(channels), len(squares)),
        cost=5.0,
        grid=(length // CHUNK,),
        in_specs=[
            row_spec(width),
            row_spec(width),
            row_spec(width),
            row_spec(width),
            row_spec(LANES, last),
            row_spec(LANES),
            whole((1, width)),
            whole((LANES, width)),
        ]
        + [stat] * (2 * len(squares)),
        out_specs=[
            row_spec(width),
            row_spec(width),
            row_spec(width),
            whole((8, width)),
            whole((LANES, width)),
        ],
        out_shape=[
            jax.ShapeDtypeStruct((length, width), BF16),
            jax.ShapeDtypeStruct((length, width), BF16),
            jax.ShapeDtypeStruct((length, width), F32),
            jax.ShapeDtypeStruct((8, width), F32),
            jax.ShapeDtypeStruct((LANES, width), BF16),
        ],
        scratch_shapes=[pltpu.VMEM((LANES, width), F32)],
        compiler_params=params(),
    )(grad, y, gate, z, z, growth, consts["gain"], consts["exp"], *squares, *dots)


def scan_backward_kernel(
    heads, width, chunks, dy_ref, z_ref, p_ref, before_ref, rim_ref, aux_ref, segr_ref, cw_ref,
    hp_ref, skip_ref, exp_ref, red_ref, st_ref, sin_ref, grprev_ref, dend_ref,
    dproj_ref, wacc_ref, hacc_ref, tail_ref, drim_ref, vbuf, zbuf, dstate,
):
    step_at = pl.program_id(0)
    chunk = chunks - 1 - step_at

    @pl.when(step_at == 0)
    def _():
        dstate[...] = dend_ref[...].astype(F32)
        zbuf[...] = jnp.zeros_like(zbuf)
        wacc_ref[...] = jnp.zeros_like(wacc_ref)
        hacc_ref[...] = jnp.zeros_like(hacc_ref)

    @pl.when(chunk == 0)
    def _():
        vbuf[0:8] = rim_ref[...].astype(F32)

    @pl.when(chunk > 0)
    def _():
        vbuf[0:8, :width] = rounded(before_ref[:, :width])
        vbuf[0:8, width:] = rounded(before_ref[:, width + LANES :])

    vbuf[8:, :width] = rounded(p_ref[:, :width])
    vbuf[8:, width:] = rounded(p_ref[:, width + LANES :])

    z = z_ref[...]
    act, sig = silu_parts(z)
    slope = sig * (1.0 + z * (1.0 - sig))
    x = act[:, :width]
    b_val, c_val = act[:, width : width + LANES], act[:, width + LANES :]
    lane = iota(1)
    pre = p_ref[:, width : width + LANES] + hp_ref[0:1]
    step = jnp.where(lane < heads, softplus(pre), 0.0)
    decay = hp_ref[1:2] * step
    cum = lax.dot_general(
        (iota(0) >= iota(1)).astype(F32), decay, NN, precision=HIGH, preferred_element_type=F32
    )
    cum_t = cum.T
    seg_col = aux_ref[:, 5:6]
    link = jnp.where((seg_col == segr_ref[0]) & (iota(0) <= iota(1)), 0.0, NO_LINK)
    growth = jnp.exp(cum) * aux_ref[:, 3:4]
    last = cum[CHUNK - 1 : CHUNK]
    weight = jnp.exp(last - cum) * (seg_col == seg_col[CHUNK - 1 : CHUNK]).astype(F32)
    reach = jnp.where(chunk == 0, 1.0, grprev_ref[7:8])
    wide = split_dot(
        jnp.concatenate([step, growth, weight, jnp.broadcast_to(reach, (8, LANES))], axis=0),
        exp_ref[...],
    )
    step_e, growth_e = wide[:CHUNK], wide[CHUNK : 2 * CHUNK]
    weight_e, reach_e = wide[2 * CHUNK : 3 * CHUNK], wide[3 * CHUNK : 3 * CHUNK + 1]
    held = st_ref[0] + sin_ref[...].astype(F32) * reach_e
    after = dstate[...]
    xd = x * step_e
    dy = dy_ref[...]
    scores = bmm(b_val, c_val, NT)
    carried = bmm(c_val, held) * growth_e
    fed = bmm(b_val, after) * weight_e
    dy_grown = dy * growth_e
    lower = lane < LANES // 2
    dscores = jnp.zeros((CHUNK, CHUNK), F32)
    into = jnp.zeros((CHUNK, CHUNK), F32)
    rows, pieces = [], []
    for pair in range(heads // 2):
        at = slice(pair * LANES, (pair + 1) * LANES)
        products = bmm(head_halves(xd[:, at], lower), dy[:, at], NT)
        mats = []
        for side, head in enumerate((2 * pair, 2 * pair + 1)):
            spread = cum_t[head : head + 1, :] - cum[:, head : head + 1]
            reachable = jnp.exp(spread + link)
            product = products[side * CHUNK : (side + 1) * CHUNK]
            mat = reachable * scores
            dscores = dscores + reachable * product
            energy = mat * product
            rows.append(jnp.sum(energy, axis=0, keepdims=True))
            into = jnp.where(lane == head, jnp.sum(energy, axis=1, keepdims=True), into)
            mats.append(mat)
        pieces.append(bmm(jnp.concatenate(mats, axis=1), head_halves(dy[:, at], lower)))
    dxd = jnp.concatenate(pieces, axis=1) + fed
    kept = jnp.sum(after * held, axis=0, keepdims=True) * growth_e[CHUNK - 1 : CHUNK]
    sums = split_dot(
        jnp.concatenate(
            [dy * carried, xd * fed, dxd * x, jnp.broadcast_to(kept, (8, width))], axis=0
        ),
        red_ref[...],
    )
    out_of, fed_sum = sums[:CHUNK], sums[CHUNK : 2 * CHUNK]
    dstep, kept_sum = sums[2 * CHUNK : 3 * CHUNK], sums[3 * CHUNK : 3 * CHUNK + 1]
    rows = column_of(jnp.concatenate(rows, axis=0))
    dcum = rows - into + out_of - fed_sum
    end_term = kept_sum + jnp.sum(fed_sum, axis=0, keepdims=True)
    ddecay = (
        lax.dot_general(
            (iota(0) <= iota(1)).astype(F32), dcum, NN, precision=HIGH, preferred_element_type=F32
        )
        + end_term
    )
    ddecay = jnp.where(lane < heads, ddecay, 0.0)
    dpre = jnp.where(lane < heads, (dstep + hp_ref[1:2] * ddecay) * jax.nn.sigmoid(pre), 0.0)
    hacc_ref[0:1] += jnp.sum(dpre, axis=0, keepdims=True)
    hacc_ref[1:2] += jnp.sum(ddecay * decay, axis=0, keepdims=True)
    dx = dxd * step_e + skip_ref[...] * dy
    db = wide_mm(dscores, c_val) + wide_mm(xd * weight_e, after, NT)
    dc = wide_mm(dscores, b_val, TN) + wide_mm(dy_grown, held, NT)
    dstate[...] = after * growth_e[CHUNK - 1 : CHUNK] + bmm(c_val, dy_grown, TN)

    dz = jnp.concatenate([dx, db, dc], axis=1) * slope
    wacc_ref[3:4] += jnp.sum(dz * vbuf[8:], axis=0, keepdims=True)
    wacc_ref[4:5] += jnp.sum(dz, axis=0, keepdims=True)
    dv = cw_ref[3:4] * dz
    for k in range(3):
        masked = dz * aux_ref[:, k : k + 1]
        wacc_ref[k : k + 1] += jnp.sum(
            masked * vbuf[5 + k : 5 + k + CHUNK], axis=0, keepdims=True
        )
        zbuf[k, 8 : 8 + CHUNK] = masked
        dv = dv + cw_ref[k : k + 1] * zbuf[k, 11 - k : 11 - k + CHUNK]
    dproj_ref[:, :width] = dv[:, :width].astype(BF16)
    dproj_ref[:, width : width + LANES] = dpre.astype(BF16)
    dproj_ref[:, width + LANES :] = dv[:, width:].astype(BF16)

    @pl.when(step_at == 0)
    def _():
        tail_ref[...] = dv[CHUNK - 16 :]

    @pl.when(chunk == 0)
    def _():
        drim = cw_ref[0:1] * zbuf[0, 3:11]
        for k in (1, 2):
            drim = drim + cw_ref[k : k + 1] * zbuf[k, 3 - k : 11 - k]
        drim_ref[0:8] = jnp.zeros_like(drim)
        drim_ref[8:] = drim

    for k in range(3):
        zbuf[k, 8 + CHUNK :] = zbuf[k, 8:16]


def scan_backward(dy, z, proj, rim, aux, seg_rows, states, carried, growth, dend, consts):
    length, total = proj.shape
    heads, width = consts["heads"], consts["width"]
    chunks, conv = length // CHUNK, total - LANES
    eights = CHUNK // 8

    def back(columns):
        return pl.BlockSpec((CHUNK, columns), lambda i: (chunks - 1 - i, 0))

    def previous(columns):
        return pl.BlockSpec(
            (8, columns), lambda i: (jnp.maximum((chunks - 1 - i) * eights - 1, 0), 0)
        )

    return kernel_call(
        functools.partial(scan_backward_kernel, heads, width, chunks),
        cost=18.0,
        grid=(chunks,),
        in_specs=[
            back(width),
            back(conv),
            back(total),
            previous(total),
            whole((8, conv)),
            back(8),
            pl.BlockSpec((1, 1, CHUNK), lambda i: (chunks - 1 - i, 0, 0)),
            whole((8, conv)),
            whole((8, LANES)),
            whole((1, width)),
            whole((LANES, width)),
            whole((width, LANES)),
            pl.BlockSpec((1, LANES, width), lambda i: (chunks - 1 - i, 0, 0)),
            whole((LANES, width)),
            previous(LANES),
            whole((LANES, width)),
        ],
        out_specs=[
            back(total),
            whole((8, conv)),
            whole((8, LANES)),
            whole((16, conv)),
            whole((16, conv)),
        ],
        out_shape=[
            jax.ShapeDtypeStruct((length, total), BF16),
            jax.ShapeDtypeStruct((8, conv), F32),
            jax.ShapeDtypeStruct((8, LANES), F32),
            jax.ShapeDtypeStruct((16, conv), F32),
            jax.ShapeDtypeStruct((16, conv), F32),
        ],
        scratch_shapes=[
            pltpu.VMEM((CHUNK + 8, conv), F32),
            pltpu.VMEM((3, CHUNK + 16, conv), F32),
            pltpu.VMEM((LANES, width), F32),
        ],
        compiler_params=params(),
    )(
        dy, z, proj, proj, rim, aux, seg_rows, consts["cw"], consts["hp"], consts["skip"],
        consts["exp"], consts["red"], states, carried, growth, dend,
    )


def local(
    stream,
    seg_ids,
    input_weight,
    step_size_weight,
    coefficient_weight,
    pre_gain,
    conv_bc,
    bias_bc,
    output_weight,
    conv_x,
    bias_x,
    dt_bias,
    a_log,
    skip,
    gate_gain,
    cotangent,
):
    PRECEDING.clear()
    layers, rows_in, _, width = input_weight.shape
    sequences, length, model = stream.shape
    heads = dt_bias.shape[1]
    depth = width // heads
    shared = coefficient_weight.shape[2]
    dp, context, tensor = (lax.axis_size(a) for a in ("dp", "context", "tensor"))
    channels = width * tensor
    rows_bc = rows_in // tensor
    conv, total = width + shared, width + LANES + shared
    layer_range, seq_range = range(layers), range(sequences)

    own_gain, own_conv = pre_gain.shape[1], conv_bc.shape[2]
    small = jnp.concatenate([pre_gain, conv_bc.reshape(layers, -1), bias_bc], axis=1)
    small = jnp.pad(small, ((0, 0), (0, shared - small.shape[1])))[:, None]
    bc_rows = gather_small(jnp.concatenate([coefficient_weight, small], axis=1), ("tensor",))
    small, bc_rows = bc_rows[:, :, rows_bc], bc_rows[:, :, :rows_bc]
    taps = small[:, :, own_gain : own_gain + 5 * own_conv].reshape(tensor, layers, 5, own_conv)
    taps = jnp.moveaxis(taps, 0, 2).reshape(layers, -1)
    small = jnp.concatenate(
        [
            jnp.moveaxis(small[:, :, :own_gain], 0, 1).reshape(layers, rows_in),
            jnp.pad(taps, ((0, 0), (0, rows_in - taps.shape[1]))),
        ],
        axis=0,
    ).T

    def first_piece(layer):
        tile = jnp.concatenate(
            [
                step_size_weight[layer],
                small,
                jnp.zeros((rows_in, LANES - heads - 2 * layers), BF16),
                bc_rows[:, layer].reshape(rows_in, shared),
            ],
            axis=1,
        )
        return [input_weight[layer, :, 1], tile]

    def second_piece(layer):
        return [input_weight[layer, :, 0], output_weight[layer].T]

    edge_ids = shifted(seg_ids[:, -3:], "context", 1)
    ext_ids = jnp.concatenate([edge_ids, seg_ids], axis=1)
    prior = ext_ids[:, 2 : 2 + length].reshape(sequences, length // CHUNK, CHUNK)[:, :, 0]
    prior = jnp.repeat(prior, CHUNK, axis=1)
    aux_all = jnp.stack(
        [ext_ids[:, k : k + length] == seg_ids for k in range(3)]
        + [seg_ids == prior, seg_ids == edge_ids[:, 2:3], seg_ids, seg_ids, seg_ids],
        axis=2,
    ).astype(F32)
    seg_rows = seg_ids.astype(F32).reshape(sequences, length // CHUNK, 1, CHUNK)

    spread_table = (jnp.arange(LANES)[:, None] == jnp.arange(width)[None, :] // depth).astype(BF16)

    table = ring_pieces(jnp.concatenate(first_piece(0), axis=1))
    first, tile_rows = placed(table, [total], width)
    weights, before = [], table[min(1, dp - 1)][0][:16, :LANES]
    for layer in layer_range:
        front = first
        if layer:
            part = after(jnp.concatenate(first_piece(layer), axis=1), before)
            front = lax.all_gather(part, ("dp", "context"), axis=0, tiled=True)
            before = front[:8, :LANES]
        part = after(jnp.concatenate(second_piece(layer), axis=1), before)
        rest = lax.all_gather(part, ("dp", "context"), axis=0, tiled=True)
        before = rest[:8, :LANES]
        weights.append({"front": (front, 0), "gate": (rest, 0), "out": (rest, 1)})
    small = tile_rows[heads : heads + 2 * layers]
    gains = small[:layers]
    taps = small[layers:].reshape(layers, dp * context, rows_in)[:, :, : 5 * tensor * own_conv]
    taps = taps.reshape(layers, dp * context, 5, tensor * own_conv)
    taps = jnp.moveaxis(taps, 1, 2).reshape(layers, 5, shared)

    consts = []
    for layer in layer_range:
        cw = jnp.concatenate(
            [
                jnp.concatenate(
                    [jnp.concatenate([conv_x[layer], bias_x[layer][None]], axis=0), taps[layer]],
                    axis=1,
                ),
                jnp.zeros((3, conv), F32),
            ],
            axis=0,
        )
        pad = jnp.zeros((LANES - heads,), F32)
        hp = jnp.stack(
            [
                jnp.concatenate([dt_bias[layer], pad]),
                jnp.concatenate([-jnp.exp(a_log[layer]), pad]),
            ]
            + [jnp.zeros((LANES,), F32)] * 6
        )
        consts.append(
            {
                "heads": heads,
                "width": width,
                "cw": cw,
                "hp": hp,
                "skip": jnp.repeat(skip[layer], depth)[None],
                "gain": gate_gain[layer][None],
                "exp": spread_table,
                "red": spread_table.T,
                **weights[layer],
            }
        )

    def chain(value, total, steps):
        carried = shifted(value, "context", steps)
        for _ in range(context - 2):
            passed = value.astype(F32) + carried.astype(F32) * total
            carried = shifted(passed.astype(value.dtype), "context", steps)
        return carried

    def through(growth):
        return jnp.repeat(growth[length - 1, :heads], depth)[None]

    places = jnp.arange(length // CHUNK, dtype=jnp.int32)
    arrived, sending = rows_order(False), rows_order(True)
    streams = [own_rows(stream[s]).astype(F32) for s in seq_range]
    grads = [own_rows(cotangent[s]).astype(F32) for s in seq_range]
    halo = shifted(stream[:, length - 16 :], "context", 1)
    incoming = [(stream, halo, s) for s in seq_range]
    work = [[{} for _ in seq_range] for _ in layer_range]
    outputs = []
    top = layers - 1
    def step_project(layer, s):
        k = work[layer][s]
        k["stream"] = streams[s]
        k["normed"], k["proj"], tail = project(
            incoming[s],
            None if layer else gains[0:1],
            arrived if layer else places,
            consts[layer]["front"],
            width,
            total,
        )
        k["rim"] = shifted(tail, "context", 1) if layer else tail

    def step_scan(layer, s):
        k = work[layer][s]
        k["z"], k["y0"], k["states"], end, k["growth"] = scan_forward(
            k["proj"], k["rim"], aux_all[s], seg_rows[s], consts[layer]
        )
        k["carried"] = chain(end, through(k["growth"]), 1)

    def step_gate(layer, s):
        k = work[layer][s]
        k["gate"] = plain_product(k["normed"], consts[layer]["gate"], width)

    def step_mix(layer, s):
        k = work[layer][s]
        k["y"], squares = mix_forward(
            k["y0"], k["z"], k["growth"], k["carried"], k["gate"], consts[layer]
        )
        k["squares"] = from_others(squares, "tensor")

    def step_out(layer, s):
        k = work[layer][s]
        kind = BF16 if layer == top else F32
        sent, own = project_out(
            k["y"], k["gate"], k["squares"], channels, kind, sending, consts[layer]
        )
        k["out"] = [own, flipped(sent, "tensor", 0)]

    def step_pass(layer, s, name):
        terms = work[layer][s][name]
        terms.append(flipped(pass_on(*terms), "tensor", 1))

    def step_norm(layer, s):
        k = work[layer][s]
        gain = None if layer == top else gains[layer + 1 : layer + 2]
        streams[s], low = norm_forward(streams[s], k["out"], gain)
        return gathered(low)

    def step_grad(layer, s):
        k = work[layer][s]
        source = (cotangent, s) if layer == top else incoming[s]
        k["grad"], dots, k["low"] = grad_scaled(
            source, k["y"], k["gate"], places if layer == top else arrived, consts[layer]
        )
        k["dots"] = from_others(dots, "tensor")

    def step_mix_back(layer, s):
        k = work[layer][s]
        k["scaled"], k["dgate"], k["dy"], k["acc"], dsin = mix_backward(
            k["grad"], k["y"], k["gate"], k["z"], k["growth"], k["squares"], k["dots"],
            channels, consts[layer],
        )
        k["dend"] = chain(dsin, through(k["growth"]), -1)

    def step_scan_back(layer, s):
        k = work[layer][s]
        k["dproj"], k["wacc"], k["hacc"], k["tail"], drim = scan_backward(
            k["dy"], k["z"], k["proj"], k["rim"], aux_all[s], seg_rows[s], k["states"],
            k["carried"], k["growth"], k["dend"], consts[layer],
        )
        k["drim"] = shifted(drim, "context", -1)

    def step_input_grad(layer, s):
        k = work[layer][s]
        sent, own, k["dproj"] = input_grad(
            k["dproj"], k["dgate"], k["tail"], k["drim"], consts[layer]["front"],
            consts[layer]["gate"], sending,
        )
        k["back"] = [own, flipped(sent, "tensor", 0)]

    def step_norm_back(layer, s):
        k = work[layer][s]
        grads[s], low, k["dgain"] = norm_backward(
            k["stream"], k["back"], grads[s], gains[layer : layer + 1]
        )
        return gathered(low)

    def every(layer, name):
        return [k[name] for k in work[layer]]

    def step_second_grad(layer):
        return weight_grad(
            [
                (every(layer, "normed"), every(layer, "dgate")),
                (every(layer, "low"), every(layer, "scaled")),
            ],
            layer == 0,
        )

    def step_first_grad(layer):
        return weight_grad([(every(layer, "normed"), every(layer, "dproj"))], layer == 0)

    def scattered(value):
        return lax.psum_scatter(
            value[0], ("dp", "context"), scatter_dimension=0, tiled=True
        ).astype(F32)

    second_sums, first_sums = [None] * layers, [None] * layers
    final = sequences - 1
    for s in seq_range:
        step_project(0, s)
        if s == 0:
            step_scan(0, s)
    for layer in layer_range:
        if layer:
            for s in seq_range:
                step_project(layer, s)
                step_scan(layer, s)
            for s in seq_range:
                step_gate(layer, s)
                step_mix(layer, s)
        else:
            for s in seq_range:
                step_gate(layer, s)
                step_mix(layer, s)
                if s < final:
                    step_scan(layer, s + 1)
                if layer < top:
                    step_out(layer, s)
                    step_pass(layer, s, "out")
        if layer < top:
            for s in seq_range:
                incoming[s] = step_norm(layer, s)

    def rest_of(layer):
        incoming[final] = step_norm_back(layer, final)
        first_sums[layer] = scattered(step_first_grad(layer))

    for layer in reversed(layer_range):
        for s in seq_range:
            step_grad(layer, s)
            if s == 0 and layer < top:
                rest_of(layer + 1)
        for s in seq_range:
            step_mix_back(layer, s)
        grad = step_second_grad(layer)
        if layer:
            second_sums[layer] = scattered(grad)
        steps = iter(()) if layer else ring_steps(grad)
        for s in seq_range:
            step_scan_back(layer, s)
            if s == final:
                for earlier in range(s):
                    incoming[earlier] = step_norm_back(layer, earlier)
            next(steps, None)
            if layer == top:
                step_out(layer, s)
            elif layer == top - 1 and s == 0:
                outputs.extend(step_norm(top, s) for s in seq_range)
            step_input_grad(layer, s)
            step_pass(layer, s, "back")
            if layer == top:
                step_pass(layer, s, "out")
    next(steps, None)
    grad = step_first_grad(0)
    for value in steps:
        second_sums[0] = value
    steps = ring_steps(grad)
    next(steps)
    incoming[final] = step_norm_back(0, final)
    next(steps)
    layer_out = assembled(outputs, arrived)
    for value in steps:
        first_sums[0] = value
    grad_stream = assembled(incoming, arrived)

    out, small_local, small_shared = [], [], []
    for layer in layer_range:
        second_sum, first_sum = second_sums[layer], first_sums[layer]
        out.append(
            (
                jnp.stack([second_sum[:, :width], first_sum[:, :width]], axis=1),
                first_sum[:, width : width + heads],
                scatter_places(first_sum[:, width + LANES :]),
                second_sum[:, width:].T,
            )
        )
        acc, wacc, hacc, dgain = (
            sum(every(layer, name)) for name in ("acc", "wacc", "hacc", "dgain")
        )
        small_local.append(
            jnp.concatenate(
                [
                    wacc[:5, :width].reshape(-1),
                    acc[0],
                    acc[1].reshape(heads, depth).sum(axis=1),
                    hacc[0, :heads],
                    hacc[1, :heads],
                ]
            )
        )
        small_shared.append(jnp.concatenate([wacc[:5, width:].reshape(-1), dgain[0]]))

    shared_sum = summed_over(jnp.stack(small_shared), ("tensor",))
    local_sum = jnp.stack(small_local)
    cut = local_sum.shape[1]
    both = summed_over(
        jnp.concatenate([local_sum, shared_sum], axis=1), ("context", "dp")
    )
    local_sum, shared_sum = both[:, :cut], both[:, cut:]
    place = (lax.axis_index("dp") * context + lax.axis_index("context")) * tensor
    place = place + lax.axis_index("tensor")
    taps = shared_sum[:, : 5 * shared].reshape(layers, 5, shared)
    taps = lax.dynamic_slice_in_dim(taps, place * own_conv, own_conv, 2)
    grad_gain = lax.dynamic_slice_in_dim(
        shared_sum[:, 5 * shared :], place * own_gain, own_gain, 1
    )
    taps_x = local_sum[:, : 5 * width].reshape(layers, 5, width)
    heads_at = 6 * width
    return (
        layer_out,
        grad_stream,
        jnp.stack([o[0] for o in out]),
        jnp.stack([o[1] for o in out]),
        jnp.stack([o[2] for o in out]),
        grad_gain,
        taps[:, :4],
        taps[:, 4],
        jnp.stack([o[3] for o in out]),
        taps_x[:, :4],
        taps_x[:, 4],
        local_sum[:, heads_at + heads : heads_at + 2 * heads],
        local_sum[:, heads_at + 2 * heads : heads_at + 3 * heads],
        local_sum[:, heads_at : heads_at + heads],
        local_sum[:, 5 * width : 6 * width],
    )


def solution(mesh):
    in_specs = (
        P("dp", "context", None),
        P("dp", "context"),
        P(None, ("dp", "context"), None, "tensor"),
        P(None, ("dp", "context"), "tensor"),
        P(None, ("dp", "context", "tensor"), None),
        P(None, ("dp", "context", "tensor")),
        P(None, None, ("dp", "context", "tensor")),
        P(None, ("dp", "context", "tensor")),
        P(None, "tensor", ("dp", "context")),
        P(None, None, "tensor"),
        P(None, "tensor"),
        P(None, "tensor"),
        P(None, "tensor"),
        P(None, "tensor"),
        P(None, "tensor"),
        P("dp", "context", None),
    )
    out_specs = (
        P("dp", "context", None),
        P("dp", "context", None),
        P(None, ("dp", "context"), None, "tensor"),
        P(None, ("dp", "context"), "tensor"),
        P(None, ("dp", "context", "tensor"), None),
        P(None, ("dp", "context", "tensor")),
        P(None, None, ("dp", "context", "tensor")),
        P(None, ("dp", "context", "tensor")),
        P(None, "tensor", ("dp", "context")),
        P(None, None, "tensor"),
        P(None, "tensor"),
        P(None, "tensor"),
        P(None, "tensor"),
        P(None, "tensor"),
        P(None, "tensor"),
        P("dp", "context", None),
    )
    return jax.shard_map(
        local, mesh=mesh, in_specs=in_specs, out_specs=out_specs[:15], check_vma=False
    )
```

```python
import functools

import jax
import jax.numpy as jnp
from jax import lax
from jax.experimental import pallas as pl
from jax.experimental.pallas import tpu as pltpu
from jax.sharding import PartitionSpec as P

CHUNK = 128
LANES = 128
eps = 1e-05
F32 = jnp.float32
BF16 = jnp.bfloat16
HIGH = lax.Precision.HIGHEST
NN = (((1,), (0,)), ((), ()))
NT = (((1,), (1,)), ((), ()))
TN = (((0,), (0,)), ((), ()))
NO_LINK = -1e30
COST_SCALE = 0.5


def mm(a, b, dims=NN):
    return lax.dot_general(a, b, dims, preferred_element_type=F32)


def params(mib=48):
    return pltpu.CompilerParams(
        dimension_semantics=("arbitrary",), vmem_limit_bytes=mib * 1024 * 1024
    )


PRECEDING = []


def kernel_call(body, cost=2.0, **spec):
    def call(*inputs):
        tokens = list(PRECEDING)
        options = dict(spec)
        grid_spec = options.pop("grid_spec", None)
        unread = [pl.BlockSpec(memory_space=pl.ANY)] * len(tokens)
        prefetched = 0
        if grid_spec is None:
            options["in_specs"] = list(options["in_specs"]) + unread
        else:
            prefetched = grid_spec.num_scalar_prefetch
            options["grid_spec"] = pltpu.PrefetchScalarGridSpec(
                num_scalar_prefetch=prefetched,
                grid=grid_spec.grid,
                in_specs=list(grid_spec.in_specs) + unread,
                out_specs=grid_spec.out_specs,
                scratch_shapes=grid_spec.scratch_shapes,
            )
        first = len(inputs)

        def without_tokens(*refs):
            body(*refs[:first], *refs[first + len(tokens) :])

        out = pl.pallas_call(
            without_tokens,
            cost_estimate=pl.CostEstimate(
                flops=int(cost * 1.0e9 * COST_SCALE), transcendentals=0, bytes_accessed=1024
            ),
            **options,
        )(*inputs, *tokens)
        PRECEDING[:] = [min(jax.tree.leaves(out), key=lambda one: one.size * one.dtype.itemsize)]
        return out

    return call


def precede(*tokens):
    PRECEDING.extend(token for token in tokens if token is not None)


def flipped(value, axis, bit):
    count = lax.axis_size(axis)
    return lax.ppermute(value, axis, [(i, i ^ (1 << bit)) for i in range(count)])


def bits(axis):
    return (lax.axis_size(axis) - 1).bit_length()


def shifted(value, axis, steps):
    count = lax.axis_size(axis)
    leading, last = (max(0, -steps), min(count, count - steps))
    return lax.ppermute(value, axis, [(source, source + steps) for source in range(leading, last)])


def ring(value, axis):
    count = lax.axis_size(axis)
    return lax.ppermute(value, axis, [(i, (i - 1) % count) for i in range(count)])


def summed_over(value, axes):
    for axis in axes:
        for bit in range(bits(axis)):
            value = value + flipped(value, axis, bit)
    return value


def gather_small(value, axes):
    value = value[None]
    for axis in axes:
        index = lax.axis_index(axis)
        for bit in range(bits(axis)):
            other = flipped(value, axis, bit)
            upper = (index >> bit) & 1
            value = jnp.concatenate(
                [jnp.where(upper == 0, value, other), jnp.where(upper == 0, other, value)], axis=0
            )
    return value


def slots():
    count, places = bits("tensor"), []
    for m in range(lax.axis_size("tensor")):
        places.append(sum(((m >> b) & 1) << (count - 1 - b) for b in range(count)))
    return places


def rows_order(first):
    places = slots()
    if first:
        half = len(places) // 2
        places = places[half:] + places[:half]
    return jnp.array(places, jnp.int32) ^ lax.axis_index("tensor")


def own_rows(value):
    rows = value.shape[0] // lax.axis_size("tensor")
    return lax.dynamic_slice_in_dim(value, lax.axis_index("tensor") * rows, rows, 0)


def relay_kernel(from_ref, to_ref):
    to_ref[...] = from_ref[...]


def widen_kernel(from_ref, to_ref):
    to_ref[...] = from_ref[...].astype(F32)


def widened(value):
    return kernel_call(
        widen_kernel,
        grid=(1,),
        in_specs=[fixed_block(value.shape)],
        out_specs=fixed_block(value.shape),
        out_shape=jax.ShapeDtypeStruct(value.shape, F32),
        compiler_params=params(),
    )(value)


def relayed(piece, *tokens):
    precede(*tokens)
    return kernel_call(
        relay_kernel,
        grid=(1,),
        in_specs=[fixed_block(piece.shape)],
        out_specs=fixed_block(piece.shape),
        out_shape=jax.ShapeDtypeStruct(piece.shape, piece.dtype),
        compiler_params=params(),
    )(piece)


def ring_pieces(table, piece):
    def over_context(arrived):
        row = [arrived]
        for _ in range(lax.axis_size("context") - 1):
            row.append(ring(row[-1], "context"))
        return row

    arrived = piece
    table.append(over_context(piece))
    for k in range(1, lax.axis_size("dp")):
        arrived = ring(arrived, "dp")
        yield
        arrived = relayed(arrived, table[k - 1][-1])
        table.append(over_context(arrived))
    yield


def place_kernel(count, widths, tile_at, index_ref, *refs):
    pieces, outs = refs[:count], refs[count:]
    for i in range(count):
        at = 0
        for out, width in zip(outs, widths):
            out[index_ref[i]] = pieces[i][:, at : at + width]
            at += width
    if tile_at is not None:
        first, tiles = outs[0], outs[-1]
        rows = first.shape[1]
        whole_rows = jnp.concatenate(
            [first[i, :, tile_at : tile_at + LANES] for i in range(count)], axis=0
        )
        for at in range(0, count * rows, LANES):
            tiles[:, at : at + LANES] = whole_rows[at : at + LANES].astype(F32).T


def placed(table, widths, tile_at=None):
    dp, context = lax.axis_size("dp"), lax.axis_size("context")
    z, x = lax.axis_index("dp"), lax.axis_index("context")
    pieces, index = [], []
    for k, row in enumerate(table):
        for j, piece in enumerate(row):
            pieces.append(piece)
            index.append(((z + k) % dp) * context + (x + j) % context)
    count, rows = len(pieces), pieces[0].shape[0]
    out_specs = [
        pl.BlockSpec((count, rows, width), lambda i, index: (0, 0, 0)) for width in widths
    ]
    out_shape = [jax.ShapeDtypeStruct((count, rows, width), BF16) for width in widths]
    if tile_at is not None:
        out_specs.append(pl.BlockSpec((LANES, count * rows), lambda i, index: (0, 0)))
        out_shape.append(jax.ShapeDtypeStruct((LANES, count * rows), F32))
    outs = kernel_call(
        functools.partial(place_kernel, count, widths, tile_at),
        cost=3.5,
        grid_spec=pltpu.PrefetchScalarGridSpec(
            num_scalar_prefetch=1,
            grid=(1,),
            in_specs=[pl.BlockSpec(piece.shape, lambda i, index: (0, 0)) for piece in pieces],
            out_specs=out_specs,
        ),
        out_shape=out_shape,
        compiler_params=params(),
    )(jnp.stack(index).astype(jnp.int32), *pieces)
    return [
        out.reshape(count * rows, -1) if i < len(widths) else out for i, out in enumerate(outs)
    ]


def after(value, *tokens):
    tokens = tuple(token for token in tokens if token is not None)
    return lax.optimization_barrier((value, *tokens))[0] if tokens else value


def from_others(value, axis):
    count = lax.axis_size(axis)
    return [value] + [
        lax.ppermute(value, axis, [(i, i ^ step) for i in range(count)])
        for step in range(1, count)
    ]


def scatter_places(value):
    count, index = lax.axis_size("tensor"), lax.axis_index("tensor")
    value = value.reshape(count, -1, value.shape[1])
    total = lax.dynamic_index_in_dim(value, index, 0, keepdims=False)
    for step in range(1, count):
        sent = lax.dynamic_index_in_dim(value, index ^ step, 0, keepdims=False)
        total = total + lax.ppermute(sent, "tensor", [(i, i ^ step) for i in range(count)])
    return total


def pack_kernel(layers, sequences, width, *refs):
    inputs, (local_ref, shared_ref) = refs[:-2], refs[-2:]
    local_ref[...] = jnp.zeros_like(local_ref)
    shared_ref[...] = jnp.zeros_like(shared_ref)
    for layer in range(layers):
        mine = inputs[layer * sequences * 4 : (layer + 1) * sequences * 4]
        taps, acc, small, gain = (sum(one[...] for one in mine[i::4]) for i in range(4))
        local_ref[layer, 0:5, :width] = taps[0:5, :width]
        local_ref[layer, 5:7, :width] = acc[0:2]
        local_ref[layer, 0:2, width:] = small[0:2]
        shared = taps.shape[1] - width
        shared_ref[layer, 0:5, :shared] = taps[0:5, width:]
        for i, (row, at) in enumerate(gain_places(gain.shape[1], shared)):
            shared_ref[layer, row : row + 1, at : at + shared] = gain[
                0:1, i * shared : (i + 1) * shared
            ]


def gain_places(model, shared):
    places = [(5, 0), (6, 0), (7, 0)] + [(row, shared) for row in range(8)]
    return places[: model // shared]


def share_kernel(local_ref, *refs):
    cut = local_ref.shape[2]
    refs[-1][:, :, :cut] = local_ref[...]
    refs[-1][:, :, cut:] = sum(one[...] for one in refs[:-1])


def unpack_kernel(width, heads, shared, model, place_ref, a_ref, b_ref, red_ref, *outs):
    taps_x, bias_x, dt_bias, rate, skip, gate_gain, taps_bc, bias_bc, pre_gain = outs
    own_conv, own_gain = taps_bc.shape[2], pre_gain.shape[1]
    cut = width + LANES
    for layer in range(a_ref.shape[0]):
        total = a_ref[layer] + b_ref[layer]
        at = slice(layer, layer + 1)
        taps_x[layer] = total[0:4, :width]
        bias_x[at] = total[4:5, :width]
        gate_gain[at] = total[5:6, :width]
        dt_bias[at] = total[0:1, width : width + heads]
        rate[at] = total[1:2, width : width + heads]
        skip[at] = split_dot(total[:, :width], red_ref[...])[6:7, :heads]
        part = total[:, cut : cut + shared]
        part = pltpu.roll(part, shared - place_ref[0] * own_conv, axis=1)
        taps_bc[layer] = part[0:4, :own_conv]
        bias_bc[at] = part[4:5, :own_conv]
        rows = [
            total[row : row + 1, cut + col : cut + col + shared]
            for row, col in gain_places(model, shared)
        ]
        gain = jnp.broadcast_to(jnp.concatenate(rows, axis=1), (8, model))
        gain = pltpu.roll(gain, model - place_ref[0] * own_gain, axis=1)
        pre_gain[at] = gain[0:1, :own_gain]


def add_kernel(*refs):
    refs[-1][...] = sum(one[...] for one in refs[:-1])


def add_up(terms):
    shape = terms[0].shape
    return kernel_call(
        add_kernel,
        cost=1.0,
        grid=(1,),
        in_specs=[whole(shape)] * len(terms),
        out_specs=whole(shape),
        out_shape=jax.ShapeDtypeStruct(shape, terms[0].dtype),
        compiler_params=params(),
    )(*terms)


def small_sums(work, width, heads, model, red):
    layers, sequences = len(work), len(work[0])
    inputs = [k[name] for ks in work for k in ks for name in ("wacc", "acc", "hacc", "dgain")]
    shared = inputs[0].shape[1] - width
    shapes = [(layers, 8, width + LANES), (layers, 8, 2 * shared)]
    own, every = kernel_call(
        functools.partial(pack_kernel, layers, sequences, width),
        grid=(1,),
        in_specs=[whole(one.shape) for one in inputs],
        out_specs=[whole(shape) for shape in shapes],
        out_shape=[jax.ShapeDtypeStruct(shape, F32) for shape in shapes],
        compiler_params=params(),
    )(*inputs)
    parts = from_others(every, "tensor")
    yield None
    shape = (layers, 8, width + LANES + 2 * shared)
    total = kernel_call(
        share_kernel,
        cost=1.0,
        grid=(1,),
        in_specs=[whole(one.shape) for one in (own, *parts)],
        out_specs=whole(shape),
        out_shape=jax.ShapeDtypeStruct(shape, F32),
        compiler_params=params(),
    )(own, *parts)
    hops = [(axis, bit) for axis in ("context", "dp") for bit in range(bits(axis))]
    for axis, bit in hops:
        other = flipped(total, axis, bit)
        yield None
        if (axis, bit) != hops[-1]:
            total = add_up([total, other])
    devices = lax.axis_size("dp") * lax.axis_size("context") * lax.axis_size("tensor")
    place = lax.axis_index("dp") * lax.axis_size("context") + lax.axis_index("context")
    place = place * lax.axis_size("tensor") + lax.axis_index("tensor")
    own_conv, own_gain = shared // devices, model // devices
    shapes = [
        (layers, 4, width), (layers, width), (layers, heads), (layers, heads), (layers, heads),
        (layers, width), (layers, 4, own_conv), (layers, own_conv), (layers, own_gain),
    ]
    yield kernel_call(
        functools.partial(unpack_kernel, width, heads, shared, model),
        grid_spec=pltpu.PrefetchScalarGridSpec(
            num_scalar_prefetch=1,
            grid=(1,),
            in_specs=[fixed_block(one.shape) for one in (total, other, red)],
            out_specs=[fixed_block(one) for one in shapes],
        ),
        out_shape=[jax.ShapeDtypeStruct(one, F32) for one in shapes],
        compiler_params=params(),
    )(place.astype(jnp.int32)[None], total, other, red)


def silu_parts(value):
    sig = jax.nn.sigmoid(value)
    return value * sig, sig


def softplus(value):
    return jnp.maximum(value, 0.0) + jnp.log1p(jnp.exp(-jnp.abs(value)))


def split_dot(value, table):
    high = value.astype(BF16)
    low = (value - high.astype(F32)).astype(BF16)
    return mm(high, table) + mm(low, table)


def wide_mm(a, b, dims=NN):
    a_high, b_high = a.astype(BF16), b.astype(BF16)
    a_low = (a - a_high.astype(F32)).astype(BF16)
    b_low = (b - b_high.astype(F32)).astype(BF16)
    return mm(a_high, b_high, dims) + (mm(a_low, b_high, dims) + mm(a_high, b_low, dims))


def low_mm(a, b, dims=NN):
    return mm(a.astype(BF16), b.astype(BF16), dims)


def iota(axis):
    return lax.broadcasted_iota(jnp.int32, (CHUNK, CHUNK), axis)


def rounded(value):
    return value.astype(BF16).astype(F32)


def head_halves(tile, lower):
    zero = jnp.zeros_like(tile)
    return jnp.concatenate([jnp.where(lower, tile, zero), jnp.where(lower, zero, tile)], axis=0)


def column_of(rows):
    pad = jnp.zeros((CHUNK - rows.shape[0], CHUNK), F32)
    return jnp.concatenate([rows, pad], axis=0).T


def row_norm(wide):
    return lax.rsqrt(jnp.mean(wide * wide, axis=-1, keepdims=True) + eps)


def columns(array, at, width):
    return pl.BlockSpec((array.shape[0], width), lambda i, *_: (0, at))


def fixed_block(shape):
    return pl.BlockSpec(shape, lambda i, *_: (0,) * len(shape))


def project_kernel(norm, count, width, order_ref, *refs):
    pieces, rest = refs[:count], refs[count:]
    if norm:
        gain_ref, halo_ref, rest = rest[0], rest[1], rest[2:]
    w_ref, normed_ref, proj_ref, rim_ref, halo = rest
    step = pl.program_id(0)
    length, size = proj_ref.shape

    @pl.when(step == 0)
    def _():
        for m in range(length // CHUNK):
            if norm:
                wide = pieces[0][0, m * CHUNK : (m + 1) * CHUNK].astype(F32)
                rows = (wide * row_norm(wide) * gain_ref[...]).astype(BF16)
                normed_ref[m * CHUNK : (m + 1) * CHUNK] = rows
            else:
                place = pl.ds(pl.multiple_of(order_ref[m] * CHUNK, CHUNK), CHUNK)
                normed_ref[place] = pieces[m][...]
        if norm:
            wide = halo_ref[0].astype(F32)
            halo[...] = (wide * row_norm(wide) * gain_ref[...]).astype(BF16)
        else:
            halo[...] = normed_ref[length - 16 :]

    weight = w_ref[...]
    proj_ref[...] = mm(normed_ref[...], weight)
    tail = mm(halo[...], weight)[8:].astype(BF16)
    for i in range(width // size):

        @pl.when(step == i)
        def _(i=i):
            rim_ref[:, i * size : (i + 1) * size] = tail

    @pl.when(step == width // size)
    def _():
        rim_ref[:, width:] = tail[:, LANES:]


def project(source, gain, order, front, width, total):
    weights, at = front
    third = total // 3
    norm = gain is not None
    if norm:
        stream, halo, sequence = source
        model, length = stream.shape[2], stream.shape[1]
        inputs, count = [stream, gain, halo], 1
        specs = [
            pl.BlockSpec((1, length, model), lambda i, order: (sequence, 0, 0)),
            fixed_block((1, model)),
            pl.BlockSpec((1, 16, model), lambda i, order: (sequence, 0, 0)),
        ]
    else:
        model, count = source[0][0].shape[1], len(source)
        length = count * CHUNK
        inputs, specs = [one for one, _ in source], piece_specs(source, CHUNK)
    conv = total - LANES
    return kernel_call(
        functools.partial(project_kernel, norm, count, width),
        cost=5.0,
        grid_spec=pltpu.PrefetchScalarGridSpec(
            num_scalar_prefetch=1,
            grid=(3,),
            in_specs=specs + [pl.BlockSpec((model, third), lambda i, order: (0, at + i))],
            out_specs=[
                fixed_block((length, model)),
                pl.BlockSpec((length, third), lambda i, order: (0, i)),
                fixed_block((8, conv)),
            ],
            scratch_shapes=[pltpu.VMEM((16, model), BF16)],
        ),
        out_shape=[
            jax.ShapeDtypeStruct((length, model), BF16),
            jax.ShapeDtypeStruct((length, total), F32),
            jax.ShapeDtypeStruct((8, conv), BF16),
        ],
        compiler_params=params(),
    )(order, *inputs, weights)


def plain_kernel(a_ref, w_ref, out_ref):
    out_ref[...] = mm(a_ref[...], w_ref[...])


def plain_product(a, weight, width):
    weights, at = weight
    length, model = a.shape
    half = width // 2
    return kernel_call(
        plain_kernel,
        cost=3.0,
        grid=(2,),
        in_specs=[
            fixed_block((length, model)),
            pl.BlockSpec((model, half), lambda i: (0, 2 * at + i)),
        ],
        out_specs=pl.BlockSpec((length, half), lambda i: (0, i)),
        out_shape=jax.ShapeDtypeStruct((length, width), F32),
        compiler_params=params(),
    )(a, weights)


def rows_of(ref):
    return (ref[...] if len(ref.shape) == 2 else ref[0]).astype(F32)


def norm_forward_kernel(place_ref, stream_ref, keep_ref, first_ref, second_ref, *refs):
    total = keep_ref[0].astype(F32) + first_ref[0].astype(F32) + second_ref[...].astype(F32)
    new = rows_of(stream_ref) + total
    if len(refs) == 1:
        refs[0][...] = new.astype(BF16)
    else:
        gain_ref, new_ref, low_ref = refs
        new_ref[...] = new
        low_ref[...] = (new * row_norm(new) * gain_ref[...]).astype(BF16)


def join_kernel(own_ref, other_ref, out_ref):
    rows = own_ref.shape[0]
    out_ref[:rows] = own_ref[...]
    out_ref[rows:] = other_ref[...]


def joined_rows(own, other):
    rows, model = own.shape
    return kernel_call(
        join_kernel,
        grid=(1,),
        in_specs=[fixed_block((rows, model))] * 2,
        out_specs=fixed_block((2 * rows, model)),
        out_shape=jax.ShapeDtypeStruct((2 * rows, model), own.dtype),
        compiler_params=params(),
    )(own, other)


def piece_specs(pieces, rows):
    return [pl.BlockSpec((rows, one.shape[1]), lambda i, *_, at=at: (at, 0)) for one, at in pieces]


def pass_on_kernel(keep_ref, first_ref, out_ref):
    total = keep_ref[0].astype(F32) + first_ref[0].astype(F32)
    out_ref[...] = total.astype(out_ref.dtype)


def pass_on(kept, first):
    _, rows, model = kept.shape
    spec = pl.BlockSpec((1, rows, model), lambda i: (1, 0, 0))
    return kernel_call(
        pass_on_kernel,
        grid=(1,),
        in_specs=[spec, spec],
        out_specs=fixed_block((rows, model)),
        out_shape=jax.ShapeDtypeStruct((rows, model), kept.dtype),
        compiler_params=params(),
    )(kept, first)


def rows_spec(one, rows):
    if isinstance(one, tuple):
        array, s = one
        return array, pl.BlockSpec((1, rows, array.shape[2]), lambda i, place: (s, place[0], 0))
    return one, fixed_block(one.shape)


def term_specs(rows, model):
    part = fixed_block((1, rows, model))
    return [part, part, fixed_block((rows, model))]


def norm_forward(stream, terms, gain, place):
    rows, model = terms[2].shape
    stream, spec = rows_spec(stream, rows)
    low = jax.ShapeDtypeStruct((rows, model), BF16)
    last = gain is None
    return kernel_call(
        norm_forward_kernel,
        grid_spec=pltpu.PrefetchScalarGridSpec(
            num_scalar_prefetch=1,
            grid=(1,),
            in_specs=[spec]
            + term_specs(rows, model)
            + ([] if last else [fixed_block((1, model))]),
            out_specs=[fixed_block((rows, model))] * (1 if last else 2),
        ),
        out_shape=[low] if last else [jax.ShapeDtypeStruct((rows, model), F32), low],
        compiler_params=params(),
    )(place, stream, *terms, *([] if last else [gain]))


def norm_backward_kernel(
    place_ref, stream_ref, keep_ref, first_ref, second_ref, grad_ref, gain_ref, new_ref, low_ref,
    dgain_ref,
):
    total = keep_ref[0].astype(F32) + first_ref[0].astype(F32) + second_ref[...].astype(F32)
    current = rows_of(stream_ref)
    scale = row_norm(current)
    unit = current * scale
    dgain_ref[...] = jnp.broadcast_to(
        jnp.sum(total * unit, axis=0, keepdims=True), dgain_ref.shape
    )
    pulled = total * gain_ref[...]
    shift = jnp.mean(pulled * unit, axis=-1, keepdims=True)
    new = rows_of(grad_ref) + scale * (pulled - unit * shift)
    new_ref[...] = new
    low_ref[...] = new.astype(BF16)


def norm_backward(stream, terms, grad, gain, place):
    rows, model = terms[2].shape
    stream, stream_spec = rows_spec(stream, rows)
    grad, grad_spec = rows_spec(grad, rows)
    return kernel_call(
        norm_backward_kernel,
        grid_spec=pltpu.PrefetchScalarGridSpec(
            num_scalar_prefetch=1,
            grid=(1,),
            in_specs=[stream_spec]
            + term_specs(rows, model)
            + [grad_spec, fixed_block((1, model))],
            out_specs=[fixed_block((rows, model))] * 2 + [fixed_block((8, model))],
        ),
        out_shape=[
            jax.ShapeDtypeStruct((rows, model), F32),
            jax.ShapeDtypeStruct((rows, model), BF16),
            jax.ShapeDtypeStruct((8, model), F32),
        ],
        compiler_params=params(),
    )(place, stream, *terms, grad, gain)


def assemble_kernel(count, order_ref, *refs):
    step = pl.program_id(0)
    for m in range(count):

        @pl.when(step == m)
        def _(m=m):
            refs[-1][0] = refs[m][...]


def assembled(groups, order):
    each, (rows, model) = len(groups[0]), groups[0][0][0].shape
    pieces = [piece for group in groups for piece in group]
    count = len(pieces)
    return kernel_call(
        functools.partial(assemble_kernel, count),
        cost=5.0,
        grid_spec=pltpu.PrefetchScalarGridSpec(
            num_scalar_prefetch=1,
            grid=(count,),
            in_specs=piece_specs(pieces, rows),
            out_specs=pl.BlockSpec(
                (1, rows, model), lambda i, order: (i // each, order[i % each], 0)
            ),
        ),
        out_shape=jax.ShapeDtypeStruct((len(groups), each * rows, model), BF16),
        compiler_params=params(),
    )(order, *[one for one, _ in pieces])


def input_grad_kernel(parts, width, order_ref, dproj_ref, dgate_ref, tail_ref, rim_ref, *refs):
    w_refs, gate_ref, sent_ref, kept_ref, fixed_ref, rows_p, rows_g = refs[:3], *refs[3:]
    half = parts // 2

    @pl.when(pl.program_id(0) == 0)
    def _():
        fixed_ref[...] = dproj_ref[...]
        tail = (tail_ref[...] + rim_ref[...]).astype(BF16)
        fixed_ref[parts * CHUNK - 16 :, :width] = tail[:, :width]
        fixed_ref[parts * CHUNK - 16 :, width + LANES :] = tail[:, width:]
        for m in range(parts):
            source = pl.ds(pl.multiple_of(order_ref[m] * CHUNK, CHUNK), CHUNK)
            rows_p[m * CHUNK : (m + 1) * CHUNK] = fixed_ref[source]
            rows_g[m * CHUNK : (m + 1) * CHUNK] = dgate_ref[source]

    total = mm(rows_g[...], gate_ref[...], NT)
    for j, w_ref in enumerate(w_refs):
        size = w_ref.shape[1]
        total = total + mm(rows_p[:, j * size : (j + 1) * size], w_ref[...], NT)
    total = total.astype(BF16)
    for m in range(half):
        sent_ref[m] = total[m * CHUNK : (m + 1) * CHUNK]
        kept_ref[m] = total[(half + m) * CHUNK : (half + m + 1) * CHUNK]


def input_grad(dproj, dgate, tail, rim, front, gate, order):
    length, total = dproj.shape
    width = dgate.shape[1]
    (front_w, at), (gate_w, gate_at) = front, gate
    model, third, parts = front_w.shape[0], total // 3, length // CHUNK
    cut = model // 4
    half = pl.BlockSpec((parts // 2, CHUNK, cut), lambda i, order: (0, 0, i))

    def rows(offset, size):
        return pl.BlockSpec((cut, size), lambda i, order: (i, offset))

    return kernel_call(
        functools.partial(input_grad_kernel, parts, width),
        cost=7.6,
        grid_spec=pltpu.PrefetchScalarGridSpec(
            num_scalar_prefetch=1,
            grid=(4,),
            in_specs=[fixed_block(one.shape) for one in (dproj, dgate, tail, rim)]
            + [rows(at + j, third) for j in range(3)]
            + [rows(gate_at, width)],
            out_specs=[half, half, fixed_block((length, total))],
            scratch_shapes=[
                pltpu.VMEM((length, total), BF16),
                pltpu.VMEM((length, width), BF16),
            ],
        ),
        out_shape=[jax.ShapeDtypeStruct((parts // 2, CHUNK, model), BF16)] * 2
        + [jax.ShapeDtypeStruct((length, total), BF16)],
        compiler_params=params(),
    )(order, dproj, dgate, tail, rim, front_w, front_w, front_w, gate_w)


def weight_grad_kernel(segments, sequences, rows, places, order_ref, *refs):
    lefts, rights = refs[: segments * sequences], refs[segments * sequences :]
    rights, outs, total = rights[: segments * sequences], rights[segments * sequences : -1], refs[-1]
    at = 0
    for g in range(segments):
        width = rights[g * sequences].shape[1]
        part = None
        for s in range(sequences):
            left = lefts[g * sequences + s]
            left = left[...] if len(left.shape) == 2 else left[0]
            one = mm(left, rights[g * sequences + s][...], TN)
            part = one if part is None else part + one
        total[:, at : at + width] = part
        at += width
    if places is None:
        outs[0][...] = total[...].astype(BF16)
        return
    dp, context = places
    slot = lax.rem(pl.program_id(0) - order_ref[1] + dp, dp)

    def block(j):
        start = lax.rem(order_ref[0] + j, context) * rows
        return total[pl.ds(pl.multiple_of(start, 8), rows)].astype(BF16)

    outs[0][0] = block(0)
    for j in range(1, context):
        for k in range(dp):

            @pl.when(slot == k)
            def _(j=j, k=k):
                outs[1 + (j - 1) * dp + k][...] = block(j)


def weight_grad(pairs, ordered):
    dp, context = lax.axis_size("dp"), lax.axis_size("context")
    sequences, length = len(pairs[0][0]), pairs[0][1][0].shape[0]
    widths = [right[0].shape[1] for _, right in pairs]
    lefts = [one for left, _ in pairs for one in left]
    rights = [one for _, right in pairs for one in right]
    model = lefts[0].shape[-1]
    total, cut = sum(widths), model // dp
    rows = cut // context
    order = jnp.stack([lax.axis_index("context"), lax.axis_index("dp")]).astype(jnp.int32)
    if ordered:
        others = (context - 1) * dp
        out_specs = [
            pl.BlockSpec(
                (1, rows, total), lambda i, order: (lax.rem(i - order[1] + dp, dp), 0, 0)
            )
        ] + [fixed_block((rows, total))] * others
        out_shape = [jax.ShapeDtypeStruct((dp, rows, total), BF16)] + [
            jax.ShapeDtypeStruct((rows, total), BF16)
        ] * others
    else:
        out_specs = [pl.BlockSpec((cut, total), lambda i, order: (i, 0))]
        out_shape = [jax.ShapeDtypeStruct((model, total), BF16)]
    left_specs, left_arrays = [], []
    for left in lefts:
        if isinstance(left, tuple):
            left_arrays.append(left[0])
            left_specs.append(
                pl.BlockSpec((1, length, cut), lambda i, order, s=left[1]: (s, 0, i))
            )
        else:
            left_arrays.append(left)
            left_specs.append(pl.BlockSpec((length, cut), lambda i, order: (0, i)))
    return kernel_call(
        functools.partial(
            weight_grad_kernel, len(pairs), sequences, rows, (dp, context) if ordered else None
        ),
        cost=10.0,
        grid_spec=pltpu.PrefetchScalarGridSpec(
            num_scalar_prefetch=1,
            grid=(dp,),
            in_specs=left_specs + [fixed_block(one.shape) for one in rights],
            out_specs=out_specs,
            scratch_shapes=[pltpu.VMEM((cut, total), F32)],
        ),
        out_shape=out_shape,
        compiler_params=params(56),
    )(order, *left_arrays, *rights)


def ring_add_kernel(own_ref, *refs):
    total = own_ref[0].astype(F32)
    for one in refs[:-1]:
        total = total + one[...].astype(F32)
    refs[-1][...] = total.astype(refs[-1].dtype)


def ring_add(own, k, terms, kind):
    _, rows, width = own.shape
    return kernel_call(
        ring_add_kernel,
        cost=1.5,
        grid=(1,),
        in_specs=[pl.BlockSpec((1, rows, width), lambda i: (k, 0, 0))]
        + [fixed_block((rows, width))] * len(terms),
        out_specs=fixed_block((rows, width)),
        out_shape=jax.ShapeDtypeStruct((rows, width), kind),
        compiler_params=params(),
    )(own, *terms)


def ring_steps(blocks):
    dp, context = lax.axis_size("dp"), lax.axis_size("context")
    own, others = blocks[0], blocks[1:]
    places = list(range(1, dp)) + [0]
    sides = []
    for k in places:
        side = None
        for j in range(1, context):
            part = others[(j - 1) * dp + k]
            if side is not None:
                part = (side.astype(F32) + part.astype(F32)).astype(BF16)
            side = ring(part, "context")
        sides.append([] if side is None else [side])
    passed = []
    for k, side in zip(places, sides):
        value = ring_add(own, k, side + passed, BF16 if k else F32)
        if k:
            passed = [ring(value, "dp")]
            yield None
        else:
            yield value


def scan_forward_kernel(
    heads, width, p_ref, rim_ref, marks_ref, cw_ref, hp_ref, skip_ref, exp_ref,
    z_ref, y_ref, st_ref, end_ref, gr_ref, vbuf, state, offset,
):
    chunk = pl.program_id(0)
    aux = column_of(marks_ref[...])

    @pl.when(chunk == 0)
    def _():
        vbuf[0:8] = rim_ref[...].astype(F32)
        state[...] = jnp.zeros_like(state)
        offset[...] = jnp.zeros_like(offset)

    @pl.when(chunk > 0)
    def _():
        vbuf[0:8] = vbuf[CHUNK : CHUNK + 8]

    vbuf[8:, :width] = rounded(p_ref[:, :width])
    vbuf[8:, width:] = rounded(p_ref[:, width + LANES :])
    z = cw_ref[4:5] + cw_ref[3:4] * vbuf[8:]
    for k in range(3):
        z = z + cw_ref[k : k + 1] * vbuf[5 + k : 5 + k + CHUNK] * aux[:, k : k + 1]
    z_ref[...] = z
    act = z * jax.nn.sigmoid(z)
    x = act[:, :width]
    b_val, c_val = act[:, width : width + LANES], act[:, width + LANES :]
    lane = iota(1)
    step = jnp.where(
        lane < heads, softplus(p_ref[:, width : width + LANES] + hp_ref[0:1]), 0.0
    )
    decay = hp_ref[1:2] * step
    cum = lax.dot_general(
        (iota(0) >= iota(1)).astype(F32), decay, NN, precision=HIGH, preferred_element_type=F32
    )
    cum_t = cum.T
    seg_col = aux[:, 5:6]
    link = jnp.where((seg_col == marks_ref[5:6]) & (iota(0) >= iota(1)), 0.0, NO_LINK)
    scores = wide_mm(c_val, b_val, NT)
    growth = jnp.exp(cum) * aux[:, 3:4]
    last = cum[CHUNK - 1 : CHUNK]
    weight = jnp.exp(last - cum) * (seg_col == seg_col[CHUNK - 1 : CHUNK]).astype(F32)
    wide = split_dot(jnp.concatenate([step, growth, weight], axis=0), exp_ref[...])
    step_e, growth_e, weight_e = wide[:CHUNK], wide[CHUNK : 2 * CHUNK], wide[2 * CHUNK :]
    xd = x * step_e
    lower = lane < LANES // 2
    pieces = []
    for pair in range(heads // 2):
        mats = []
        for head in (2 * pair, 2 * pair + 1):
            spread = cum[:, head : head + 1] - cum_t[head : head + 1, :]
            mats.append(jnp.exp(spread + link) * scores)
        tile = xd[:, pair * LANES : (pair + 1) * LANES]
        pieces.append(wide_mm(jnp.concatenate(mats, axis=1), head_halves(tile, lower)))
    held = state[...]
    st_ref[0] = held
    carried = wide_mm(c_val, held) * growth_e
    y_ref[...] = jnp.concatenate(pieces, axis=1) + carried + skip_ref[...] * x
    new = held * growth_e[CHUNK - 1 : CHUNK] + wide_mm(b_val, xd * weight_e, TN)
    state[...] = new
    end_ref[...] = new
    gr_ref[...] = jnp.exp(offset[...] + cum) * aux[:, 4:5]
    offset[...] = offset[...] + last


def row_spec(width, at=None, rows=CHUNK):
    if at is None:
        return pl.BlockSpec((rows, width), lambda i: (i, 0))
    return pl.BlockSpec((rows, width), lambda i: (i, at))


def whole(shape):
    return pl.BlockSpec(shape, lambda i: (0,) * len(shape))


def scan_forward(proj, rim, marks, consts):
    length, total = proj.shape
    heads, width = consts["heads"], consts["width"]
    chunks, conv = length // CHUNK, total - LANES
    return kernel_call(
        functools.partial(scan_forward_kernel, heads, width),
        cost=9.5,
        grid=(chunks,),
        in_specs=[
            row_spec(total),
            whole((8, conv)),
            pl.BlockSpec((8, CHUNK), lambda i: (0, i)),
            whole((8, conv)),
            whole((8, LANES)),
            whole((1, width)),
            whole((LANES, width)),
        ],
        out_specs=[
            row_spec(conv),
            row_spec(width),
            pl.BlockSpec((1, LANES, width), lambda i: (i, 0, 0)),
            whole((LANES, width)),
            row_spec(LANES),
        ],
        out_shape=[
            jax.ShapeDtypeStruct((length, conv), F32),
            jax.ShapeDtypeStruct((length, width), F32),
            jax.ShapeDtypeStruct((chunks, LANES, width), F32),
            jax.ShapeDtypeStruct((LANES, width), F32),
            jax.ShapeDtypeStruct((length, LANES), F32),
        ],
        scratch_shapes=[
            pltpu.VMEM((CHUNK + 8, conv), F32),
            pltpu.VMEM((LANES, width), F32),
            pltpu.VMEM((1, LANES), F32),
        ],
        compiler_params=params(),
    )(proj, rim, marks, consts["cw"], consts["hp"], consts["skip"], consts["exp"])


def mix_forward_kernel(y0_ref, zc_ref, gr_ref, sin_ref, gate_ref, exp_ref, y_ref, sq_ref):
    c_val = zc_ref[...] * jax.nn.sigmoid(zc_ref[...])
    carried = wide_mm(c_val, sin_ref[...].astype(F32))
    y = y0_ref[...] + carried * split_dot(gr_ref[...], exp_ref[...])
    y_ref[...] = y
    gate = gate_ref[...]
    gated = y * (gate * jax.nn.sigmoid(gate))
    square = jnp.sum(gated * gated, axis=1, keepdims=True)
    sq_ref[...] = jnp.broadcast_to(square, (CHUNK, CHUNK)).T[:8]


def mix_forward(y0, z, growth, carried, gate, consts):
    length, width = y0.shape
    last = z.shape[1] // LANES - 1
    return kernel_call(
        mix_forward_kernel,
        cost=3.6,
        grid=(length // CHUNK,),
        in_specs=[
            row_spec(width),
            row_spec(LANES, last),
            row_spec(LANES),
            whole((LANES, width)),
            row_spec(width),
            whole((LANES, width)),
        ],
        out_specs=[row_spec(width), pl.BlockSpec((8, CHUNK), lambda i: (0, i))],
        out_shape=[
            jax.ShapeDtypeStruct((length, width), F32),
            jax.ShapeDtypeStruct((8, length), F32),
        ],
        compiler_params=params(),
    )(y0, z, growth, carried, gate, consts["exp"])


def project_out_kernel(channels, parts, order_ref, y_ref, gate_ref, gain_ref, w_ref, *refs):
    squares, (sent_ref, kept_ref, rows) = refs[:-3], refs[-3:]
    half = parts // 2

    @pl.when(pl.program_id(0) == 0)
    def _():
        for m in range(parts):
            source = pl.ds(pl.multiple_of(order_ref[m] * CHUNK, CHUNK), CHUNK)
            square = sum(one[:, source] for one in squares)
            scale = lax.rsqrt(column_of(square)[:, 1:2] / channels + eps)
            gate = gate_ref[source]
            gated = y_ref[source] * (gate * jax.nn.sigmoid(gate))
            rows[m * CHUNK : (m + 1) * CHUNK] = (gated * scale * gain_ref[...]).astype(BF16)

    total = mm(rows[...], w_ref[...], NT).astype(sent_ref.dtype)
    for m in range(half):
        sent_ref[m] = total[m * CHUNK : (m + 1) * CHUNK]
        kept_ref[m] = total[(half + m) * CHUNK : (half + m + 1) * CHUNK]


def project_out(y, gate, squares, channels, kind, order, consts):
    length, width = y.shape
    weights, at = consts["out"]
    model, parts = weights.shape[0], length // CHUNK
    cut = model // 4
    half = pl.BlockSpec((parts // 2, CHUNK, cut), lambda i, order: (0, 0, i))
    return kernel_call(
        functools.partial(project_out_kernel, float(channels), parts),
        cost=5.7,
        grid_spec=pltpu.PrefetchScalarGridSpec(
            num_scalar_prefetch=1,
            grid=(4,),
            in_specs=[
                fixed_block((length, width)),
                fixed_block((length, width)),
                fixed_block((1, width)),
                pl.BlockSpec((cut, width), lambda i, order: (i, at)),
            ]
            + [fixed_block((8, length))] * len(squares),
            out_specs=[half, half],
            scratch_shapes=[pltpu.VMEM((length, width), BF16)],
        ),
        out_shape=[jax.ShapeDtypeStruct((parts // 2, CHUNK, model), kind)] * 2,
        compiler_params=params(),
    )(order, y, gate, consts["gain"], weights, *squares)


def grad_scaled_kernel(count, order_ref, *refs):
    pieces, rest = refs[:count], refs[count:]
    w_ref, y_ref, gate_ref, gain_ref, gs_ref, dot_ref = rest[:6]
    sums = rest[-1]
    step = pl.program_id(0)
    length = gs_ref.shape[0]
    if count > 1:

        @pl.when(step == 0)
        def _():
            for m in range(count):
                place = pl.ds(pl.multiple_of(order_ref[m] * CHUNK, CHUNK), CHUNK)
                rest[6][place] = pieces[m][...]

        rows = rest[6][...]
    else:
        rows = pieces[0][0]
    grad = mm(rows, w_ref[...])
    gs_ref[...] = grad
    gate = gate_ref[...]
    gated = y_ref[...] * (gate * jax.nn.sigmoid(gate))
    product = jnp.sum(grad * gain_ref[...] * gated, axis=1, keepdims=True)
    square = jnp.sum(gated * gated, axis=1, keepdims=True)
    lane = lax.broadcasted_iota(jnp.int32, (length, LANES), 1)
    part = jnp.where(lane == 0, product, square)

    @pl.when(step == 0)
    def _():
        sums[...] = part

    @pl.when(step > 0)
    def _():
        sums[...] += part

    @pl.when(step == pl.num_programs(0) - 1)
    def _():
        for m in range(length // CHUNK):
            at = slice(m * CHUNK, (m + 1) * CHUNK)
            dot_ref[:, at] = sums[at].T[:8]


def grad_scaled(source, y, gate, order, consts):
    length, width = y.shape
    weights, at = consts["out"]
    model, half = weights.shape[0], width // 2
    part = pl.BlockSpec((length, half), lambda i, order: (0, i))
    out_specs = [part, fixed_block((8, length))]
    out_shape = [
        jax.ShapeDtypeStruct((length, width), F32),
        jax.ShapeDtypeStruct((8, length), F32),
    ]
    if len(source) == 2:
        stream, sequence = source
        inputs, count = [stream], 1
        specs = [pl.BlockSpec((1, length, model), lambda i, order: (sequence, 0, 0))]
    else:
        inputs, count = [one for one, _ in source], len(source)
        specs = piece_specs(source, CHUNK)
        out_specs.append(fixed_block((length, model)))
        out_shape.append(jax.ShapeDtypeStruct((length, model), BF16))
    out = kernel_call(
        functools.partial(grad_scaled_kernel, count),
        cost=4.5,
        grid_spec=pltpu.PrefetchScalarGridSpec(
            num_scalar_prefetch=1,
            grid=(2,),
            in_specs=specs
            + [
                pl.BlockSpec((model, half), lambda i, order: (0, 2 * at + i)),
                part,
                part,
                pl.BlockSpec((1, half), lambda i, order: (0, i)),
            ],
            out_specs=out_specs,
            scratch_shapes=[pltpu.VMEM((length, LANES), F32)],
        ),
        out_shape=out_shape,
        compiler_params=params(),
    )(order, *inputs, weights, y, gate, consts["gain"])
    return out if count > 1 else (*out, source)


def mix_backward_kernel(
    channels, shares, gs_ref, y_ref, gate_ref, zx_ref, zc_ref, gr_ref, gain_ref, exp_ref, *refs
):
    shared, refs = refs[:shares], refs[shares:]
    scaled_ref, dgate_ref, dy_ref, acc_ref, dsin_ref, dsin = refs
    at = pl.program_id(0)

    @pl.when(at == 0)
    def _():
        acc_ref[...] = jnp.zeros_like(acc_ref)
        dsin[...] = jnp.zeros_like(dsin)

    stats = column_of(sum(one[...] for one in shared))
    scale = lax.rsqrt(stats[:, 1:2] / channels + eps)
    pull = scale * scale * scale * stats[:, 0:1] / channels
    grad, y, gate = gs_ref[...], y_ref[...], gate_ref[...]
    silu, sig = silu_parts(gate)
    gated = y * silu
    unit = gated * scale
    scaled_ref[...] = (unit * gain_ref[...]).astype(BF16)
    dgated = grad * gain_ref[...] * scale - gated * pull
    dy = dgated * silu
    dy_ref[...] = dy
    dgate_ref[...] = (dgated * y * (sig * (1.0 + gate * (1.0 - sig)))).astype(BF16)
    x = zx_ref[...] * jax.nn.sigmoid(zx_ref[...])
    acc_ref[0:1] += jnp.sum(grad * unit, axis=0, keepdims=True)
    acc_ref[1:2] += jnp.sum(dy * x, axis=0, keepdims=True)
    c_low = (zc_ref[...] * jax.nn.sigmoid(zc_ref[...])).astype(BF16)
    dsin[...] += mm(c_low, (dy * split_dot(gr_ref[...], exp_ref[...])).astype(BF16), TN)

    @pl.when(at == pl.num_programs(0) - 1)
    def _():
        dsin_ref[...] = dsin[...].astype(BF16)


def mix_backward(grad, y, gate, z, growth, stats, channels, consts):
    length, width = y.shape
    last = z.shape[1] // LANES - 1
    stat = pl.BlockSpec((8, CHUNK), lambda i: (0, i))
    return kernel_call(
        functools.partial(mix_backward_kernel, float(channels), len(stats)),
        cost=5.0,
        grid=(length // CHUNK,),
        in_specs=[
            row_spec(width),
            row_spec(width),
            row_spec(width),
            row_spec(width),
            row_spec(LANES, last),
            row_spec(LANES),
            whole((1, width)),
            whole((LANES, width)),
        ]
        + [stat] * len(stats),
        out_specs=[
            row_spec(width),
            row_spec(width),
            row_spec(width),
            whole((8, width)),
            whole((LANES, width)),
        ],
        out_shape=[
            jax.ShapeDtypeStruct((length, width), BF16),
            jax.ShapeDtypeStruct((length, width), BF16),
            jax.ShapeDtypeStruct((length, width), F32),
            jax.ShapeDtypeStruct((8, width), F32),
            jax.ShapeDtypeStruct((LANES, width), BF16),
        ],
        scratch_shapes=[pltpu.VMEM((LANES, width), F32)],
        compiler_params=params(),
    )(grad, y, gate, z, z, growth, consts["gain"], consts["exp"], *stats)


def scan_backward_kernel(
    heads, width, chunks, dy_ref, z_ref, p_ref, before_ref, rim_ref, marks_ref, cw_ref,
    hp_ref, skip_ref, exp_ref, red_ref, st_ref, sin_ref, grprev_ref, dend_ref,
    dproj_ref, wacc_ref, hacc_ref, tail_ref, drim_ref, vbuf, zbuf, dstate,
):
    step_at = pl.program_id(0)
    chunk = chunks - 1 - step_at
    aux = column_of(marks_ref[...])

    @pl.when(step_at == 0)
    def _():
        dstate[...] = dend_ref[...].astype(F32)
        zbuf[...] = jnp.zeros_like(zbuf)
        wacc_ref[...] = jnp.zeros_like(wacc_ref)
        hacc_ref[...] = jnp.zeros_like(hacc_ref)

    @pl.when(chunk == 0)
    def _():
        vbuf[0:8] = rim_ref[...].astype(F32)

    @pl.when(chunk > 0)
    def _():
        vbuf[0:8, :width] = rounded(before_ref[:, :width])
        vbuf[0:8, width:] = rounded(before_ref[:, width + LANES :])

    vbuf[8:, :width] = rounded(p_ref[:, :width])
    vbuf[8:, width:] = rounded(p_ref[:, width + LANES :])

    z = z_ref[...]
    act, sig = silu_parts(z)
    slope = sig * (1.0 + z * (1.0 - sig))
    x = act[:, :width]
    b_val, c_val = act[:, width : width + LANES], act[:, width + LANES :]
    lane = iota(1)
    pre = p_ref[:, width : width + LANES] + hp_ref[0:1]
    step = jnp.where(lane < heads, softplus(pre), 0.0)
    decay = hp_ref[1:2] * step
    cum = lax.dot_general(
        (iota(0) >= iota(1)).astype(F32), decay, NN, precision=HIGH, preferred_element_type=F32
    )
    cum_t = cum.T
    seg_col = aux[:, 5:6]
    link = jnp.where((seg_col == marks_ref[5:6]) & (iota(0) <= iota(1)), 0.0, NO_LINK)
    growth = jnp.exp(cum) * aux[:, 3:4]
    last = cum[CHUNK - 1 : CHUNK]
    weight = jnp.exp(last - cum) * (seg_col == seg_col[CHUNK - 1 : CHUNK]).astype(F32)
    reach = jnp.where(chunk == 0, 1.0, grprev_ref[7:8])
    wide = split_dot(
        jnp.concatenate([step, growth, weight, jnp.broadcast_to(reach, (8, LANES))], axis=0),
        exp_ref[...],
    )
    step_e, growth_e = wide[:CHUNK], wide[CHUNK : 2 * CHUNK]
    weight_e, reach_e = wide[2 * CHUNK : 3 * CHUNK], wide[3 * CHUNK : 3 * CHUNK + 1]
    held = st_ref[0] + sin_ref[...].astype(F32) * reach_e
    after = dstate[...]
    xd = x * step_e
    dy = dy_ref[...]
    scores = wide_mm(b_val, c_val, NT)
    carried = low_mm(c_val, held) * growth_e
    fed = low_mm(b_val, after) * weight_e
    dy_grown = dy * growth_e
    lower = lane < LANES // 2
    dscores = jnp.zeros((CHUNK, CHUNK), F32)
    into = jnp.zeros((CHUNK, CHUNK), F32)
    rows, pieces = [], []
    for pair in range(heads // 2):
        at = slice(pair * LANES, (pair + 1) * LANES)
        products = wide_mm(head_halves(xd[:, at], lower), dy[:, at], NT)
        mats = []
        for side, head in enumerate((2 * pair, 2 * pair + 1)):
            spread = cum_t[head : head + 1, :] - cum[:, head : head + 1]
            reachable = jnp.exp(spread + link)
            product = products[side * CHUNK : (side + 1) * CHUNK]
            mat = reachable * scores
            dscores = dscores + reachable * product
            energy = mat * product
            rows.append(jnp.sum(energy, axis=0, keepdims=True))
            into = jnp.where(lane == head, jnp.sum(energy, axis=1, keepdims=True), into)
            mats.append(mat)
        pieces.append(low_mm(jnp.concatenate(mats, axis=1), head_halves(dy[:, at], lower)))
    dxd = jnp.concatenate(pieces, axis=1) + fed
    kept = jnp.sum(after * held, axis=0, keepdims=True) * growth_e[CHUNK - 1 : CHUNK]
    sums = split_dot(
        jnp.concatenate(
            [dy * carried, xd * fed, dxd * x, jnp.broadcast_to(kept, (8, width))], axis=0
        ),
        red_ref[...],
    )
    out_of, fed_sum = sums[:CHUNK], sums[CHUNK : 2 * CHUNK]
    dstep, kept_sum = sums[2 * CHUNK : 3 * CHUNK], sums[3 * CHUNK : 3 * CHUNK + 1]
    rows = column_of(jnp.concatenate(rows, axis=0))
    dcum = rows - into + out_of - fed_sum
    end_term = kept_sum + jnp.sum(fed_sum, axis=0, keepdims=True)
    ddecay = (
        lax.dot_general(
            (iota(0) <= iota(1)).astype(F32), dcum, NN, precision=HIGH, preferred_element_type=F32
        )
        + end_term
    )
    ddecay = jnp.where(lane < heads, ddecay, 0.0)
    dpre = jnp.where(lane < heads, (dstep + hp_ref[1:2] * ddecay) * jax.nn.sigmoid(pre), 0.0)
    hacc_ref[0:1] += jnp.sum(dpre, axis=0, keepdims=True)
    hacc_ref[1:2] += jnp.sum(ddecay * decay, axis=0, keepdims=True)
    dx = dxd * step_e + skip_ref[...] * dy
    db = wide_mm(dscores, c_val) + wide_mm(xd * weight_e, after, NT)
    dc = wide_mm(dscores, b_val, TN) + wide_mm(dy_grown, held, NT)
    dstate[...] = after * growth_e[CHUNK - 1 : CHUNK] + wide_mm(c_val, dy_grown, TN)

    dz = jnp.concatenate([dx, db, dc], axis=1) * slope
    wacc_ref[3:4] += jnp.sum(dz * vbuf[8:], axis=0, keepdims=True)
    wacc_ref[4:5] += jnp.sum(dz, axis=0, keepdims=True)
    dv = cw_ref[3:4] * dz
    for k in range(3):
        masked = dz * aux[:, k : k + 1]
        wacc_ref[k : k + 1] += jnp.sum(
            masked * vbuf[5 + k : 5 + k + CHUNK], axis=0, keepdims=True
        )
        zbuf[k, 8 : 8 + CHUNK] = masked
        dv = dv + cw_ref[k : k + 1] * zbuf[k, 11 - k : 11 - k + CHUNK]
    dproj_ref[:, :width] = dv[:, :width].astype(BF16)
    dproj_ref[:, width : width + LANES] = dpre.astype(BF16)
    dproj_ref[:, width + LANES :] = dv[:, width:].astype(BF16)

    @pl.when(step_at == 0)
    def _():
        tail_ref[...] = dv[CHUNK - 16 :]

    @pl.when(chunk == 0)
    def _():
        drim = cw_ref[0:1] * zbuf[0, 3:11]
        for k in (1, 2):
            drim = drim + cw_ref[k : k + 1] * zbuf[k, 3 - k : 11 - k]
        drim_ref[0:8] = jnp.zeros_like(drim)
        drim_ref[8:] = drim

    for k in range(3):
        zbuf[k, 8 + CHUNK :] = zbuf[k, 8:16]


def scan_backward(dy, z, proj, rim, marks, states, carried, growth, dend, consts):
    length, total = proj.shape
    heads, width = consts["heads"], consts["width"]
    chunks, conv = length // CHUNK, total - LANES
    eights = CHUNK // 8

    def back(columns):
        return pl.BlockSpec((CHUNK, columns), lambda i: (chunks - 1 - i, 0))

    def previous(columns):
        return pl.BlockSpec(
            (8, columns), lambda i: (jnp.maximum((chunks - 1 - i) * eights - 1, 0), 0)
        )

    return kernel_call(
        functools.partial(scan_backward_kernel, heads, width, chunks),
        cost=18.0,
        grid=(chunks,),
        in_specs=[
            back(width),
            back(conv),
            back(total),
            previous(total),
            whole((8, conv)),
            pl.BlockSpec((8, CHUNK), lambda i: (0, chunks - 1 - i)),
            whole((8, conv)),
            whole((8, LANES)),
            whole((1, width)),
            whole((LANES, width)),
            whole((width, LANES)),
            pl.BlockSpec((1, LANES, width), lambda i: (chunks - 1 - i, 0, 0)),
            whole((LANES, width)),
            previous(LANES),
            whole((LANES, width)),
        ],
        out_specs=[
            back(total),
            whole((8, conv)),
            whole((8, LANES)),
            whole((16, conv)),
            whole((16, conv)),
        ],
        out_shape=[
            jax.ShapeDtypeStruct((length, total), BF16),
            jax.ShapeDtypeStruct((8, conv), F32),
            jax.ShapeDtypeStruct((8, LANES), F32),
            jax.ShapeDtypeStruct((16, conv), F32),
            jax.ShapeDtypeStruct((16, conv), F32),
        ],
        scratch_shapes=[
            pltpu.VMEM((CHUNK + 8, conv), F32),
            pltpu.VMEM((3, CHUNK + 16, conv), F32),
            pltpu.VMEM((LANES, width), F32),
        ],
        compiler_params=params(),
    )(
        dy, z, proj, proj, rim, marks, consts["cw"], consts["hp"], consts["skip"],
        consts["exp"], consts["red"], states, carried, growth, dend,
    )


def local(
    stream,
    seg_ids,
    input_weight,
    step_size_weight,
    coefficient_weight,
    pre_gain,
    conv_bc,
    bias_bc,
    output_weight,
    conv_x,
    bias_x,
    dt_bias,
    a_log,
    skip,
    gate_gain,
    cotangent,
):
    PRECEDING.clear()
    layers, rows_in, _, width = input_weight.shape
    sequences, length, model = stream.shape
    heads = dt_bias.shape[1]
    depth = width // heads
    shared = coefficient_weight.shape[2]
    dp, context, tensor = (lax.axis_size(a) for a in ("dp", "context", "tensor"))
    channels = width * tensor
    rows_bc = rows_in // tensor
    conv, total = width + shared, width + LANES + shared
    layer_range, seq_range = range(layers), range(sequences)

    own_gain, own_conv = pre_gain.shape[1], conv_bc.shape[2]
    small = jnp.concatenate([pre_gain, conv_bc.reshape(layers, -1), bias_bc], axis=1)
    small = jnp.pad(small, ((0, 0), (0, shared - small.shape[1])))[:, None]
    bc_rows = gather_small(jnp.concatenate([coefficient_weight, small], axis=1), ("tensor",))
    small, bc_rows = bc_rows[:, :, rows_bc], bc_rows[:, :, :rows_bc]
    taps = small[:, :, own_gain : own_gain + 5 * own_conv].reshape(tensor, layers, 5, own_conv)
    taps = jnp.moveaxis(taps, 0, 2).reshape(layers, -1)
    small = jnp.concatenate(
        [
            jnp.moveaxis(small[:, :, :own_gain], 0, 1).reshape(layers, rows_in),
            jnp.pad(taps, ((0, 0), (0, rows_in - taps.shape[1]))),
        ],
        axis=0,
    ).T

    def first_piece(layer):
        tile = jnp.concatenate(
            [
                step_size_weight[layer],
                small,
                jnp.zeros((rows_in, LANES - heads - 2 * layers), BF16),
                bc_rows[:, layer].reshape(rows_in, shared),
            ],
            axis=1,
        )
        return [input_weight[layer, :, 1], tile]

    def second_piece(layer):
        return [input_weight[layer, :, 0], output_weight[layer].T]

    edge_ids = shifted(seg_ids[:, -3:], "context", 1)
    ext_ids = jnp.concatenate([edge_ids, seg_ids], axis=1)
    prior = ext_ids[:, 2 : 2 + length].reshape(sequences, length // CHUNK, CHUNK)[:, :, 0]
    prior = jnp.repeat(prior, CHUNK, axis=1)
    aux_all = jnp.stack(
        [ext_ids[:, k : k + length] == seg_ids for k in range(3)]
        + [seg_ids == prior, seg_ids == edge_ids[:, 2:3], seg_ids, seg_ids, seg_ids],
        axis=1,
    ).astype(F32)

    spread_table = (jnp.arange(LANES)[:, None] == jnp.arange(width)[None, :] // depth).astype(BF16)

    def joined(*parts):
        return jnp.concatenate([one for part in parts for one in part], axis=1)

    third = total // 3
    upper_piece = joined(second_piece(1), first_piece(1))
    table, second_table = [], []
    halo = shifted(stream[:, length - 16 :], "context", 1)
    precede(halo, edge_ids)
    for _ in ring_pieces(table, joined(first_piece(0))):
        pass
    second_ring = ring_pieces(second_table, relayed(joined(second_piece(0))))
    next(second_ring)
    places = jnp.arange(length // CHUNK, dtype=jnp.int32)
    arrived, sending = rows_order(False), rows_order(True)
    own_place = lax.axis_index("tensor").astype(jnp.int32)[None]
    precede(aux_all, spread_table, spread_table.T, arrived, sending)
    first, tile_rows = placed(table, [total], width)

    def every_row(part):
        return lax.all_gather(part, ("dp", "context"), axis=0, tiled=True)

    weights = [
        {"front": (first, 0)},
        {},
    ]
    streams = [(stream, s) for s in seq_range]
    grads = [(cotangent, s) for s in seq_range]
    small = tile_rows[heads : heads + 2 * layers]
    gains = small[:layers]
    taps = small[layers:].reshape(layers, dp * context, rows_in)[:, :, : 5 * tensor * own_conv]
    taps = taps.reshape(layers, dp * context, 5, tensor * own_conv)
    taps = jnp.moveaxis(taps, 1, 2).reshape(layers, 5, shared)

    consts = []
    for layer in layer_range:
        cw = jnp.concatenate(
            [
                jnp.concatenate(
                    [jnp.concatenate([conv_x[layer], bias_x[layer][None]], axis=0), taps[layer]],
                    axis=1,
                ),
                jnp.zeros((3, conv), F32),
            ],
            axis=0,
        )
        pad = jnp.zeros((LANES - heads,), F32)
        hp = jnp.stack(
            [
                jnp.concatenate([dt_bias[layer], pad]),
                jnp.concatenate([-jnp.exp(a_log[layer]), pad]),
            ]
            + [jnp.zeros((LANES,), F32)] * 6
        )
        consts.append(
            {
                "heads": heads,
                "width": width,
                "cw": cw,
                "hp": hp,
                "skip": jnp.repeat(skip[layer], depth)[None],
                "gain": gate_gain[layer][None],
                "exp": spread_table,
                "red": spread_table.T,
                **weights[layer],
            }
        )

    def chain(value, total, steps):
        carried = shifted(value, "context", steps)
        for _ in range(context - 2):
            passed = value.astype(F32) + carried.astype(F32) * total
            carried = shifted(passed.astype(value.dtype), "context", steps)
        return carried

    def through(growth):
        return jnp.repeat(growth[length - 1, :heads], depth)[None]

    for const in consts:
        precede(const["cw"], const["hp"], const["skip"], const["gain"])
    precede(gains)
    incoming = [(stream, halo, s) for s in seq_range]
    work = [[{} for _ in seq_range] for _ in layer_range]
    outputs = []
    top = layers - 1
    def step_project(layer, s):
        k = work[layer][s]
        k["stream"] = streams[s]
        k["normed"], k["proj"], tail = project(
            incoming[s],
            None if layer else gains[0:1],
            arrived if layer else places,
            consts[layer]["front"],
            width,
            total,
        )
        k["rim"] = shifted(tail, "context", 1) if layer else tail

    def step_scan(layer, s):
        k = work[layer][s]
        k["z"], k["y0"], k["states"], end, k["growth"] = scan_forward(
            k["proj"], k["rim"], aux_all[s], consts[layer]
        )
        k["carried"] = chain(end, through(k["growth"]), 1)

    def step_gate(layer, s):
        k = work[layer][s]
        k["gate"] = plain_product(k["normed"], consts[layer]["gate"], width)

    def step_mix(layer, s):
        k = work[layer][s]
        k["y"], squares = mix_forward(
            k["y0"], k["z"], k["growth"], k["carried"], k["gate"], consts[layer]
        )
        if layer < top:
            k["squares"] = from_others(squares, "tensor")

    def step_out(layer, s):
        k = work[layer][s]
        kind = BF16 if layer == top else F32
        sent, own = project_out(
            k["y"], k["gate"], k["squares" if layer < top else "stats"], channels, kind, sending,
            consts[layer],
        )
        k["out"] = [own, flipped(sent, "tensor", 0)]

    def step_pass(layer, s, name):
        terms = work[layer][s][name]
        terms.append(flipped(pass_on(*terms), "tensor", 1))

    def step_norm(layer, s):
        k = work[layer][s]
        gain = None if layer == top else gains[layer + 1 : layer + 2]
        *new, low = norm_forward(streams[s], k["out"], gain, own_place)
        streams[s] = new[0] if new else None
        k["rows"] = [low, flipped(low, "tensor", 1)]

    def step_join(layer, s, name):
        own, other = work[layer][s][name]
        across = flipped(joined_rows(own, other), "tensor", 0)
        return [(own, 0), (other, 0), (across, 0), (across, 1)]

    def step_grad(layer, s):
        k = work[layer][s]
        source = (cotangent, s) if layer == top else incoming[s]
        k["grad"], dots, k["low"] = grad_scaled(
            source, k["y"], k["gate"], places if layer == top else arrived, consts[layer]
        )
        k["stats"] = from_others(dots, "tensor")

    def step_mix_back(layer, s):
        k = work[layer][s]
        k["scaled"], k["dgate"], k["dy"], k["acc"], dsin = mix_backward(
            k["grad"], k["y"], k["gate"], k["z"], k["growth"], k["stats"], channels, consts[layer],
        )
        k["dend"] = chain(dsin, through(k["growth"]), -1)

    def step_scan_back(layer, s):
        k = work[layer][s]
        k["dproj"], k["wacc"], k["hacc"], k["tail"], drim = scan_backward(
            k["dy"], k["z"], k["proj"], k["rim"], aux_all[s], k["states"],
            k["carried"], k["growth"], k["dend"], consts[layer],
        )
        k["drim"] = shifted(drim, "context", -1)

    def step_input_grad(layer, s):
        k = work[layer][s]
        sent, own, k["dproj"] = input_grad(
            k["dproj"], k["dgate"], k["tail"], k["drim"], consts[layer]["front"],
            consts[layer]["gate"], sending,
        )
        k["back"] = [own, flipped(sent, "tensor", 0)]

    def step_norm_back(layer, s):
        k = work[layer][s]
        grads[s], low, k["dgain"] = norm_backward(
            k["stream"], k["back"], grads[s], gains[layer : layer + 1], own_place
        )
        k["grad_low"] = [low, flipped(low, "tensor", 1)]

    def every(layer, name):
        return [k[name] for k in work[layer]]

    def step_second_grad(layer):
        return weight_grad(
            [
                (every(layer, "normed"), every(layer, "dgate")),
                (every(layer, "low"), every(layer, "scaled")),
            ],
            layer == 0,
        )

    def step_first_grad(layer):
        return weight_grad([(every(layer, "normed"), every(layer, "dproj"))], layer == 0)

    def scattered(value):
        return lax.psum_scatter(value, ("dp", "context"), scatter_dimension=0, tiled=True)

    second_sums, first_sums = [None] * layers, [None] * layers
    project_0, scan_0, gate_0, mix_0, out_0, grad_0, mixed_0, scanned_0, input_0 = (
        functools.partial(step, 0)
        for step in (
            step_project, step_scan, step_gate, step_mix, step_out, step_grad, step_mix_back,
            step_scan_back, step_input_grad,
        )
    )
    project_1, scan_1, gate_1, mix_1, out_1, grad_1, mixed_1, scanned_1, input_1 = (
        functools.partial(step, 1)
        for step in (
            step_project, step_scan, step_gate, step_mix, step_out, step_grad, step_mix_back,
            step_scan_back, step_input_grad,
        )
    )

    project_0(0)
    next(second_ring)
    scan_0(0)
    next(second_ring)
    project_0(1)
    next(second_ring, None)
    upper = every_row(relayed(upper_piece))
    consts[1].update(front=(upper, 2 * width // third), gate=(upper, 0), out=(upper, 1))
    scan_0(1)
    precede(work[0][0]["carried"])
    (second,) = placed(second_table, [2 * width])
    consts[0].update(gate=(second, 0), out=(second, 1))
    gate_0(0)
    mix_0(0)
    gate_0(1)
    mix_0(1)
    out_0(0)
    step_pass(0, 0, "out")
    out_0(1)
    step_pass(0, 1, "out")
    step_norm(0, 0)
    step_norm(0, 1)
    incoming[0] = step_join(0, 0, "rows")
    project_1(0)
    incoming[1] = step_join(0, 1, "rows")
    project_1(1)
    scan_1(0)
    scan_1(1)
    gate_1(0)
    mix_1(0)
    gate_1(1)
    mix_1(1)
    grad_1(0)
    grad_1(1)
    mixed_1(0)
    mixed_1(1)
    second_sums[1] = scattered(step_second_grad(1)[0])
    scanned_1(0)
    out_1(0)
    input_1(0)
    step_pass(1, 0, "back")
    scanned_1(1)
    step_norm_back(1, 0)
    out_1(1)
    input_1(1)
    incoming[0] = step_join(1, 0, "grad_low")
    grad_0(0)
    step_pass(1, 1, "back")
    first_grad = step_first_grad(1)
    mixed_0(0)
    step_norm_back(1, 1)
    precede(second_sums[1])
    step_pass(1, 0, "out")
    step_pass(1, 1, "out")
    first_sums[1] = scattered(first_grad[0])
    scanned_0(0)
    incoming[1] = step_join(1, 1, "grad_low")
    grad_0(1)
    input_0(0)
    mixed_0(1)
    second_steps = ring_steps(step_second_grad(0))
    step_pass(0, 0, "back")
    scanned_0(1)
    next(second_steps)
    step_norm_back(0, 0)
    for s in seq_range:
        step_norm(1, s)
    input_0(1)
    next(second_steps)
    step_pass(0, 1, "back")
    precede(first_sums[1])
    first_steps = ring_steps(step_first_grad(0))
    next(second_steps)
    step_norm_back(0, 1)
    small_steps = small_sums(work, width, heads, model, consts[0]["red"])
    next(small_steps)
    next(first_steps)
    outputs.extend(step_join(1, s, "rows") for s in seq_range)
    layer_out = assembled(outputs, arrived)
    next(first_steps)
    next(small_steps)
    second_sums[0] = next(second_steps)
    second_sums[1], first_sums[1] = widened(second_sums[1]), widened(first_sums[1])
    incoming[0] = step_join(0, 0, "grad_low")
    next(first_steps)
    next(small_steps)
    incoming[1] = step_join(0, 1, "grad_low")
    grad_stream = assembled(incoming, arrived)
    first_sums[0] = next(first_steps)
    for value in small_steps:
        small_out = value

    out = []
    for layer in layer_range:
        second_sum, first_sum = second_sums[layer], first_sums[layer]
        out.append(
            (
                jnp.stack([second_sum[:, :width], first_sum[:, :width]], axis=1),
                first_sum[:, width : width + heads],
                scatter_places(first_sum[:, width + LANES :]),
                second_sum[:, width:].T,
            )
        )
    taps_x, sum_bias_x, dt_sum, rate_sum, skip_sum, gate_sum, taps_bc, sum_bias_bc, gain_sum = (
        small_out
    )
    return (
        layer_out,
        grad_stream,
        jnp.stack([o[0] for o in out]),
        jnp.stack([o[1] for o in out]),
        jnp.stack([o[2] for o in out]),
        gain_sum,
        taps_bc,
        sum_bias_bc,
        jnp.stack([o[3] for o in out]),
        taps_x,
        sum_bias_x,
        dt_sum,
        rate_sum,
        skip_sum,
        gate_sum,
    )


def solution(mesh):
    in_specs = (
        P("dp", "context", None),
        P("dp", "context"),
        P(None, ("dp", "context"), None, "tensor"),
        P(None, ("dp", "context"), "tensor"),
        P(None, ("dp", "context", "tensor"), None),
        P(None, ("dp", "context", "tensor")),
        P(None, None, ("dp", "context", "tensor")),
        P(None, ("dp", "context", "tensor")),
        P(None, "tensor", ("dp", "context")),
        P(None, None, "tensor"),
        P(None, "tensor"),
        P(None, "tensor"),
        P(None, "tensor"),
        P(None, "tensor"),
        P(None, "tensor"),
        P("dp", "context", None),
    )
    out_specs = (
        P("dp", "context", None),
        P("dp", "context", None),
        P(None, ("dp", "context"), None, "tensor"),
        P(None, ("dp", "context"), "tensor"),
        P(None, ("dp", "context", "tensor"), None),
        P(None, ("dp", "context", "tensor")),
        P(None, None, ("dp", "context", "tensor")),
        P(None, ("dp", "context", "tensor")),
        P(None, "tensor", ("dp", "context")),
        P(None, None, "tensor"),
        P(None, "tensor"),
        P(None, "tensor"),
        P(None, "tensor"),
        P(None, "tensor"),
        P(None, "tensor"),
        P("dp", "context", None),
    )
    return jax.shard_map(
        local, mesh=mesh, in_specs=in_specs, out_specs=out_specs[:15], check_vma=False
    )
```

```python
import functools

import jax
import jax.numpy as jnp
from jax import lax
from jax.experimental import pallas as pl
from jax.experimental.pallas import tpu as pltpu
from jax.sharding import PartitionSpec as P

CHUNK = 128
LANES = 128
eps = 1e-05
F32 = jnp.float32
BF16 = jnp.bfloat16
HIGH = lax.Precision.HIGHEST
NN = (((1,), (0,)), ((), ()))
NT = (((1,), (1,)), ((), ()))
TN = (((0,), (0,)), ((), ()))
NO_LINK = -1e30
COST_SCALE = 0.5


def mm(a, b, dims=NN):
    return lax.dot_general(a, b, dims, preferred_element_type=F32)


def params(mib=48):
    return pltpu.CompilerParams(
        dimension_semantics=("arbitrary",), vmem_limit_bytes=mib * 1024 * 1024
    )


PRECEDING = []


def kernel_call(body, cost=2.0, **spec):
    def call(*inputs):
        tokens = list(PRECEDING)
        options = dict(spec)
        grid_spec = options.pop("grid_spec", None)
        unread = [pl.BlockSpec(memory_space=pl.ANY)] * len(tokens)
        prefetched = 0
        if grid_spec is None:
            options["in_specs"] = list(options["in_specs"]) + unread
        else:
            prefetched = grid_spec.num_scalar_prefetch
            options["grid_spec"] = pltpu.PrefetchScalarGridSpec(
                num_scalar_prefetch=prefetched,
                grid=grid_spec.grid,
                in_specs=list(grid_spec.in_specs) + unread,
                out_specs=grid_spec.out_specs,
                scratch_shapes=grid_spec.scratch_shapes,
            )
        first = len(inputs)

        def without_tokens(*refs):
            body(*refs[:first], *refs[first + len(tokens) :])

        out = pl.pallas_call(
            without_tokens,
            cost_estimate=pl.CostEstimate(
                flops=int(cost * 1.0e9 * COST_SCALE), transcendentals=0, bytes_accessed=1024
            ),
            **options,
        )(*inputs, *tokens)
        PRECEDING[:] = [min(jax.tree.leaves(out), key=lambda one: one.size * one.dtype.itemsize)]
        return out

    return call


def precede(*tokens):
    PRECEDING.extend(token for token in tokens if token is not None)


def flipped(value, axis, bit):
    count = lax.axis_size(axis)
    return lax.ppermute(value, axis, [(i, i ^ (1 << bit)) for i in range(count)])


def bits(axis):
    return (lax.axis_size(axis) - 1).bit_length()


def shifted(value, axis, steps):
    count = lax.axis_size(axis)
    leading, last = (max(0, -steps), min(count, count - steps))
    return lax.ppermute(value, axis, [(source, source + steps) for source in range(leading, last)])


def ring(value, axis):
    count = lax.axis_size(axis)
    return lax.ppermute(value, axis, [(i, (i - 1) % count) for i in range(count)])


def summed_over(value, axes):
    for axis in axes:
        for bit in range(bits(axis)):
            value = value + flipped(value, axis, bit)
    return value


def gather_small(value, axes):
    value = value[None]
    for axis in axes:
        index = lax.axis_index(axis)
        for bit in range(bits(axis)):
            other = flipped(value, axis, bit)
            upper = (index >> bit) & 1
            value = jnp.concatenate(
                [jnp.where(upper == 0, value, other), jnp.where(upper == 0, other, value)], axis=0
            )
    return value


def slots():
    count, places = bits("tensor"), []
    for m in range(lax.axis_size("tensor")):
        places.append(sum(((m >> b) & 1) << (count - 1 - b) for b in range(count)))
    return places


def rows_order(first):
    places = slots()
    if first:
        half = len(places) // 2
        places = places[half:] + places[:half]
    return jnp.array(places, jnp.int32) ^ lax.axis_index("tensor")


def own_rows(value):
    rows = value.shape[0] // lax.axis_size("tensor")
    return lax.dynamic_slice_in_dim(value, lax.axis_index("tensor") * rows, rows, 0)


def relay_kernel(from_ref, to_ref):
    to_ref[...] = from_ref[...]


def widen_kernel(from_ref, to_ref):
    to_ref[...] = from_ref[...].astype(F32)


def widened(value):
    return kernel_call(
        widen_kernel,
        grid=(1,),
        in_specs=[fixed_block(value.shape)],
        out_specs=fixed_block(value.shape),
        out_shape=jax.ShapeDtypeStruct(value.shape, F32),
        compiler_params=params(),
    )(value)


def relayed(piece, *tokens):
    precede(*tokens)
    return kernel_call(
        relay_kernel,
        grid=(1,),
        in_specs=[fixed_block(piece.shape)],
        out_specs=fixed_block(piece.shape),
        out_shape=jax.ShapeDtypeStruct(piece.shape, piece.dtype),
        compiler_params=params(),
    )(piece)


def ring_pieces(table, piece):
    def over_context(arrived):
        row = [arrived]
        for _ in range(lax.axis_size("context") - 1):
            row.append(ring(row[-1], "context"))
        return row

    arrived = piece
    table.append(over_context(piece))
    for k in range(1, lax.axis_size("dp")):
        arrived = ring(arrived, "dp")
        yield
        arrived = relayed(arrived, table[k - 1][-1])
        table.append(over_context(arrived))
    yield


def place_kernel(count, widths, tile_at, index_ref, *refs):
    pieces, outs = refs[:count], refs[count:]
    for i in range(count):
        at = 0
        for out, width in zip(outs, widths):
            out[index_ref[i]] = pieces[i][:, at : at + width]
            at += width
    if tile_at is not None:
        first, tiles = outs[0], outs[-1]
        rows = first.shape[1]
        whole_rows = jnp.concatenate(
            [first[i, :, tile_at : tile_at + LANES] for i in range(count)], axis=0
        )
        for at in range(0, count * rows, LANES):
            tiles[:, at : at + LANES] = whole_rows[at : at + LANES].astype(F32).T


def placed(table, widths, tile_at=None):
    dp, context = lax.axis_size("dp"), lax.axis_size("context")
    z, x = lax.axis_index("dp"), lax.axis_index("context")
    pieces, index = [], []
    for k, row in enumerate(table):
        for j, piece in enumerate(row):
            pieces.append(piece)
            index.append(((z + k) % dp) * context + (x + j) % context)
    count, rows = len(pieces), pieces[0].shape[0]
    out_specs = [
        pl.BlockSpec((count, rows, width), lambda i, index: (0, 0, 0)) for width in widths
    ]
    out_shape = [jax.ShapeDtypeStruct((count, rows, width), BF16) for width in widths]
    if tile_at is not None:
        out_specs.append(pl.BlockSpec((LANES, count * rows), lambda i, index: (0, 0)))
        out_shape.append(jax.ShapeDtypeStruct((LANES, count * rows), F32))
    outs = kernel_call(
        functools.partial(place_kernel, count, widths, tile_at),
        cost=3.5,
        grid_spec=pltpu.PrefetchScalarGridSpec(
            num_scalar_prefetch=1,
            grid=(1,),
            in_specs=[pl.BlockSpec(piece.shape, lambda i, index: (0, 0)) for piece in pieces],
            out_specs=out_specs,
        ),
        out_shape=out_shape,
        compiler_params=params(),
    )(jnp.stack(index).astype(jnp.int32), *pieces)
    return [
        out.reshape(count * rows, -1) if i < len(widths) else out for i, out in enumerate(outs)
    ]


def after(value, *tokens):
    tokens = tuple(token for token in tokens if token is not None)
    return lax.optimization_barrier((value, *tokens))[0] if tokens else value


def from_others(value, axis):
    count = lax.axis_size(axis)
    return [value] + [
        lax.ppermute(value, axis, [(i, i ^ step) for i in range(count)])
        for step in range(1, count)
    ]


def scatter_places(value):
    count, index = lax.axis_size("tensor"), lax.axis_index("tensor")
    value = value.reshape(count, -1, value.shape[1])
    total = lax.dynamic_index_in_dim(value, index, 0, keepdims=False)
    for step in range(1, count):
        sent = lax.dynamic_index_in_dim(value, index ^ step, 0, keepdims=False)
        total = total + lax.ppermute(sent, "tensor", [(i, i ^ step) for i in range(count)])
    return total


def pack_kernel(layers, sequences, width, *refs):
    inputs, (local_ref, shared_ref) = refs[:-2], refs[-2:]
    local_ref[...] = jnp.zeros_like(local_ref)
    shared_ref[...] = jnp.zeros_like(shared_ref)
    for layer in range(layers):
        mine = inputs[layer * sequences * 4 : (layer + 1) * sequences * 4]
        taps, acc, small, gain = (sum(one[...] for one in mine[i::4]) for i in range(4))
        local_ref[layer, 0:5, :width] = taps[0:5, :width]
        local_ref[layer, 5:7, :width] = acc[0:2]
        local_ref[layer, 0:2, width:] = small[0:2]
        shared = taps.shape[1] - width
        shared_ref[layer, 0:5, :shared] = taps[0:5, width:]
        for i, (row, at) in enumerate(gain_places(gain.shape[1], shared)):
            shared_ref[layer, row : row + 1, at : at + shared] = gain[
                0:1, i * shared : (i + 1) * shared
            ]


def gain_places(model, shared):
    places = [(5, 0), (6, 0), (7, 0)] + [(row, shared) for row in range(8)]
    return places[: model // shared]


def share_kernel(local_ref, *refs):
    cut = local_ref.shape[2]
    refs[-1][:, :, :cut] = local_ref[...]
    refs[-1][:, :, cut:] = sum(one[...] for one in refs[:-1])


def unpack_kernel(width, heads, shared, model, place_ref, a_ref, b_ref, red_ref, *outs):
    taps_x, bias_x, dt_bias, rate, skip, gate_gain, taps_bc, bias_bc, pre_gain = outs
    own_conv, own_gain = taps_bc.shape[2], pre_gain.shape[1]
    cut = width + LANES
    for layer in range(a_ref.shape[0]):
        total = a_ref[layer] + b_ref[layer]
        at = slice(layer, layer + 1)
        taps_x[layer] = total[0:4, :width]
        bias_x[at] = total[4:5, :width]
        gate_gain[at] = total[5:6, :width]
        dt_bias[at] = total[0:1, width : width + heads]
        rate[at] = total[1:2, width : width + heads]
        skip[at] = split_dot(total[:, :width], red_ref[...])[6:7, :heads]
        part = total[:, cut : cut + shared]
        part = pltpu.roll(part, shared - place_ref[0] * own_conv, axis=1)
        taps_bc[layer] = part[0:4, :own_conv]
        bias_bc[at] = part[4:5, :own_conv]
        rows = [
            total[row : row + 1, cut + col : cut + col + shared]
            for row, col in gain_places(model, shared)
        ]
        gain = jnp.broadcast_to(jnp.concatenate(rows, axis=1), (8, model))
        gain = pltpu.roll(gain, model - place_ref[0] * own_gain, axis=1)
        pre_gain[at] = gain[0:1, :own_gain]


def add_kernel(*refs):
    refs[-1][...] = sum(one[...] for one in refs[:-1])


def add_up(terms):
    shape = terms[0].shape
    return kernel_call(
        add_kernel,
        cost=1.0,
        grid=(1,),
        in_specs=[whole(shape)] * len(terms),
        out_specs=whole(shape),
        out_shape=jax.ShapeDtypeStruct(shape, terms[0].dtype),
        compiler_params=params(),
    )(*terms)


def small_sums(work, width, heads, model, red):
    layers, sequences = len(work), len(work[0])
    inputs = [k[name] for ks in work for k in ks for name in ("wacc", "acc", "hacc", "dgain")]
    shared = inputs[0].shape[1] - width
    shapes = [(layers, 8, width + LANES), (layers, 8, 2 * shared)]
    own, every = kernel_call(
        functools.partial(pack_kernel, layers, sequences, width),
        grid=(1,),
        in_specs=[whole(one.shape) for one in inputs],
        out_specs=[whole(shape) for shape in shapes],
        out_shape=[jax.ShapeDtypeStruct(shape, F32) for shape in shapes],
        compiler_params=params(),
    )(*inputs)
    parts = from_others(every, "tensor")
    yield None
    shape = (layers, 8, width + LANES + 2 * shared)
    total = kernel_call(
        share_kernel,
        cost=1.0,
        grid=(1,),
        in_specs=[whole(one.shape) for one in (own, *parts)],
        out_specs=whole(shape),
        out_shape=jax.ShapeDtypeStruct(shape, F32),
        compiler_params=params(),
    )(own, *parts)
    hops = [(axis, bit) for axis in ("context", "dp") for bit in range(bits(axis))]
    for axis, bit in hops:
        other = flipped(total, axis, bit)
        yield None
        if (axis, bit) != hops[-1]:
            total = add_up([total, other])
    devices = lax.axis_size("dp") * lax.axis_size("context") * lax.axis_size("tensor")
    place = lax.axis_index("dp") * lax.axis_size("context") + lax.axis_index("context")
    place = place * lax.axis_size("tensor") + lax.axis_index("tensor")
    own_conv, own_gain = shared // devices, model // devices
    shapes = [
        (layers, 4, width), (layers, width), (layers, heads), (layers, heads), (layers, heads),
        (layers, width), (layers, 4, own_conv), (layers, own_conv), (layers, own_gain),
    ]
    yield kernel_call(
        functools.partial(unpack_kernel, width, heads, shared, model),
        grid_spec=pltpu.PrefetchScalarGridSpec(
            num_scalar_prefetch=1,
            grid=(1,),
            in_specs=[fixed_block(one.shape) for one in (total, other, red)],
            out_specs=[fixed_block(one) for one in shapes],
        ),
        out_shape=[jax.ShapeDtypeStruct(one, F32) for one in shapes],
        compiler_params=params(),
    )(place.astype(jnp.int32)[None], total, other, red)


def silu_parts(value):
    sig = jax.nn.sigmoid(value)
    return value * sig, sig


def softplus(value):
    return jnp.maximum(value, 0.0) + jnp.log1p(jnp.exp(-jnp.abs(value)))


def split_dot(value, table):
    high = value.astype(BF16)
    low = (value - high.astype(F32)).astype(BF16)
    return mm(high, table) + mm(low, table)


def wide_mm(a, b, dims=NN):
    a_high, b_high = a.astype(BF16), b.astype(BF16)
    a_low = (a - a_high.astype(F32)).astype(BF16)
    b_low = (b - b_high.astype(F32)).astype(BF16)
    return mm(a_high, b_high, dims) + (mm(a_low, b_high, dims) + mm(a_high, b_low, dims))


def low_mm(a, b, dims=NN):
    return mm(a.astype(BF16), b.astype(BF16), dims)


def iota(axis):
    return lax.broadcasted_iota(jnp.int32, (CHUNK, CHUNK), axis)


def rounded(value):
    return value.astype(BF16).astype(F32)


def head_halves(tile, lower):
    zero = jnp.zeros_like(tile)
    return jnp.concatenate([jnp.where(lower, tile, zero), jnp.where(lower, zero, tile)], axis=0)


def column_of(rows):
    pad = jnp.zeros((CHUNK - rows.shape[0], CHUNK), F32)
    return jnp.concatenate([rows, pad], axis=0).T


def row_norm(wide):
    return lax.rsqrt(jnp.mean(wide * wide, axis=-1, keepdims=True) + eps)


def columns(array, at, width):
    return pl.BlockSpec((array.shape[0], width), lambda i, *_: (0, at))


def fixed_block(shape):
    return pl.BlockSpec(shape, lambda i, *_: (0,) * len(shape))


def project_kernel(norm, count, width, order_ref, *refs):
    pieces, rest = refs[:count], refs[count:]
    if norm:
        gain_ref, halo_ref, rest = rest[0], rest[1], rest[2:]
    w_ref, normed_ref, proj_ref, rim_ref, halo = rest
    step = pl.program_id(0)
    length, size = proj_ref.shape

    @pl.when(step == 0)
    def _():
        for m in range(length // CHUNK):
            if norm:
                wide = pieces[0][0, m * CHUNK : (m + 1) * CHUNK].astype(F32)
                rows = (wide * row_norm(wide) * gain_ref[...]).astype(BF16)
                normed_ref[m * CHUNK : (m + 1) * CHUNK] = rows
            else:
                place = pl.ds(pl.multiple_of(order_ref[m] * CHUNK, CHUNK), CHUNK)
                normed_ref[place] = pieces[m][...]
        if norm:
            wide = halo_ref[0].astype(F32)
            halo[...] = (wide * row_norm(wide) * gain_ref[...]).astype(BF16)
        else:
            halo[...] = normed_ref[length - 16 :]

    weight = w_ref[...]
    proj_ref[...] = mm(normed_ref[...], weight)
    tail = mm(halo[...], weight)[8:].astype(BF16)
    for i in range(width // size):

        @pl.when(step == i)
        def _(i=i):
            rim_ref[:, i * size : (i + 1) * size] = tail

    @pl.when(step == width // size)
    def _():
        rim_ref[:, width:] = tail[:, LANES:]


def project(source, gain, order, front, width, total):
    weights, at = front
    third = total // 3
    norm = gain is not None
    if norm:
        stream, halo, sequence = source
        model, length = stream.shape[2], stream.shape[1]
        inputs, count = [stream, gain, halo], 1
        specs = [
            pl.BlockSpec((1, length, model), lambda i, order: (sequence, 0, 0)),
            fixed_block((1, model)),
            pl.BlockSpec((1, 16, model), lambda i, order: (sequence, 0, 0)),
        ]
    else:
        model, count = source[0][0].shape[1], len(source)
        length = count * CHUNK
        inputs, specs = [one for one, _ in source], piece_specs(source, CHUNK)
    conv = total - LANES
    return kernel_call(
        functools.partial(project_kernel, norm, count, width),
        cost=5.0,
        grid_spec=pltpu.PrefetchScalarGridSpec(
            num_scalar_prefetch=1,
            grid=(3,),
            in_specs=specs + [pl.BlockSpec((model, third), lambda i, order: (0, at + i))],
            out_specs=[
                fixed_block((length, model)),
                pl.BlockSpec((length, third), lambda i, order: (0, i)),
                fixed_block((8, conv)),
            ],
            scratch_shapes=[pltpu.VMEM((16, model), BF16)],
        ),
        out_shape=[
            jax.ShapeDtypeStruct((length, model), BF16),
            jax.ShapeDtypeStruct((length, total), F32),
            jax.ShapeDtypeStruct((8, conv), BF16),
        ],
        compiler_params=params(),
    )(order, *inputs, weights)


def plain_kernel(a_ref, w_ref, out_ref):
    out_ref[...] = mm(a_ref[...], w_ref[...])


def plain_product(a, weight, width):
    weights, at = weight
    length, model = a.shape
    half = width // 2
    return kernel_call(
        plain_kernel,
        cost=3.0,
        grid=(2,),
        in_specs=[
            fixed_block((length, model)),
            pl.BlockSpec((model, half), lambda i: (0, 2 * at + i)),
        ],
        out_specs=pl.BlockSpec((length, half), lambda i: (0, i)),
        out_shape=jax.ShapeDtypeStruct((length, width), F32),
        compiler_params=params(),
    )(a, weights)


def rows_of(ref):
    return (ref[...] if len(ref.shape) == 2 else ref[0]).astype(F32)


def norm_forward_kernel(place_ref, stream_ref, keep_ref, first_ref, second_ref, *refs):
    total = keep_ref[0].astype(F32) + first_ref[0].astype(F32) + second_ref[...].astype(F32)
    new = rows_of(stream_ref) + total
    if len(refs) == 1:
        refs[0][...] = new.astype(BF16)
    else:
        gain_ref, new_ref, low_ref = refs
        new_ref[...] = new
        low_ref[...] = (new * row_norm(new) * gain_ref[...]).astype(BF16)


def join_kernel(own_ref, other_ref, out_ref):
    rows = own_ref.shape[0]
    out_ref[:rows] = own_ref[...]
    out_ref[rows:] = other_ref[...]


def joined_rows(own, other):
    rows, model = own.shape
    return kernel_call(
        join_kernel,
        grid=(1,),
        in_specs=[fixed_block((rows, model))] * 2,
        out_specs=fixed_block((2 * rows, model)),
        out_shape=jax.ShapeDtypeStruct((2 * rows, model), own.dtype),
        compiler_params=params(),
    )(own, other)


def piece_specs(pieces, rows):
    return [pl.BlockSpec((rows, one.shape[1]), lambda i, *_, at=at: (at, 0)) for one, at in pieces]


def pass_on_kernel(keep_ref, first_ref, out_ref):
    total = keep_ref[0].astype(F32) + first_ref[0].astype(F32)
    out_ref[...] = total.astype(out_ref.dtype)


def pass_on(kept, first):
    _, rows, model = kept.shape
    spec = pl.BlockSpec((1, rows, model), lambda i: (1, 0, 0))
    return kernel_call(
        pass_on_kernel,
        grid=(1,),
        in_specs=[spec, spec],
        out_specs=fixed_block((rows, model)),
        out_shape=jax.ShapeDtypeStruct((rows, model), kept.dtype),
        compiler_params=params(),
    )(kept, first)


def rows_spec(one, rows):
    if isinstance(one, tuple):
        array, s = one
        return array, pl.BlockSpec((1, rows, array.shape[2]), lambda i, place: (s, place[0], 0))
    return one, fixed_block(one.shape)


def term_specs(rows, model):
    part = fixed_block((1, rows, model))
    return [part, part, fixed_block((rows, model))]


def norm_forward(stream, terms, gain, place):
    rows, model = terms[2].shape
    stream, spec = rows_spec(stream, rows)
    low = jax.ShapeDtypeStruct((rows, model), BF16)
    last = gain is None
    return kernel_call(
        norm_forward_kernel,
        grid_spec=pltpu.PrefetchScalarGridSpec(
            num_scalar_prefetch=1,
            grid=(1,),
            in_specs=[spec]
            + term_specs(rows, model)
            + ([] if last else [fixed_block((1, model))]),
            out_specs=[fixed_block((rows, model))] * (1 if last else 2),
        ),
        out_shape=[low] if last else [jax.ShapeDtypeStruct((rows, model), F32), low],
        compiler_params=params(),
    )(place, stream, *terms, *([] if last else [gain]))


def norm_backward_kernel(
    place_ref, stream_ref, keep_ref, first_ref, second_ref, grad_ref, gain_ref, new_ref, low_ref,
    dgain_ref,
):
    total = keep_ref[0].astype(F32) + first_ref[0].astype(F32) + second_ref[...].astype(F32)
    current = rows_of(stream_ref)
    scale = row_norm(current)
    unit = current * scale
    dgain_ref[...] = jnp.broadcast_to(
        jnp.sum(total * unit, axis=0, keepdims=True), dgain_ref.shape
    )
    pulled = total * gain_ref[...]
    shift = jnp.mean(pulled * unit, axis=-1, keepdims=True)
    new = rows_of(grad_ref) + scale * (pulled - unit * shift)
    new_ref[...] = new
    low_ref[...] = new.astype(BF16)


def norm_backward(stream, terms, grad, gain, place):
    rows, model = terms[2].shape
    stream, stream_spec = rows_spec(stream, rows)
    grad, grad_spec = rows_spec(grad, rows)
    return kernel_call(
        norm_backward_kernel,
        grid_spec=pltpu.PrefetchScalarGridSpec(
            num_scalar_prefetch=1,
            grid=(1,),
            in_specs=[stream_spec]
            + term_specs(rows, model)
            + [grad_spec, fixed_block((1, model))],
            out_specs=[fixed_block((rows, model))] * 2 + [fixed_block((8, model))],
        ),
        out_shape=[
            jax.ShapeDtypeStruct((rows, model), F32),
            jax.ShapeDtypeStruct((rows, model), BF16),
            jax.ShapeDtypeStruct((8, model), F32),
        ],
        compiler_params=params(),
    )(place, stream, *terms, grad, gain)


def assemble_kernel(count, order_ref, *refs):
    step = pl.program_id(0)
    for m in range(count):

        @pl.when(step == m)
        def _(m=m):
            refs[-1][0] = refs[m][...]


def assembled(groups, order):
    each, (rows, model) = len(groups[0]), groups[0][0][0].shape
    pieces = [piece for group in groups for piece in group]
    count = len(pieces)
    return kernel_call(
        functools.partial(assemble_kernel, count),
        cost=5.0,
        grid_spec=pltpu.PrefetchScalarGridSpec(
            num_scalar_prefetch=1,
            grid=(count,),
            in_specs=piece_specs(pieces, rows),
            out_specs=pl.BlockSpec(
                (1, rows, model), lambda i, order: (i // each, order[i % each], 0)
            ),
        ),
        out_shape=jax.ShapeDtypeStruct((len(groups), each * rows, model), BF16),
        compiler_params=params(),
    )(order, *[one for one, _ in pieces])


def input_grad_kernel(parts, width, order_ref, dproj_ref, dgate_ref, tail_ref, rim_ref, *refs):
    w_refs, gate_ref, sent_ref, kept_ref, fixed_ref, rows_p, rows_g = refs[:3], *refs[3:]
    half = parts // 2

    @pl.when(pl.program_id(0) == 0)
    def _():
        fixed_ref[...] = dproj_ref[...]
        tail = (tail_ref[...] + rim_ref[...]).astype(BF16)
        fixed_ref[parts * CHUNK - 16 :, :width] = tail[:, :width]
        fixed_ref[parts * CHUNK - 16 :, width + LANES :] = tail[:, width:]
        for m in range(parts):
            source = pl.ds(pl.multiple_of(order_ref[m] * CHUNK, CHUNK), CHUNK)
            rows_p[m * CHUNK : (m + 1) * CHUNK] = fixed_ref[source]
            rows_g[m * CHUNK : (m + 1) * CHUNK] = dgate_ref[source]

    total = mm(rows_g[...], gate_ref[...], NT)
    for j, w_ref in enumerate(w_refs):
        size = w_ref.shape[1]
        total = total + mm(rows_p[:, j * size : (j + 1) * size], w_ref[...], NT)
    total = total.astype(BF16)
    for m in range(half):
        sent_ref[m] = total[m * CHUNK : (m + 1) * CHUNK]
        kept_ref[m] = total[(half + m) * CHUNK : (half + m + 1) * CHUNK]


def input_grad(dproj, dgate, tail, rim, front, gate, order):
    length, total = dproj.shape
    width = dgate.shape[1]
    (front_w, at), (gate_w, gate_at) = front, gate
    model, third, parts = front_w.shape[0], total // 3, length // CHUNK
    cut = model // 4
    half = pl.BlockSpec((parts // 2, CHUNK, cut), lambda i, order: (0, 0, i))

    def rows(offset, size):
        return pl.BlockSpec((cut, size), lambda i, order: (i, offset))

    return kernel_call(
        functools.partial(input_grad_kernel, parts, width),
        cost=7.6,
        grid_spec=pltpu.PrefetchScalarGridSpec(
            num_scalar_prefetch=1,
            grid=(4,),
            in_specs=[fixed_block(one.shape) for one in (dproj, dgate, tail, rim)]
            + [rows(at + j, third) for j in range(3)]
            + [rows(gate_at, width)],
            out_specs=[half, half, fixed_block((length, total))],
            scratch_shapes=[
                pltpu.VMEM((length, total), BF16),
                pltpu.VMEM((length, width), BF16),
            ],
        ),
        out_shape=[jax.ShapeDtypeStruct((parts // 2, CHUNK, model), BF16)] * 2
        + [jax.ShapeDtypeStruct((length, total), BF16)],
        compiler_params=params(),
    )(order, dproj, dgate, tail, rim, front_w, front_w, front_w, gate_w)


def weight_grad_kernel(segments, sequences, rows, places, order_ref, *refs):
    lefts, rights = refs[: segments * sequences], refs[segments * sequences :]
    rights, outs, total = rights[: segments * sequences], rights[segments * sequences : -1], refs[-1]
    at = 0
    for g in range(segments):
        width = rights[g * sequences].shape[1]
        part = None
        for s in range(sequences):
            left = lefts[g * sequences + s]
            left = left[...] if len(left.shape) == 2 else left[0]
            one = mm(left, rights[g * sequences + s][...], TN)
            part = one if part is None else part + one
        total[:, at : at + width] = part
        at += width
    if places is None:
        outs[0][...] = total[...].astype(BF16)
        return
    dp, context = places
    slot = lax.rem(pl.program_id(0) - order_ref[1] + dp, dp)

    def block(j):
        start = lax.rem(order_ref[0] + j, context) * rows
        return total[pl.ds(pl.multiple_of(start, 8), rows)].astype(BF16)

    outs[0][0] = block(0)
    for j in range(1, context):
        for k in range(dp):

            @pl.when(slot == k)
            def _(j=j, k=k):
                outs[1 + (j - 1) * dp + k][...] = block(j)


def weight_grad(pairs, ordered):
    dp, context = lax.axis_size("dp"), lax.axis_size("context")
    sequences, length = len(pairs[0][0]), pairs[0][1][0].shape[0]
    widths = [right[0].shape[1] for _, right in pairs]
    lefts = [one for left, _ in pairs for one in left]
    rights = [one for _, right in pairs for one in right]
    model = lefts[0].shape[-1]
    total, cut = sum(widths), model // dp
    rows = cut // context
    order = jnp.stack([lax.axis_index("context"), lax.axis_index("dp")]).astype(jnp.int32)
    if ordered:
        others = (context - 1) * dp
        out_specs = [
            pl.BlockSpec(
                (1, rows, total), lambda i, order: (lax.rem(i - order[1] + dp, dp), 0, 0)
            )
        ] + [fixed_block((rows, total))] * others
        out_shape = [jax.ShapeDtypeStruct((dp, rows, total), BF16)] + [
            jax.ShapeDtypeStruct((rows, total), BF16)
        ] * others
    else:
        out_specs = [pl.BlockSpec((cut, total), lambda i, order: (i, 0))]
        out_shape = [jax.ShapeDtypeStruct((model, total), BF16)]
    left_specs, left_arrays = [], []
    for left in lefts:
        if isinstance(left, tuple):
            left_arrays.append(left[0])
            left_specs.append(
                pl.BlockSpec((1, length, cut), lambda i, order, s=left[1]: (s, 0, i))
            )
        else:
            left_arrays.append(left)
            left_specs.append(pl.BlockSpec((length, cut), lambda i, order: (0, i)))
    return kernel_call(
        functools.partial(
            weight_grad_kernel, len(pairs), sequences, rows, (dp, context) if ordered else None
        ),
        cost=10.0,
        grid_spec=pltpu.PrefetchScalarGridSpec(
            num_scalar_prefetch=1,
            grid=(dp,),
            in_specs=left_specs + [fixed_block(one.shape) for one in rights],
            out_specs=out_specs,
            scratch_shapes=[pltpu.VMEM((cut, total), F32)],
        ),
        out_shape=out_shape,
        compiler_params=params(56),
    )(order, *left_arrays, *rights)


def ring_add_kernel(own_ref, *refs):
    total = own_ref[0].astype(F32)
    for one in refs[:-1]:
        total = total + one[...].astype(F32)
    refs[-1][...] = total.astype(refs[-1].dtype)


def ring_add(own, k, terms, kind):
    _, rows, width = own.shape
    return kernel_call(
        ring_add_kernel,
        cost=1.5,
        grid=(1,),
        in_specs=[pl.BlockSpec((1, rows, width), lambda i: (k, 0, 0))]
        + [fixed_block((rows, width))] * len(terms),
        out_specs=fixed_block((rows, width)),
        out_shape=jax.ShapeDtypeStruct((rows, width), kind),
        compiler_params=params(),
    )(own, *terms)


def ring_steps(blocks):
    dp, context = lax.axis_size("dp"), lax.axis_size("context")
    own, others = blocks[0], blocks[1:]
    places = list(range(1, dp)) + [0]
    sides = []
    for k in places:
        side = None
        for j in range(1, context):
            part = others[(j - 1) * dp + k]
            if side is not None:
                part = (side.astype(F32) + part.astype(F32)).astype(BF16)
            side = ring(part, "context")
        sides.append([] if side is None else [side])
    passed = []
    for k, side in zip(places, sides):
        value = ring_add(own, k, side + passed, BF16 if k else F32)
        if k:
            passed = [ring(value, "dp")]
            yield None
        else:
            yield value


def scan_forward_kernel(
    heads, width, p_ref, rim_ref, marks_ref, cw_ref, hp_ref, skip_ref, exp_ref,
    z_ref, y_ref, st_ref, end_ref, gr_ref, vbuf, state, offset,
):
    chunk = pl.program_id(0)
    aux = column_of(marks_ref[...])

    @pl.when(chunk == 0)
    def _():
        vbuf[0:8] = rim_ref[...].astype(F32)
        state[...] = jnp.zeros_like(state)
        offset[...] = jnp.zeros_like(offset)

    @pl.when(chunk > 0)
    def _():
        vbuf[0:8] = vbuf[CHUNK : CHUNK + 8]

    vbuf[8:, :width] = rounded(p_ref[:, :width])
    vbuf[8:, width:] = rounded(p_ref[:, width + LANES :])
    z = cw_ref[4:5] + cw_ref[3:4] * vbuf[8:]
    for k in range(3):
        z = z + cw_ref[k : k + 1] * vbuf[5 + k : 5 + k + CHUNK] * aux[:, k : k + 1]
    z_ref[...] = z
    act = z * jax.nn.sigmoid(z)
    x = act[:, :width]
    b_val, c_val = act[:, width : width + LANES], act[:, width + LANES :]
    lane = iota(1)
    step = jnp.where(
        lane < heads, softplus(p_ref[:, width : width + LANES] + hp_ref[0:1]), 0.0
    )
    decay = hp_ref[1:2] * step
    cum = lax.dot_general(
        (iota(0) >= iota(1)).astype(F32), decay, NN, precision=HIGH, preferred_element_type=F32
    )
    cum_t = cum.T
    seg_col = aux[:, 5:6]
    link = jnp.where((seg_col == marks_ref[5:6]) & (iota(0) >= iota(1)), 0.0, NO_LINK)
    scores = wide_mm(c_val, b_val, NT)
    growth = jnp.exp(cum) * aux[:, 3:4]
    last = cum[CHUNK - 1 : CHUNK]
    weight = jnp.exp(last - cum) * (seg_col == seg_col[CHUNK - 1 : CHUNK]).astype(F32)
    wide = split_dot(jnp.concatenate([step, growth, weight], axis=0), exp_ref[...])
    step_e, growth_e, weight_e = wide[:CHUNK], wide[CHUNK : 2 * CHUNK], wide[2 * CHUNK :]
    xd = x * step_e
    lower = lane < LANES // 2
    pieces = []
    for pair in range(heads // 2):
        mats = []
        for head in (2 * pair, 2 * pair + 1):
            spread = cum[:, head : head + 1] - cum_t[head : head + 1, :]
            mats.append(jnp.exp(spread + link) * scores)
        tile = xd[:, pair * LANES : (pair + 1) * LANES]
        pieces.append(wide_mm(jnp.concatenate(mats, axis=1), head_halves(tile, lower)))
    held = state[...]
    st_ref[0] = held
    carried = wide_mm(c_val, held) * growth_e
    y_ref[...] = jnp.concatenate(pieces, axis=1) + carried + skip_ref[...] * x
    new = held * growth_e[CHUNK - 1 : CHUNK] + wide_mm(b_val, xd * weight_e, TN)
    state[...] = new
    end_ref[...] = new
    gr_ref[...] = jnp.exp(offset[...] + cum) * aux[:, 4:5]
    offset[...] = offset[...] + last


def row_spec(width, at=None, rows=CHUNK):
    if at is None:
        return pl.BlockSpec((rows, width), lambda i: (i, 0))
    return pl.BlockSpec((rows, width), lambda i: (i, at))


def whole(shape):
    return pl.BlockSpec(shape, lambda i: (0,) * len(shape))


def scan_forward(proj, rim, marks, consts):
    length, total = proj.shape
    heads, width = consts["heads"], consts["width"]
    chunks, conv = length // CHUNK, total - LANES
    return kernel_call(
        functools.partial(scan_forward_kernel, heads, width),
        cost=9.5,
        grid=(chunks,),
        in_specs=[
            row_spec(total),
            whole((8, conv)),
            pl.BlockSpec((8, CHUNK), lambda i: (0, i)),
            whole((8, conv)),
            whole((8, LANES)),
            whole((1, width)),
            whole((LANES, width)),
        ],
        out_specs=[
            row_spec(conv),
            row_spec(width),
            pl.BlockSpec((1, LANES, width), lambda i: (i, 0, 0)),
            whole((LANES, width)),
            row_spec(LANES),
        ],
        out_shape=[
            jax.ShapeDtypeStruct((length, conv), F32),
            jax.ShapeDtypeStruct((length, width), F32),
            jax.ShapeDtypeStruct((chunks, LANES, width), F32),
            jax.ShapeDtypeStruct((LANES, width), F32),
            jax.ShapeDtypeStruct((length, LANES), F32),
        ],
        scratch_shapes=[
            pltpu.VMEM((CHUNK + 8, conv), F32),
            pltpu.VMEM((LANES, width), F32),
            pltpu.VMEM((1, LANES), F32),
        ],
        compiler_params=params(),
    )(proj, rim, marks, consts["cw"], consts["hp"], consts["skip"], consts["exp"])


def mix_forward_kernel(y0_ref, zc_ref, gr_ref, sin_ref, gate_ref, exp_ref, y_ref, sq_ref):
    c_val = zc_ref[...] * jax.nn.sigmoid(zc_ref[...])
    carried = wide_mm(c_val, sin_ref[...].astype(F32))
    y = y0_ref[...] + carried * split_dot(gr_ref[...], exp_ref[...])
    y_ref[...] = y
    gate = gate_ref[...]
    gated = y * (gate * jax.nn.sigmoid(gate))
    square = jnp.sum(gated * gated, axis=1, keepdims=True)
    sq_ref[...] = jnp.broadcast_to(square, (CHUNK, CHUNK)).T[:8]


def mix_forward(y0, z, growth, carried, gate, consts):
    length, width = y0.shape
    last = z.shape[1] // LANES - 1
    return kernel_call(
        mix_forward_kernel,
        cost=3.6,
        grid=(length // CHUNK,),
        in_specs=[
            row_spec(width),
            row_spec(LANES, last),
            row_spec(LANES),
            whole((LANES, width)),
            row_spec(width),
            whole((LANES, width)),
        ],
        out_specs=[row_spec(width), pl.BlockSpec((8, CHUNK), lambda i: (0, i))],
        out_shape=[
            jax.ShapeDtypeStruct((length, width), F32),
            jax.ShapeDtypeStruct((8, length), F32),
        ],
        compiler_params=params(),
    )(y0, z, growth, carried, gate, consts["exp"])


def project_out_kernel(channels, parts, order_ref, y_ref, gate_ref, gain_ref, w_ref, *refs):
    squares, (sent_ref, kept_ref, rows) = refs[:-3], refs[-3:]
    half = parts // 2

    @pl.when(pl.program_id(0) == 0)
    def _():
        for m in range(parts):
            source = pl.ds(pl.multiple_of(order_ref[m] * CHUNK, CHUNK), CHUNK)
            square = sum(one[:, source] for one in squares)
            scale = lax.rsqrt(column_of(square)[:, 1:2] / channels + eps)
            gate = gate_ref[source]
            gated = y_ref[source] * (gate * jax.nn.sigmoid(gate))
            rows[m * CHUNK : (m + 1) * CHUNK] = (gated * scale * gain_ref[...]).astype(BF16)

    total = mm(rows[...], w_ref[...], NT).astype(sent_ref.dtype)
    for m in range(half):
        sent_ref[m] = total[m * CHUNK : (m + 1) * CHUNK]
        kept_ref[m] = total[(half + m) * CHUNK : (half + m + 1) * CHUNK]


def project_out(y, gate, squares, channels, kind, order, consts):
    length, width = y.shape
    weights, at = consts["out"]
    model, parts = weights.shape[0], length // CHUNK
    cut = model // 4
    half = pl.BlockSpec((parts // 2, CHUNK, cut), lambda i, order: (0, 0, i))
    return kernel_call(
        functools.partial(project_out_kernel, float(channels), parts),
        cost=5.7,
        grid_spec=pltpu.PrefetchScalarGridSpec(
            num_scalar_prefetch=1,
            grid=(4,),
            in_specs=[
                fixed_block((length, width)),
                fixed_block((length, width)),
                fixed_block((1, width)),
                pl.BlockSpec((cut, width), lambda i, order: (i, at)),
            ]
            + [fixed_block((8, length))] * len(squares),
            out_specs=[half, half],
            scratch_shapes=[pltpu.VMEM((length, width), BF16)],
        ),
        out_shape=[jax.ShapeDtypeStruct((parts // 2, CHUNK, model), kind)] * 2,
        compiler_params=params(),
    )(order, y, gate, consts["gain"], weights, *squares)


def grad_scaled_kernel(count, order_ref, *refs):
    pieces, rest = refs[:count], refs[count:]
    w_ref, y_ref, gate_ref, gain_ref, gs_ref, dot_ref = rest[:6]
    sums = rest[-1]
    step = pl.program_id(0)
    length = gs_ref.shape[0]
    if count > 1:

        @pl.when(step == 0)
        def _():
            for m in range(count):
                place = pl.ds(pl.multiple_of(order_ref[m] * CHUNK, CHUNK), CHUNK)
                rest[6][place] = pieces[m][...]

        rows = rest[6][...]
    else:
        rows = pieces[0][0]
    grad = mm(rows, w_ref[...])
    gs_ref[...] = grad
    gate = gate_ref[...]
    gated = y_ref[...] * (gate * jax.nn.sigmoid(gate))
    product = jnp.sum(grad * gain_ref[...] * gated, axis=1, keepdims=True)
    square = jnp.sum(gated * gated, axis=1, keepdims=True)
    lane = lax.broadcasted_iota(jnp.int32, (length, LANES), 1)
    part = jnp.where(lane == 0, product, square)

    @pl.when(step == 0)
    def _():
        sums[...] = part

    @pl.when(step > 0)
    def _():
        sums[...] += part

    @pl.when(step == pl.num_programs(0) - 1)
    def _():
        for m in range(length // CHUNK):
            at = slice(m * CHUNK, (m + 1) * CHUNK)
            dot_ref[:, at] = sums[at].T[:8]


def grad_scaled(source, y, gate, order, consts):
    length, width = y.shape
    weights, at = consts["out"]
    model, half = weights.shape[0], width // 2
    part = pl.BlockSpec((length, half), lambda i, order: (0, i))
    out_specs = [part, fixed_block((8, length))]
    out_shape = [
        jax.ShapeDtypeStruct((length, width), F32),
        jax.ShapeDtypeStruct((8, length), F32),
    ]
    if len(source) == 2:
        stream, sequence = source
        inputs, count = [stream], 1
        specs = [pl.BlockSpec((1, length, model), lambda i, order: (sequence, 0, 0))]
    else:
        inputs, count = [one for one, _ in source], len(source)
        specs = piece_specs(source, CHUNK)
        out_specs.append(fixed_block((length, model)))
        out_shape.append(jax.ShapeDtypeStruct((length, model), BF16))
    out = kernel_call(
        functools.partial(grad_scaled_kernel, count),
        cost=4.5,
        grid_spec=pltpu.PrefetchScalarGridSpec(
            num_scalar_prefetch=1,
            grid=(2,),
            in_specs=specs
            + [
                pl.BlockSpec((model, half), lambda i, order: (0, 2 * at + i)),
                part,
                part,
                pl.BlockSpec((1, half), lambda i, order: (0, i)),
            ],
            out_specs=out_specs,
            scratch_shapes=[pltpu.VMEM((length, LANES), F32)],
        ),
        out_shape=out_shape,
        compiler_params=params(),
    )(order, *inputs, weights, y, gate, consts["gain"])
    return out if count > 1 else (*out, source)


def mix_backward_kernel(
    channels, shares, gs_ref, y_ref, gate_ref, zx_ref, zc_ref, gr_ref, gain_ref, exp_ref, *refs
):
    shared, refs = refs[:shares], refs[shares:]
    scaled_ref, dgate_ref, dy_ref, acc_ref, dsin_ref, dsin = refs
    at = pl.program_id(0)

    @pl.when(at == 0)
    def _():
        acc_ref[...] = jnp.zeros_like(acc_ref)
        dsin[...] = jnp.zeros_like(dsin)

    stats = column_of(sum(one[...] for one in shared))
    scale = lax.rsqrt(stats[:, 1:2] / channels + eps)
    pull = scale * scale * scale * stats[:, 0:1] / channels
    grad, y, gate = gs_ref[...], y_ref[...], gate_ref[...]
    silu, sig = silu_parts(gate)
    gated = y * silu
    unit = gated * scale
    scaled_ref[...] = (unit * gain_ref[...]).astype(BF16)
    dgated = grad * gain_ref[...] * scale - gated * pull
    dy = dgated * silu
    dy_ref[...] = dy
    dgate_ref[...] = (dgated * y * (sig * (1.0 + gate * (1.0 - sig)))).astype(BF16)
    x = zx_ref[...] * jax.nn.sigmoid(zx_ref[...])
    acc_ref[0:1] += jnp.sum(grad * unit, axis=0, keepdims=True)
    acc_ref[1:2] += jnp.sum(dy * x, axis=0, keepdims=True)
    c_low = (zc_ref[...] * jax.nn.sigmoid(zc_ref[...])).astype(BF16)
    dsin[...] += mm(c_low, (dy * split_dot(gr_ref[...], exp_ref[...])).astype(BF16), TN)

    @pl.when(at == pl.num_programs(0) - 1)
    def _():
        dsin_ref[...] = dsin[...].astype(BF16)


def mix_backward(grad, y, gate, z, growth, stats, channels, consts):
    length, width = y.shape
    last = z.shape[1] // LANES - 1
    stat = pl.BlockSpec((8, CHUNK), lambda i: (0, i))
    return kernel_call(
        functools.partial(mix_backward_kernel, float(channels), len(stats)),
        cost=5.0,
        grid=(length // CHUNK,),
        in_specs=[
            row_spec(width),
            row_spec(width),
            row_spec(width),
            row_spec(width),
            row_spec(LANES, last),
            row_spec(LANES),
            whole((1, width)),
            whole((LANES, width)),
        ]
        + [stat] * len(stats),
        out_specs=[
            row_spec(width),
            row_spec(width),
            row_spec(width),
            whole((8, width)),
            whole((LANES, width)),
        ],
        out_shape=[
            jax.ShapeDtypeStruct((length, width), BF16),
            jax.ShapeDtypeStruct((length, width), BF16),
            jax.ShapeDtypeStruct((length, width), F32),
            jax.ShapeDtypeStruct((8, width), F32),
            jax.ShapeDtypeStruct((LANES, width), BF16),
        ],
        scratch_shapes=[pltpu.VMEM((LANES, width), F32)],
        compiler_params=params(),
    )(grad, y, gate, z, z, growth, consts["gain"], consts["exp"], *stats)


def scan_backward_kernel(
    heads, width, chunks, dy_ref, z_ref, p_ref, before_ref, rim_ref, marks_ref, cw_ref,
    hp_ref, skip_ref, exp_ref, red_ref, st_ref, sin_ref, grprev_ref, dend_ref,
    dproj_ref, wacc_ref, hacc_ref, tail_ref, drim_ref, vbuf, zbuf, dstate,
):
    step_at = pl.program_id(0)
    chunk = chunks - 1 - step_at
    aux = column_of(marks_ref[...])

    @pl.when(step_at == 0)
    def _():
        dstate[...] = dend_ref[...].astype(F32)
        zbuf[...] = jnp.zeros_like(zbuf)
        wacc_ref[...] = jnp.zeros_like(wacc_ref)
        hacc_ref[...] = jnp.zeros_like(hacc_ref)

    @pl.when(chunk == 0)
    def _():
        vbuf[0:8] = rim_ref[...].astype(F32)

    @pl.when(chunk > 0)
    def _():
        vbuf[0:8, :width] = rounded(before_ref[:, :width])
        vbuf[0:8, width:] = rounded(before_ref[:, width + LANES :])

    vbuf[8:, :width] = rounded(p_ref[:, :width])
    vbuf[8:, width:] = rounded(p_ref[:, width + LANES :])

    z = z_ref[...]
    act, sig = silu_parts(z)
    slope = sig * (1.0 + z * (1.0 - sig))
    x = act[:, :width]
    b_val, c_val = act[:, width : width + LANES], act[:, width + LANES :]
    lane = iota(1)
    pre = p_ref[:, width : width + LANES] + hp_ref[0:1]
    step = jnp.where(lane < heads, softplus(pre), 0.0)
    decay = hp_ref[1:2] * step
    cum = lax.dot_general(
        (iota(0) >= iota(1)).astype(F32), decay, NN, precision=HIGH, preferred_element_type=F32
    )
    cum_t = cum.T
    seg_col = aux[:, 5:6]
    link = jnp.where((seg_col == marks_ref[5:6]) & (iota(0) <= iota(1)), 0.0, NO_LINK)
    growth = jnp.exp(cum) * aux[:, 3:4]
    last = cum[CHUNK - 1 : CHUNK]
    weight = jnp.exp(last - cum) * (seg_col == seg_col[CHUNK - 1 : CHUNK]).astype(F32)
    reach = jnp.where(chunk == 0, 1.0, grprev_ref[7:8])
    wide = split_dot(
        jnp.concatenate([step, growth, weight, jnp.broadcast_to(reach, (8, LANES))], axis=0),
        exp_ref[...],
    )
    step_e, growth_e = wide[:CHUNK], wide[CHUNK : 2 * CHUNK]
    weight_e, reach_e = wide[2 * CHUNK : 3 * CHUNK], wide[3 * CHUNK : 3 * CHUNK + 1]
    held = st_ref[0] + sin_ref[...].astype(F32) * reach_e
    after = dstate[...]
    xd = x * step_e
    dy = dy_ref[...]
    scores = wide_mm(b_val, c_val, NT)
    carried = low_mm(c_val, held) * growth_e
    fed = low_mm(b_val, after) * weight_e
    dy_grown = dy * growth_e
    lower = lane < LANES // 2
    dscores = jnp.zeros((CHUNK, CHUNK), F32)
    into = jnp.zeros((CHUNK, CHUNK), F32)
    rows, pieces = [], []
    for pair in range(heads // 2):
        at = slice(pair * LANES, (pair + 1) * LANES)
        products = wide_mm(head_halves(xd[:, at], lower), dy[:, at], NT)
        mats = []
        for side, head in enumerate((2 * pair, 2 * pair + 1)):
            spread = cum_t[head : head + 1, :] - cum[:, head : head + 1]
            reachable = jnp.exp(spread + link)
            product = products[side * CHUNK : (side + 1) * CHUNK]
            mat = reachable * scores
            dscores = dscores + reachable * product
            energy = mat * product
            rows.append(jnp.sum(energy, axis=0, keepdims=True))
            into = jnp.where(lane == head, jnp.sum(energy, axis=1, keepdims=True), into)
            mats.append(mat)
        pieces.append(low_mm(jnp.concatenate(mats, axis=1), head_halves(dy[:, at], lower)))
    dxd = jnp.concatenate(pieces, axis=1) + fed
    kept = jnp.sum(after * held, axis=0, keepdims=True) * growth_e[CHUNK - 1 : CHUNK]
    sums = split_dot(
        jnp.concatenate(
            [dy * carried, xd * fed, dxd * x, jnp.broadcast_to(kept, (8, width))], axis=0
        ),
        red_ref[...],
    )
    out_of, fed_sum = sums[:CHUNK], sums[CHUNK : 2 * CHUNK]
    dstep, kept_sum = sums[2 * CHUNK : 3 * CHUNK], sums[3 * CHUNK : 3 * CHUNK + 1]
    rows = column_of(jnp.concatenate(rows, axis=0))
    dcum = rows - into + out_of - fed_sum
    end_term = kept_sum + jnp.sum(fed_sum, axis=0, keepdims=True)
    ddecay = (
        lax.dot_general(
            (iota(0) <= iota(1)).astype(F32), dcum, NN, precision=HIGH, preferred_element_type=F32
        )
        + end_term
    )
    ddecay = jnp.where(lane < heads, ddecay, 0.0)
    dpre = jnp.where(lane < heads, (dstep + hp_ref[1:2] * ddecay) * jax.nn.sigmoid(pre), 0.0)
    hacc_ref[0:1] += jnp.sum(dpre, axis=0, keepdims=True)
    hacc_ref[1:2] += jnp.sum(ddecay * decay, axis=0, keepdims=True)
    dx = dxd * step_e + skip_ref[...] * dy
    db = wide_mm(dscores, c_val) + wide_mm(xd * weight_e, after, NT)
    dc = wide_mm(dscores, b_val, TN) + wide_mm(dy_grown, held, NT)
    dstate[...] = after * growth_e[CHUNK - 1 : CHUNK] + wide_mm(c_val, dy_grown, TN)

    dz = jnp.concatenate([dx, db, dc], axis=1) * slope
    wacc_ref[3:4] += jnp.sum(dz * vbuf[8:], axis=0, keepdims=True)
    wacc_ref[4:5] += jnp.sum(dz, axis=0, keepdims=True)
    dv = cw_ref[3:4] * dz
    for k in range(3):
        masked = dz * aux[:, k : k + 1]
        wacc_ref[k : k + 1] += jnp.sum(
            masked * vbuf[5 + k : 5 + k + CHUNK], axis=0, keepdims=True
        )
        zbuf[k, 8 : 8 + CHUNK] = masked
        dv = dv + cw_ref[k : k + 1] * zbuf[k, 11 - k : 11 - k + CHUNK]
    dproj_ref[:, :width] = dv[:, :width].astype(BF16)
    dproj_ref[:, width : width + LANES] = dpre.astype(BF16)
    dproj_ref[:, width + LANES :] = dv[:, width:].astype(BF16)

    @pl.when(step_at == 0)
    def _():
        tail_ref[...] = dv[CHUNK - 16 :]

    @pl.when(chunk == 0)
    def _():
        drim = cw_ref[0:1] * zbuf[0, 3:11]
        for k in (1, 2):
            drim = drim + cw_ref[k : k + 1] * zbuf[k, 3 - k : 11 - k]
        drim_ref[0:8] = jnp.zeros_like(drim)
        drim_ref[8:] = drim

    for k in range(3):
        zbuf[k, 8 + CHUNK :] = zbuf[k, 8:16]


def scan_backward(dy, z, proj, rim, marks, states, carried, growth, dend, consts):
    length, total = proj.shape
    heads, width = consts["heads"], consts["width"]
    chunks, conv = length // CHUNK, total - LANES
    eights = CHUNK // 8

    def back(columns):
        return pl.BlockSpec((CHUNK, columns), lambda i: (chunks - 1 - i, 0))

    def previous(columns):
        return pl.BlockSpec(
            (8, columns), lambda i: (jnp.maximum((chunks - 1 - i) * eights - 1, 0), 0)
        )

    return kernel_call(
        functools.partial(scan_backward_kernel, heads, width, chunks),
        cost=18.0,
        grid=(chunks,),
        in_specs=[
            back(width),
            back(conv),
            back(total),
            previous(total),
            whole((8, conv)),
            pl.BlockSpec((8, CHUNK), lambda i: (0, chunks - 1 - i)),
            whole((8, conv)),
            whole((8, LANES)),
            whole((1, width)),
            whole((LANES, width)),
            whole((width, LANES)),
            pl.BlockSpec((1, LANES, width), lambda i: (chunks - 1 - i, 0, 0)),
            whole((LANES, width)),
            previous(LANES),
            whole((LANES, width)),
        ],
        out_specs=[
            back(total),
            whole((8, conv)),
            whole((8, LANES)),
            whole((16, conv)),
            whole((16, conv)),
        ],
        out_shape=[
            jax.ShapeDtypeStruct((length, total), BF16),
            jax.ShapeDtypeStruct((8, conv), F32),
            jax.ShapeDtypeStruct((8, LANES), F32),
            jax.ShapeDtypeStruct((16, conv), F32),
            jax.ShapeDtypeStruct((16, conv), F32),
        ],
        scratch_shapes=[
            pltpu.VMEM((CHUNK + 8, conv), F32),
            pltpu.VMEM((3, CHUNK + 16, conv), F32),
            pltpu.VMEM((LANES, width), F32),
        ],
        compiler_params=params(),
    )(
        dy, z, proj, proj, rim, marks, consts["cw"], consts["hp"], consts["skip"],
        consts["exp"], consts["red"], states, carried, growth, dend,
    )


def local(
    stream,
    seg_ids,
    input_weight,
    step_size_weight,
    coefficient_weight,
    pre_gain,
    conv_bc,
    bias_bc,
    output_weight,
    conv_x,
    bias_x,
    dt_bias,
    a_log,
    skip,
    gate_gain,
    cotangent,
):
    PRECEDING.clear()
    layers, rows_in, _, width = input_weight.shape
    sequences, length, model = stream.shape
    heads = dt_bias.shape[1]
    depth = width // heads
    shared = coefficient_weight.shape[2]
    dp, context, tensor = (lax.axis_size(a) for a in ("dp", "context", "tensor"))
    channels = width * tensor
    rows_bc = rows_in // tensor
    conv, total = width + shared, width + LANES + shared
    layer_range, seq_range = range(layers), range(sequences)

    own_gain, own_conv = pre_gain.shape[1], conv_bc.shape[2]
    small = jnp.concatenate([pre_gain, conv_bc.reshape(layers, -1), bias_bc], axis=1)
    small = jnp.pad(small, ((0, 0), (0, shared - small.shape[1])))[:, None]
    bc_rows = gather_small(jnp.concatenate([coefficient_weight, small], axis=1), ("tensor",))
    small, bc_rows = bc_rows[:, :, rows_bc], bc_rows[:, :, :rows_bc]
    taps = small[:, :, own_gain : own_gain + 5 * own_conv].reshape(tensor, layers, 5, own_conv)
    taps = jnp.moveaxis(taps, 0, 2).reshape(layers, -1)
    small = jnp.concatenate(
        [
            jnp.moveaxis(small[:, :, :own_gain], 0, 1).reshape(layers, rows_in),
            jnp.pad(taps, ((0, 0), (0, rows_in - taps.shape[1]))),
        ],
        axis=0,
    ).T

    def first_piece(layer):
        tile = jnp.concatenate(
            [
                step_size_weight[layer],
                small,
                jnp.zeros((rows_in, LANES - heads - 2 * layers), BF16),
                bc_rows[:, layer].reshape(rows_in, shared),
            ],
            axis=1,
        )
        return [input_weight[layer, :, 1], tile]

    def second_piece(layer):
        return [input_weight[layer, :, 0], output_weight[layer].T]

    edge_ids = shifted(seg_ids[:, -3:], "context", 1)
    ext_ids = jnp.concatenate([edge_ids, seg_ids], axis=1)
    prior = ext_ids[:, 2 : 2 + length].reshape(sequences, length // CHUNK, CHUNK)[:, :, 0]
    prior = jnp.repeat(prior, CHUNK, axis=1)
    aux_all = jnp.stack(
        [ext_ids[:, k : k + length] == seg_ids for k in range(3)]
        + [seg_ids == prior, seg_ids == edge_ids[:, 2:3], seg_ids, seg_ids, seg_ids],
        axis=1,
    ).astype(F32)

    spread_table = (jnp.arange(LANES)[:, None] == jnp.arange(width)[None, :] // depth).astype(BF16)

    def joined(*parts):
        return jnp.concatenate([one for part in parts for one in part], axis=1)

    third = total // 3
    upper_piece = joined(second_piece(1), first_piece(1))
    table, second_table = [], []
    halo = shifted(stream[:, length - 16 :], "context", 1)
    precede(halo, edge_ids)
    for _ in ring_pieces(table, joined(first_piece(0))):
        pass
    second_ring = ring_pieces(second_table, relayed(joined(second_piece(0))))
    next(second_ring)
    places = jnp.arange(length // CHUNK, dtype=jnp.int32)
    arrived, sending = rows_order(False), rows_order(True)
    own_place = lax.axis_index("tensor").astype(jnp.int32)[None]
    precede(aux_all, spread_table, spread_table.T, arrived, sending)
    first, tile_rows = placed(table, [total], width)

    def every_row(part):
        return lax.all_gather(part, ("dp", "context"), axis=0, tiled=True)

    weights = [
        {"front": (first, 0)},
        {},
    ]
    streams = [(stream, s) for s in seq_range]
    grads = [(cotangent, s) for s in seq_range]
    small = tile_rows[heads : heads + 2 * layers]
    gains = small[:layers]
    taps = small[layers:].reshape(layers, dp * context, rows_in)[:, :, : 5 * tensor * own_conv]
    taps = taps.reshape(layers, dp * context, 5, tensor * own_conv)
    taps = jnp.moveaxis(taps, 1, 2).reshape(layers, 5, shared)

    consts = []
    for layer in layer_range:
        cw = jnp.concatenate(
            [
                jnp.concatenate(
                    [jnp.concatenate([conv_x[layer], bias_x[layer][None]], axis=0), taps[layer]],
                    axis=1,
                ),
                jnp.zeros((3, conv), F32),
            ],
            axis=0,
        )
        pad = jnp.zeros((LANES - heads,), F32)
        hp = jnp.stack(
            [
                jnp.concatenate([dt_bias[layer], pad]),
                jnp.concatenate([-jnp.exp(a_log[layer]), pad]),
            ]
            + [jnp.zeros((LANES,), F32)] * 6
        )
        consts.append(
            {
                "heads": heads,
                "width": width,
                "cw": cw,
                "hp": hp,
                "skip": jnp.repeat(skip[layer], depth)[None],
                "gain": gate_gain[layer][None],
                "exp": spread_table,
                "red": spread_table.T,
                **weights[layer],
            }
        )

    def chain(value, total, steps):
        carried = shifted(value, "context", steps)
        for _ in range(context - 2):
            passed = value.astype(F32) + carried.astype(F32) * total
            carried = shifted(passed.astype(value.dtype), "context", steps)
        return carried

    def through(growth):
        return jnp.repeat(growth[length - 1, :heads], depth)[None]

    for const in consts:
        precede(const["cw"], const["hp"], const["skip"], const["gain"])
    precede(gains)
    incoming = [(stream, halo, s) for s in seq_range]
    work = [[{} for _ in seq_range] for _ in layer_range]
    outputs = []
    top = layers - 1
    def step_project(layer, s):
        k = work[layer][s]
        k["stream"] = streams[s]
        k["normed"], k["proj"], tail = project(
            incoming[s],
            None if layer else gains[0:1],
            arrived if layer else places,
            consts[layer]["front"],
            width,
            total,
        )
        k["rim"] = shifted(tail, "context", 1) if layer else tail

    def step_scan(layer, s):
        k = work[layer][s]
        k["z"], k["y0"], k["states"], end, k["growth"] = scan_forward(
            k["proj"], k["rim"], aux_all[s], consts[layer]
        )
        k["carried"] = chain(end, through(k["growth"]), 1)

    def step_gate(layer, s):
        k = work[layer][s]
        k["gate"] = plain_product(k["normed"], consts[layer]["gate"], width)

    def step_mix(layer, s):
        k = work[layer][s]
        k["y"], squares = mix_forward(
            k["y0"], k["z"], k["growth"], k["carried"], k["gate"], consts[layer]
        )
        if layer < top:
            k["squares"] = from_others(squares, "tensor")

    def step_out(layer, s):
        k = work[layer][s]
        kind = BF16 if layer == top else F32
        sent, own = project_out(
            k["y"], k["gate"], k["squares" if layer < top else "stats"], channels, kind, sending,
            consts[layer],
        )
        k["out"] = [own, flipped(sent, "tensor", 0)]

    def step_pass(layer, s, name):
        terms = work[layer][s][name]
        terms.append(flipped(pass_on(*terms), "tensor", 1))

    def step_norm(layer, s):
        k = work[layer][s]
        gain = None if layer == top else gains[layer + 1 : layer + 2]
        *new, low = norm_forward(streams[s], k["out"], gain, own_place)
        streams[s] = new[0] if new else None
        k["rows"] = [low, flipped(low, "tensor", 1)]

    def step_join(layer, s, name):
        own, other = work[layer][s][name]
        across = flipped(joined_rows(own, other), "tensor", 0)
        return [(own, 0), (other, 0), (across, 0), (across, 1)]

    def step_grad(layer, s):
        k = work[layer][s]
        source = (cotangent, s) if layer == top else incoming[s]
        k["grad"], dots, k["low"] = grad_scaled(
            source, k["y"], k["gate"], places if layer == top else arrived, consts[layer]
        )
        k["stats"] = from_others(dots, "tensor")

    def step_mix_back(layer, s):
        k = work[layer][s]
        k["scaled"], k["dgate"], k["dy"], k["acc"], dsin = mix_backward(
            k["grad"], k["y"], k["gate"], k["z"], k["growth"], k["stats"], channels, consts[layer],
        )
        k["dend"] = chain(dsin, through(k["growth"]), -1)

    def step_scan_back(layer, s):
        k = work[layer][s]
        k["dproj"], k["wacc"], k["hacc"], k["tail"], drim = scan_backward(
            k["dy"], k["z"], k["proj"], k["rim"], aux_all[s], k["states"],
            k["carried"], k["growth"], k["dend"], consts[layer],
        )
        k["drim"] = shifted(drim, "context", -1)

    def step_input_grad(layer, s):
        k = work[layer][s]
        sent, own, k["dproj"] = input_grad(
            k["dproj"], k["dgate"], k["tail"], k["drim"], consts[layer]["front"],
            consts[layer]["gate"], sending,
        )
        k["back"] = [own, flipped(sent, "tensor", 0)]

    def step_norm_back(layer, s):
        k = work[layer][s]
        grads[s], low, k["dgain"] = norm_backward(
            k["stream"], k["back"], grads[s], gains[layer : layer + 1], own_place
        )
        k["grad_low"] = [low, flipped(low, "tensor", 1)]

    def every(layer, name):
        return [k[name] for k in work[layer]]

    def step_second_grad(layer):
        return weight_grad(
            [
                (every(layer, "normed"), every(layer, "dgate")),
                (every(layer, "low"), every(layer, "scaled")),
            ],
            layer == 0,
        )

    def step_first_grad(layer):
        return weight_grad([(every(layer, "normed"), every(layer, "dproj"))], layer == 0)

    def scattered(value):
        return lax.psum_scatter(value, ("dp", "context"), scatter_dimension=0, tiled=True)

    second_sums, first_sums = [None] * layers, [None] * layers
    project_0, scan_0, gate_0, mix_0, out_0, grad_0, mixed_0, scanned_0, input_0 = (
        functools.partial(step, 0)
        for step in (
            step_project, step_scan, step_gate, step_mix, step_out, step_grad, step_mix_back,
            step_scan_back, step_input_grad,
        )
    )
    project_1, scan_1, gate_1, mix_1, out_1, grad_1, mixed_1, scanned_1, input_1 = (
        functools.partial(step, 1)
        for step in (
            step_project, step_scan, step_gate, step_mix, step_out, step_grad, step_mix_back,
            step_scan_back, step_input_grad,
        )
    )

    project_0(0)
    next(second_ring)
    scan_0(0)
    next(second_ring)
    upper = every_row(relayed(upper_piece))
    consts[1].update(front=(upper, 2 * width // third), gate=(upper, 0), out=(upper, 1))
    project_0(1)
    next(second_ring, None)
    scan_0(1)
    precede(work[0][0]["carried"])
    (second,) = placed(second_table, [2 * width])
    consts[0].update(gate=(second, 0), out=(second, 1))
    gate_0(0)
    mix_0(0)
    gate_0(1)
    mix_0(1)
    out_0(0)
    step_pass(0, 0, "out")
    out_0(1)
    step_norm(0, 0)
    step_pass(0, 1, "out")
    incoming[0] = step_join(0, 0, "rows")
    project_1(0)
    step_norm(0, 1)
    incoming[1] = step_join(0, 1, "rows")
    scan_1(0)
    project_1(1)
    gate_1(0)
    scan_1(1)
    mix_1(0)
    gate_1(1)
    grad_1(0)
    mix_1(1)
    grad_1(1)
    mixed_1(0)
    mixed_1(1)
    precede(work[1][0]["dend"])
    second_sums[1] = scattered(step_second_grad(1)[0])
    scanned_1(0)
    out_1(0)
    precede(work[1][1]["dend"])
    input_1(0)
    step_pass(1, 0, "back")
    scanned_1(1)
    step_norm_back(1, 0)
    out_1(1)
    input_1(1)
    incoming[0] = step_join(1, 0, "grad_low")
    step_pass(1, 1, "back")
    grad_0(0)
    step_pass(1, 0, "out")
    step_pass(1, 1, "out")
    precede(*work[0][0]["stats"])
    first_grad = step_first_grad(1)
    mixed_0(0)
    step_norm_back(1, 1)
    precede(second_sums[1])
    first_sums[1] = scattered(first_grad[0])
    scanned_0(0)
    for s in seq_range:
        step_norm(1, s)
    incoming[1] = step_join(1, 1, "grad_low")
    grad_0(1)
    input_0(0)
    mixed_0(1)
    second_steps = ring_steps(step_second_grad(0))
    step_pass(0, 0, "back")
    precede(first_sums[1])
    scanned_0(1)
    outputs.extend(step_join(1, s, "rows") for s in seq_range)
    next(second_steps)
    step_norm_back(0, 0)
    input_0(1)
    first_steps = ring_steps(step_first_grad(0))
    step_pass(0, 1, "back")
    next(second_steps)
    incoming[0] = step_join(0, 0, "grad_low")
    next(first_steps)
    layer_out = assembled(outputs, arrived)
    step_norm_back(0, 1)
    small_steps = small_sums(work, width, heads, model, consts[0]["red"])
    next(small_steps)
    next(first_steps)
    next(small_steps)
    next(second_steps)
    second_sums[1], first_sums[1] = widened(second_sums[1]), widened(first_sums[1])
    incoming[1] = step_join(0, 1, "grad_low")
    next(first_steps)
    next(small_steps)
    grad_stream = assembled(incoming, arrived)
    first_sums[0] = next(first_steps)
    next(small_steps)
    second_sums[0] = next(second_steps)
    for value in small_steps:
        small_out = value

    out = []
    for layer in layer_range:
        second_sum, first_sum = second_sums[layer], first_sums[layer]
        out.append(
            (
                jnp.stack([second_sum[:, :width], first_sum[:, :width]], axis=1),
                first_sum[:, width : width + heads],
                scatter_places(first_sum[:, width + LANES :]),
                second_sum[:, width:].T,
            )
        )
    taps_x, sum_bias_x, dt_sum, rate_sum, skip_sum, gate_sum, taps_bc, sum_bias_bc, gain_sum = (
        small_out
    )
    return (
        layer_out,
        grad_stream,
        jnp.stack([o[0] for o in out]),
        jnp.stack([o[1] for o in out]),
        jnp.stack([o[2] for o in out]),
        gain_sum,
        taps_bc,
        sum_bias_bc,
        jnp.stack([o[3] for o in out]),
        taps_x,
        sum_bias_x,
        dt_sum,
        rate_sum,
        skip_sum,
        gate_sum,
    )


def solution(mesh):
    in_specs = (
        P("dp", "context", None),
        P("dp", "context"),
        P(None, ("dp", "context"), None, "tensor"),
        P(None, ("dp", "context"), "tensor"),
        P(None, ("dp", "context", "tensor"), None),
        P(None, ("dp", "context", "tensor")),
        P(None, None, ("dp", "context", "tensor")),
        P(None, ("dp", "context", "tensor")),
        P(None, "tensor", ("dp", "context")),
        P(None, None, "tensor"),
        P(None, "tensor"),
        P(None, "tensor"),
        P(None, "tensor"),
        P(None, "tensor"),
        P(None, "tensor"),
        P("dp", "context", None),
    )
    out_specs = (
        P("dp", "context", None),
        P("dp", "context", None),
        P(None, ("dp", "context"), None, "tensor"),
        P(None, ("dp", "context"), "tensor"),
        P(None, ("dp", "context", "tensor"), None),
        P(None, ("dp", "context", "tensor")),
        P(None, None, ("dp", "context", "tensor")),
        P(None, ("dp", "context", "tensor")),
        P(None, "tensor", ("dp", "context")),
        P(None, None, "tensor"),
        P(None, "tensor"),
        P(None, "tensor"),
        P(None, "tensor"),
        P(None, "tensor"),
        P(None, "tensor"),
        P("dp", "context", None),
    )
    return jax.shard_map(
        local, mesh=mesh, in_specs=in_specs, out_specs=out_specs[:15], check_vma=False
    )
```

```python
import functools

import jax
import jax.numpy as jnp
from jax import lax
from jax.experimental import pallas as pl
from jax.experimental.pallas import tpu as pltpu
from jax.sharding import PartitionSpec as P

CHUNK = 128
LANES = 128
eps = 1e-05
F32 = jnp.float32
BF16 = jnp.bfloat16
HIGH = lax.Precision.HIGHEST
NN = (((1,), (0,)), ((), ()))
NT = (((1,), (1,)), ((), ()))
TN = (((0,), (0,)), ((), ()))
NO_LINK = -1e30
COST_SCALE = 0.5


def mm(a, b, dims=NN):
    return lax.dot_general(a, b, dims, preferred_element_type=F32)


def params(mib=48):
    return pltpu.CompilerParams(
        dimension_semantics=("arbitrary",), vmem_limit_bytes=mib * 1024 * 1024
    )


PRECEDING = []


def kernel_call(body, cost=2.0, **spec):
    def call(*inputs):
        tokens = list(PRECEDING)
        options = dict(spec)
        grid_spec = options.pop("grid_spec", None)
        unread = [pl.BlockSpec(memory_space=pl.ANY)] * len(tokens)
        prefetched = 0
        if grid_spec is None:
            options["in_specs"] = list(options["in_specs"]) + unread
        else:
            prefetched = grid_spec.num_scalar_prefetch
            options["grid_spec"] = pltpu.PrefetchScalarGridSpec(
                num_scalar_prefetch=prefetched,
                grid=grid_spec.grid,
                in_specs=list(grid_spec.in_specs) + unread,
                out_specs=grid_spec.out_specs,
                scratch_shapes=grid_spec.scratch_shapes,
            )
        first = len(inputs)

        def without_tokens(*refs):
            body(*refs[:first], *refs[first + len(tokens) :])

        out = pl.pallas_call(
            without_tokens,
            cost_estimate=pl.CostEstimate(
                flops=int(cost * 1.0e9 * COST_SCALE), transcendentals=0, bytes_accessed=1024
            ),
            **options,
        )(*inputs, *tokens)
        PRECEDING[:] = [min(jax.tree.leaves(out), key=lambda one: one.size * one.dtype.itemsize)]
        return out

    return call


def precede(*tokens):
    PRECEDING.extend(token for token in tokens if token is not None)


def flipped(value, axis, bit):
    count = lax.axis_size(axis)
    return lax.ppermute(value, axis, [(i, i ^ (1 << bit)) for i in range(count)])


def bits(axis):
    return (lax.axis_size(axis) - 1).bit_length()


def shifted(value, axis, steps):
    count = lax.axis_size(axis)
    leading, last = (max(0, -steps), min(count, count - steps))
    return lax.ppermute(value, axis, [(source, source + steps) for source in range(leading, last)])


def ring(value, axis):
    count = lax.axis_size(axis)
    return lax.ppermute(value, axis, [(i, (i - 1) % count) for i in range(count)])


def summed_over(value, axes):
    for axis in axes:
        for bit in range(bits(axis)):
            value = value + flipped(value, axis, bit)
    return value


def gather_small(value, axes):
    value = value[None]
    for axis in axes:
        index = lax.axis_index(axis)
        for bit in range(bits(axis)):
            other = flipped(value, axis, bit)
            upper = (index >> bit) & 1
            value = jnp.concatenate(
                [jnp.where(upper == 0, value, other), jnp.where(upper == 0, other, value)], axis=0
            )
    return value


def slots():
    count, places = bits("tensor"), []
    for m in range(lax.axis_size("tensor")):
        places.append(sum(((m >> b) & 1) << (count - 1 - b) for b in range(count)))
    return places


def rows_order(first):
    places = slots()
    if first:
        half = len(places) // 2
        places = places[half:] + places[:half]
    return jnp.array(places, jnp.int32) ^ lax.axis_index("tensor")


def own_rows(value):
    rows = value.shape[0] // lax.axis_size("tensor")
    return lax.dynamic_slice_in_dim(value, lax.axis_index("tensor") * rows, rows, 0)


def relay_kernel(from_ref, to_ref):
    to_ref[...] = from_ref[...]


def widen_kernel(from_ref, to_ref):
    to_ref[...] = from_ref[...].astype(F32)


def widened(value):
    return kernel_call(
        widen_kernel,
        grid=(1,),
        in_specs=[fixed_block(value.shape)],
        out_specs=fixed_block(value.shape),
        out_shape=jax.ShapeDtypeStruct(value.shape, F32),
        compiler_params=params(),
    )(value)


def relayed(piece, *tokens):
    precede(*tokens)
    return kernel_call(
        relay_kernel,
        grid=(1,),
        in_specs=[fixed_block(piece.shape)],
        out_specs=fixed_block(piece.shape),
        out_shape=jax.ShapeDtypeStruct(piece.shape, piece.dtype),
        compiler_params=params(),
    )(piece)


def ring_pieces(table, piece):
    def over_context(arrived):
        row = [arrived]
        for _ in range(lax.axis_size("context") - 1):
            row.append(ring(row[-1], "context"))
        return row

    arrived = piece
    table.append(over_context(piece))
    for k in range(1, lax.axis_size("dp")):
        arrived = ring(arrived, "dp")
        yield
        arrived = relayed(arrived, table[k - 1][-1])
        table.append(over_context(arrived))
    yield


def place_kernel(count, widths, tile_at, index_ref, *refs):
    pieces, outs = refs[:count], refs[count:]
    for i in range(count):
        at = 0
        for out, width in zip(outs, widths):
            out[index_ref[i]] = pieces[i][:, at : at + width]
            at += width
    if tile_at is not None:
        first, tiles = outs[0], outs[-1]
        rows = first.shape[1]
        whole_rows = jnp.concatenate(
            [first[i, :, tile_at : tile_at + LANES] for i in range(count)], axis=0
        )
        for at in range(0, count * rows, LANES):
            tiles[:, at : at + LANES] = whole_rows[at : at + LANES].astype(F32).T


def placed(table, widths, tile_at=None):
    dp, context = lax.axis_size("dp"), lax.axis_size("context")
    z, x = lax.axis_index("dp"), lax.axis_index("context")
    pieces, index = [], []
    for k, row in enumerate(table):
        for j, piece in enumerate(row):
            pieces.append(piece)
            index.append(((z + k) % dp) * context + (x + j) % context)
    count, rows = len(pieces), pieces[0].shape[0]
    out_specs = [
        pl.BlockSpec((count, rows, width), lambda i, index: (0, 0, 0)) for width in widths
    ]
    out_shape = [jax.ShapeDtypeStruct((count, rows, width), BF16) for width in widths]
    if tile_at is not None:
        out_specs.append(pl.BlockSpec((LANES, count * rows), lambda i, index: (0, 0)))
        out_shape.append(jax.ShapeDtypeStruct((LANES, count * rows), F32))
    outs = kernel_call(
        functools.partial(place_kernel, count, widths, tile_at),
        cost=3.5,
        grid_spec=pltpu.PrefetchScalarGridSpec(
            num_scalar_prefetch=1,
            grid=(1,),
            in_specs=[pl.BlockSpec(piece.shape, lambda i, index: (0, 0)) for piece in pieces],
            out_specs=out_specs,
        ),
        out_shape=out_shape,
        compiler_params=params(),
    )(jnp.stack(index).astype(jnp.int32), *pieces)
    return [
        out.reshape(count * rows, -1) if i < len(widths) else out for i, out in enumerate(outs)
    ]


def after(value, *tokens):
    tokens = tuple(token for token in tokens if token is not None)
    return lax.optimization_barrier((value, *tokens))[0] if tokens else value


def from_others(value, axis):
    count = lax.axis_size(axis)
    return [value] + [
        lax.ppermute(value, axis, [(i, i ^ step) for i in range(count)])
        for step in range(1, count)
    ]


def scatter_places(value):
    count, index = lax.axis_size("tensor"), lax.axis_index("tensor")
    value = value.reshape(count, -1, value.shape[1])
    total = lax.dynamic_index_in_dim(value, index, 0, keepdims=False)
    for step in range(1, count):
        sent = lax.dynamic_index_in_dim(value, index ^ step, 0, keepdims=False)
        total = total + lax.ppermute(sent, "tensor", [(i, i ^ step) for i in range(count)])
    return total


def pack_kernel(layers, sequences, width, *refs):
    inputs, (local_ref, shared_ref) = refs[:-2], refs[-2:]
    local_ref[...] = jnp.zeros_like(local_ref)
    shared_ref[...] = jnp.zeros_like(shared_ref)
    for layer in range(layers):
        mine = inputs[layer * sequences * 4 : (layer + 1) * sequences * 4]
        taps, acc, small, gain = (sum(one[...] for one in mine[i::4]) for i in range(4))
        local_ref[layer, 0:5, :width] = taps[0:5, :width]
        local_ref[layer, 5:7, :width] = acc[0:2]
        local_ref[layer, 0:2, width:] = small[0:2]
        shared = taps.shape[1] - width
        shared_ref[layer, 0:5, :shared] = taps[0:5, width:]
        for i, (row, at) in enumerate(gain_places(gain.shape[1], shared)):
            shared_ref[layer, row : row + 1, at : at + shared] = gain[
                0:1, i * shared : (i + 1) * shared
            ]


def gain_places(model, shared):
    places = [(5, 0), (6, 0), (7, 0)] + [(row, shared) for row in range(8)]
    return places[: model // shared]


def share_kernel(local_ref, *refs):
    cut = local_ref.shape[2]
    refs[-1][:, :, :cut] = local_ref[...]
    refs[-1][:, :, cut:] = sum(one[...] for one in refs[:-1])


def unpack_kernel(width, heads, shared, model, place_ref, a_ref, b_ref, red_ref, *outs):
    taps_x, bias_x, dt_bias, rate, skip, gate_gain, taps_bc, bias_bc, pre_gain = outs
    own_conv, own_gain = taps_bc.shape[2], pre_gain.shape[1]
    cut = width + LANES
    for layer in range(a_ref.shape[0]):
        total = a_ref[layer] + b_ref[layer]
        at = slice(layer, layer + 1)
        taps_x[layer] = total[0:4, :width]
        bias_x[at] = total[4:5, :width]
        gate_gain[at] = total[5:6, :width]
        dt_bias[at] = total[0:1, width : width + heads]
        rate[at] = total[1:2, width : width + heads]
        skip[at] = split_dot(total[:, :width], red_ref[...])[6:7, :heads]
        part = total[:, cut : cut + shared]
        part = pltpu.roll(part, shared - place_ref[0] * own_conv, axis=1)
        taps_bc[layer] = part[0:4, :own_conv]
        bias_bc[at] = part[4:5, :own_conv]
        rows = [
            total[row : row + 1, cut + col : cut + col + shared]
            for row, col in gain_places(model, shared)
        ]
        gain = jnp.broadcast_to(jnp.concatenate(rows, axis=1), (8, model))
        gain = pltpu.roll(gain, model - place_ref[0] * own_gain, axis=1)
        pre_gain[at] = gain[0:1, :own_gain]


def add_kernel(*refs):
    refs[-1][...] = sum(one[...] for one in refs[:-1])


def add_up(terms):
    shape = terms[0].shape
    return kernel_call(
        add_kernel,
        cost=1.0,
        grid=(1,),
        in_specs=[whole(shape)] * len(terms),
        out_specs=whole(shape),
        out_shape=jax.ShapeDtypeStruct(shape, terms[0].dtype),
        compiler_params=params(),
    )(*terms)


def small_sums(work, width, heads, model, red):
    layers, sequences = len(work), len(work[0])
    inputs = [k[name] for ks in work for k in ks for name in ("wacc", "acc", "hacc", "dgain")]
    shared = inputs[0].shape[1] - width
    shapes = [(layers, 8, width + LANES), (layers, 8, 2 * shared)]
    own, every = kernel_call(
        functools.partial(pack_kernel, layers, sequences, width),
        grid=(1,),
        in_specs=[whole(one.shape) for one in inputs],
        out_specs=[whole(shape) for shape in shapes],
        out_shape=[jax.ShapeDtypeStruct(shape, F32) for shape in shapes],
        compiler_params=params(),
    )(*inputs)
    parts = from_others(every, "tensor")
    yield None
    shape = (layers, 8, width + LANES + 2 * shared)
    total = kernel_call(
        share_kernel,
        cost=1.0,
        grid=(1,),
        in_specs=[whole(one.shape) for one in (own, *parts)],
        out_specs=whole(shape),
        out_shape=jax.ShapeDtypeStruct(shape, F32),
        compiler_params=params(),
    )(own, *parts)
    hops = [(axis, bit) for axis in ("context", "dp") for bit in range(bits(axis))]
    for axis, bit in hops:
        other = flipped(total, axis, bit)
        yield None
        if (axis, bit) != hops[-1]:
            total = add_up([total, other])
    devices = lax.axis_size("dp") * lax.axis_size("context") * lax.axis_size("tensor")
    place = lax.axis_index("dp") * lax.axis_size("context") + lax.axis_index("context")
    place = place * lax.axis_size("tensor") + lax.axis_index("tensor")
    own_conv, own_gain = shared // devices, model // devices
    shapes = [
        (layers, 4, width), (layers, width), (layers, heads), (layers, heads), (layers, heads),
        (layers, width), (layers, 4, own_conv), (layers, own_conv), (layers, own_gain),
    ]
    yield kernel_call(
        functools.partial(unpack_kernel, width, heads, shared, model),
        grid_spec=pltpu.PrefetchScalarGridSpec(
            num_scalar_prefetch=1,
            grid=(1,),
            in_specs=[fixed_block(one.shape) for one in (total, other, red)],
            out_specs=[fixed_block(one) for one in shapes],
        ),
        out_shape=[jax.ShapeDtypeStruct(one, F32) for one in shapes],
        compiler_params=params(),
    )(place.astype(jnp.int32)[None], total, other, red)


def silu_parts(value):
    sig = jax.nn.sigmoid(value)
    return value * sig, sig


def softplus(value):
    return jnp.maximum(value, 0.0) + jnp.log1p(jnp.exp(-jnp.abs(value)))


def split_dot(value, table):
    high = value.astype(BF16)
    low = (value - high.astype(F32)).astype(BF16)
    return mm(high, table) + mm(low, table)


def wide_mm(a, b, dims=NN):
    a_high, b_high = a.astype(BF16), b.astype(BF16)
    a_low = (a - a_high.astype(F32)).astype(BF16)
    b_low = (b - b_high.astype(F32)).astype(BF16)
    return mm(a_high, b_high, dims) + (mm(a_low, b_high, dims) + mm(a_high, b_low, dims))


def low_mm(a, b, dims=NN):
    return mm(a.astype(BF16), b.astype(BF16), dims)


def iota(axis):
    return lax.broadcasted_iota(jnp.int32, (CHUNK, CHUNK), axis)


def rounded(value):
    return value.astype(BF16).astype(F32)


def head_halves(tile, lower):
    zero = jnp.zeros_like(tile)
    return jnp.concatenate([jnp.where(lower, tile, zero), jnp.where(lower, zero, tile)], axis=0)


def column_of(rows):
    pad = jnp.zeros((CHUNK - rows.shape[0], CHUNK), F32)
    return jnp.concatenate([rows, pad], axis=0).T


def row_norm(wide):
    return lax.rsqrt(jnp.mean(wide * wide, axis=-1, keepdims=True) + eps)


def columns(array, at, width):
    return pl.BlockSpec((array.shape[0], width), lambda i, *_: (0, at))


def fixed_block(shape):
    return pl.BlockSpec(shape, lambda i, *_: (0,) * len(shape))


def project_kernel(norm, count, width, order_ref, *refs):
    pieces, rest = refs[:count], refs[count:]
    if norm:
        gain_ref, halo_ref, rest = rest[0], rest[1], rest[2:]
    w_ref, normed_ref, proj_ref, rim_ref, halo = rest
    step = pl.program_id(0)
    length, size = proj_ref.shape

    @pl.when(step == 0)
    def _():
        for m in range(length // CHUNK):
            if norm:
                wide = pieces[0][0, m * CHUNK : (m + 1) * CHUNK].astype(F32)
                rows = (wide * row_norm(wide) * gain_ref[...]).astype(BF16)
                normed_ref[m * CHUNK : (m + 1) * CHUNK] = rows
            else:
                place = pl.ds(pl.multiple_of(order_ref[m] * CHUNK, CHUNK), CHUNK)
                normed_ref[place] = pieces[m][...]
        if norm:
            wide = halo_ref[0].astype(F32)
            halo[...] = (wide * row_norm(wide) * gain_ref[...]).astype(BF16)
        else:
            halo[...] = normed_ref[length - 16 :]

    weight = w_ref[...]
    proj_ref[...] = mm(normed_ref[...], weight)
    tail = mm(halo[...], weight)[8:].astype(BF16)
    for i in range(width // size):

        @pl.when(step == i)
        def _(i=i):
            rim_ref[:, i * size : (i + 1) * size] = tail

    @pl.when(step == width // size)
    def _():
        rim_ref[:, width:] = tail[:, LANES:]


def project(source, gain, order, front, width, total):
    weights, at = front
    third = total // 3
    norm = gain is not None
    if norm:
        stream, halo, sequence = source
        model, length = stream.shape[2], stream.shape[1]
        inputs, count = [stream, gain, halo], 1
        specs = [
            pl.BlockSpec((1, length, model), lambda i, order: (sequence, 0, 0)),
            fixed_block((1, model)),
            pl.BlockSpec((1, 16, model), lambda i, order: (sequence, 0, 0)),
        ]
    else:
        model, count = source[0][0].shape[1], len(source)
        length = count * CHUNK
        inputs, specs = [one for one, _ in source], piece_specs(source, CHUNK)
    conv = total - LANES
    return kernel_call(
        functools.partial(project_kernel, norm, count, width),
        cost=5.0,
        grid_spec=pltpu.PrefetchScalarGridSpec(
            num_scalar_prefetch=1,
            grid=(3,),
            in_specs=specs + [pl.BlockSpec((model, third), lambda i, order: (0, at + i))],
            out_specs=[
                fixed_block((length, model)),
                pl.BlockSpec((length, third), lambda i, order: (0, i)),
                fixed_block((8, conv)),
            ],
            scratch_shapes=[pltpu.VMEM((16, model), BF16)],
        ),
        out_shape=[
            jax.ShapeDtypeStruct((length, model), BF16),
            jax.ShapeDtypeStruct((length, total), F32),
            jax.ShapeDtypeStruct((8, conv), BF16),
        ],
        compiler_params=params(),
    )(order, *inputs, weights)


def plain_kernel(a_ref, w_ref, out_ref):
    out_ref[...] = mm(a_ref[...], w_ref[...])


def plain_product(a, weight, width):
    weights, at = weight
    length, model = a.shape
    half = width // 2
    return kernel_call(
        plain_kernel,
        cost=3.0,
        grid=(2,),
        in_specs=[
            fixed_block((length, model)),
            pl.BlockSpec((model, half), lambda i: (0, 2 * at + i)),
        ],
        out_specs=pl.BlockSpec((length, half), lambda i: (0, i)),
        out_shape=jax.ShapeDtypeStruct((length, width), F32),
        compiler_params=params(),
    )(a, weights)


def rows_of(ref):
    return (ref[...] if len(ref.shape) == 2 else ref[0]).astype(F32)


def norm_forward_kernel(place_ref, stream_ref, keep_ref, first_ref, second_ref, *refs):
    total = keep_ref[0].astype(F32) + first_ref[0].astype(F32) + second_ref[...].astype(F32)
    new = rows_of(stream_ref) + total
    if len(refs) == 1:
        refs[0][...] = new.astype(BF16)
    else:
        gain_ref, new_ref, low_ref = refs
        new_ref[...] = new
        low_ref[...] = (new * row_norm(new) * gain_ref[...]).astype(BF16)


def join_kernel(own_ref, other_ref, out_ref):
    rows = own_ref.shape[0]
    out_ref[:rows] = own_ref[...]
    out_ref[rows:] = other_ref[...]


def joined_rows(own, other):
    rows, model = own.shape
    return kernel_call(
        join_kernel,
        grid=(1,),
        in_specs=[fixed_block((rows, model))] * 2,
        out_specs=fixed_block((2 * rows, model)),
        out_shape=jax.ShapeDtypeStruct((2 * rows, model), own.dtype),
        compiler_params=params(),
    )(own, other)


def piece_specs(pieces, rows):
    return [pl.BlockSpec((rows, one.shape[1]), lambda i, *_, at=at: (at, 0)) for one, at in pieces]


def pass_on_kernel(keep_ref, first_ref, out_ref):
    total = keep_ref[0].astype(F32) + first_ref[0].astype(F32)
    out_ref[...] = total.astype(out_ref.dtype)


def pass_on(kept, first):
    _, rows, model = kept.shape
    spec = pl.BlockSpec((1, rows, model), lambda i: (1, 0, 0))
    return kernel_call(
        pass_on_kernel,
        grid=(1,),
        in_specs=[spec, spec],
        out_specs=fixed_block((rows, model)),
        out_shape=jax.ShapeDtypeStruct((rows, model), kept.dtype),
        compiler_params=params(),
    )(kept, first)


def rows_spec(one, rows):
    if isinstance(one, tuple):
        array, s = one
        return array, pl.BlockSpec((1, rows, array.shape[2]), lambda i, place: (s, place[0], 0))
    return one, fixed_block(one.shape)


def term_specs(rows, model):
    part = fixed_block((1, rows, model))
    return [part, part, fixed_block((rows, model))]


def norm_forward(stream, terms, gain, place):
    rows, model = terms[2].shape
    stream, spec = rows_spec(stream, rows)
    low = jax.ShapeDtypeStruct((rows, model), BF16)
    last = gain is None
    return kernel_call(
        norm_forward_kernel,
        grid_spec=pltpu.PrefetchScalarGridSpec(
            num_scalar_prefetch=1,
            grid=(1,),
            in_specs=[spec]
            + term_specs(rows, model)
            + ([] if last else [fixed_block((1, model))]),
            out_specs=[fixed_block((rows, model))] * (1 if last else 2),
        ),
        out_shape=[low] if last else [jax.ShapeDtypeStruct((rows, model), F32), low],
        compiler_params=params(),
    )(place, stream, *terms, *([] if last else [gain]))


def norm_backward_kernel(
    place_ref, stream_ref, keep_ref, first_ref, second_ref, grad_ref, gain_ref, new_ref, low_ref,
    dgain_ref,
):
    total = keep_ref[0].astype(F32) + first_ref[0].astype(F32) + second_ref[...].astype(F32)
    current = rows_of(stream_ref)
    scale = row_norm(current)
    unit = current * scale
    dgain_ref[...] = jnp.broadcast_to(
        jnp.sum(total * unit, axis=0, keepdims=True), dgain_ref.shape
    )
    pulled = total * gain_ref[...]
    shift = jnp.mean(pulled * unit, axis=-1, keepdims=True)
    new = rows_of(grad_ref) + scale * (pulled - unit * shift)
    new_ref[...] = new
    low_ref[...] = new.astype(BF16)


def norm_backward(stream, terms, grad, gain, place):
    rows, model = terms[2].shape
    stream, stream_spec = rows_spec(stream, rows)
    grad, grad_spec = rows_spec(grad, rows)
    return kernel_call(
        norm_backward_kernel,
        grid_spec=pltpu.PrefetchScalarGridSpec(
            num_scalar_prefetch=1,
            grid=(1,),
            in_specs=[stream_spec]
            + term_specs(rows, model)
            + [grad_spec, fixed_block((1, model))],
            out_specs=[fixed_block((rows, model))] * 2 + [fixed_block((8, model))],
        ),
        out_shape=[
            jax.ShapeDtypeStruct((rows, model), F32),
            jax.ShapeDtypeStruct((rows, model), BF16),
            jax.ShapeDtypeStruct((8, model), F32),
        ],
        compiler_params=params(),
    )(place, stream, *terms, grad, gain)


def assemble_kernel(count, order_ref, *refs):
    step = pl.program_id(0)
    for m in range(count):

        @pl.when(step == m)
        def _(m=m):
            refs[-1][0] = refs[m][...]


def assembled(groups, order):
    each, (rows, model) = len(groups[0]), groups[0][0][0].shape
    pieces = [piece for group in groups for piece in group]
    count = len(pieces)
    return kernel_call(
        functools.partial(assemble_kernel, count),
        cost=5.0,
        grid_spec=pltpu.PrefetchScalarGridSpec(
            num_scalar_prefetch=1,
            grid=(count,),
            in_specs=piece_specs(pieces, rows),
            out_specs=pl.BlockSpec(
                (1, rows, model), lambda i, order: (i // each, order[i % each], 0)
            ),
        ),
        out_shape=jax.ShapeDtypeStruct((len(groups), each * rows, model), BF16),
        compiler_params=params(),
    )(order, *[one for one, _ in pieces])


def input_grad_kernel(parts, width, order_ref, dproj_ref, dgate_ref, tail_ref, rim_ref, *refs):
    w_refs, gate_ref, sent_ref, kept_ref, fixed_ref, rows_p, rows_g = refs[:3], *refs[3:]
    half = parts // 2

    @pl.when(pl.program_id(0) == 0)
    def _():
        fixed_ref[...] = dproj_ref[...]
        tail = (tail_ref[...] + rim_ref[...]).astype(BF16)
        fixed_ref[parts * CHUNK - 16 :, :width] = tail[:, :width]
        fixed_ref[parts * CHUNK - 16 :, width + LANES :] = tail[:, width:]
        for m in range(parts):
            source = pl.ds(pl.multiple_of(order_ref[m] * CHUNK, CHUNK), CHUNK)
            rows_p[m * CHUNK : (m + 1) * CHUNK] = fixed_ref[source]
            rows_g[m * CHUNK : (m + 1) * CHUNK] = dgate_ref[source]

    total = mm(rows_g[...], gate_ref[...], NT)
    for j, w_ref in enumerate(w_refs):
        size = w_ref.shape[1]
        total = total + mm(rows_p[:, j * size : (j + 1) * size], w_ref[...], NT)
    total = total.astype(BF16)
    for m in range(half):
        sent_ref[m] = total[m * CHUNK : (m + 1) * CHUNK]
        kept_ref[m] = total[(half + m) * CHUNK : (half + m + 1) * CHUNK]


def input_grad(dproj, dgate, tail, rim, front, gate, order):
    length, total = dproj.shape
    width = dgate.shape[1]
    (front_w, at), (gate_w, gate_at) = front, gate
    model, third, parts = front_w.shape[0], total // 3, length // CHUNK
    cut = model // 4
    half = pl.BlockSpec((parts // 2, CHUNK, cut), lambda i, order: (0, 0, i))

    def rows(offset, size):
        return pl.BlockSpec((cut, size), lambda i, order: (i, offset))

    return kernel_call(
        functools.partial(input_grad_kernel, parts, width),
        cost=7.6,
        grid_spec=pltpu.PrefetchScalarGridSpec(
            num_scalar_prefetch=1,
            grid=(4,),
            in_specs=[fixed_block(one.shape) for one in (dproj, dgate, tail, rim)]
            + [rows(at + j, third) for j in range(3)]
            + [rows(gate_at, width)],
            out_specs=[half, half, fixed_block((length, total))],
            scratch_shapes=[
                pltpu.VMEM((length, total), BF16),
                pltpu.VMEM((length, width), BF16),
            ],
        ),
        out_shape=[jax.ShapeDtypeStruct((parts // 2, CHUNK, model), BF16)] * 2
        + [jax.ShapeDtypeStruct((length, total), BF16)],
        compiler_params=params(),
    )(order, dproj, dgate, tail, rim, front_w, front_w, front_w, gate_w)


def weight_grad_kernel(segments, sequences, rows, places, order_ref, *refs):
    lefts, rights = refs[: segments * sequences], refs[segments * sequences :]
    rights, outs, total = rights[: segments * sequences], rights[segments * sequences : -1], refs[-1]
    at = 0
    for g in range(segments):
        width = rights[g * sequences].shape[1]
        part = None
        for s in range(sequences):
            left = lefts[g * sequences + s]
            left = left[...] if len(left.shape) == 2 else left[0]
            one = mm(left, rights[g * sequences + s][...], TN)
            part = one if part is None else part + one
        total[:, at : at + width] = part
        at += width
    if places is None:
        outs[0][...] = total[...].astype(BF16)
        return
    dp, context = places
    slot = lax.rem(pl.program_id(0) - order_ref[1] + dp, dp)

    def block(j):
        start = lax.rem(order_ref[0] + j, context) * rows
        return total[pl.ds(pl.multiple_of(start, 8), rows)].astype(BF16)

    outs[0][0] = block(0)
    for j in range(1, context):
        for k in range(dp):

            @pl.when(slot == k)
            def _(j=j, k=k):
                outs[1 + (j - 1) * dp + k][...] = block(j)


def weight_grad(pairs, ordered):
    dp, context = lax.axis_size("dp"), lax.axis_size("context")
    sequences, length = len(pairs[0][0]), pairs[0][1][0].shape[0]
    widths = [right[0].shape[1] for _, right in pairs]
    lefts = [one for left, _ in pairs for one in left]
    rights = [one for _, right in pairs for one in right]
    model = lefts[0].shape[-1]
    total, cut = sum(widths), model // dp
    rows = cut // context
    order = jnp.stack([lax.axis_index("context"), lax.axis_index("dp")]).astype(jnp.int32)
    if ordered:
        others = (context - 1) * dp
        out_specs = [
            pl.BlockSpec(
                (1, rows, total), lambda i, order: (lax.rem(i - order[1] + dp, dp), 0, 0)
            )
        ] + [fixed_block((rows, total))] * others
        out_shape = [jax.ShapeDtypeStruct((dp, rows, total), BF16)] + [
            jax.ShapeDtypeStruct((rows, total), BF16)
        ] * others
    else:
        out_specs = [pl.BlockSpec((cut, total), lambda i, order: (i, 0))]
        out_shape = [jax.ShapeDtypeStruct((model, total), BF16)]
    left_specs, left_arrays = [], []
    for left in lefts:
        if isinstance(left, tuple):
            left_arrays.append(left[0])
            left_specs.append(
                pl.BlockSpec((1, length, cut), lambda i, order, s=left[1]: (s, 0, i))
            )
        else:
            left_arrays.append(left)
            left_specs.append(pl.BlockSpec((length, cut), lambda i, order: (0, i)))
    return kernel_call(
        functools.partial(
            weight_grad_kernel, len(pairs), sequences, rows, (dp, context) if ordered else None
        ),
        cost=10.0,
        grid_spec=pltpu.PrefetchScalarGridSpec(
            num_scalar_prefetch=1,
            grid=(dp,),
            in_specs=left_specs + [fixed_block(one.shape) for one in rights],
            out_specs=out_specs,
            scratch_shapes=[pltpu.VMEM((cut, total), F32)],
        ),
        out_shape=out_shape,
        compiler_params=params(56),
    )(order, *left_arrays, *rights)


def ring_add_kernel(own_ref, *refs):
    total = own_ref[0].astype(F32)
    for one in refs[:-1]:
        total = total + one[...].astype(F32)
    refs[-1][...] = total.astype(refs[-1].dtype)


def ring_add(own, k, terms, kind):
    _, rows, width = own.shape
    return kernel_call(
        ring_add_kernel,
        cost=1.5,
        grid=(1,),
        in_specs=[pl.BlockSpec((1, rows, width), lambda i: (k, 0, 0))]
        + [fixed_block((rows, width))] * len(terms),
        out_specs=fixed_block((rows, width)),
        out_shape=jax.ShapeDtypeStruct((rows, width), kind),
        compiler_params=params(),
    )(own, *terms)


def ring_steps(blocks, whole_first=False):
    dp, context = lax.axis_size("dp"), lax.axis_size("context")
    own, others = blocks[0], blocks[1:]
    places = list(range(1, dp)) + [0]
    sides = []
    for k in places:
        side = None
        for j in range(1, context):
            part = others[(j - 1) * dp + k]
            if side is not None:
                part = (side.astype(F32) + part.astype(F32)).astype(BF16)
            side = ring(part, "context")
        sides.append([] if side is None else [side])
    if whole_first:
        precede(*sides[-1])
    passed = []
    for k, side in zip(places, sides):
        value = ring_add(own, k, side + passed, BF16 if k else F32)
        if k:
            passed = [ring(value, "dp")]
            yield None
        else:
            yield value


def scan_forward_kernel(
    heads, width, p_ref, rim_ref, marks_ref, cw_ref, hp_ref, skip_ref, exp_ref,
    z_ref, y_ref, st_ref, end_ref, gr_ref, vbuf, state, offset,
):
    chunk = pl.program_id(0)
    aux = column_of(marks_ref[...])

    @pl.when(chunk == 0)
    def _():
        vbuf[0:8] = rim_ref[...].astype(F32)
        state[...] = jnp.zeros_like(state)
        offset[...] = jnp.zeros_like(offset)

    @pl.when(chunk > 0)
    def _():
        vbuf[0:8] = vbuf[CHUNK : CHUNK + 8]

    vbuf[8:, :width] = rounded(p_ref[:, :width])
    vbuf[8:, width:] = rounded(p_ref[:, width + LANES :])
    z = cw_ref[4:5] + cw_ref[3:4] * vbuf[8:]
    for k in range(3):
        z = z + cw_ref[k : k + 1] * vbuf[5 + k : 5 + k + CHUNK] * aux[:, k : k + 1]
    z_ref[...] = z
    act = z * jax.nn.sigmoid(z)
    x = act[:, :width]
    b_val, c_val = act[:, width : width + LANES], act[:, width + LANES :]
    lane = iota(1)
    step = jnp.where(
        lane < heads, softplus(p_ref[:, width : width + LANES] + hp_ref[0:1]), 0.0
    )
    decay = hp_ref[1:2] * step
    cum = lax.dot_general(
        (iota(0) >= iota(1)).astype(F32), decay, NN, precision=HIGH, preferred_element_type=F32
    )
    cum_t = cum.T
    seg_col = aux[:, 5:6]
    link = jnp.where((seg_col == marks_ref[5:6]) & (iota(0) >= iota(1)), 0.0, NO_LINK)
    scores = wide_mm(c_val, b_val, NT)
    growth = jnp.exp(cum) * aux[:, 3:4]
    last = cum[CHUNK - 1 : CHUNK]
    weight = jnp.exp(last - cum) * (seg_col == seg_col[CHUNK - 1 : CHUNK]).astype(F32)
    wide = split_dot(jnp.concatenate([step, growth, weight], axis=0), exp_ref[...])
    step_e, growth_e, weight_e = wide[:CHUNK], wide[CHUNK : 2 * CHUNK], wide[2 * CHUNK :]
    xd = x * step_e
    lower = lane < LANES // 2
    pieces = []
    for pair in range(heads // 2):
        mats = []
        for head in (2 * pair, 2 * pair + 1):
            spread = cum[:, head : head + 1] - cum_t[head : head + 1, :]
            mats.append(jnp.exp(spread + link) * scores)
        tile = xd[:, pair * LANES : (pair + 1) * LANES]
        pieces.append(wide_mm(jnp.concatenate(mats, axis=1), head_halves(tile, lower)))
    held = state[...]
    st_ref[0] = held
    carried = wide_mm(c_val, held) * growth_e
    y_ref[...] = jnp.concatenate(pieces, axis=1) + carried + skip_ref[...] * x
    new = held * growth_e[CHUNK - 1 : CHUNK] + wide_mm(b_val, xd * weight_e, TN)
    state[...] = new
    end_ref[...] = new
    gr_ref[...] = jnp.exp(offset[...] + cum) * aux[:, 4:5]
    offset[...] = offset[...] + last


def row_spec(width, at=None, rows=CHUNK):
    if at is None:
        return pl.BlockSpec((rows, width), lambda i: (i, 0))
    return pl.BlockSpec((rows, width), lambda i: (i, at))


def whole(shape):
    return pl.BlockSpec(shape, lambda i: (0,) * len(shape))


def scan_forward(proj, rim, marks, consts):
    length, total = proj.shape
    heads, width = consts["heads"], consts["width"]
    chunks, conv = length // CHUNK, total - LANES
    return kernel_call(
        functools.partial(scan_forward_kernel, heads, width),
        cost=9.5,
        grid=(chunks,),
        in_specs=[
            row_spec(total),
            whole((8, conv)),
            pl.BlockSpec((8, CHUNK), lambda i: (0, i)),
            whole((8, conv)),
            whole((8, LANES)),
            whole((1, width)),
            whole((LANES, width)),
        ],
        out_specs=[
            row_spec(conv),
            row_spec(width),
            pl.BlockSpec((1, LANES, width), lambda i: (i, 0, 0)),
            whole((LANES, width)),
            row_spec(LANES),
        ],
        out_shape=[
            jax.ShapeDtypeStruct((length, conv), F32),
            jax.ShapeDtypeStruct((length, width), F32),
            jax.ShapeDtypeStruct((chunks, LANES, width), F32),
            jax.ShapeDtypeStruct((LANES, width), F32),
            jax.ShapeDtypeStruct((length, LANES), F32),
        ],
        scratch_shapes=[
            pltpu.VMEM((CHUNK + 8, conv), F32),
            pltpu.VMEM((LANES, width), F32),
            pltpu.VMEM((1, LANES), F32),
        ],
        compiler_params=params(),
    )(proj, rim, marks, consts["cw"], consts["hp"], consts["skip"], consts["exp"])


def mix_forward_kernel(y0_ref, zc_ref, gr_ref, sin_ref, gate_ref, exp_ref, y_ref, sq_ref):
    c_val = zc_ref[...] * jax.nn.sigmoid(zc_ref[...])
    carried = wide_mm(c_val, sin_ref[...].astype(F32))
    y = y0_ref[...] + carried * split_dot(gr_ref[...], exp_ref[...])
    y_ref[...] = y
    gate = gate_ref[...]
    gated = y * (gate * jax.nn.sigmoid(gate))
    square = jnp.sum(gated * gated, axis=1, keepdims=True)
    sq_ref[...] = jnp.broadcast_to(square, (CHUNK, CHUNK)).T[:8]


def mix_forward(y0, z, growth, carried, gate, consts):
    length, width = y0.shape
    last = z.shape[1] // LANES - 1
    return kernel_call(
        mix_forward_kernel,
        cost=3.6,
        grid=(length // CHUNK,),
        in_specs=[
            row_spec(width),
            row_spec(LANES, last),
            row_spec(LANES),
            whole((LANES, width)),
            row_spec(width),
            whole((LANES, width)),
        ],
        out_specs=[row_spec(width), pl.BlockSpec((8, CHUNK), lambda i: (0, i))],
        out_shape=[
            jax.ShapeDtypeStruct((length, width), F32),
            jax.ShapeDtypeStruct((8, length), F32),
        ],
        compiler_params=params(),
    )(y0, z, growth, carried, gate, consts["exp"])


def project_out_kernel(channels, parts, order_ref, y_ref, gate_ref, gain_ref, w_ref, *refs):
    squares, (sent_ref, kept_ref, rows) = refs[:-3], refs[-3:]
    half = parts // 2

    @pl.when(pl.program_id(0) == 0)
    def _():
        for m in range(parts):
            source = pl.ds(pl.multiple_of(order_ref[m] * CHUNK, CHUNK), CHUNK)
            square = sum(one[:, source] for one in squares)
            scale = lax.rsqrt(column_of(square)[:, 1:2] / channels + eps)
            gate = gate_ref[source]
            gated = y_ref[source] * (gate * jax.nn.sigmoid(gate))
            rows[m * CHUNK : (m + 1) * CHUNK] = (gated * scale * gain_ref[...]).astype(BF16)

    total = mm(rows[...], w_ref[...], NT).astype(sent_ref.dtype)
    for m in range(half):
        sent_ref[m] = total[m * CHUNK : (m + 1) * CHUNK]
        kept_ref[m] = total[(half + m) * CHUNK : (half + m + 1) * CHUNK]


def project_out(y, gate, squares, channels, kind, order, consts):
    length, width = y.shape
    weights, at = consts["out"]
    model, parts = weights.shape[0], length // CHUNK
    cut = model // 4
    half = pl.BlockSpec((parts // 2, CHUNK, cut), lambda i, order: (0, 0, i))
    return kernel_call(
        functools.partial(project_out_kernel, float(channels), parts),
        cost=5.7,
        grid_spec=pltpu.PrefetchScalarGridSpec(
            num_scalar_prefetch=1,
            grid=(4,),
            in_specs=[
                fixed_block((length, width)),
                fixed_block((length, width)),
                fixed_block((1, width)),
                pl.BlockSpec((cut, width), lambda i, order: (i, at)),
            ]
            + [fixed_block((8, length))] * len(squares),
            out_specs=[half, half],
            scratch_shapes=[pltpu.VMEM((length, width), BF16)],
        ),
        out_shape=[jax.ShapeDtypeStruct((parts // 2, CHUNK, model), kind)] * 2,
        compiler_params=params(),
    )(order, y, gate, consts["gain"], weights, *squares)


def grad_scaled_kernel(count, order_ref, *refs):
    pieces, rest = refs[:count], refs[count:]
    w_ref, y_ref, gate_ref, gain_ref, gs_ref, dot_ref = rest[:6]
    sums = rest[-1]
    step = pl.program_id(0)
    length = gs_ref.shape[0]
    if count > 1:

        @pl.when(step == 0)
        def _():
            for m in range(count):
                place = pl.ds(pl.multiple_of(order_ref[m] * CHUNK, CHUNK), CHUNK)
                rest[6][place] = pieces[m][...]

        rows = rest[6][...]
    else:
        rows = pieces[0][0]
    grad = mm(rows, w_ref[...])
    gs_ref[...] = grad
    gate = gate_ref[...]
    gated = y_ref[...] * (gate * jax.nn.sigmoid(gate))
    product = jnp.sum(grad * gain_ref[...] * gated, axis=1, keepdims=True)
    square = jnp.sum(gated * gated, axis=1, keepdims=True)
    lane = lax.broadcasted_iota(jnp.int32, (length, LANES), 1)
    part = jnp.where(lane == 0, product, square)

    @pl.when(step == 0)
    def _():
        sums[...] = part

    @pl.when(step > 0)
    def _():
        sums[...] += part

    @pl.when(step == pl.num_programs(0) - 1)
    def _():
        for m in range(length // CHUNK):
            at = slice(m * CHUNK, (m + 1) * CHUNK)
            dot_ref[:, at] = sums[at].T[:8]


def grad_scaled(source, y, gate, order, consts):
    length, width = y.shape
    weights, at = consts["out"]
    model, half = weights.shape[0], width // 2
    part = pl.BlockSpec((length, half), lambda i, order: (0, i))
    out_specs = [part, fixed_block((8, length))]
    out_shape = [
        jax.ShapeDtypeStruct((length, width), F32),
        jax.ShapeDtypeStruct((8, length), F32),
    ]
    if len(source) == 2:
        stream, sequence = source
        inputs, count = [stream], 1
        specs = [pl.BlockSpec((1, length, model), lambda i, order: (sequence, 0, 0))]
    else:
        inputs, count = [one for one, _ in source], len(source)
        specs = piece_specs(source, CHUNK)
        out_specs.append(fixed_block((length, model)))
        out_shape.append(jax.ShapeDtypeStruct((length, model), BF16))
    out = kernel_call(
        functools.partial(grad_scaled_kernel, count),
        cost=4.5,
        grid_spec=pltpu.PrefetchScalarGridSpec(
            num_scalar_prefetch=1,
            grid=(2,),
            in_specs=specs
            + [
                pl.BlockSpec((model, half), lambda i, order: (0, 2 * at + i)),
                part,
                part,
                pl.BlockSpec((1, half), lambda i, order: (0, i)),
            ],
            out_specs=out_specs,
            scratch_shapes=[pltpu.VMEM((length, LANES), F32)],
        ),
        out_shape=out_shape,
        compiler_params=params(),
    )(order, *inputs, weights, y, gate, consts["gain"])
    return out if count > 1 else (*out, source)


def mix_backward_kernel(
    channels, shares, gs_ref, y_ref, gate_ref, zx_ref, zc_ref, gr_ref, gain_ref, exp_ref, *refs
):
    shared, refs = refs[:shares], refs[shares:]
    scaled_ref, dgate_ref, dy_ref, acc_ref, dsin_ref, dsin = refs
    at = pl.program_id(0)

    @pl.when(at == 0)
    def _():
        acc_ref[...] = jnp.zeros_like(acc_ref)
        dsin[...] = jnp.zeros_like(dsin)

    stats = column_of(sum(one[...] for one in shared))
    scale = lax.rsqrt(stats[:, 1:2] / channels + eps)
    pull = scale * scale * scale * stats[:, 0:1] / channels
    grad, y, gate = gs_ref[...], y_ref[...], gate_ref[...]
    silu, sig = silu_parts(gate)
    gated = y * silu
    unit = gated * scale
    scaled_ref[...] = (unit * gain_ref[...]).astype(BF16)
    dgated = grad * gain_ref[...] * scale - gated * pull
    dy = dgated * silu
    dy_ref[...] = dy
    dgate_ref[...] = (dgated * y * (sig * (1.0 + gate * (1.0 - sig)))).astype(BF16)
    x = zx_ref[...] * jax.nn.sigmoid(zx_ref[...])
    acc_ref[0:1] += jnp.sum(grad * unit, axis=0, keepdims=True)
    acc_ref[1:2] += jnp.sum(dy * x, axis=0, keepdims=True)
    c_low = (zc_ref[...] * jax.nn.sigmoid(zc_ref[...])).astype(BF16)
    dsin[...] += mm(c_low, (dy * split_dot(gr_ref[...], exp_ref[...])).astype(BF16), TN)

    @pl.when(at == pl.num_programs(0) - 1)
    def _():
        dsin_ref[...] = dsin[...].astype(BF16)


def mix_backward(grad, y, gate, z, growth, stats, channels, consts):
    length, width = y.shape
    last = z.shape[1] // LANES - 1
    stat = pl.BlockSpec((8, CHUNK), lambda i: (0, i))
    return kernel_call(
        functools.partial(mix_backward_kernel, float(channels), len(stats)),
        cost=5.0,
        grid=(length // CHUNK,),
        in_specs=[
            row_spec(width),
            row_spec(width),
            row_spec(width),
            row_spec(width),
            row_spec(LANES, last),
            row_spec(LANES),
            whole((1, width)),
            whole((LANES, width)),
        ]
        + [stat] * len(stats),
        out_specs=[
            row_spec(width),
            row_spec(width),
            row_spec(width),
            whole((8, width)),
            whole((LANES, width)),
        ],
        out_shape=[
            jax.ShapeDtypeStruct((length, width), BF16),
            jax.ShapeDtypeStruct((length, width), BF16),
            jax.ShapeDtypeStruct((length, width), F32),
            jax.ShapeDtypeStruct((8, width), F32),
            jax.ShapeDtypeStruct((LANES, width), BF16),
        ],
        scratch_shapes=[pltpu.VMEM((LANES, width), F32)],
        compiler_params=params(),
    )(grad, y, gate, z, z, growth, consts["gain"], consts["exp"], *stats)


def scan_backward_kernel(
    heads, width, chunks, dy_ref, z_ref, p_ref, before_ref, rim_ref, marks_ref, cw_ref,
    hp_ref, skip_ref, exp_ref, red_ref, st_ref, sin_ref, grprev_ref, dend_ref,
    dproj_ref, wacc_ref, hacc_ref, tail_ref, drim_ref, vbuf, zbuf, dstate,
):
    step_at = pl.program_id(0)
    chunk = chunks - 1 - step_at
    aux = column_of(marks_ref[...])

    @pl.when(step_at == 0)
    def _():
        dstate[...] = dend_ref[...].astype(F32)
        zbuf[...] = jnp.zeros_like(zbuf)
        wacc_ref[...] = jnp.zeros_like(wacc_ref)
        hacc_ref[...] = jnp.zeros_like(hacc_ref)

    @pl.when(chunk == 0)
    def _():
        vbuf[0:8] = rim_ref[...].astype(F32)

    @pl.when(chunk > 0)
    def _():
        vbuf[0:8, :width] = rounded(before_ref[:, :width])
        vbuf[0:8, width:] = rounded(before_ref[:, width + LANES :])

    vbuf[8:, :width] = rounded(p_ref[:, :width])
    vbuf[8:, width:] = rounded(p_ref[:, width + LANES :])

    z = z_ref[...]
    act, sig = silu_parts(z)
    slope = sig * (1.0 + z * (1.0 - sig))
    x = act[:, :width]
    b_val, c_val = act[:, width : width + LANES], act[:, width + LANES :]
    lane = iota(1)
    pre = p_ref[:, width : width + LANES] + hp_ref[0:1]
    step = jnp.where(lane < heads, softplus(pre), 0.0)
    decay = hp_ref[1:2] * step
    cum = lax.dot_general(
        (iota(0) >= iota(1)).astype(F32), decay, NN, precision=HIGH, preferred_element_type=F32
    )
    cum_t = cum.T
    seg_col = aux[:, 5:6]
    link = jnp.where((seg_col == marks_ref[5:6]) & (iota(0) <= iota(1)), 0.0, NO_LINK)
    growth = jnp.exp(cum) * aux[:, 3:4]
    last = cum[CHUNK - 1 : CHUNK]
    weight = jnp.exp(last - cum) * (seg_col == seg_col[CHUNK - 1 : CHUNK]).astype(F32)
    reach = jnp.where(chunk == 0, 1.0, grprev_ref[7:8])
    wide = split_dot(
        jnp.concatenate([step, growth, weight, jnp.broadcast_to(reach, (8, LANES))], axis=0),
        exp_ref[...],
    )
    step_e, growth_e = wide[:CHUNK], wide[CHUNK : 2 * CHUNK]
    weight_e, reach_e = wide[2 * CHUNK : 3 * CHUNK], wide[3 * CHUNK : 3 * CHUNK + 1]
    held = st_ref[0] + sin_ref[...].astype(F32) * reach_e
    after = dstate[...]
    xd = x * step_e
    dy = dy_ref[...]
    scores = wide_mm(b_val, c_val, NT)
    carried = low_mm(c_val, held) * growth_e
    fed = low_mm(b_val, after) * weight_e
    dy_grown = dy * growth_e
    lower = lane < LANES // 2
    dscores = jnp.zeros((CHUNK, CHUNK), F32)
    into = jnp.zeros((CHUNK, CHUNK), F32)
    rows, pieces = [], []
    for pair in range(heads // 2):
        at = slice(pair * LANES, (pair + 1) * LANES)
        products = wide_mm(head_halves(xd[:, at], lower), dy[:, at], NT)
        mats = []
        for side, head in enumerate((2 * pair, 2 * pair + 1)):
            spread = cum_t[head : head + 1, :] - cum[:, head : head + 1]
            reachable = jnp.exp(spread + link)
            product = products[side * CHUNK : (side + 1) * CHUNK]
            mat = reachable * scores
            dscores = dscores + reachable * product
            energy = mat * product
            rows.append(jnp.sum(energy, axis=0, keepdims=True))
            into = jnp.where(lane == head, jnp.sum(energy, axis=1, keepdims=True), into)
            mats.append(mat)
        pieces.append(low_mm(jnp.concatenate(mats, axis=1), head_halves(dy[:, at], lower)))
    dxd = jnp.concatenate(pieces, axis=1) + fed
    kept = jnp.sum(after * held, axis=0, keepdims=True) * growth_e[CHUNK - 1 : CHUNK]
    sums = split_dot(
        jnp.concatenate(
            [dy * carried, xd * fed, dxd * x, jnp.broadcast_to(kept, (8, width))], axis=0
        ),
        red_ref[...],
    )
    out_of, fed_sum = sums[:CHUNK], sums[CHUNK : 2 * CHUNK]
    dstep, kept_sum = sums[2 * CHUNK : 3 * CHUNK], sums[3 * CHUNK : 3 * CHUNK + 1]
    rows = column_of(jnp.concatenate(rows, axis=0))
    dcum = rows - into + out_of - fed_sum
    end_term = kept_sum + jnp.sum(fed_sum, axis=0, keepdims=True)
    ddecay = (
        lax.dot_general(
            (iota(0) <= iota(1)).astype(F32), dcum, NN, precision=HIGH, preferred_element_type=F32
        )
        + end_term
    )
    ddecay = jnp.where(lane < heads, ddecay, 0.0)
    dpre = jnp.where(lane < heads, (dstep + hp_ref[1:2] * ddecay) * jax.nn.sigmoid(pre), 0.0)
    hacc_ref[0:1] += jnp.sum(dpre, axis=0, keepdims=True)
    hacc_ref[1:2] += jnp.sum(ddecay * decay, axis=0, keepdims=True)
    dx = dxd * step_e + skip_ref[...] * dy
    db = wide_mm(dscores, c_val) + wide_mm(xd * weight_e, after, NT)
    dc = wide_mm(dscores, b_val, TN) + wide_mm(dy_grown, held, NT)
    dstate[...] = after * growth_e[CHUNK - 1 : CHUNK] + wide_mm(c_val, dy_grown, TN)

    dz = jnp.concatenate([dx, db, dc], axis=1) * slope
    wacc_ref[3:4] += jnp.sum(dz * vbuf[8:], axis=0, keepdims=True)
    wacc_ref[4:5] += jnp.sum(dz, axis=0, keepdims=True)
    dv = cw_ref[3:4] * dz
    for k in range(3):
        masked = dz * aux[:, k : k + 1]
        wacc_ref[k : k + 1] += jnp.sum(
            masked * vbuf[5 + k : 5 + k + CHUNK], axis=0, keepdims=True
        )
        zbuf[k, 8 : 8 + CHUNK] = masked
        dv = dv + cw_ref[k : k + 1] * zbuf[k, 11 - k : 11 - k + CHUNK]
    dproj_ref[:, :width] = dv[:, :width].astype(BF16)
    dproj_ref[:, width : width + LANES] = dpre.astype(BF16)
    dproj_ref[:, width + LANES :] = dv[:, width:].astype(BF16)

    @pl.when(step_at == 0)
    def _():
        tail_ref[...] = dv[CHUNK - 16 :]

    @pl.when(chunk == 0)
    def _():
        drim = cw_ref[0:1] * zbuf[0, 3:11]
        for k in (1, 2):
            drim = drim + cw_ref[k : k + 1] * zbuf[k, 3 - k : 11 - k]
        drim_ref[0:8] = jnp.zeros_like(drim)
        drim_ref[8:] = drim

    for k in range(3):
        zbuf[k, 8 + CHUNK :] = zbuf[k, 8:16]


def scan_backward(dy, z, proj, rim, marks, states, carried, growth, dend, consts):
    length, total = proj.shape
    heads, width = consts["heads"], consts["width"]
    chunks, conv = length // CHUNK, total - LANES
    eights = CHUNK // 8

    def back(columns):
        return pl.BlockSpec((CHUNK, columns), lambda i: (chunks - 1 - i, 0))

    def previous(columns):
        return pl.BlockSpec(
            (8, columns), lambda i: (jnp.maximum((chunks - 1 - i) * eights - 1, 0), 0)
        )

    return kernel_call(
        functools.partial(scan_backward_kernel, heads, width, chunks),
        cost=18.0,
        grid=(chunks,),
        in_specs=[
            back(width),
            back(conv),
            back(total),
            previous(total),
            whole((8, conv)),
            pl.BlockSpec((8, CHUNK), lambda i: (0, chunks - 1 - i)),
            whole((8, conv)),
            whole((8, LANES)),
            whole((1, width)),
            whole((LANES, width)),
            whole((width, LANES)),
            pl.BlockSpec((1, LANES, width), lambda i: (chunks - 1 - i, 0, 0)),
            whole((LANES, width)),
            previous(LANES),
            whole((LANES, width)),
        ],
        out_specs=[
            back(total),
            whole((8, conv)),
            whole((8, LANES)),
            whole((16, conv)),
            whole((16, conv)),
        ],
        out_shape=[
            jax.ShapeDtypeStruct((length, total), BF16),
            jax.ShapeDtypeStruct((8, conv), F32),
            jax.ShapeDtypeStruct((8, LANES), F32),
            jax.ShapeDtypeStruct((16, conv), F32),
            jax.ShapeDtypeStruct((16, conv), F32),
        ],
        scratch_shapes=[
            pltpu.VMEM((CHUNK + 8, conv), F32),
            pltpu.VMEM((3, CHUNK + 16, conv), F32),
            pltpu.VMEM((LANES, width), F32),
        ],
        compiler_params=params(),
    )(
        dy, z, proj, proj, rim, marks, consts["cw"], consts["hp"], consts["skip"],
        consts["exp"], consts["red"], states, carried, growth, dend,
    )


def local(
    stream,
    seg_ids,
    input_weight,
    step_size_weight,
    coefficient_weight,
    pre_gain,
    conv_bc,
    bias_bc,
    output_weight,
    conv_x,
    bias_x,
    dt_bias,
    a_log,
    skip,
    gate_gain,
    cotangent,
):
    PRECEDING.clear()
    layers, rows_in, _, width = input_weight.shape
    sequences, length, model = stream.shape
    heads = dt_bias.shape[1]
    depth = width // heads
    shared = coefficient_weight.shape[2]
    dp, context, tensor = (lax.axis_size(a) for a in ("dp", "context", "tensor"))
    channels = width * tensor
    rows_bc = rows_in // tensor
    conv, total = width + shared, width + LANES + shared
    layer_range, seq_range = range(layers), range(sequences)

    own_gain, own_conv = pre_gain.shape[1], conv_bc.shape[2]
    small = jnp.concatenate([pre_gain, conv_bc.reshape(layers, -1), bias_bc], axis=1)
    small = jnp.pad(small, ((0, 0), (0, shared - small.shape[1])))[:, None]
    bc_rows = gather_small(jnp.concatenate([coefficient_weight, small], axis=1), ("tensor",))
    small, bc_rows = bc_rows[:, :, rows_bc], bc_rows[:, :, :rows_bc]
    taps = small[:, :, own_gain : own_gain + 5 * own_conv].reshape(tensor, layers, 5, own_conv)
    taps = jnp.moveaxis(taps, 0, 2).reshape(layers, -1)
    small = jnp.concatenate(
        [
            jnp.moveaxis(small[:, :, :own_gain], 0, 1).reshape(layers, rows_in),
            jnp.pad(taps, ((0, 0), (0, rows_in - taps.shape[1]))),
        ],
        axis=0,
    ).T

    def first_piece(layer):
        tile = jnp.concatenate(
            [
                step_size_weight[layer],
                small,
                jnp.zeros((rows_in, LANES - heads - 2 * layers), BF16),
                bc_rows[:, layer].reshape(rows_in, shared),
            ],
            axis=1,
        )
        return [input_weight[layer, :, 1], tile]

    def second_piece(layer):
        return [input_weight[layer, :, 0], output_weight[layer].T]

    edge_ids = shifted(seg_ids[:, -3:], "context", 1)
    ext_ids = jnp.concatenate([edge_ids, seg_ids], axis=1)
    prior = ext_ids[:, 2 : 2 + length].reshape(sequences, length // CHUNK, CHUNK)[:, :, 0]
    prior = jnp.repeat(prior, CHUNK, axis=1)
    aux_all = jnp.stack(
        [ext_ids[:, k : k + length] == seg_ids for k in range(3)]
        + [seg_ids == prior, seg_ids == edge_ids[:, 2:3], seg_ids, seg_ids, seg_ids],
        axis=1,
    ).astype(F32)

    spread_table = (jnp.arange(LANES)[:, None] == jnp.arange(width)[None, :] // depth).astype(BF16)

    def joined(*parts):
        return jnp.concatenate([one for part in parts for one in part], axis=1)

    third = total // 3
    upper_piece = joined(second_piece(1), first_piece(1))
    table, second_table = [], []
    halo = shifted(stream[:, length - 16 :], "context", 1)
    precede(halo, edge_ids)
    for _ in ring_pieces(table, joined(first_piece(0))):
        pass
    second_ring = ring_pieces(second_table, relayed(joined(second_piece(0))))
    next(second_ring)
    places = jnp.arange(length // CHUNK, dtype=jnp.int32)
    arrived, sending = rows_order(False), rows_order(True)
    own_place = lax.axis_index("tensor").astype(jnp.int32)[None]
    precede(aux_all, spread_table, spread_table.T, arrived, sending)
    first, tile_rows = placed(table, [total], width)

    def every_row(part):
        return lax.all_gather(part, ("dp", "context"), axis=0, tiled=True)

    weights = [
        {"front": (first, 0)},
        {},
    ]
    streams = [(stream, s) for s in seq_range]
    grads = [(cotangent, s) for s in seq_range]
    small = tile_rows[heads : heads + 2 * layers]
    gains = small[:layers]
    taps = small[layers:].reshape(layers, dp * context, rows_in)[:, :, : 5 * tensor * own_conv]
    taps = taps.reshape(layers, dp * context, 5, tensor * own_conv)
    taps = jnp.moveaxis(taps, 1, 2).reshape(layers, 5, shared)

    consts = []
    for layer in layer_range:
        cw = jnp.concatenate(
            [
                jnp.concatenate(
                    [jnp.concatenate([conv_x[layer], bias_x[layer][None]], axis=0), taps[layer]],
                    axis=1,
                ),
                jnp.zeros((3, conv), F32),
            ],
            axis=0,
        )
        pad = jnp.zeros((LANES - heads,), F32)
        hp = jnp.stack(
            [
                jnp.concatenate([dt_bias[layer], pad]),
                jnp.concatenate([-jnp.exp(a_log[layer]), pad]),
            ]
            + [jnp.zeros((LANES,), F32)] * 6
        )
        consts.append(
            {
                "heads": heads,
                "width": width,
                "cw": cw,
                "hp": hp,
                "skip": jnp.repeat(skip[layer], depth)[None],
                "gain": gate_gain[layer][None],
                "exp": spread_table,
                "red": spread_table.T,
                **weights[layer],
            }
        )

    def chain(value, total, steps):
        carried = shifted(value, "context", steps)
        for _ in range(context - 2):
            passed = value.astype(F32) + carried.astype(F32) * total
            carried = shifted(passed.astype(value.dtype), "context", steps)
        return carried

    def through(growth):
        return jnp.repeat(growth[length - 1, :heads], depth)[None]

    for const in consts:
        precede(const["cw"], const["hp"], const["skip"], const["gain"])
    precede(gains)
    incoming = [(stream, halo, s) for s in seq_range]
    work = [[{} for _ in seq_range] for _ in layer_range]
    outputs = []
    top = layers - 1
    def step_project(layer, s):
        k = work[layer][s]
        k["stream"] = streams[s]
        k["normed"], k["proj"], tail = project(
            incoming[s],
            None if layer else gains[0:1],
            arrived if layer else places,
            consts[layer]["front"],
            width,
            total,
        )
        k["rim"] = shifted(tail, "context", 1) if layer else tail

    def step_scan(layer, s):
        k = work[layer][s]
        k["z"], k["y0"], k["states"], end, k["growth"] = scan_forward(
            k["proj"], k["rim"], aux_all[s], consts[layer]
        )
        k["carried"] = chain(end, through(k["growth"]), 1)

    def step_gate(layer, s):
        k = work[layer][s]
        k["gate"] = plain_product(k["normed"], consts[layer]["gate"], width)

    def step_mix(layer, s):
        k = work[layer][s]
        k["y"], squares = mix_forward(
            k["y0"], k["z"], k["growth"], k["carried"], k["gate"], consts[layer]
        )
        if layer < top:
            k["squares"] = from_others(squares, "tensor")

    def step_out(layer, s):
        k = work[layer][s]
        kind = BF16 if layer == top else F32
        sent, own = project_out(
            k["y"], k["gate"], k["squares" if layer < top else "stats"], channels, kind, sending,
            consts[layer],
        )
        k["out"] = [own, flipped(sent, "tensor", 0)]

    def step_pass(layer, s, name):
        terms = work[layer][s][name]
        terms.append(flipped(pass_on(*terms), "tensor", 1))

    def step_norm(layer, s):
        k = work[layer][s]
        gain = None if layer == top else gains[layer + 1 : layer + 2]
        *new, low = norm_forward(streams[s], k["out"], gain, own_place)
        streams[s] = new[0] if new else None
        k["rows"] = [low, flipped(low, "tensor", 1)]

    def step_join(layer, s, name):
        own, other = work[layer][s][name]
        across = flipped(joined_rows(own, other), "tensor", 0)
        return [(own, 0), (other, 0), (across, 0), (across, 1)]

    def step_grad(layer, s):
        k = work[layer][s]
        source = (cotangent, s) if layer == top else incoming[s]
        k["grad"], dots, k["low"] = grad_scaled(
            source, k["y"], k["gate"], places if layer == top else arrived, consts[layer]
        )
        k["stats"] = from_others(dots, "tensor")

    def step_mix_back(layer, s):
        k = work[layer][s]
        k["scaled"], k["dgate"], k["dy"], k["acc"], dsin = mix_backward(
            k["grad"], k["y"], k["gate"], k["z"], k["growth"], k["stats"], channels, consts[layer],
        )
        k["dend"] = chain(dsin, through(k["growth"]), -1)

    def step_scan_back(layer, s):
        k = work[layer][s]
        k["dproj"], k["wacc"], k["hacc"], k["tail"], drim = scan_backward(
            k["dy"], k["z"], k["proj"], k["rim"], aux_all[s], k["states"],
            k["carried"], k["growth"], k["dend"], consts[layer],
        )
        k["drim"] = shifted(drim, "context", -1)

    def step_input_grad(layer, s):
        k = work[layer][s]
        sent, own, k["dproj"] = input_grad(
            k["dproj"], k["dgate"], k["tail"], k["drim"], consts[layer]["front"],
            consts[layer]["gate"], sending,
        )
        k["back"] = [own, flipped(sent, "tensor", 0)]

    def step_norm_back(layer, s):
        k = work[layer][s]
        grads[s], low, k["dgain"] = norm_backward(
            k["stream"], k["back"], grads[s], gains[layer : layer + 1], own_place
        )
        k["grad_low"] = [low, flipped(low, "tensor", 1)]

    def every(layer, name):
        return [k[name] for k in work[layer]]

    def step_second_grad(layer):
        return weight_grad(
            [
                (every(layer, "normed"), every(layer, "dgate")),
                (every(layer, "low"), every(layer, "scaled")),
            ],
            layer == 0,
        )

    def step_first_grad(layer):
        return weight_grad([(every(layer, "normed"), every(layer, "dproj"))], layer == 0)

    def scattered(value):
        return lax.psum_scatter(value, ("dp", "context"), scatter_dimension=0, tiled=True)

    second_sums, first_sums = [None] * layers, [None] * layers
    project_0, scan_0, gate_0, mix_0, out_0, grad_0, mixed_0, scanned_0, input_0 = (
        functools.partial(step, 0)
        for step in (
            step_project, step_scan, step_gate, step_mix, step_out, step_grad, step_mix_back,
            step_scan_back, step_input_grad,
        )
    )
    project_1, scan_1, gate_1, mix_1, out_1, grad_1, mixed_1, scanned_1, input_1 = (
        functools.partial(step, 1)
        for step in (
            step_project, step_scan, step_gate, step_mix, step_out, step_grad, step_mix_back,
            step_scan_back, step_input_grad,
        )
    )

    project_0(0)
    next(second_ring)
    scan_0(0)
    next(second_ring)
    upper = every_row(relayed(upper_piece))
    consts[1].update(front=(upper, 2 * width // third), gate=(upper, 0), out=(upper, 1))
    project_0(1)
    next(second_ring, None)
    scan_0(1)
    precede(work[0][0]["carried"])
    (second,) = placed(second_table, [2 * width])
    consts[0].update(gate=(second, 0), out=(second, 1))
    gate_0(0)
    mix_0(0)
    gate_0(1)
    mix_0(1)
    out_0(0)
    step_pass(0, 0, "out")
    out_0(1)
    step_norm(0, 0)
    step_pass(0, 1, "out")
    incoming[0] = step_join(0, 0, "rows")
    project_1(0)
    step_norm(0, 1)
    incoming[1] = step_join(0, 1, "rows")
    scan_1(0)
    project_1(1)
    gate_1(0)
    scan_1(1)
    mix_1(0)
    gate_1(1)
    grad_1(0)
    mix_1(1)
    grad_1(1)
    mixed_1(0)
    mixed_1(1)
    precede(work[1][0]["dend"])
    second_sums[1] = scattered(step_second_grad(1)[0])
    scanned_1(0)
    out_1(0)
    precede(work[1][1]["dend"])
    input_1(0)
    step_pass(1, 0, "back")
    scanned_1(1)
    step_norm_back(1, 0)
    out_1(1)
    input_1(1)
    incoming[0] = step_join(1, 0, "grad_low")
    step_pass(1, 1, "back")
    grad_0(0)
    step_pass(1, 0, "out")
    step_pass(1, 1, "out")
    precede(*work[0][0]["stats"])
    first_grad = step_first_grad(1)
    mixed_0(0)
    step_norm_back(1, 1)
    precede(second_sums[1])
    first_sums[1] = scattered(first_grad[0])
    scanned_0(0)
    for s in seq_range:
        step_norm(1, s)
    incoming[1] = step_join(1, 1, "grad_low")
    grad_0(1)
    input_0(0)
    mixed_0(1)
    second_steps = ring_steps(step_second_grad(0), True)
    step_pass(0, 0, "back")
    precede(first_sums[1])
    scanned_0(1)
    outputs.extend(step_join(1, s, "rows") for s in seq_range)
    next(second_steps)
    step_norm_back(0, 0)
    input_0(1)
    next(second_steps)
    first_steps = ring_steps(step_first_grad(0))
    step_pass(0, 1, "back")
    next(second_steps)
    incoming[0] = step_join(0, 0, "grad_low")
    next(first_steps)
    second_sums[0] = next(second_steps)
    layer_out = assembled(outputs, arrived)
    step_norm_back(0, 1)
    small_steps = small_sums(work, width, heads, model, consts[0]["red"])
    next(small_steps)
    next(first_steps)
    next(small_steps)
    second_sums[1], first_sums[1] = widened(second_sums[1]), widened(first_sums[1])
    incoming[1] = step_join(0, 1, "grad_low")
    next(small_steps)
    next(first_steps)
    grad_stream = assembled(incoming, arrived)
    first_sums[0] = next(first_steps)
    next(small_steps)
    for value in small_steps:
        small_out = value

    out = []
    for layer in layer_range:
        second_sum, first_sum = second_sums[layer], first_sums[layer]
        out.append(
            (
                jnp.stack([second_sum[:, :width], first_sum[:, :width]], axis=1),
                first_sum[:, width : width + heads],
                scatter_places(first_sum[:, width + LANES :]),
                second_sum[:, width:].T,
            )
        )
    taps_x, sum_bias_x, dt_sum, rate_sum, skip_sum, gate_sum, taps_bc, sum_bias_bc, gain_sum = (
        small_out
    )
    return (
        layer_out,
        grad_stream,
        jnp.stack([o[0] for o in out]),
        jnp.stack([o[1] for o in out]),
        jnp.stack([o[2] for o in out]),
        gain_sum,
        taps_bc,
        sum_bias_bc,
        jnp.stack([o[3] for o in out]),
        taps_x,
        sum_bias_x,
        dt_sum,
        rate_sum,
        skip_sum,
        gate_sum,
    )


def solution(mesh):
    in_specs = (
        P("dp", "context", None),
        P("dp", "context"),
        P(None, ("dp", "context"), None, "tensor"),
        P(None, ("dp", "context"), "tensor"),
        P(None, ("dp", "context", "tensor"), None),
        P(None, ("dp", "context", "tensor")),
        P(None, None, ("dp", "context", "tensor")),
        P(None, ("dp", "context", "tensor")),
        P(None, "tensor", ("dp", "context")),
        P(None, None, "tensor"),
        P(None, "tensor"),
        P(None, "tensor"),
        P(None, "tensor"),
        P(None, "tensor"),
        P(None, "tensor"),
        P("dp", "context", None),
    )
    out_specs = (
        P("dp", "context", None),
        P("dp", "context", None),
        P(None, ("dp", "context"), None, "tensor"),
        P(None, ("dp", "context"), "tensor"),
        P(None, ("dp", "context", "tensor"), None),
        P(None, ("dp", "context", "tensor")),
        P(None, None, ("dp", "context", "tensor")),
        P(None, ("dp", "context", "tensor")),
        P(None, "tensor", ("dp", "context")),
        P(None, None, "tensor"),
        P(None, "tensor"),
        P(None, "tensor"),
        P(None, "tensor"),
        P(None, "tensor"),
        P(None, "tensor"),
        P("dp", "context", None),
    )
    return jax.shard_map(
        local, mesh=mesh, in_specs=in_specs, out_specs=out_specs[:15], check_vma=False
    )
```

```python
import functools

import jax
import jax.numpy as jnp
from jax import lax
from jax.experimental import pallas as pl
from jax.experimental.pallas import tpu as pltpu
from jax.sharding import PartitionSpec as P

CHUNK = 128
LANES = 128
eps = 1e-05
F32 = jnp.float32
BF16 = jnp.bfloat16
HIGH = lax.Precision.HIGHEST
NN = (((1,), (0,)), ((), ()))
NT = (((1,), (1,)), ((), ()))
TN = (((0,), (0,)), ((), ()))
NO_LINK = -1e30
COST_SCALE = 0.5


def mm(a, b, dims=NN):
    return lax.dot_general(a, b, dims, preferred_element_type=F32)


def params(mib=48):
    return pltpu.CompilerParams(
        dimension_semantics=("arbitrary",), vmem_limit_bytes=mib * 1024 * 1024
    )


PRECEDING = []


def kernel_call(body, cost=2.0, **spec):
    def call(*inputs):
        tokens = list(PRECEDING)
        options = dict(spec)
        grid_spec = options.pop("grid_spec", None)
        unread = [pl.BlockSpec(memory_space=pl.ANY)] * len(tokens)
        prefetched = 0
        if grid_spec is None:
            options["in_specs"] = list(options["in_specs"]) + unread
        else:
            prefetched = grid_spec.num_scalar_prefetch
            options["grid_spec"] = pltpu.PrefetchScalarGridSpec(
                num_scalar_prefetch=prefetched,
                grid=grid_spec.grid,
                in_specs=list(grid_spec.in_specs) + unread,
                out_specs=grid_spec.out_specs,
                scratch_shapes=grid_spec.scratch_shapes,
            )
        first = len(inputs)

        def without_tokens(*refs):
            body(*refs[:first], *refs[first + len(tokens) :])

        out = pl.pallas_call(
            without_tokens,
            cost_estimate=pl.CostEstimate(
                flops=int(cost * 1.0e9 * COST_SCALE), transcendentals=0, bytes_accessed=1024
            ),
            **options,
        )(*inputs, *tokens)
        PRECEDING[:] = [min(jax.tree.leaves(out), key=lambda one: one.size * one.dtype.itemsize)]
        return out

    return call


def precede(*tokens):
    PRECEDING.extend(token for token in tokens if token is not None)


def flipped(value, axis, bit):
    count = lax.axis_size(axis)
    return lax.ppermute(value, axis, [(i, i ^ (1 << bit)) for i in range(count)])


def bits(axis):
    return (lax.axis_size(axis) - 1).bit_length()


def shifted(value, axis, steps):
    count = lax.axis_size(axis)
    leading, last = (max(0, -steps), min(count, count - steps))
    return lax.ppermute(value, axis, [(source, source + steps) for source in range(leading, last)])


def ring(value, axis):
    count = lax.axis_size(axis)
    return lax.ppermute(value, axis, [(i, (i - 1) % count) for i in range(count)])


def summed_over(value, axes):
    for axis in axes:
        for bit in range(bits(axis)):
            value = value + flipped(value, axis, bit)
    return value


def gather_small(value, axes):
    value = value[None]
    for axis in axes:
        index = lax.axis_index(axis)
        for bit in range(bits(axis)):
            other = flipped(value, axis, bit)
            upper = (index >> bit) & 1
            value = jnp.concatenate(
                [jnp.where(upper == 0, value, other), jnp.where(upper == 0, other, value)], axis=0
            )
    return value


def slots():
    count, places = bits("tensor"), []
    for m in range(lax.axis_size("tensor")):
        places.append(sum(((m >> b) & 1) << (count - 1 - b) for b in range(count)))
    return places


def rows_order(first):
    places = slots()
    if first:
        half = len(places) // 2
        places = places[half:] + places[:half]
    return jnp.array(places, jnp.int32) ^ lax.axis_index("tensor")


def own_rows(value):
    rows = value.shape[0] // lax.axis_size("tensor")
    return lax.dynamic_slice_in_dim(value, lax.axis_index("tensor") * rows, rows, 0)


def relay_kernel(from_ref, to_ref):
    to_ref[...] = from_ref[...]


def widen_kernel(from_ref, to_ref):
    to_ref[...] = from_ref[...].astype(F32)


def widened(value):
    return kernel_call(
        widen_kernel,
        grid=(1,),
        in_specs=[fixed_block(value.shape)],
        out_specs=fixed_block(value.shape),
        out_shape=jax.ShapeDtypeStruct(value.shape, F32),
        compiler_params=params(),
    )(value)


def relayed(piece, *tokens):
    precede(*tokens)
    return kernel_call(
        relay_kernel,
        grid=(1,),
        in_specs=[fixed_block(piece.shape)],
        out_specs=fixed_block(piece.shape),
        out_shape=jax.ShapeDtypeStruct(piece.shape, piece.dtype),
        compiler_params=params(),
    )(piece)


def ring_pieces(table, piece):
    def over_context(arrived):
        row = [arrived]
        for _ in range(lax.axis_size("context") - 1):
            row.append(ring(row[-1], "context"))
        return row

    arrived = piece
    table.append(over_context(piece))
    for k in range(1, lax.axis_size("dp")):
        arrived = ring(arrived, "dp")
        yield
        arrived = relayed(arrived, table[k - 1][-1])
        table.append(over_context(arrived))
    yield


def place_kernel(count, widths, tile_at, index_ref, *refs):
    pieces, outs = refs[:count], refs[count:]
    for i in range(count):
        at = 0
        for out, width in zip(outs, widths):
            out[index_ref[i]] = pieces[i][:, at : at + width]
            at += width
    if tile_at is not None:
        first, tiles = outs[0], outs[-1]
        rows = first.shape[1]
        whole_rows = jnp.concatenate(
            [first[i, :, tile_at : tile_at + LANES] for i in range(count)], axis=0
        )
        for at in range(0, count * rows, LANES):
            tiles[:, at : at + LANES] = whole_rows[at : at + LANES].astype(F32).T


def placed(table, widths, tile_at=None):
    dp, context = lax.axis_size("dp"), lax.axis_size("context")
    z, x = lax.axis_index("dp"), lax.axis_index("context")
    pieces, index = [], []
    for k, row in enumerate(table):
        for j, piece in enumerate(row):
            pieces.append(piece)
            index.append(((z + k) % dp) * context + (x + j) % context)
    count, rows = len(pieces), pieces[0].shape[0]
    out_specs = [
        pl.BlockSpec((count, rows, width), lambda i, index: (0, 0, 0)) for width in widths
    ]
    out_shape = [jax.ShapeDtypeStruct((count, rows, width), BF16) for width in widths]
    if tile_at is not None:
        out_specs.append(pl.BlockSpec((LANES, count * rows), lambda i, index: (0, 0)))
        out_shape.append(jax.ShapeDtypeStruct((LANES, count * rows), F32))
    outs = kernel_call(
        functools.partial(place_kernel, count, widths, tile_at),
        cost=3.5,
        grid_spec=pltpu.PrefetchScalarGridSpec(
            num_scalar_prefetch=1,
            grid=(1,),
            in_specs=[pl.BlockSpec(piece.shape, lambda i, index: (0, 0)) for piece in pieces],
            out_specs=out_specs,
        ),
        out_shape=out_shape,
        compiler_params=params(),
    )(jnp.stack(index).astype(jnp.int32), *pieces)
    return [
        out.reshape(count * rows, -1) if i < len(widths) else out for i, out in enumerate(outs)
    ]


def after(value, *tokens):
    tokens = tuple(token for token in tokens if token is not None)
    return lax.optimization_barrier((value, *tokens))[0] if tokens else value


def from_others(value, axis):
    count = lax.axis_size(axis)
    return [value] + [
        lax.ppermute(value, axis, [(i, i ^ step) for i in range(count)])
        for step in range(1, count)
    ]


def scatter_places(value):
    count, index = lax.axis_size("tensor"), lax.axis_index("tensor")
    value = value.reshape(count, -1, value.shape[1])
    total = lax.dynamic_index_in_dim(value, index, 0, keepdims=False)
    for step in range(1, count):
        sent = lax.dynamic_index_in_dim(value, index ^ step, 0, keepdims=False)
        total = total + lax.ppermute(sent, "tensor", [(i, i ^ step) for i in range(count)])
    return total


def pack_kernel(layers, sequences, width, *refs):
    inputs, (local_ref, shared_ref) = refs[:-2], refs[-2:]
    local_ref[...] = jnp.zeros_like(local_ref)
    shared_ref[...] = jnp.zeros_like(shared_ref)
    for layer in range(layers):
        mine = inputs[layer * sequences * 4 : (layer + 1) * sequences * 4]
        taps, acc, small, gain = (sum(one[...] for one in mine[i::4]) for i in range(4))
        local_ref[layer, 0:5, :width] = taps[0:5, :width]
        local_ref[layer, 5:7, :width] = acc[0:2]
        local_ref[layer, 0:2, width:] = small[0:2]
        shared = taps.shape[1] - width
        shared_ref[layer, 0:5, :shared] = taps[0:5, width:]
        for i, (row, at) in enumerate(gain_places(gain.shape[1], shared)):
            shared_ref[layer, row : row + 1, at : at + shared] = gain[
                0:1, i * shared : (i + 1) * shared
            ]


def gain_places(model, shared):
    places = [(5, 0), (6, 0), (7, 0)] + [(row, shared) for row in range(8)]
    return places[: model // shared]


def share_kernel(local_ref, *refs):
    cut = local_ref.shape[2]
    refs[-1][:, :, :cut] = local_ref[...]
    refs[-1][:, :, cut:] = sum(one[...] for one in refs[:-1])


def unpack_kernel(width, heads, shared, model, place_ref, a_ref, b_ref, red_ref, *outs):
    taps_x, bias_x, dt_bias, rate, skip, gate_gain, taps_bc, bias_bc, pre_gain = outs
    own_conv, own_gain = taps_bc.shape[2], pre_gain.shape[1]
    cut = width + LANES
    for layer in range(a_ref.shape[0]):
        total = a_ref[layer] + b_ref[layer]
        at = slice(layer, layer + 1)
        taps_x[layer] = total[0:4, :width]
        bias_x[at] = total[4:5, :width]
        gate_gain[at] = total[5:6, :width]
        dt_bias[at] = total[0:1, width : width + heads]
        rate[at] = total[1:2, width : width + heads]
        skip[at] = split_dot(total[:, :width], red_ref[...])[6:7, :heads]
        part = total[:, cut : cut + shared]
        part = pltpu.roll(part, shared - place_ref[0] * own_conv, axis=1)
        taps_bc[layer] = part[0:4, :own_conv]
        bias_bc[at] = part[4:5, :own_conv]
        rows = [
            total[row : row + 1, cut + col : cut + col + shared]
            for row, col in gain_places(model, shared)
        ]
        gain = jnp.broadcast_to(jnp.concatenate(rows, axis=1), (8, model))
        gain = pltpu.roll(gain, model - place_ref[0] * own_gain, axis=1)
        pre_gain[at] = gain[0:1, :own_gain]


def add_kernel(*refs):
    refs[-1][...] = sum(one[...] for one in refs[:-1])


def add_up(terms):
    shape = terms[0].shape
    return kernel_call(
        add_kernel,
        cost=1.0,
        grid=(1,),
        in_specs=[whole(shape)] * len(terms),
        out_specs=whole(shape),
        out_shape=jax.ShapeDtypeStruct(shape, terms[0].dtype),
        compiler_params=params(),
    )(*terms)


def small_sums(work, width, heads, model, red):
    layers, sequences = len(work), len(work[0])
    inputs = [k[name] for ks in work for k in ks for name in ("wacc", "acc", "hacc", "dgain")]
    shared = inputs[0].shape[1] - width
    shapes = [(layers, 8, width + LANES), (layers, 8, 2 * shared)]
    own, every = kernel_call(
        functools.partial(pack_kernel, layers, sequences, width),
        grid=(1,),
        in_specs=[whole(one.shape) for one in inputs],
        out_specs=[whole(shape) for shape in shapes],
        out_shape=[jax.ShapeDtypeStruct(shape, F32) for shape in shapes],
        compiler_params=params(),
    )(*inputs)
    parts = from_others(every, "tensor")
    yield None
    shape = (layers, 8, width + LANES + 2 * shared)
    total = kernel_call(
        share_kernel,
        cost=1.0,
        grid=(1,),
        in_specs=[whole(one.shape) for one in (own, *parts)],
        out_specs=whole(shape),
        out_shape=jax.ShapeDtypeStruct(shape, F32),
        compiler_params=params(),
    )(own, *parts)
    hops = [(axis, bit) for axis in ("context", "dp") for bit in range(bits(axis))]
    for axis, bit in hops:
        other = flipped(total, axis, bit)
        yield None
        if (axis, bit) != hops[-1]:
            total = add_up([total, other])
    devices = lax.axis_size("dp") * lax.axis_size("context") * lax.axis_size("tensor")
    place = lax.axis_index("dp") * lax.axis_size("context") + lax.axis_index("context")
    place = place * lax.axis_size("tensor") + lax.axis_index("tensor")
    own_conv, own_gain = shared // devices, model // devices
    shapes = [
        (layers, 4, width), (layers, width), (layers, heads), (layers, heads), (layers, heads),
        (layers, width), (layers, 4, own_conv), (layers, own_conv), (layers, own_gain),
    ]
    yield kernel_call(
        functools.partial(unpack_kernel, width, heads, shared, model),
        grid_spec=pltpu.PrefetchScalarGridSpec(
            num_scalar_prefetch=1,
            grid=(1,),
            in_specs=[fixed_block(one.shape) for one in (total, other, red)],
            out_specs=[fixed_block(one) for one in shapes],
        ),
        out_shape=[jax.ShapeDtypeStruct(one, F32) for one in shapes],
        compiler_params=params(),
    )(place.astype(jnp.int32)[None], total, other, red)


def silu_parts(value):
    sig = jax.nn.sigmoid(value)
    return value * sig, sig


def softplus(value):
    return jnp.maximum(value, 0.0) + jnp.log1p(jnp.exp(-jnp.abs(value)))


def split_dot(value, table):
    high = value.astype(BF16)
    low = (value - high.astype(F32)).astype(BF16)
    return mm(high, table) + mm(low, table)


def wide_mm(a, b, dims=NN):
    a_high, b_high = a.astype(BF16), b.astype(BF16)
    a_low = (a - a_high.astype(F32)).astype(BF16)
    b_low = (b - b_high.astype(F32)).astype(BF16)
    return mm(a_high, b_high, dims) + (mm(a_low, b_high, dims) + mm(a_high, b_low, dims))


def low_mm(a, b, dims=NN):
    return mm(a.astype(BF16), b.astype(BF16), dims)


def iota(axis):
    return lax.broadcasted_iota(jnp.int32, (CHUNK, CHUNK), axis)


def rounded(value):
    return value.astype(BF16).astype(F32)


def head_halves(tile, lower):
    zero = jnp.zeros_like(tile)
    return jnp.concatenate([jnp.where(lower, tile, zero), jnp.where(lower, zero, tile)], axis=0)


def column_of(rows):
    pad = jnp.zeros((CHUNK - rows.shape[0], CHUNK), F32)
    return jnp.concatenate([rows, pad], axis=0).T


def row_norm(wide):
    return lax.rsqrt(jnp.mean(wide * wide, axis=-1, keepdims=True) + eps)


def columns(array, at, width):
    return pl.BlockSpec((array.shape[0], width), lambda i, *_: (0, at))


def fixed_block(shape):
    return pl.BlockSpec(shape, lambda i, *_: (0,) * len(shape))


def project_kernel(norm, count, width, order_ref, *refs):
    pieces, rest = refs[:count], refs[count:]
    if norm:
        gain_ref, halo_ref, rest = rest[0], rest[1], rest[2:]
    w_ref, normed_ref, proj_ref, rim_ref, halo = rest
    step = pl.program_id(0)
    length, size = proj_ref.shape

    @pl.when(step == 0)
    def _():
        for m in range(length // CHUNK):
            if norm:
                wide = pieces[0][0, m * CHUNK : (m + 1) * CHUNK].astype(F32)
                rows = (wide * row_norm(wide) * gain_ref[...]).astype(BF16)
                normed_ref[m * CHUNK : (m + 1) * CHUNK] = rows
            else:
                place = pl.ds(pl.multiple_of(order_ref[m] * CHUNK, CHUNK), CHUNK)
                normed_ref[place] = pieces[m][...]
        if norm:
            wide = halo_ref[0].astype(F32)
            halo[...] = (wide * row_norm(wide) * gain_ref[...]).astype(BF16)
        else:
            halo[...] = normed_ref[length - 16 :]

    weight = w_ref[...]
    proj_ref[...] = mm(normed_ref[...], weight)
    tail = mm(halo[...], weight)[8:].astype(BF16)
    for i in range(width // size):

        @pl.when(step == i)
        def _(i=i):
            rim_ref[:, i * size : (i + 1) * size] = tail

    @pl.when(step == width // size)
    def _():
        rim_ref[:, width:] = tail[:, LANES:]


def project(source, gain, order, front, width, total):
    weights, at = front
    third = total // 3
    norm = gain is not None
    if norm:
        stream, halo, sequence = source
        model, length = stream.shape[2], stream.shape[1]
        inputs, count = [stream, gain, halo], 1
        specs = [
            pl.BlockSpec((1, length, model), lambda i, order: (sequence, 0, 0)),
            fixed_block((1, model)),
            pl.BlockSpec((1, 16, model), lambda i, order: (sequence, 0, 0)),
        ]
    else:
        model, count = source[0][0].shape[1], len(source)
        length = count * CHUNK
        inputs, specs = [one for one, _ in source], piece_specs(source, CHUNK)
    conv = total - LANES
    return kernel_call(
        functools.partial(project_kernel, norm, count, width),
        cost=5.0,
        grid_spec=pltpu.PrefetchScalarGridSpec(
            num_scalar_prefetch=1,
            grid=(3,),
            in_specs=specs + [pl.BlockSpec((model, third), lambda i, order: (0, at + i))],
            out_specs=[
                fixed_block((length, model)),
                pl.BlockSpec((length, third), lambda i, order: (0, i)),
                fixed_block((8, conv)),
            ],
            scratch_shapes=[pltpu.VMEM((16, model), BF16)],
        ),
        out_shape=[
            jax.ShapeDtypeStruct((length, model), BF16),
            jax.ShapeDtypeStruct((length, total), F32),
            jax.ShapeDtypeStruct((8, conv), BF16),
        ],
        compiler_params=params(),
    )(order, *inputs, weights)


def plain_kernel(a_ref, w_ref, out_ref):
    out_ref[...] = mm(a_ref[...], w_ref[...])


def plain_product(a, weight, width):
    weights, at = weight
    length, model = a.shape
    half = width // 2
    return kernel_call(
        plain_kernel,
        cost=3.0,
        grid=(2,),
        in_specs=[
            fixed_block((length, model)),
            pl.BlockSpec((model, half), lambda i: (0, 2 * at + i)),
        ],
        out_specs=pl.BlockSpec((length, half), lambda i: (0, i)),
        out_shape=jax.ShapeDtypeStruct((length, width), F32),
        compiler_params=params(),
    )(a, weights)


def rows_of(ref):
    return (ref[...] if len(ref.shape) == 2 else ref[0]).astype(F32)


def norm_forward_kernel(place_ref, stream_ref, keep_ref, first_ref, second_ref, *refs):
    total = keep_ref[0].astype(F32) + first_ref[0].astype(F32) + second_ref[...].astype(F32)
    new = rows_of(stream_ref) + total
    if len(refs) == 1:
        refs[0][...] = new.astype(BF16)
    else:
        gain_ref, new_ref, low_ref = refs
        new_ref[...] = new
        low_ref[...] = (new * row_norm(new) * gain_ref[...]).astype(BF16)


def join_kernel(own_ref, other_ref, out_ref):
    rows = own_ref.shape[0]
    out_ref[:rows] = own_ref[...]
    out_ref[rows:] = other_ref[...]


def joined_rows(own, other):
    rows, model = own.shape
    return kernel_call(
        join_kernel,
        grid=(1,),
        in_specs=[fixed_block((rows, model))] * 2,
        out_specs=fixed_block((2 * rows, model)),
        out_shape=jax.ShapeDtypeStruct((2 * rows, model), own.dtype),
        compiler_params=params(),
    )(own, other)


def piece_specs(pieces, rows):
    return [pl.BlockSpec((rows, one.shape[1]), lambda i, *_, at=at: (at, 0)) for one, at in pieces]


def pass_on_kernel(keep_ref, first_ref, out_ref):
    total = keep_ref[0].astype(F32) + first_ref[0].astype(F32)
    out_ref[...] = total.astype(out_ref.dtype)


def pass_on(kept, first):
    _, rows, model = kept.shape
    spec = pl.BlockSpec((1, rows, model), lambda i: (1, 0, 0))
    return kernel_call(
        pass_on_kernel,
        grid=(1,),
        in_specs=[spec, spec],
        out_specs=fixed_block((rows, model)),
        out_shape=jax.ShapeDtypeStruct((rows, model), kept.dtype),
        compiler_params=params(),
    )(kept, first)


def rows_spec(one, rows):
    if isinstance(one, tuple):
        array, s = one
        return array, pl.BlockSpec((1, rows, array.shape[2]), lambda i, place: (s, place[0], 0))
    return one, fixed_block(one.shape)


def term_specs(rows, model):
    part = fixed_block((1, rows, model))
    return [part, part, fixed_block((rows, model))]


def norm_forward(stream, terms, gain, place):
    rows, model = terms[2].shape
    stream, spec = rows_spec(stream, rows)
    low = jax.ShapeDtypeStruct((rows, model), BF16)
    last = gain is None
    return kernel_call(
        norm_forward_kernel,
        grid_spec=pltpu.PrefetchScalarGridSpec(
            num_scalar_prefetch=1,
            grid=(1,),
            in_specs=[spec]
            + term_specs(rows, model)
            + ([] if last else [fixed_block((1, model))]),
            out_specs=[fixed_block((rows, model))] * (1 if last else 2),
        ),
        out_shape=[low] if last else [jax.ShapeDtypeStruct((rows, model), F32), low],
        compiler_params=params(),
    )(place, stream, *terms, *([] if last else [gain]))


def norm_backward_kernel(
    place_ref, stream_ref, keep_ref, first_ref, second_ref, grad_ref, gain_ref, new_ref, low_ref,
    dgain_ref,
):
    total = keep_ref[0].astype(F32) + first_ref[0].astype(F32) + second_ref[...].astype(F32)
    current = rows_of(stream_ref)
    scale = row_norm(current)
    unit = current * scale
    dgain_ref[...] = jnp.broadcast_to(
        jnp.sum(total * unit, axis=0, keepdims=True), dgain_ref.shape
    )
    pulled = total * gain_ref[...]
    shift = jnp.mean(pulled * unit, axis=-1, keepdims=True)
    new = rows_of(grad_ref) + scale * (pulled - unit * shift)
    new_ref[...] = new
    low_ref[...] = new.astype(BF16)


def norm_backward(stream, terms, grad, gain, place):
    rows, model = terms[2].shape
    stream, stream_spec = rows_spec(stream, rows)
    grad, grad_spec = rows_spec(grad, rows)
    return kernel_call(
        norm_backward_kernel,
        grid_spec=pltpu.PrefetchScalarGridSpec(
            num_scalar_prefetch=1,
            grid=(1,),
            in_specs=[stream_spec]
            + term_specs(rows, model)
            + [grad_spec, fixed_block((1, model))],
            out_specs=[fixed_block((rows, model))] * 2 + [fixed_block((8, model))],
        ),
        out_shape=[
            jax.ShapeDtypeStruct((rows, model), F32),
            jax.ShapeDtypeStruct((rows, model), BF16),
            jax.ShapeDtypeStruct((8, model), F32),
        ],
        compiler_params=params(),
    )(place, stream, *terms, grad, gain)


def assemble_kernel(count, order_ref, *refs):
    step = pl.program_id(0)
    for m in range(count):

        @pl.when(step == m)
        def _(m=m):
            refs[-1][0] = refs[m][...]


def assembled(groups, order):
    each, (rows, model) = len(groups[0]), groups[0][0][0].shape
    pieces = [piece for group in groups for piece in group]
    count = len(pieces)
    return kernel_call(
        functools.partial(assemble_kernel, count),
        cost=5.0,
        grid_spec=pltpu.PrefetchScalarGridSpec(
            num_scalar_prefetch=1,
            grid=(count,),
            in_specs=piece_specs(pieces, rows),
            out_specs=pl.BlockSpec(
                (1, rows, model), lambda i, order: (i // each, order[i % each], 0)
            ),
        ),
        out_shape=jax.ShapeDtypeStruct((len(groups), each * rows, model), BF16),
        compiler_params=params(),
    )(order, *[one for one, _ in pieces])


def input_grad_kernel(parts, width, order_ref, dproj_ref, dgate_ref, tail_ref, rim_ref, *refs):
    w_refs, gate_ref, sent_ref, kept_ref, fixed_ref, rows_p, rows_g = refs[:3], *refs[3:]
    half = parts // 2

    @pl.when(pl.program_id(0) == 0)
    def _():
        fixed_ref[...] = dproj_ref[...]
        tail = (tail_ref[...] + rim_ref[...]).astype(BF16)
        fixed_ref[parts * CHUNK - 16 :, :width] = tail[:, :width]
        fixed_ref[parts * CHUNK - 16 :, width + LANES :] = tail[:, width:]
        for m in range(parts):
            source = pl.ds(pl.multiple_of(order_ref[m] * CHUNK, CHUNK), CHUNK)
            rows_p[m * CHUNK : (m + 1) * CHUNK] = fixed_ref[source]
            rows_g[m * CHUNK : (m + 1) * CHUNK] = dgate_ref[source]

    total = mm(rows_g[...], gate_ref[...], NT)
    for j, w_ref in enumerate(w_refs):
        size = w_ref.shape[1]
        total = total + mm(rows_p[:, j * size : (j + 1) * size], w_ref[...], NT)
    total = total.astype(BF16)
    for m in range(half):
        sent_ref[m] = total[m * CHUNK : (m + 1) * CHUNK]
        kept_ref[m] = total[(half + m) * CHUNK : (half + m + 1) * CHUNK]


def input_grad(dproj, dgate, tail, rim, front, gate, order):
    length, total = dproj.shape
    width = dgate.shape[1]
    (front_w, at), (gate_w, gate_at) = front, gate
    model, third, parts = front_w.shape[0], total // 3, length // CHUNK
    cut = model // 4
    half = pl.BlockSpec((parts // 2, CHUNK, cut), lambda i, order: (0, 0, i))

    def rows(offset, size):
        return pl.BlockSpec((cut, size), lambda i, order: (i, offset))

    return kernel_call(
        functools.partial(input_grad_kernel, parts, width),
        cost=7.6,
        grid_spec=pltpu.PrefetchScalarGridSpec(
            num_scalar_prefetch=1,
            grid=(4,),
            in_specs=[fixed_block(one.shape) for one in (dproj, dgate, tail, rim)]
            + [rows(at + j, third) for j in range(3)]
            + [rows(gate_at, width)],
            out_specs=[half, half, fixed_block((length, total))],
            scratch_shapes=[
                pltpu.VMEM((length, total), BF16),
                pltpu.VMEM((length, width), BF16),
            ],
        ),
        out_shape=[jax.ShapeDtypeStruct((parts // 2, CHUNK, model), BF16)] * 2
        + [jax.ShapeDtypeStruct((length, total), BF16)],
        compiler_params=params(),
    )(order, dproj, dgate, tail, rim, front_w, front_w, front_w, gate_w)


def weight_grad_kernel(segments, sequences, rows, places, order_ref, *refs):
    lefts, rights = refs[: segments * sequences], refs[segments * sequences :]
    rights, outs, total = rights[: segments * sequences], rights[segments * sequences : -1], refs[-1]
    at = 0
    for g in range(segments):
        width = rights[g * sequences].shape[1]
        part = None
        for s in range(sequences):
            left = lefts[g * sequences + s]
            left = left[...] if len(left.shape) == 2 else left[0]
            one = mm(left, rights[g * sequences + s][...], TN)
            part = one if part is None else part + one
        total[:, at : at + width] = part
        at += width
    if places is None:
        outs[0][...] = total[...].astype(BF16)
        return
    dp, context = places
    slot = lax.rem(pl.program_id(0) - order_ref[1] + dp, dp)

    def block(j):
        start = lax.rem(order_ref[0] + j, context) * rows
        return total[pl.ds(pl.multiple_of(start, 8), rows)].astype(BF16)

    outs[0][0] = block(0)
    for j in range(1, context):
        for k in range(dp):

            @pl.when(slot == k)
            def _(j=j, k=k):
                outs[1 + (j - 1) * dp + k][...] = block(j)


def weight_grad(pairs, ordered):
    dp, context = lax.axis_size("dp"), lax.axis_size("context")
    sequences, length = len(pairs[0][0]), pairs[0][1][0].shape[0]
    widths = [right[0].shape[1] for _, right in pairs]
    lefts = [one for left, _ in pairs for one in left]
    rights = [one for _, right in pairs for one in right]
    model = lefts[0].shape[-1]
    total, cut = sum(widths), model // dp
    rows = cut // context
    order = jnp.stack([lax.axis_index("context"), lax.axis_index("dp")]).astype(jnp.int32)
    if ordered:
        others = (context - 1) * dp
        out_specs = [
            pl.BlockSpec(
                (1, rows, total), lambda i, order: (lax.rem(i - order[1] + dp, dp), 0, 0)
            )
        ] + [fixed_block((rows, total))] * others
        out_shape = [jax.ShapeDtypeStruct((dp, rows, total), BF16)] + [
            jax.ShapeDtypeStruct((rows, total), BF16)
        ] * others
    else:
        out_specs = [pl.BlockSpec((cut, total), lambda i, order: (i, 0))]
        out_shape = [jax.ShapeDtypeStruct((model, total), BF16)]
    left_specs, left_arrays = [], []
    for left in lefts:
        if isinstance(left, tuple):
            left_arrays.append(left[0])
            left_specs.append(
                pl.BlockSpec((1, length, cut), lambda i, order, s=left[1]: (s, 0, i))
            )
        else:
            left_arrays.append(left)
            left_specs.append(pl.BlockSpec((length, cut), lambda i, order: (0, i)))
    return kernel_call(
        functools.partial(
            weight_grad_kernel, len(pairs), sequences, rows, (dp, context) if ordered else None
        ),
        cost=10.0,
        grid_spec=pltpu.PrefetchScalarGridSpec(
            num_scalar_prefetch=1,
            grid=(dp,),
            in_specs=left_specs + [fixed_block(one.shape) for one in rights],
            out_specs=out_specs,
            scratch_shapes=[pltpu.VMEM((cut, total), F32)],
        ),
        out_shape=out_shape,
        compiler_params=params(56),
    )(order, *left_arrays, *rights)


def ring_add_kernel(own_ref, *refs):
    total = own_ref[0].astype(F32)
    for one in refs[:-1]:
        total = total + one[...].astype(F32)
    refs[-1][...] = total.astype(refs[-1].dtype)


def ring_add(own, k, terms, kind):
    _, rows, width = own.shape
    return kernel_call(
        ring_add_kernel,
        cost=1.5,
        grid=(1,),
        in_specs=[pl.BlockSpec((1, rows, width), lambda i: (k, 0, 0))]
        + [fixed_block((rows, width))] * len(terms),
        out_specs=fixed_block((rows, width)),
        out_shape=jax.ShapeDtypeStruct((rows, width), kind),
        compiler_params=params(),
    )(own, *terms)


def ring_steps(blocks, whole_first=False):
    dp, context = lax.axis_size("dp"), lax.axis_size("context")
    own, others = blocks[0], blocks[1:]
    places = list(range(1, dp)) + [0]
    sides = []
    for k in places:
        side = None
        for j in range(1, context):
            part = others[(j - 1) * dp + k]
            if side is not None:
                part = (side.astype(F32) + part.astype(F32)).astype(BF16)
            side = ring(part, "context")
        sides.append([] if side is None else [side])
    if whole_first:
        precede(*sides[-1])
    passed = []
    for k, side in zip(places, sides):
        value = ring_add(own, k, side + passed, BF16 if k else F32)
        if k:
            passed = [ring(value, "dp")]
            yield None
        else:
            yield value


def scan_forward_kernel(
    heads, width, p_ref, rim_ref, marks_ref, cw_ref, hp_ref, skip_ref, exp_ref,
    z_ref, y_ref, st_ref, end_ref, gr_ref, vbuf, state, offset,
):
    chunk = pl.program_id(0)
    aux = column_of(marks_ref[...])

    @pl.when(chunk == 0)
    def _():
        vbuf[0:8] = rim_ref[...].astype(F32)
        state[...] = jnp.zeros_like(state)
        offset[...] = jnp.zeros_like(offset)

    @pl.when(chunk > 0)
    def _():
        vbuf[0:8] = vbuf[CHUNK : CHUNK + 8]

    vbuf[8:, :width] = rounded(p_ref[:, :width])
    vbuf[8:, width:] = rounded(p_ref[:, width + LANES :])
    z = cw_ref[4:5] + cw_ref[3:4] * vbuf[8:]
    for k in range(3):
        z = z + cw_ref[k : k + 1] * vbuf[5 + k : 5 + k + CHUNK] * aux[:, k : k + 1]
    z_ref[...] = z
    act = z * jax.nn.sigmoid(z)
    x = act[:, :width]
    b_val, c_val = act[:, width : width + LANES], act[:, width + LANES :]
    lane = iota(1)
    step = jnp.where(
        lane < heads, softplus(p_ref[:, width : width + LANES] + hp_ref[0:1]), 0.0
    )
    decay = hp_ref[1:2] * step
    cum = lax.dot_general(
        (iota(0) >= iota(1)).astype(F32), decay, NN, precision=HIGH, preferred_element_type=F32
    )
    cum_t = cum.T
    seg_col = aux[:, 5:6]
    link = jnp.where((seg_col == marks_ref[5:6]) & (iota(0) >= iota(1)), 0.0, NO_LINK)
    scores = wide_mm(c_val, b_val, NT)
    growth = jnp.exp(cum) * aux[:, 3:4]
    last = cum[CHUNK - 1 : CHUNK]
    weight = jnp.exp(last - cum) * (seg_col == seg_col[CHUNK - 1 : CHUNK]).astype(F32)
    wide = split_dot(jnp.concatenate([step, growth, weight], axis=0), exp_ref[...])
    step_e, growth_e, weight_e = wide[:CHUNK], wide[CHUNK : 2 * CHUNK], wide[2 * CHUNK :]
    xd = x * step_e
    lower = lane < LANES // 2
    pieces = []
    for pair in range(heads // 2):
        mats = []
        for head in (2 * pair, 2 * pair + 1):
            spread = cum[:, head : head + 1] - cum_t[head : head + 1, :]
            mats.append(jnp.exp(spread + link) * scores)
        tile = xd[:, pair * LANES : (pair + 1) * LANES]
        pieces.append(wide_mm(jnp.concatenate(mats, axis=1), head_halves(tile, lower)))
    held = state[...]
    st_ref[0] = held
    carried = wide_mm(c_val, held) * growth_e
    y_ref[...] = jnp.concatenate(pieces, axis=1) + carried + skip_ref[...] * x
    new = held * growth_e[CHUNK - 1 : CHUNK] + wide_mm(b_val, xd * weight_e, TN)
    state[...] = new
    end_ref[...] = new
    gr_ref[...] = jnp.exp(offset[...] + cum) * aux[:, 4:5]
    offset[...] = offset[...] + last


def row_spec(width, at=None, rows=CHUNK):
    if at is None:
        return pl.BlockSpec((rows, width), lambda i: (i, 0))
    return pl.BlockSpec((rows, width), lambda i: (i, at))


def whole(shape):
    return pl.BlockSpec(shape, lambda i: (0,) * len(shape))


def scan_forward(proj, rim, marks, consts):
    length, total = proj.shape
    heads, width = consts["heads"], consts["width"]
    chunks, conv = length // CHUNK, total - LANES
    return kernel_call(
        functools.partial(scan_forward_kernel, heads, width),
        cost=9.5,
        grid=(chunks,),
        in_specs=[
            row_spec(total),
            whole((8, conv)),
            pl.BlockSpec((8, CHUNK), lambda i: (0, i)),
            whole((8, conv)),
            whole((8, LANES)),
            whole((1, width)),
            whole((LANES, width)),
        ],
        out_specs=[
            row_spec(conv),
            row_spec(width),
            pl.BlockSpec((1, LANES, width), lambda i: (i, 0, 0)),
            whole((LANES, width)),
            row_spec(LANES),
        ],
        out_shape=[
            jax.ShapeDtypeStruct((length, conv), F32),
            jax.ShapeDtypeStruct((length, width), F32),
            jax.ShapeDtypeStruct((chunks, LANES, width), F32),
            jax.ShapeDtypeStruct((LANES, width), F32),
            jax.ShapeDtypeStruct((length, LANES), F32),
        ],
        scratch_shapes=[
            pltpu.VMEM((CHUNK + 8, conv), F32),
            pltpu.VMEM((LANES, width), F32),
            pltpu.VMEM((1, LANES), F32),
        ],
        compiler_params=params(),
    )(proj, rim, marks, consts["cw"], consts["hp"], consts["skip"], consts["exp"])


def mix_forward_kernel(y0_ref, zc_ref, gr_ref, sin_ref, gate_ref, exp_ref, y_ref, sq_ref):
    c_val = zc_ref[...] * jax.nn.sigmoid(zc_ref[...])
    carried = wide_mm(c_val, sin_ref[...].astype(F32))
    y = y0_ref[...] + carried * split_dot(gr_ref[...], exp_ref[...])
    y_ref[...] = y
    gate = gate_ref[...]
    gated = y * (gate * jax.nn.sigmoid(gate))
    square = jnp.sum(gated * gated, axis=1, keepdims=True)
    sq_ref[...] = jnp.broadcast_to(square, (CHUNK, CHUNK)).T[:8]


def mix_forward(y0, z, growth, carried, gate, consts):
    length, width = y0.shape
    last = z.shape[1] // LANES - 1
    return kernel_call(
        mix_forward_kernel,
        cost=3.6,
        grid=(length // CHUNK,),
        in_specs=[
            row_spec(width),
            row_spec(LANES, last),
            row_spec(LANES),
            whole((LANES, width)),
            row_spec(width),
            whole((LANES, width)),
        ],
        out_specs=[row_spec(width), pl.BlockSpec((8, CHUNK), lambda i: (0, i))],
        out_shape=[
            jax.ShapeDtypeStruct((length, width), F32),
            jax.ShapeDtypeStruct((8, length), F32),
        ],
        compiler_params=params(),
    )(y0, z, growth, carried, gate, consts["exp"])


def project_out_kernel(channels, parts, order_ref, y_ref, gate_ref, gain_ref, w_ref, *refs):
    squares, (sent_ref, kept_ref, rows) = refs[:-3], refs[-3:]
    half = parts // 2

    @pl.when(pl.program_id(0) == 0)
    def _():
        for m in range(parts):
            source = pl.ds(pl.multiple_of(order_ref[m] * CHUNK, CHUNK), CHUNK)
            square = sum(one[:, source] for one in squares)
            scale = lax.rsqrt(column_of(square)[:, 1:2] / channels + eps)
            gate = gate_ref[source]
            gated = y_ref[source] * (gate * jax.nn.sigmoid(gate))
            rows[m * CHUNK : (m + 1) * CHUNK] = (gated * scale * gain_ref[...]).astype(BF16)

    total = mm(rows[...], w_ref[...], NT).astype(sent_ref.dtype)
    for m in range(half):
        sent_ref[m] = total[m * CHUNK : (m + 1) * CHUNK]
        kept_ref[m] = total[(half + m) * CHUNK : (half + m + 1) * CHUNK]


def project_out(y, gate, squares, channels, kind, order, consts):
    length, width = y.shape
    weights, at = consts["out"]
    model, parts = weights.shape[0], length // CHUNK
    cut = model // 4
    half = pl.BlockSpec((parts // 2, CHUNK, cut), lambda i, order: (0, 0, i))
    return kernel_call(
        functools.partial(project_out_kernel, float(channels), parts),
        cost=5.7,
        grid_spec=pltpu.PrefetchScalarGridSpec(
            num_scalar_prefetch=1,
            grid=(4,),
            in_specs=[
                fixed_block((length, width)),
                fixed_block((length, width)),
                fixed_block((1, width)),
                pl.BlockSpec((cut, width), lambda i, order: (i, at)),
            ]
            + [fixed_block((8, length))] * len(squares),
            out_specs=[half, half],
            scratch_shapes=[pltpu.VMEM((length, width), BF16)],
        ),
        out_shape=[jax.ShapeDtypeStruct((parts // 2, CHUNK, model), kind)] * 2,
        compiler_params=params(),
    )(order, y, gate, consts["gain"], weights, *squares)


def grad_scaled_kernel(count, order_ref, *refs):
    pieces, rest = refs[:count], refs[count:]
    w_ref, y_ref, gate_ref, gain_ref, gs_ref, dot_ref = rest[:6]
    sums = rest[-1]
    step = pl.program_id(0)
    length = gs_ref.shape[0]
    if count > 1:

        @pl.when(step == 0)
        def _():
            for m in range(count):
                place = pl.ds(pl.multiple_of(order_ref[m] * CHUNK, CHUNK), CHUNK)
                rest[6][place] = pieces[m][...]

        rows = rest[6][...]
    else:
        rows = pieces[0][0]
    grad = mm(rows, w_ref[...])
    gs_ref[...] = grad
    gate = gate_ref[...]
    gated = y_ref[...] * (gate * jax.nn.sigmoid(gate))
    product = jnp.sum(grad * gain_ref[...] * gated, axis=1, keepdims=True)
    square = jnp.sum(gated * gated, axis=1, keepdims=True)
    lane = lax.broadcasted_iota(jnp.int32, (length, LANES), 1)
    part = jnp.where(lane == 0, product, square)

    @pl.when(step == 0)
    def _():
        sums[...] = part

    @pl.when(step > 0)
    def _():
        sums[...] += part

    @pl.when(step == pl.num_programs(0) - 1)
    def _():
        for m in range(length // CHUNK):
            at = slice(m * CHUNK, (m + 1) * CHUNK)
            dot_ref[:, at] = sums[at].T[:8]


def grad_scaled(source, y, gate, order, consts):
    length, width = y.shape
    weights, at = consts["out"]
    model, half = weights.shape[0], width // 2
    part = pl.BlockSpec((length, half), lambda i, order: (0, i))
    out_specs = [part, fixed_block((8, length))]
    out_shape = [
        jax.ShapeDtypeStruct((length, width), F32),
        jax.ShapeDtypeStruct((8, length), F32),
    ]
    if len(source) == 2:
        stream, sequence = source
        inputs, count = [stream], 1
        specs = [pl.BlockSpec((1, length, model), lambda i, order: (sequence, 0, 0))]
    else:
        inputs, count = [one for one, _ in source], len(source)
        specs = piece_specs(source, CHUNK)
        out_specs.append(fixed_block((length, model)))
        out_shape.append(jax.ShapeDtypeStruct((length, model), BF16))
    out = kernel_call(
        functools.partial(grad_scaled_kernel, count),
        cost=4.5,
        grid_spec=pltpu.PrefetchScalarGridSpec(
            num_scalar_prefetch=1,
            grid=(2,),
            in_specs=specs
            + [
                pl.BlockSpec((model, half), lambda i, order: (0, 2 * at + i)),
                part,
                part,
                pl.BlockSpec((1, half), lambda i, order: (0, i)),
            ],
            out_specs=out_specs,
            scratch_shapes=[pltpu.VMEM((length, LANES), F32)],
        ),
        out_shape=out_shape,
        compiler_params=params(),
    )(order, *inputs, weights, y, gate, consts["gain"])
    return out if count > 1 else (*out, source)


def mix_backward_kernel(
    channels, shares, gs_ref, y_ref, gate_ref, zx_ref, zc_ref, gr_ref, gain_ref, exp_ref, *refs
):
    shared, refs = refs[:shares], refs[shares:]
    scaled_ref, dgate_ref, dy_ref, acc_ref, dsin_ref, dsin = refs
    at = pl.program_id(0)

    @pl.when(at == 0)
    def _():
        acc_ref[...] = jnp.zeros_like(acc_ref)
        dsin[...] = jnp.zeros_like(dsin)

    stats = column_of(sum(one[...] for one in shared))
    scale = lax.rsqrt(stats[:, 1:2] / channels + eps)
    pull = scale * scale * scale * stats[:, 0:1] / channels
    grad, y, gate = gs_ref[...], y_ref[...], gate_ref[...]
    silu, sig = silu_parts(gate)
    gated = y * silu
    unit = gated * scale
    scaled_ref[...] = (unit * gain_ref[...]).astype(BF16)
    dgated = grad * gain_ref[...] * scale - gated * pull
    dy = dgated * silu
    dy_ref[...] = dy
    dgate_ref[...] = (dgated * y * (sig * (1.0 + gate * (1.0 - sig)))).astype(BF16)
    x = zx_ref[...] * jax.nn.sigmoid(zx_ref[...])
    acc_ref[0:1] += jnp.sum(grad * unit, axis=0, keepdims=True)
    acc_ref[1:2] += jnp.sum(dy * x, axis=0, keepdims=True)
    c_low = (zc_ref[...] * jax.nn.sigmoid(zc_ref[...])).astype(BF16)
    dsin[...] += mm(c_low, (dy * split_dot(gr_ref[...], exp_ref[...])).astype(BF16), TN)

    @pl.when(at == pl.num_programs(0) - 1)
    def _():
        dsin_ref[...] = dsin[...].astype(BF16)


def mix_backward(grad, y, gate, z, growth, stats, channels, consts):
    length, width = y.shape
    last = z.shape[1] // LANES - 1
    stat = pl.BlockSpec((8, CHUNK), lambda i: (0, i))
    return kernel_call(
        functools.partial(mix_backward_kernel, float(channels), len(stats)),
        cost=5.0,
        grid=(length // CHUNK,),
        in_specs=[
            row_spec(width),
            row_spec(width),
            row_spec(width),
            row_spec(width),
            row_spec(LANES, last),
            row_spec(LANES),
            whole((1, width)),
            whole((LANES, width)),
        ]
        + [stat] * len(stats),
        out_specs=[
            row_spec(width),
            row_spec(width),
            row_spec(width),
            whole((8, width)),
            whole((LANES, width)),
        ],
        out_shape=[
            jax.ShapeDtypeStruct((length, width), BF16),
            jax.ShapeDtypeStruct((length, width), BF16),
            jax.ShapeDtypeStruct((length, width), F32),
            jax.ShapeDtypeStruct((8, width), F32),
            jax.ShapeDtypeStruct((LANES, width), BF16),
        ],
        scratch_shapes=[pltpu.VMEM((LANES, width), F32)],
        compiler_params=params(),
    )(grad, y, gate, z, z, growth, consts["gain"], consts["exp"], *stats)


def scan_backward_kernel(
    heads, width, chunks, dy_ref, z_ref, p_ref, before_ref, rim_ref, marks_ref, cw_ref,
    hp_ref, skip_ref, exp_ref, red_ref, st_ref, sin_ref, grprev_ref, dend_ref,
    dproj_ref, wacc_ref, hacc_ref, tail_ref, drim_ref, vbuf, zbuf, dstate,
):
    step_at = pl.program_id(0)
    chunk = chunks - 1 - step_at
    aux = column_of(marks_ref[...])

    @pl.when(step_at == 0)
    def _():
        dstate[...] = dend_ref[...].astype(F32)
        zbuf[...] = jnp.zeros_like(zbuf)
        wacc_ref[...] = jnp.zeros_like(wacc_ref)
        hacc_ref[...] = jnp.zeros_like(hacc_ref)

    @pl.when(chunk == 0)
    def _():
        vbuf[0:8] = rim_ref[...].astype(F32)

    @pl.when(chunk > 0)
    def _():
        vbuf[0:8, :width] = rounded(before_ref[:, :width])
        vbuf[0:8, width:] = rounded(before_ref[:, width + LANES :])

    vbuf[8:, :width] = rounded(p_ref[:, :width])
    vbuf[8:, width:] = rounded(p_ref[:, width + LANES :])

    z = z_ref[...]
    act, sig = silu_parts(z)
    slope = sig * (1.0 + z * (1.0 - sig))
    x = act[:, :width]
    b_val, c_val = act[:, width : width + LANES], act[:, width + LANES :]
    lane = iota(1)
    pre = p_ref[:, width : width + LANES] + hp_ref[0:1]
    step = jnp.where(lane < heads, softplus(pre), 0.0)
    decay = hp_ref[1:2] * step
    cum = lax.dot_general(
        (iota(0) >= iota(1)).astype(F32), decay, NN, precision=HIGH, preferred_element_type=F32
    )
    cum_t = cum.T
    seg_col = aux[:, 5:6]
    link = jnp.where((seg_col == marks_ref[5:6]) & (iota(0) <= iota(1)), 0.0, NO_LINK)
    growth = jnp.exp(cum) * aux[:, 3:4]
    last = cum[CHUNK - 1 : CHUNK]
    weight = jnp.exp(last - cum) * (seg_col == seg_col[CHUNK - 1 : CHUNK]).astype(F32)
    reach = jnp.where(chunk == 0, 1.0, grprev_ref[7:8])
    wide = split_dot(
        jnp.concatenate([step, growth, weight, jnp.broadcast_to(reach, (8, LANES))], axis=0),
        exp_ref[...],
    )
    step_e, growth_e = wide[:CHUNK], wide[CHUNK : 2 * CHUNK]
    weight_e, reach_e = wide[2 * CHUNK : 3 * CHUNK], wide[3 * CHUNK : 3 * CHUNK + 1]
    held = st_ref[0] + sin_ref[...].astype(F32) * reach_e
    after = dstate[...]
    xd = x * step_e
    dy = dy_ref[...]
    scores = wide_mm(b_val, c_val, NT)
    carried = low_mm(c_val, held) * growth_e
    fed = low_mm(b_val, after) * weight_e
    dy_grown = dy * growth_e
    lower = lane < LANES // 2
    dscores = jnp.zeros((CHUNK, CHUNK), F32)
    into = jnp.zeros((CHUNK, CHUNK), F32)
    rows, pieces = [], []
    for pair in range(heads // 2):
        at = slice(pair * LANES, (pair + 1) * LANES)
        products = wide_mm(head_halves(xd[:, at], lower), dy[:, at], NT)
        mats = []
        for side, head in enumerate((2 * pair, 2 * pair + 1)):
            spread = cum_t[head : head + 1, :] - cum[:, head : head + 1]
            reachable = jnp.exp(spread + link)
            product = products[side * CHUNK : (side + 1) * CHUNK]
            mat = reachable * scores
            dscores = dscores + reachable * product
            energy = mat * product
            rows.append(jnp.sum(energy, axis=0, keepdims=True))
            into = jnp.where(lane == head, jnp.sum(energy, axis=1, keepdims=True), into)
            mats.append(mat)
        pieces.append(low_mm(jnp.concatenate(mats, axis=1), head_halves(dy[:, at], lower)))
    dxd = jnp.concatenate(pieces, axis=1) + fed
    kept = jnp.sum(after * held, axis=0, keepdims=True) * growth_e[CHUNK - 1 : CHUNK]
    sums = split_dot(
        jnp.concatenate(
            [dy * carried, xd * fed, dxd * x, jnp.broadcast_to(kept, (8, width))], axis=0
        ),
        red_ref[...],
    )
    out_of, fed_sum = sums[:CHUNK], sums[CHUNK : 2 * CHUNK]
    dstep, kept_sum = sums[2 * CHUNK : 3 * CHUNK], sums[3 * CHUNK : 3 * CHUNK + 1]
    rows = column_of(jnp.concatenate(rows, axis=0))
    dcum = rows - into + out_of - fed_sum
    end_term = kept_sum + jnp.sum(fed_sum, axis=0, keepdims=True)
    ddecay = (
        lax.dot_general(
            (iota(0) <= iota(1)).astype(F32), dcum, NN, precision=HIGH, preferred_element_type=F32
        )
        + end_term
    )
    ddecay = jnp.where(lane < heads, ddecay, 0.0)
    dpre = jnp.where(lane < heads, (dstep + hp_ref[1:2] * ddecay) * jax.nn.sigmoid(pre), 0.0)
    hacc_ref[0:1] += jnp.sum(dpre, axis=0, keepdims=True)
    hacc_ref[1:2] += jnp.sum(ddecay * decay, axis=0, keepdims=True)
    dx = dxd * step_e + skip_ref[...] * dy
    db = wide_mm(dscores, c_val) + wide_mm(xd * weight_e, after, NT)
    dc = wide_mm(dscores, b_val, TN) + wide_mm(dy_grown, held, NT)
    dstate[...] = after * growth_e[CHUNK - 1 : CHUNK] + wide_mm(c_val, dy_grown, TN)

    dz = jnp.concatenate([dx, db, dc], axis=1) * slope
    wacc_ref[3:4] += jnp.sum(dz * vbuf[8:], axis=0, keepdims=True)
    wacc_ref[4:5] += jnp.sum(dz, axis=0, keepdims=True)
    dv = cw_ref[3:4] * dz
    for k in range(3):
        masked = dz * aux[:, k : k + 1]
        wacc_ref[k : k + 1] += jnp.sum(
            masked * vbuf[5 + k : 5 + k + CHUNK], axis=0, keepdims=True
        )
        zbuf[k, 8 : 8 + CHUNK] = masked
        dv = dv + cw_ref[k : k + 1] * zbuf[k, 11 - k : 11 - k + CHUNK]
    dproj_ref[:, :width] = dv[:, :width].astype(BF16)
    dproj_ref[:, width : width + LANES] = dpre.astype(BF16)
    dproj_ref[:, width + LANES :] = dv[:, width:].astype(BF16)

    @pl.when(step_at == 0)
    def _():
        tail_ref[...] = dv[CHUNK - 16 :]

    @pl.when(chunk == 0)
    def _():
        drim = cw_ref[0:1] * zbuf[0, 3:11]
        for k in (1, 2):
            drim = drim + cw_ref[k : k + 1] * zbuf[k, 3 - k : 11 - k]
        drim_ref[0:8] = jnp.zeros_like(drim)
        drim_ref[8:] = drim

    for k in range(3):
        zbuf[k, 8 + CHUNK :] = zbuf[k, 8:16]


def scan_backward(dy, z, proj, rim, marks, states, carried, growth, dend, consts):
    length, total = proj.shape
    heads, width = consts["heads"], consts["width"]
    chunks, conv = length // CHUNK, total - LANES
    eights = CHUNK // 8

    def back(columns):
        return pl.BlockSpec((CHUNK, columns), lambda i: (chunks - 1 - i, 0))

    def previous(columns):
        return pl.BlockSpec(
            (8, columns), lambda i: (jnp.maximum((chunks - 1 - i) * eights - 1, 0), 0)
        )

    return kernel_call(
        functools.partial(scan_backward_kernel, heads, width, chunks),
        cost=18.0,
        grid=(chunks,),
        in_specs=[
            back(width),
            back(conv),
            back(total),
            previous(total),
            whole((8, conv)),
            pl.BlockSpec((8, CHUNK), lambda i: (0, chunks - 1 - i)),
            whole((8, conv)),
            whole((8, LANES)),
            whole((1, width)),
            whole((LANES, width)),
            whole((width, LANES)),
            pl.BlockSpec((1, LANES, width), lambda i: (chunks - 1 - i, 0, 0)),
            whole((LANES, width)),
            previous(LANES),
            whole((LANES, width)),
        ],
        out_specs=[
            back(total),
            whole((8, conv)),
            whole((8, LANES)),
            whole((16, conv)),
            whole((16, conv)),
        ],
        out_shape=[
            jax.ShapeDtypeStruct((length, total), BF16),
            jax.ShapeDtypeStruct((8, conv), F32),
            jax.ShapeDtypeStruct((8, LANES), F32),
            jax.ShapeDtypeStruct((16, conv), F32),
            jax.ShapeDtypeStruct((16, conv), F32),
        ],
        scratch_shapes=[
            pltpu.VMEM((CHUNK + 8, conv), F32),
            pltpu.VMEM((3, CHUNK + 16, conv), F32),
            pltpu.VMEM((LANES, width), F32),
        ],
        compiler_params=params(),
    )(
        dy, z, proj, proj, rim, marks, consts["cw"], consts["hp"], consts["skip"],
        consts["exp"], consts["red"], states, carried, growth, dend,
    )


def local(
    stream,
    seg_ids,
    input_weight,
    step_size_weight,
    coefficient_weight,
    pre_gain,
    conv_bc,
    bias_bc,
    output_weight,
    conv_x,
    bias_x,
    dt_bias,
    a_log,
    skip,
    gate_gain,
    cotangent,
):
    PRECEDING.clear()
    layers, rows_in, _, width = input_weight.shape
    sequences, length, model = stream.shape
    heads = dt_bias.shape[1]
    depth = width // heads
    shared = coefficient_weight.shape[2]
    dp, context, tensor = (lax.axis_size(a) for a in ("dp", "context", "tensor"))
    channels = width * tensor
    rows_bc = rows_in // tensor
    conv, total = width + shared, width + LANES + shared
    layer_range, seq_range = range(layers), range(sequences)

    own_gain, own_conv = pre_gain.shape[1], conv_bc.shape[2]
    small = jnp.concatenate([pre_gain, conv_bc.reshape(layers, -1), bias_bc], axis=1)
    small = jnp.pad(small, ((0, 0), (0, shared - small.shape[1])))[:, None]
    bc_rows = gather_small(jnp.concatenate([coefficient_weight, small], axis=1), ("tensor",))
    small, bc_rows = bc_rows[:, :, rows_bc], bc_rows[:, :, :rows_bc]
    taps = small[:, :, own_gain : own_gain + 5 * own_conv].reshape(tensor, layers, 5, own_conv)
    taps = jnp.moveaxis(taps, 0, 2).reshape(layers, -1)
    small = jnp.concatenate(
        [
            jnp.moveaxis(small[:, :, :own_gain], 0, 1).reshape(layers, rows_in),
            jnp.pad(taps, ((0, 0), (0, rows_in - taps.shape[1]))),
        ],
        axis=0,
    ).T

    def first_piece(layer):
        tile = jnp.concatenate(
            [
                step_size_weight[layer],
                small,
                jnp.zeros((rows_in, LANES - heads - 2 * layers), BF16),
                bc_rows[:, layer].reshape(rows_in, shared),
            ],
            axis=1,
        )
        return [input_weight[layer, :, 1], tile]

    def second_piece(layer):
        return [input_weight[layer, :, 0], output_weight[layer].T]

    edge_ids = shifted(seg_ids[:, -3:], "context", 1)
    ext_ids = jnp.concatenate([edge_ids, seg_ids], axis=1)
    prior = ext_ids[:, 2 : 2 + length].reshape(sequences, length // CHUNK, CHUNK)[:, :, 0]
    prior = jnp.repeat(prior, CHUNK, axis=1)
    aux_all = jnp.stack(
        [ext_ids[:, k : k + length] == seg_ids for k in range(3)]
        + [seg_ids == prior, seg_ids == edge_ids[:, 2:3], seg_ids, seg_ids, seg_ids],
        axis=1,
    ).astype(F32)

    spread_table = (jnp.arange(LANES)[:, None] == jnp.arange(width)[None, :] // depth).astype(BF16)

    def joined(*parts):
        return jnp.concatenate([one for part in parts for one in part], axis=1)

    third = total // 3
    upper_piece = joined(second_piece(1), first_piece(1))
    table, second_table = [], []
    halo = shifted(stream[:, length - 16 :], "context", 1)
    precede(halo, edge_ids)
    for _ in ring_pieces(table, joined(first_piece(0))):
        pass
    second_ring = ring_pieces(second_table, relayed(joined(second_piece(0))))
    next(second_ring)
    places = jnp.arange(length // CHUNK, dtype=jnp.int32)
    arrived, sending = rows_order(False), rows_order(True)
    own_place = lax.axis_index("tensor").astype(jnp.int32)[None]
    precede(aux_all, spread_table, spread_table.T, arrived, sending)
    first, tile_rows = placed(table, [total], width)

    def every_row(part):
        return lax.all_gather(part, ("dp", "context"), axis=0, tiled=True)

    weights = [
        {"front": (first, 0)},
        {},
    ]
    streams = [(stream, s) for s in seq_range]
    grads = [(cotangent, s) for s in seq_range]
    small = tile_rows[heads : heads + 2 * layers]
    gains = small[:layers]
    taps = small[layers:].reshape(layers, dp * context, rows_in)[:, :, : 5 * tensor * own_conv]
    taps = taps.reshape(layers, dp * context, 5, tensor * own_conv)
    taps = jnp.moveaxis(taps, 1, 2).reshape(layers, 5, shared)

    consts = []
    for layer in layer_range:
        cw = jnp.concatenate(
            [
                jnp.concatenate(
                    [jnp.concatenate([conv_x[layer], bias_x[layer][None]], axis=0), taps[layer]],
                    axis=1,
                ),
                jnp.zeros((3, conv), F32),
            ],
            axis=0,
        )
        pad = jnp.zeros((LANES - heads,), F32)
        hp = jnp.stack(
            [
                jnp.concatenate([dt_bias[layer], pad]),
                jnp.concatenate([-jnp.exp(a_log[layer]), pad]),
            ]
            + [jnp.zeros((LANES,), F32)] * 6
        )
        consts.append(
            {
                "heads": heads,
                "width": width,
                "cw": cw,
                "hp": hp,
                "skip": jnp.repeat(skip[layer], depth)[None],
                "gain": gate_gain[layer][None],
                "exp": spread_table,
                "red": spread_table.T,
                **weights[layer],
            }
        )

    def chain(value, total, steps):
        carried = shifted(value, "context", steps)
        for _ in range(context - 2):
            passed = value.astype(F32) + carried.astype(F32) * total
            carried = shifted(passed.astype(value.dtype), "context", steps)
        return carried

    def through(growth):
        return jnp.repeat(growth[length - 1, :heads], depth)[None]

    for const in consts:
        precede(const["cw"], const["hp"], const["skip"], const["gain"])
    precede(gains)
    incoming = [(stream, halo, s) for s in seq_range]
    work = [[{} for _ in seq_range] for _ in layer_range]
    outputs = []
    top = layers - 1
    def step_project(layer, s):
        k = work[layer][s]
        k["stream"] = streams[s]
        k["normed"], k["proj"], tail = project(
            incoming[s],
            None if layer else gains[0:1],
            arrived if layer else places,
            consts[layer]["front"],
            width,
            total,
        )
        k["rim"] = shifted(tail, "context", 1) if layer else tail

    def step_scan(layer, s):
        k = work[layer][s]
        k["z"], k["y0"], k["states"], end, k["growth"] = scan_forward(
            k["proj"], k["rim"], aux_all[s], consts[layer]
        )
        k["carried"] = chain(end, through(k["growth"]), 1)

    def step_gate(layer, s):
        k = work[layer][s]
        k["gate"] = plain_product(k["normed"], consts[layer]["gate"], width)

    def step_mix(layer, s):
        k = work[layer][s]
        k["y"], squares = mix_forward(
            k["y0"], k["z"], k["growth"], k["carried"], k["gate"], consts[layer]
        )
        if layer < top:
            k["squares"] = from_others(squares, "tensor")

    def step_out(layer, s):
        k = work[layer][s]
        kind = BF16 if layer == top else F32
        sent, own = project_out(
            k["y"], k["gate"], k["squares" if layer < top else "stats"], channels, kind, sending,
            consts[layer],
        )
        k["out"] = [own, flipped(sent, "tensor", 0)]

    def step_pass(layer, s, name):
        terms = work[layer][s][name]
        terms.append(flipped(pass_on(*terms), "tensor", 1))

    def step_norm(layer, s):
        k = work[layer][s]
        gain = None if layer == top else gains[layer + 1 : layer + 2]
        *new, low = norm_forward(streams[s], k["out"], gain, own_place)
        streams[s] = new[0] if new else None
        k["rows"] = [low, flipped(low, "tensor", 1)]

    def step_join(layer, s, name):
        own, other = work[layer][s][name]
        across = flipped(joined_rows(own, other), "tensor", 0)
        return [(own, 0), (other, 0), (across, 0), (across, 1)]

    def step_grad(layer, s):
        k = work[layer][s]
        source = (cotangent, s) if layer == top else incoming[s]
        k["grad"], dots, k["low"] = grad_scaled(
            source, k["y"], k["gate"], places if layer == top else arrived, consts[layer]
        )
        k["stats"] = from_others(dots, "tensor")

    def step_mix_back(layer, s):
        k = work[layer][s]
        k["scaled"], k["dgate"], k["dy"], k["acc"], dsin = mix_backward(
            k["grad"], k["y"], k["gate"], k["z"], k["growth"], k["stats"], channels, consts[layer],
        )
        k["dend"] = chain(dsin, through(k["growth"]), -1)

    def step_scan_back(layer, s):
        k = work[layer][s]
        k["dproj"], k["wacc"], k["hacc"], k["tail"], drim = scan_backward(
            k["dy"], k["z"], k["proj"], k["rim"], aux_all[s], k["states"],
            k["carried"], k["growth"], k["dend"], consts[layer],
        )
        k["drim"] = shifted(drim, "context", -1)

    def step_input_grad(layer, s):
        k = work[layer][s]
        sent, own, k["dproj"] = input_grad(
            k["dproj"], k["dgate"], k["tail"], k["drim"], consts[layer]["front"],
            consts[layer]["gate"], sending,
        )
        k["back"] = [own, flipped(sent, "tensor", 0)]

    def step_norm_back(layer, s):
        k = work[layer][s]
        grads[s], low, k["dgain"] = norm_backward(
            k["stream"], k["back"], grads[s], gains[layer : layer + 1], own_place
        )
        k["grad_low"] = [low, flipped(low, "tensor", 1)]

    def every(layer, name):
        return [k[name] for k in work[layer]]

    def step_second_grad(layer):
        return weight_grad(
            [
                (every(layer, "normed"), every(layer, "dgate")),
                (every(layer, "low"), every(layer, "scaled")),
            ],
            layer == 0,
        )

    def step_first_grad(layer):
        return weight_grad([(every(layer, "normed"), every(layer, "dproj"))], layer == 0)

    def scattered(value):
        return lax.psum_scatter(value, ("dp", "context"), scatter_dimension=0, tiled=True)

    second_sums, first_sums = [None] * layers, [None] * layers
    project_0, scan_0, gate_0, mix_0, out_0, grad_0, mixed_0, scanned_0, input_0 = (
        functools.partial(step, 0)
        for step in (
            step_project, step_scan, step_gate, step_mix, step_out, step_grad, step_mix_back,
            step_scan_back, step_input_grad,
        )
    )
    project_1, scan_1, gate_1, mix_1, out_1, grad_1, mixed_1, scanned_1, input_1 = (
        functools.partial(step, 1)
        for step in (
            step_project, step_scan, step_gate, step_mix, step_out, step_grad, step_mix_back,
            step_scan_back, step_input_grad,
        )
    )

    project_0(0)
    next(second_ring)
    scan_0(0)
    next(second_ring)
    upper = every_row(relayed(upper_piece))
    consts[1].update(front=(upper, 2 * width // third), gate=(upper, 0), out=(upper, 1))
    project_0(1)
    next(second_ring, None)
    scan_0(1)
    precede(work[0][0]["carried"])
    (second,) = placed(second_table, [2 * width])
    consts[0].update(gate=(second, 0), out=(second, 1))
    gate_0(0)
    mix_0(0)
    gate_0(1)
    mix_0(1)
    out_0(0)
    step_pass(0, 0, "out")
    out_0(1)
    step_norm(0, 0)
    step_pass(0, 1, "out")
    incoming[0] = step_join(0, 0, "rows")
    project_1(0)
    step_norm(0, 1)
    scan_1(0)
    incoming[1] = step_join(0, 1, "rows")
    project_1(1)
    gate_1(0)
    scan_1(1)
    mix_1(0)
    gate_1(1)
    grad_1(0)
    mix_1(1)
    grad_1(1)
    mixed_1(0)
    mixed_1(1)
    precede(work[1][0]["dend"])
    second_sums[1] = scattered(step_second_grad(1)[0])
    scanned_1(0)
    out_1(0)
    precede(work[1][1]["dend"])
    input_1(0)
    step_pass(1, 0, "back")
    scanned_1(1)
    step_norm_back(1, 0)
    out_1(1)
    input_1(1)
    incoming[0] = step_join(1, 0, "grad_low")
    step_pass(1, 1, "back")
    grad_0(0)
    step_pass(1, 0, "out")
    step_pass(1, 1, "out")
    precede(*work[0][0]["stats"])
    first_grad = step_first_grad(1)
    mixed_0(0)
    step_norm_back(1, 1)
    precede(second_sums[1])
    first_sums[1] = scattered(first_grad[0])
    scanned_0(0)
    for s in seq_range:
        step_norm(1, s)
    incoming[1] = step_join(1, 1, "grad_low")
    grad_0(1)
    input_0(0)
    mixed_0(1)
    second_steps = ring_steps(step_second_grad(0), True)
    step_pass(0, 0, "back")
    precede(first_sums[1])
    scanned_0(1)
    outputs.extend(step_join(1, s, "rows") for s in seq_range)
    next(second_steps)
    step_norm_back(0, 0)
    input_0(1)
    next(second_steps)
    first_steps = ring_steps(step_first_grad(0))
    step_pass(0, 1, "back")
    next(second_steps)
    incoming[0] = step_join(0, 0, "grad_low")
    next(first_steps)
    second_sums[0] = next(second_steps)
    layer_out = assembled(outputs, arrived)
    step_norm_back(0, 1)
    small_steps = small_sums(work, width, heads, model, consts[0]["red"])
    next(small_steps)
    next(first_steps)
    next(small_steps)
    second_sums[1], first_sums[1] = widened(second_sums[1]), widened(first_sums[1])
    incoming[1] = step_join(0, 1, "grad_low")
    next(small_steps)
    next(first_steps)
    grad_stream = assembled(incoming, arrived)
    first_sums[0] = next(first_steps)
    next(small_steps)
    for value in small_steps:
        small_out = value

    out = []
    for layer in layer_range:
        second_sum, first_sum = second_sums[layer], first_sums[layer]
        out.append(
            (
                jnp.stack([second_sum[:, :width], first_sum[:, :width]], axis=1),
                first_sum[:, width : width + heads],
                scatter_places(first_sum[:, width + LANES :]),
                second_sum[:, width:].T,
            )
        )
    taps_x, sum_bias_x, dt_sum, rate_sum, skip_sum, gate_sum, taps_bc, sum_bias_bc, gain_sum = (
        small_out
    )
    return (
        layer_out,
        grad_stream,
        jnp.stack([o[0] for o in out]),
        jnp.stack([o[1] for o in out]),
        jnp.stack([o[2] for o in out]),
        gain_sum,
        taps_bc,
        sum_bias_bc,
        jnp.stack([o[3] for o in out]),
        taps_x,
        sum_bias_x,
        dt_sum,
        rate_sum,
        skip_sum,
        gate_sum,
    )


def solution(mesh):
    in_specs = (
        P("dp", "context", None),
        P("dp", "context"),
        P(None, ("dp", "context"), None, "tensor"),
        P(None, ("dp", "context"), "tensor"),
        P(None, ("dp", "context", "tensor"), None),
        P(None, ("dp", "context", "tensor")),
        P(None, None, ("dp", "context", "tensor")),
        P(None, ("dp", "context", "tensor")),
        P(None, "tensor", ("dp", "context")),
        P(None, None, "tensor"),
        P(None, "tensor"),
        P(None, "tensor"),
        P(None, "tensor"),
        P(None, "tensor"),
        P(None, "tensor"),
        P("dp", "context", None),
    )
    out_specs = (
        P("dp", "context", None),
        P("dp", "context", None),
        P(None, ("dp", "context"), None, "tensor"),
        P(None, ("dp", "context"), "tensor"),
        P(None, ("dp", "context", "tensor"), None),
        P(None, ("dp", "context", "tensor")),
        P(None, None, ("dp", "context", "tensor")),
        P(None, ("dp", "context", "tensor")),
        P(None, "tensor", ("dp", "context")),
        P(None, None, "tensor"),
        P(None, "tensor"),
        P(None, "tensor"),
        P(None, "tensor"),
        P(None, "tensor"),
        P(None, "tensor"),
        P("dp", "context", None),
    )
    return jax.shard_map(
        local, mesh=mesh, in_specs=in_specs, out_specs=out_specs[:15], check_vma=False
    )
```
